32 devices in a mesh: ctx: 4 (over x, core), fsdp: 8 (over z, y).
Axes of the slice: x: 2, y: 2, z: 4, core: 2. Of those that a mesh axis runs over, the one named last changes fastest.
Arguments:
- hidden_in: bfloat16 [8, 512, 1536], P('fsdp', 'ctx'), may hold values from -6 to 6
- w_query: bfloat16 [2, 1536, 1536], P(None, ('ctx', 'fsdp')), may hold values from -0.15625 to 0.15625
- w_key_value: bfloat16 [2, 1536, 1024], P(None, ('ctx', 'fsdp')), may hold values from -0.15625 to 0.15625
- w_output: bfloat16 [2, 1536, 1536], P(None, ('ctx', 'fsdp')), may hold values from -1.25 to 1.25
- w_router: bfloat16 [2, 1536, 16], P(None, ('ctx', 'fsdp')), may hold values from -0.078125 to 0.078125
- norm_gains: bfloat16 [2, 1536, 2], P(None, ('ctx', 'fsdp')), may hold values from 0.5 to 1.5
- w_gate_up: bfloat16 [2, 16, 1536, 1024], P(None, 'fsdp', 'ctx'), may hold values from -0.15625 to 0.15625
- w_down: bfloat16 [2, 16, 512, 1536], P(None, 'fsdp', 'ctx'), may hold values from -1 to 1
- expert_ids: int32 [2, 8, 512, 8], P(None, 'fsdp', 'ctx'), may hold values from 0 to 15, all different within a row; in each aligned block of 128 rows (0 to 127, 128 to 255, ..., all dimensions but the last counted through in order) at most 96 rows name the same one
- out_grad: bfloat16 [8, 512, 1536], P('fsdp', 'ctx'), may hold values from -6 to 6
Outputs:
- hidden_out: bfloat16 [8, 512, 1536], P('fsdp', 'ctx')
- grad_hidden: float32 [8, 512, 1536], P('fsdp', 'ctx')
- grad_query: float32 [2, 1536, 1536], P(None, ('ctx', 'fsdp'))
- grad_key_value: float32 [2, 1536, 1024], P(None, ('ctx', 'fsdp'))
- grad_output: float32 [2, 1536, 1536], P(None, ('ctx', 'fsdp'))
- grad_router: float32 [2, 1536, 16], P(None, ('ctx', 'fsdp'))
- grad_gains: float32 [2, 1536, 2], P(None, ('ctx', 'fsdp'))
- grad_gate_up: float32 [2, 16, 1536, 1024], P(None, 'fsdp', 'ctx')
- grad_down: float32 [2, 16, 512, 1536], P(None, 'fsdp', 'ctx')
The draws below stay inside these ranges and needn't reach their ends.
Inputs may be any that keep to these rules, and one draw needn't show every extreme that they name: `expert_ids`: 8 different experts for each token and layer; of the 128 rows of one device in a layer, at most 96 choose one expert, and some expert is chosen by exactly 96 of them.
All inputs are finite; a program needn't handle non-finite values.
Results may differ from the reference program's by a relative error of at most 0.033.
Values may be sent and summed in bfloat16 or wider, within the bound.
No kernel may reach another device: no remote copies, remote signals or barrier semaphores. Data moves between devices by JAX's collectives and lax.ppermute only.
A program may use at most 384 MiB of HBM per device.

```python
import math
import jax
import jax.numpy as jnp
import numpy as np
from jax import lax

D = 1536
HEADS = 24
KV_HEADS = 8
HEAD_DIM = 64
FE = 512
TOP = 8
LAYERS = 2
TOK_DEV = 128
EXPERTS = 16
CAP = 96
SEQ = 512
NSEQ = 8
N_CTX = 4


def block_scale(stream_key, shape, split, low, top_value):
    loudness = 1.0
    for dim, parts in split:
        heights = jax.random.uniform(jax.random.fold_in(jax.random.fold_in(stream_key, 6), dim), (parts,), jnp.float32, low / len(split), top_value / len(split))
        loudness = loudness * jnp.repeat(jnp.exp(heights), shape[dim] // parts).reshape((-1,) + (1,) * (len(shape) - 1 - dim))
    return loudness


def routed_block(stream_key, own, number, rows, number_of, top, reach, slope):
    order = jax.random.permutation(stream_key, number_of)
    crowded, ordinary = load_shares(number_of, rows * top, reach, slope, True), load_shares(number_of, rows * top, reach, slope, False)
    places = jnp.arange(number_of)

    def named(tallies, offset_by):
        used = int((tallies > 0).sum())
        fixed = max(1, used // 4)
        moved = fixed + (places - fixed + offset_by * (used - fixed)) % max(1, number_of - fixed)
        return jnp.zeros((number_of,), jnp.int32).at[order[jnp.where(places < fixed, places, moved)]].set(jnp.asarray(tallies, jnp.int32))

    tallies = jnp.where(number % 4 == 0, named(crowded, number // 4), named(ordinary, number - number // 4 - 1))
    mixed = jax.random.permutation(jax.random.fold_in(own, 3), number_of)
    donor, taker = mixed[0:number_of // 2 * 2:2], mixed[1:number_of // 2 * 2:2]
    margin = jnp.minimum(tallies[donor] - 1, reach - tallies[taker]) // 2
    margin = jnp.where((donor == order[0]) | (taker == order[0]) | (tallies[taker] == 0), 0, jnp.maximum(margin, 0))
    moved = jax.random.randint(jax.random.fold_in(own, 4), (number_of // 2,), 0, 1 << 20) % (margin + 1)
    tallies = tallies.at[donor].add(-moved).at[taker].add(moved)
    members = jnp.searchsorted(jnp.cumsum(tallies), jnp.arange(rows * top), side="right").astype(jnp.int32)
    grid = members.reshape(top, rows).T
    grid = grid[jax.random.permutation(jax.random.fold_in(own, 1), rows)]
    offset_by = jax.random.randint(jax.random.fold_in(own, 2), (rows, 1), 0, top)
    return jnp.take_along_axis(grid, (jnp.arange(top)[None, :] + offset_by) % top, axis=1)


def load_shares(number_of, total, most, skew, full):
    weights = [(1 << 20) // math.isqrt(grade ** skew) + 1 for grade in range(1, number_of + 1)]
    largest = most if full else min(most, max(-(-total // number_of), total * weights[0] // sum(weights)))
    least = 1 if total - largest >= number_of - 1 else 0
    given, rest = [largest] + [least] * (number_of - 1), total - largest - least * (number_of - 1)
    while rest > 0:
        movable = [i for i in range(1, number_of) if given[i] < largest] or [i for i in range(1, number_of) if given[i] < most]
        pool, budget = sum([weights[i] for i in movable]), rest
        for i in movable:
            addition = min(most - given[i], max(1, budget * weights[i] // pool), rest)
            given[i] = given[i] + addition
            rest = rest - addition
    return np.array(given)


def gaussian(rng, extent, scale, most, cuts=(), held_as=jnp.bfloat16):
    drawn = jax.random.normal(rng, extent, jnp.float32) * scale
    if len(cuts) > 0:
        drawn = block_scale(rng, extent, cuts, -0.22, 0.18) * drawn
    return jnp.clip(drawn, min=-most, max=most).astype(held_as)


def setup_inputs(seed: int = 0) -> dict:
    streams_of = jax.random.split(jax.random.key(seed), 11)
    hidden_in = gaussian(streams_of[0], (NSEQ, SEQ, D), 1.0, 6.0, ((0, 8), (1, 4)))
    w_query = gaussian(streams_of[1], (LAYERS, D, D), D ** -0.5, 0.15625, ((1, 32),))
    w_key_value = gaussian(streams_of[2], (LAYERS, D, 2 * KV_HEADS * HEAD_DIM), D ** -0.5, 0.15625, ((1, 32),))
    w_output = gaussian(streams_of[3], (LAYERS, D, D), (D // 64) ** -0.5, 1.25, ((1, 32),))
    w_router = gaussian(streams_of[4], (LAYERS, D, EXPERTS), (4 * D) ** -0.5, 0.078125, ((1, 32),))
    norm_gains = jnp.clip(1.0 + 0.1 * jax.random.normal(streams_of[5], (LAYERS, D, 2), jnp.float32), 0.5, 1.5).astype(jnp.bfloat16)
    w_gate_up = gaussian(streams_of[6], (LAYERS, EXPERTS, D, 2 * FE), D ** -0.5, 0.15625, ((1, 8), (2, 4)))
    w_down = gaussian(streams_of[7], (LAYERS, EXPERTS, FE, D), (FE // 16) ** -0.5, 1.0, ((1, 8), (2, 4)))
    expert_ids_keys = jax.random.split(jax.random.fold_in(streams_of[8], 1), LAYERS * NSEQ * SEQ // TOK_DEV)
    expert_ids_turns = jax.random.permutation(jax.random.fold_in(streams_of[8], 3), LAYERS * NSEQ * SEQ // TOK_DEV)
    expert_ids = jax.vmap(lambda own, number: routed_block(jax.random.fold_in(streams_of[8], 2), own, number, TOK_DEV, EXPERTS, TOP, CAP, 1))(expert_ids_keys, expert_ids_turns).reshape((LAYERS, NSEQ, SEQ, TOP))
    out_grad = gaussian(streams_of[9], (NSEQ, SEQ, D), 1.0, 6.0, ((0, 8), (1, 4)))
    return {"hidden_in": hidden_in, "w_query": w_query, "w_key_value": w_key_value, "w_output": w_output, "w_router": w_router, "norm_gains": norm_gains, "w_gate_up": w_gate_up, "w_down": w_down, "expert_ids": expert_ids, "out_grad": out_grad}


@jax.custom_vjp
def low(v):
    return lax.optimization_barrier(v.astype(jnp.bfloat16)).astype(jnp.float32)

@jax.custom_vjp
def low_back(v):
    return v

def low_keep(v):
    return (low(v), None)

def low_pass(kept, grad):
    return (grad,)

def back_keep(v):
    return (v, None)

def back_low(kept, grad):
    return (low(grad),)
low.defvjp(low_keep, low_pass)
low_back.defvjp(back_keep, back_low)
highest = lax.Precision.HIGHEST
epsilon = 1e-06
rope_base = 10000.0

def row_positions(first_row, row_total, row_count, shards):
    indices = first_row + jnp.arange(row_total, dtype=jnp.int32)
    shard_of = indices // row_count
    within = indices % row_count
    half_rows = row_count // 2
    return jnp.where(within < half_rows, shard_of * half_rows + within, (2 * shards - 1 - shard_of) * half_rows + within - half_rows)

def rotate(values_in, places, direction):
    half_dim = values_in.shape[-1] // 2
    frequency = rope_base ** (-jnp.arange(half_dim, dtype=jnp.float32) / half_dim)
    angles = places.astype(jnp.float32)[:, None] * frequency[None, :]
    cosine_part = jnp.cos(angles)[:, None, :]
    sine_part = direction * jnp.sin(angles)[:, None, :]
    front_half = values_in[..., :half_dim]
    back_half = values_in[..., half_dim:]
    return jnp.concatenate([front_half * cosine_part - back_half * sine_part, back_half * cosine_part + front_half * sine_part], -1)

def rms_scaled(residual, gain_vector):
    inverse_root = lax.rsqrt(lax.optimization_barrier(jnp.mean(residual * residual, -1, keepdims=True)) + epsilon)
    return residual * inverse_root * gain_vector

def attend_sequence(queries, key_rows, value_rows, places):
    group_size = HEADS // KV_HEADS
    block_rows = math.gcd(SEQ, 512)
    block_count = SEQ // block_rows
    grouped = queries.reshape(block_count, block_rows, KV_HEADS, group_size, HEAD_DIM)
    block_places = places.reshape(block_count, block_rows)

    def one_block(inputs):
        query_block, query_places = inputs
        scores = jnp.einsum('qhgd,khd->hgqk', query_block, key_rows, precision=highest) * HEAD_DIM ** (-0.5)
        scores = low_back(scores)
        visible = query_places[:, None] >= places[None, :]
        scores = jnp.where(visible, scores, -1e+30)
        top_score = lax.optimization_barrier(jnp.max(scores, -1, keepdims=True))
        weights = jnp.exp(scores - top_score)
        probabilities = weights / lax.optimization_barrier(jnp.sum(weights, -1, keepdims=True))
        return jnp.einsum('hgqk,khd->qhgd', low(probabilities), value_rows, precision=highest)
    outputs = lax.map(jax.checkpoint(one_block), (grouped, block_places))
    return outputs.reshape(SEQ, HEADS * HEAD_DIM)

def one_layer(residual, weights, routing, places):
    query_weight, key_value_weight, output_weight, router_weight, gains, gate_up_weight, down_weight = weights
    key_width = KV_HEADS * HEAD_DIM
    normed = low(rms_scaled(residual, gains[:, 0]))
    queries = low_back(jnp.einsum('nsd,de->nse', normed, query_weight, precision=highest))
    key_value = low_back(jnp.einsum('nsd,de->nse', normed, key_value_weight, precision=highest))
    queries = low(rotate(queries.reshape(NSEQ, SEQ, HEADS, HEAD_DIM), places, 1.0))
    key_rows = low(rotate(key_value[..., :key_width].reshape(NSEQ, SEQ, KV_HEADS, HEAD_DIM), places, 1.0))
    value_rows = low(key_value[..., key_width:].reshape(NSEQ, SEQ, KV_HEADS, HEAD_DIM))

    def attend_one(inputs):
        return attend_sequence(inputs[0], inputs[1], inputs[2], places)
    attended = lax.map(jax.checkpoint(attend_one), (queries, key_rows, value_rows))
    attended = low(low_back(attended))
    middle = residual + low_back(jnp.einsum('nsd,de->nse', attended, output_weight, precision=highest))
    normed_second = low(rms_scaled(middle, gains[:, 1]))
    flat_rows = normed_second.reshape(NSEQ * SEQ, D)
    logits = jnp.dot(flat_rows, router_weight, precision=highest)
    chosen_mask = (routing.reshape(NSEQ * SEQ, TOP)[:, :, None] == jnp.arange(EXPERTS, dtype=jnp.int32)[None, None, :]).astype(jnp.float32)
    chosen = jnp.einsum('nke,ne->nk', chosen_mask, logits, precision=highest)
    gate_probs = jax.nn.softmax(chosen, axis=-1)
    gate_table = jnp.einsum('nke,nk->ne', chosen_mask, gate_probs, precision=highest)

    def one_expert(inputs):
        expert_gate_up, expert_down, expert_gates = inputs
        entering = low_back(flat_rows)
        gate_up = low_back(jnp.dot(entering, expert_gate_up, precision=highest))
        hidden = low(jax.nn.silu(gate_up[:, :FE]) * gate_up[:, FE:])
        leaving = low(low_back(jnp.dot(hidden, expert_down, precision=highest)))
        return expert_gates[:, None] * leaving

    def add_expert(running_sum, inputs):
        return (running_sum + jax.checkpoint(one_expert)(inputs), None)
    expert_sum, _ = lax.scan(add_expert, jnp.zeros_like(flat_rows), (gate_up_weight, down_weight, gate_table.T))
    return middle + expert_sum.reshape(NSEQ, SEQ, D)

def reference(hidden_in, w_query, w_key_value, w_output, w_router, norm_gains, w_gate_up, w_down, expert_ids, out_grad):
    places = row_positions(0, SEQ, TOK_DEV, N_CTX)
    weights = tuple((each_weight.astype(jnp.float32) for each_weight in (w_query, w_key_value, w_output, w_router, norm_gains, w_gate_up, w_down)))

    def forward(residual, weight_set):
        for layer_index in range(LAYERS):
            residual = one_layer(residual, tuple((each_weight[layer_index] for each_weight in weight_set)), expert_ids[layer_index], places)
        return residual
    result, pull_back = jax.vjp(forward, hidden_in.astype(jnp.float32), weights)
    grad_residual, grad_weights = pull_back(out_grad.astype(jnp.float32))
    return (result.astype(jnp.bfloat16), grad_residual, grad_weights[0], grad_weights[1], grad_weights[2], grad_weights[3], grad_weights[4], grad_weights[5], grad_weights[6])
```

```python
import math

import jax
import jax.numpy as jnp
from jax import lax
from jax.sharding import PartitionSpec as P

HEADS = 24
KV_HEADS = 8
HEAD_DIM = 64
FE = 512
TOP = 8


highest = lax.Precision.HIGHEST
epsilon = 1e-06
rope_base = 10000.0
masked_score = -1e30


def row_positions(first_row, row_total, row_count, shards):
    indices = first_row + jnp.arange(row_total, dtype=jnp.int32)
    shard_of = indices // row_count
    within = indices % row_count
    half_rows = row_count // 2
    return jnp.where(
        within < half_rows,
        shard_of * half_rows + within,
        (2 * shards - 1 - shard_of) * half_rows + within - half_rows,
    )


def rotate(values_in, places, direction):
    half_dim = values_in.shape[-1] // 2
    frequency = rope_base ** (-jnp.arange(half_dim, dtype=jnp.float32) / half_dim)
    angles = places.astype(jnp.float32)[:, None] * frequency[None, :]
    cosine_part = jnp.cos(angles)[:, None, :]
    sine_part = direction * jnp.sin(angles)[:, None, :]
    front_half = values_in[..., :half_dim]
    back_half = values_in[..., half_dim:]
    return jnp.concatenate(
        [
            front_half * cosine_part - back_half * sine_part,
            back_half * cosine_part + front_half * sine_part,
        ],
        -1,
    )


def rms_scaled(residual, gain_vector):
    inverse_root = lax.rsqrt(jnp.mean(residual * residual, -1, keepdims=True) + epsilon)
    return (residual * inverse_root * gain_vector, inverse_root)


def rms_back(residual, inverse_root, gain_vector, grad_normed):
    grad_gain = jnp.sum(grad_normed * residual * inverse_root, 0)
    weighted = gain_vector * grad_normed
    cubed = inverse_root * inverse_root * inverse_root
    grad_residual = inverse_root * weighted - residual * cubed * jnp.mean(
        residual * weighted, -1, keepdims=True
    )
    return (grad_residual, grad_gain)


def route_table(routing_rows, expert_total, row_count, capacity):
    top_count = routing_rows.shape[1]
    chosen_mask = (
        routing_rows[:, :, None] == jnp.arange(expert_total, dtype=jnp.int32)[None, None, :]
    )
    expert_used = jnp.sum(chosen_mask.astype(jnp.int32), 1)
    slot_all = jnp.cumsum(expert_used, 0) - expert_used
    slot_taken = jnp.sum(jnp.where(chosen_mask, slot_all[:, None, :], 0), -1)
    target_slots = routing_rows * capacity + slot_taken
    entry_rows = jnp.full((expert_total * capacity,), row_count * top_count, jnp.int32)
    entry_rows = entry_rows.at[target_slots.reshape(-1)].set(
        jnp.arange(row_count * top_count, dtype=jnp.int32)
    )
    return (chosen_mask, target_slots, entry_rows)


def fold_keys(running, key_piece, queries, query_places, row_count, shards, kv_width):
    piece_rows = key_piece.shape[0]
    step_rows = math.gcd(piece_rows, row_count)
    step_total = piece_rows // step_rows
    blocks_in = key_piece.reshape(step_total, step_rows, key_piece.shape[1])
    heads_kv = queries.shape[1]
    head_size = queries.shape[3]
    score_scale = head_size ** (-0.5)

    def fold_one_step(state_in, inputs):
        block_rows, block_index = inputs
        key_places = row_positions(block_index * step_rows, step_rows, row_count, shards)
        key_rows = block_rows[:, :kv_width].reshape(step_rows, heads_kv, head_size)
        value_rows = block_rows[:, kv_width:].reshape(step_rows, heads_kv, head_size)
        scores = (
            jnp.einsum("qhgd,khd->hgqk", queries, key_rows, preferred_element_type=jnp.float32)
            * score_scale
        )
        visible = query_places[:, None] >= key_places[None, :]
        scores = jnp.where(visible, scores, masked_score)
        old_top, old_total, old_sum = state_in
        new_top = jnp.maximum(old_top, jnp.max(scores, -1))
        shrink = jnp.exp(old_top - new_top)
        weights = jnp.where(visible, jnp.exp(scores - new_top[..., None]), 0.0)
        new_total = old_total * shrink + jnp.sum(weights, -1)
        new_sum = old_sum * shrink[..., None] + jnp.einsum(
            "hgqk,khd->hgqd",
            weights.astype(jnp.bfloat16),
            value_rows,
            preferred_element_type=jnp.float32,
        )
        return ((new_top, new_total, new_sum), None)

    running, _ = lax.scan(
        fold_one_step, running, (blocks_in, jnp.arange(step_total, dtype=jnp.int32))
    )
    return running


def attend_back(
    queries,
    query_places,
    gathered,
    out_exact,
    grad_attended,
    log_total,
    row_count,
    shards,
    kv_width,
):
    heads_kv = queries.shape[1]
    head_size = queries.shape[3]
    score_scale = head_size ** (-0.5)
    delta_rows = jnp.transpose(
        jnp.sum(grad_attended.astype(jnp.float32) * out_exact, -1), (1, 2, 0)
    )
    blocks_in = gathered.reshape(shards, row_count, gathered.shape[1])

    def attend_one_step(grad_queries, inputs):
        block_rows, block_index = inputs
        key_places = row_positions(block_index * row_count, row_count, row_count, shards)
        key_rows = block_rows[:, :kv_width].reshape(row_count, heads_kv, head_size)
        value_rows = block_rows[:, kv_width:].reshape(row_count, heads_kv, head_size)
        scores = (
            jnp.einsum("qhgd,khd->hgqk", queries, key_rows, preferred_element_type=jnp.float32)
            * score_scale
        )
        visible = query_places[:, None] >= key_places[None, :]
        probabilities = jnp.where(visible, jnp.exp(scores - log_total[..., None]), 0.0)
        rounded = probabilities.astype(jnp.bfloat16)
        grad_values = jnp.einsum(
            "hgqk,qhgd->khd", rounded, grad_attended, preferred_element_type=jnp.float32
        )
        grad_probs = jnp.einsum(
            "qhgd,khd->hgqk", grad_attended, value_rows, preferred_element_type=jnp.float32
        )
        grad_scores = (probabilities * (grad_probs - delta_rows[..., None])).astype(jnp.bfloat16)
        grad_queries = grad_queries + score_scale * jnp.einsum(
            "hgqk,khd->qhgd", grad_scores, key_rows, preferred_element_type=jnp.float32
        )
        grad_keys = score_scale * jnp.einsum(
            "hgqk,qhgd->khd", grad_scores, queries, preferred_element_type=jnp.float32
        )
        return (
            grad_queries,
            jnp.concatenate(
                [grad_keys.reshape(row_count, kv_width), grad_values.reshape(row_count, kv_width)],
                -1,
            ),
        )

    start_grad = jnp.zeros(queries.shape, jnp.float32)
    grad_queries, grad_blocks = lax.scan(
        attend_one_step, start_grad, (blocks_in, jnp.arange(shards, dtype=jnp.int32))
    )
    return (grad_queries, grad_blocks.reshape(shards * row_count, gathered.shape[1]))


def on_device(
    hidden_in,
    w_query,
    w_key_value,
    w_output,
    w_router,
    norm_gains,
    w_gate_up,
    w_down,
    expert_ids,
    out_grad,
):
    shards = lax.axis_size("ctx")
    groups = lax.axis_size("fsdp")
    shard_index = lax.axis_index("ctx")
    row_count = hidden_in.shape[1]
    model_width = hidden_in.shape[2]
    layer_total = w_query.shape[0]
    experts_here = w_gate_up.shape[1]
    expert_total = experts_here * groups
    capacity = min(row_count, 3 * row_count * TOP // (2 * expert_total))
    kv_width = w_key_value.shape[2] // 2
    group_size = HEADS // KV_HEADS
    query_places = row_positions(shard_index * row_count, row_count, row_count, shards)
    residual = hidden_in.reshape(row_count, model_width).astype(jnp.float32)
    saved = []
    for layer_index in range(layer_total):
        query_weight, key_value_weight, output_weight, router_weight, gains = (
            lax.all_gather(w_query[layer_index], ("ctx", "fsdp"), axis=0, tiled=True),
            lax.all_gather(w_key_value[layer_index], ("ctx", "fsdp"), axis=0, tiled=True),
            lax.all_gather(w_output[layer_index], ("ctx", "fsdp"), axis=0, tiled=True),
            lax.all_gather(w_router[layer_index], ("ctx", "fsdp"), axis=0, tiled=True),
            lax.all_gather(norm_gains[layer_index], ("ctx", "fsdp"), axis=0, tiled=True),
        )
        gate_up_weight, down_weight = (
            lax.all_gather(w_gate_up[layer_index], "ctx", axis=1, tiled=True),
            lax.all_gather(w_down[layer_index], "ctx", axis=1, tiled=True),
        )
        gain_pair = gains.astype(jnp.float32)
        normed_first, root_first = rms_scaled(residual, gain_pair[:, 0])
        normed_first_low = normed_first.astype(jnp.bfloat16)
        query_raw = jnp.dot(normed_first_low, query_weight, preferred_element_type=jnp.float32)
        key_value_raw = jnp.dot(
            normed_first_low, key_value_weight, preferred_element_type=jnp.float32
        )
        queries = rotate(query_raw.reshape(row_count, HEADS, HEAD_DIM), query_places, 1.0).astype(
            jnp.bfloat16
        )
        queries = queries.reshape(row_count, KV_HEADS, group_size, HEAD_DIM)
        key_turned = rotate(
            key_value_raw[:, :kv_width].reshape(row_count, KV_HEADS, HEAD_DIM), query_places, 1.0
        )
        key_value_low = jnp.concatenate(
            [key_turned.reshape(row_count, kv_width), key_value_raw[:, kv_width:]], -1
        ).astype(jnp.bfloat16)
        start_state = (
            jnp.full((KV_HEADS, group_size, row_count), masked_score, jnp.float32),
            jnp.zeros((KV_HEADS, group_size, row_count), jnp.float32),
            jnp.zeros((KV_HEADS, group_size, row_count, HEAD_DIM), jnp.float32),
        )
        top_score, score_total, accumulated = fold_keys(
            start_state,
            lax.all_gather(key_value_low, "ctx", axis=0, tiled=True),
            queries,
            query_places,
            row_count,
            shards,
            kv_width,
        )
        out_exact = jnp.transpose(accumulated / score_total[..., None], (2, 0, 1, 3))
        log_total = top_score + jnp.log(score_total)
        attended = out_exact.reshape(row_count, model_width).astype(jnp.bfloat16)
        middle = residual + jnp.dot(attended, output_weight, preferred_element_type=jnp.float32)
        normed_second, root_second = rms_scaled(middle, gain_pair[:, 1])
        normed_second_low = normed_second.astype(jnp.bfloat16)
        chosen_mask, target_slots, entry_rows = route_table(
            expert_ids[layer_index].reshape(row_count, TOP), expert_total, row_count, capacity
        )
        padded_rows = jnp.concatenate(
            [normed_second_low, jnp.zeros((1, model_width), jnp.bfloat16)], 0
        )
        send_buffer = padded_rows[jnp.minimum(entry_rows // TOP, row_count)].reshape(
            groups, experts_here, capacity, model_width
        )
        received = lax.all_to_all(send_buffer, "fsdp", split_axis=0, concat_axis=0, tiled=True)
        gate_up = jnp.einsum(
            "serd,edf->serf", received, gate_up_weight, preferred_element_type=jnp.float32
        )
        hidden = (jax.nn.silu(gate_up[..., :FE]) * gate_up[..., FE:]).astype(jnp.bfloat16)
        expert_out = jnp.einsum(
            "serf,efd->serd", hidden, down_weight, preferred_element_type=jnp.float32
        ).astype(jnp.bfloat16)
        returned = lax.all_to_all(
            expert_out, "fsdp", split_axis=0, concat_axis=0, tiled=True
        ).reshape(expert_total * capacity, model_width)
        picked = returned[target_slots]
        logits = jnp.dot(normed_second_low, router_weight, preferred_element_type=jnp.float32)
        chosen_logits = jnp.sum(jnp.where(chosen_mask, logits[:, None, :], 0.0), -1)
        gate_probs = jax.nn.softmax(chosen_logits, axis=-1)
        expert_sum = jnp.sum(gate_probs[..., None] * picked.astype(jnp.float32), 1)
        saved.append(
            (
                residual,
                root_first,
                normed_first_low,
                queries,
                key_value_low,
                out_exact,
                log_total,
                attended,
                middle,
                root_second,
                normed_second_low,
                chosen_mask,
                target_slots,
                entry_rows,
                received,
                gate_up,
                hidden,
                picked,
                gate_probs,
                query_weight,
                key_value_weight,
                output_weight,
                router_weight,
                gain_pair,
                gate_up_weight,
                down_weight,
            )
        )
        residual = middle + expert_sum
    hidden_out = residual.reshape(1, row_count, model_width).astype(jnp.bfloat16)
    grad_residual = out_grad.reshape(row_count, model_width).astype(jnp.float32)
    (
        query_parts,
        key_value_parts,
        output_parts,
        router_parts,
        gain_parts,
        gate_up_parts,
        down_parts,
    ) = ([], [], [], [], [], [], [])
    for layer_index in reversed(range(layer_total)):
        (
            layer_input,
            root_first,
            normed_first_low,
            queries,
            key_value_low,
            out_exact,
            log_total,
            attended,
            middle,
            root_second,
            normed_second_low,
            chosen_mask,
            target_slots,
            entry_rows,
            received,
            gate_up,
            hidden,
            picked,
            gate_probs,
            query_weight,
            key_value_weight,
            output_weight,
            router_weight,
            gain_pair,
            gate_up_weight,
            down_weight,
        ) = saved[layer_index]
        grad_gates = jnp.sum(grad_residual[:, None, :] * picked.astype(jnp.float32), -1)
        grad_leaving = (
            (gate_probs[..., None] * grad_residual[:, None, :])
            .astype(jnp.bfloat16)
            .reshape(row_count * TOP, model_width)
        )
        grad_padded = jnp.concatenate([grad_leaving, jnp.zeros((1, model_width), jnp.bfloat16)], 0)
        grad_send = grad_padded[entry_rows].reshape(groups, experts_here, capacity, model_width)
        grad_received = lax.all_to_all(grad_send, "fsdp", split_axis=0, concat_axis=0, tiled=True)
        grad_hidden = jnp.einsum(
            "serd,efd->serf", grad_received, down_weight, preferred_element_type=jnp.float32
        )
        grad_down_part = jnp.einsum(
            "serf,serd->efd", hidden, grad_received, preferred_element_type=jnp.float32
        )
        gate_part = gate_up[..., :FE]
        up_part = gate_up[..., FE:]
        sigmoid_gate = jax.nn.sigmoid(gate_part)
        grad_gate = grad_hidden * up_part * sigmoid_gate * (1.0 + gate_part * (1.0 - sigmoid_gate))
        grad_up = grad_hidden * gate_part * sigmoid_gate
        grad_gate_up_rows = jnp.concatenate([grad_gate, grad_up], -1).astype(jnp.bfloat16)
        grad_gate_up_part = jnp.einsum(
            "serd,serf->edf", received, grad_gate_up_rows, preferred_element_type=jnp.float32
        )
        grad_entering = jnp.einsum(
            "serf,edf->serd", grad_gate_up_rows, gate_up_weight, preferred_element_type=jnp.float32
        ).astype(jnp.bfloat16)
        grad_returned = lax.all_to_all(
            grad_entering, "fsdp", split_axis=0, concat_axis=0, tiled=True
        ).reshape(expert_total * capacity, model_width)
        grad_normed_second = jnp.sum(grad_returned[target_slots].astype(jnp.float32), 1)
        gate_mean = jnp.sum(gate_probs * grad_gates, -1, keepdims=True)
        grad_chosen = gate_probs * (grad_gates - gate_mean)
        grad_logits = jnp.sum(jnp.where(chosen_mask, grad_chosen[..., None], 0.0), 1)
        grad_router_part = jnp.dot(
            normed_second_low.astype(jnp.float32).T, grad_logits, precision=highest
        )
        grad_normed_second = grad_normed_second + jnp.dot(
            grad_logits, router_weight.astype(jnp.float32).T, precision=highest
        )
        grad_middle, grad_gain_second = rms_back(
            middle, root_second, gain_pair[:, 1], grad_normed_second
        )
        grad_middle = grad_middle + grad_residual
        grad_branch = grad_middle.astype(jnp.bfloat16)
        grad_output_part = jnp.einsum(
            "rd,re->de", attended, grad_branch, preferred_element_type=jnp.float32
        )
        grad_attended = jnp.einsum(
            "re,de->rd", grad_branch, output_weight, preferred_element_type=jnp.float32
        ).astype(jnp.bfloat16)
        grad_attended = grad_attended.reshape(row_count, KV_HEADS, group_size, HEAD_DIM)
        gathered = lax.all_gather(key_value_low, "ctx", axis=0, tiled=True)
        grad_queries, grad_key_value_all = attend_back(
            queries,
            query_places,
            gathered,
            out_exact,
            grad_attended,
            log_total,
            row_count,
            shards,
            kv_width,
        )
        grad_key_value_own = lax.psum_scatter(
            grad_key_value_all.astype(jnp.bfloat16), "ctx", scatter_dimension=0, tiled=True
        ).astype(jnp.float32)
        grad_keys = rotate(
            grad_key_value_own[:, :kv_width].reshape(row_count, KV_HEADS, HEAD_DIM),
            query_places,
            -1.0,
        )
        grad_key_value_low = jnp.concatenate(
            [grad_keys.reshape(row_count, kv_width), grad_key_value_own[:, kv_width:]], -1
        ).astype(jnp.bfloat16)
        grad_query_low = (
            rotate(grad_queries.reshape(row_count, HEADS, HEAD_DIM), query_places, -1.0)
            .reshape(row_count, model_width)
            .astype(jnp.bfloat16)
        )
        grad_query_part = jnp.einsum(
            "rd,re->de", normed_first_low, grad_query_low, preferred_element_type=jnp.float32
        )
        grad_key_value_part = jnp.einsum(
            "rd,re->de", normed_first_low, grad_key_value_low, preferred_element_type=jnp.float32
        )
        grad_normed_first = jnp.einsum(
            "re,de->rd", grad_query_low, query_weight, preferred_element_type=jnp.float32
        ) + jnp.einsum(
            "re,de->rd", grad_key_value_low, key_value_weight, preferred_element_type=jnp.float32
        )
        grad_input, grad_gain_first = rms_back(
            layer_input, root_first, gain_pair[:, 0], grad_normed_first
        )
        grad_residual = grad_input + grad_middle
        grad_gain_part = jnp.stack([grad_gain_first, grad_gain_second], -1)
        query_parts.insert(0, grad_query_part)
        key_value_parts.insert(0, grad_key_value_part)
        output_parts.insert(0, grad_output_part)
        router_parts.insert(0, grad_router_part)
        gain_parts.insert(0, grad_gain_part)
        gate_up_parts.insert(0, grad_gate_up_part)
        down_parts.insert(0, grad_down_part)
    stacked_query = jnp.stack(query_parts, 0)
    stacked_key_value = jnp.stack(key_value_parts, 0)
    stacked_output = jnp.stack(output_parts, 0)
    stacked_router = jnp.stack(router_parts, 0)
    stacked_gains = jnp.stack(gain_parts, 0)
    stacked_gate_up = jnp.stack(gate_up_parts, 0)
    stacked_down = jnp.stack(down_parts, 0)
    stacked_query, stacked_key_value, stacked_output, stacked_router, stacked_gains = (
        lax.psum_scatter(stacked_query, ("ctx", "fsdp"), scatter_dimension=1, tiled=True),
        lax.psum_scatter(stacked_key_value, ("ctx", "fsdp"), scatter_dimension=1, tiled=True),
        lax.psum_scatter(stacked_output, ("ctx", "fsdp"), scatter_dimension=1, tiled=True),
        lax.psum_scatter(stacked_router, ("ctx", "fsdp"), scatter_dimension=1, tiled=True),
        lax.psum_scatter(stacked_gains, ("ctx", "fsdp"), scatter_dimension=1, tiled=True),
    )
    stacked_gate_up, stacked_down = (
        lax.psum_scatter(
            stacked_gate_up.astype(jnp.bfloat16), "ctx", scatter_dimension=2, tiled=True
        ).astype(jnp.float32),
        lax.psum_scatter(
            stacked_down.astype(jnp.bfloat16), "ctx", scatter_dimension=2, tiled=True
        ).astype(jnp.float32),
    )
    grad_hidden = grad_residual.reshape(1, row_count, model_width)
    return (
        hidden_out,
        grad_hidden,
        stacked_query,
        stacked_key_value,
        stacked_output,
        stacked_router,
        stacked_gains,
        stacked_gate_up,
        stacked_down,
    )


def rotate_ranks(values_in, axis_name, total, target_of):
    return lax.ppermute(values_in, axis_name, [(i, target_of(i)) for i in range(total)])


def swap_y(values_in):
    return rotate_ranks(values_in, "fsdp", 8, lambda i: i ^ 1)


def move_z(values_in, steps):
    return rotate_ranks(values_in, "fsdp", 8, lambda i: (i + 2 * steps) % 8)


def swap_core(values_in):
    return rotate_ranks(values_in, "ctx", 4, lambda i: i ^ 1)


def swap_x(values_in):
    return rotate_ranks(values_in, "ctx", 4, lambda i: i ^ 2)


def fsdp_members(index):
    z, y = index // 2, index % 2
    return [((z + dz) % 4) * 2 + (y ^ dy) for dz in (0, 1, 2, 3) for dy in (0, 1)]


def gather_fsdp(block):
    half = block.shape[0] // 2
    below = move_z(block, 1)
    above = move_z(block, -1)
    own_mirror = swap_y(block)
    below_mirror = swap_y(below)
    far_first = move_z(below[:half], 1)
    above_mirror = swap_y(above)
    far_second = move_z(above[half:], -1)
    far = jnp.concatenate([far_first, far_second], 0)
    far_mirror = swap_y(far)
    return [block, own_mirror, above, above_mirror, far, far_mirror, below, below_mirror]


def scatter_fsdp(parts):
    def fold(kept, sent):
        return kept.astype(jnp.float32) + swap_y(sent).astype(jnp.float32)

    half = parts[0].shape[0] // 2
    far = fold(parts[4], parts[5]).astype(jnp.bfloat16)
    above = fold(parts[2], parts[3])
    below = fold(parts[6], parts[7])
    own = fold(parts[0], parts[1])
    first = move_z(far[:half], 1).astype(jnp.float32)
    second = move_z(far[half:], -1).astype(jnp.float32)
    above = jnp.concatenate([above[:half] + first, above[half:]], 0)
    below = jnp.concatenate([below[:half], below[half:] + second], 0)
    from_below = move_z(above.astype(jnp.bfloat16), 1).astype(jnp.float32)
    from_above = move_z(below.astype(jnp.bfloat16), -1).astype(jnp.float32)
    return own + from_below + from_above


def gather_ctx(block):
    across = swap_x(block)
    return [block, swap_core(block), across, swap_core(across)]


def scatter_ctx(parts):
    across = parts[2].astype(jnp.float32) + swap_core(parts[3]).astype(jnp.float32)
    own = parts[0].astype(jnp.float32) + swap_core(parts[1]).astype(jnp.float32)
    return own + swap_x(across.astype(jnp.bfloat16)).astype(jnp.float32)


def split_ranks(
    hidden_in,
    w_query,
    w_key_value,
    w_output,
    w_router,
    norm_gains,
    w_gate_up,
    w_down,
    expert_ids,
    out_grad,
):
    both = ("ctx", "fsdp")
    ctx_total, groups = 4, 8
    ctx_index, group_index = lax.axis_index("ctx"), lax.axis_index("fsdp")
    row_count, model_width = hidden_in.shape[1], hidden_in.shape[2]
    layer_total, share, _ = w_query.shape
    experts_here = w_gate_up.shape[1]
    expert_total = experts_here * groups
    kv_width = w_key_value.shape[2] // 2
    q_part, kv_part = model_width // ctx_total, kv_width // ctx_total
    kv_here, group_size = KV_HEADS // ctx_total, HEADS // KV_HEADS
    seq_rows = ctx_total * row_count
    low = jnp.bfloat16
    f32 = jnp.float32
    score_scale = HEAD_DIM ** (-0.5)

    def dot(a, b):
        return jnp.dot(a, b, preferred_element_type=f32)

    def dot_t(a, b):
        return lax.dot_general(a, b, (((1,), (1,)), ((), ())), preferred_element_type=f32)

    def t_dot(a, b):
        return lax.dot_general(a, b, (((0,), (0,)), ((), ())), preferred_element_type=f32)

    small = jnp.concatenate(
        [norm_gains[i] for i in range(layer_total)] + [w_router[i] for i in range(layer_total)], -1
    )
    small = lax.all_gather(small, both, axis=0, tiled=True)
    gains = [small[:, 2 * i : 2 * i + 2].astype(f32) for i in range(layer_total)]
    routers = [
        small[:, 2 * layer_total + expert_total * i : 2 * layer_total + expert_total * (i + 1)]
        for i in range(layer_total)
    ]

    attention_weights = []
    for i in range(layer_total):
        blocks = jnp.concatenate(
            [
                w_query[i].reshape(share, ctx_total, q_part),
                w_key_value[i, :, :kv_width].reshape(share, ctx_total, kv_part),
                w_key_value[i, :, kv_width:].reshape(share, ctx_total, kv_part),
            ],
            -1,
        ).transpose(1, 0, 2)
        blocks = lax.all_to_all(blocks, "ctx", split_axis=0, concat_axis=0, tiled=True)
        packed = jnp.concatenate(
            [blocks, w_output[i].reshape(share, ctx_total, q_part).transpose(1, 0, 2)], -1
        )
        gathered = lax.all_gather(packed, "fsdp", axis=0, tiled=False)
        qkv_weight = (
            gathered[..., : q_part + 2 * kv_part]
            .transpose(1, 0, 2, 3)
            .reshape(model_width, q_part + 2 * kv_part)
        )
        out_weight = (
            gathered[..., q_part + 2 * kv_part :].transpose(0, 2, 1, 3).reshape(q_part, model_width)
        )
        attention_weights.append((qkv_weight, out_weight))
    expert_weights = [
        (
            lax.all_gather(w_gate_up[i], "ctx", axis=1, tiled=True),
            lax.all_gather(w_down[i], "ctx", axis=1, tiled=True),
        )
        for i in range(layer_total)
    ]
    members = jnp.stack(fsdp_members(group_index))
    ids_all = lax.all_gather(expert_ids.reshape(layer_total, row_count, TOP), "fsdp", axis=0)
    ids_all = jnp.take(ids_all, members, axis=0)
    expert_range = jnp.arange(expert_total, dtype=jnp.int32)
    own_experts = [
        (expert_range == group_index * experts_here + j).astype(f32) for j in range(experts_here)
    ]
    places = jnp.concatenate(
        [row_positions((ctx_index ^ r) * row_count, row_count, row_count, ctx_total) for r in range(4)]
    )
    visible = (places[:, None] >= places[None, :])[None, None]

    residual = hidden_in.reshape(row_count, model_width).astype(f32)
    saved = []
    for i in range(layer_total):
        qkv_weight, out_weight = attention_weights[i]
        gate_up_weight, down_weight = expert_weights[i]
        normed, root_first = rms_scaled(residual, gains[i][:, 0])
        rows_first = jnp.concatenate(gather_ctx(normed.astype(low)), 0)
        raw = dot(rows_first, qkv_weight)
        queries = rotate(
            raw[:, :q_part].reshape(seq_rows, kv_here * group_size, HEAD_DIM), places, 1.0
        ).astype(low).reshape(seq_rows, kv_here, group_size, HEAD_DIM)
        keys = rotate(
            raw[:, q_part : q_part + kv_part].reshape(seq_rows, kv_here, HEAD_DIM), places, 1.0
        ).astype(low)
        values = raw[:, q_part + kv_part :].reshape(seq_rows, kv_here, HEAD_DIM).astype(low)
        scores = (
            jnp.einsum("qhgd,khd->hgqk", queries, keys, preferred_element_type=f32) * score_scale
        )
        scores = jnp.where(visible, scores, masked_score)
        top = jnp.max(scores, -1, keepdims=True)
        weights = jnp.exp(scores - top)
        total = jnp.sum(weights, -1, keepdims=True)
        log_total = top + jnp.log(total)
        probs = weights / total
        attended = (
            jnp.einsum("hgqk,khd->qhgd", probs.astype(low), values, preferred_element_type=f32)
            .astype(low)
            .reshape(seq_rows, q_part)
        )
        branch = dot(attended, out_weight).astype(low).reshape(ctx_total, row_count, model_width)
        middle = residual + scatter_ctx([branch[r] for r in range(4)])
        normed_second, root_second = rms_scaled(middle, gains[i][:, 1])
        rows_second = jnp.concatenate(gather_fsdp(normed_second.astype(low)), 0)
        logits = dot(rows_second, routers[i])
        ids = ids_all[:, i].reshape(groups * row_count, TOP)
        chosen = jnp.any(ids[:, :, None] == expert_range[None, None, :], 1)
        logits = jnp.where(chosen, logits, masked_score)
        gate = jnp.exp(logits - jnp.max(logits, -1, keepdims=True))
        gate = gate / jnp.sum(gate, -1, keepdims=True)
        gates = [jnp.sum(gate * own, -1, keepdims=True) for own in own_experts]
        gate_ups, hiddens = [], []
        for j in range(experts_here):
            gate_up = dot(rows_second, gate_up_weight[j])
            hidden = jax.nn.silu(gate_up[:, :FE]) * gate_up[:, FE:]
            gate_ups.append(gate_up)
            hiddens.append((gates[j] * hidden).astype(low))
        partial = sum(dot(hiddens[j], down_weight[j]) for j in range(experts_here)).astype(low)
        partial = partial.reshape(groups, row_count, model_width)
        expert_sum = scatter_fsdp([partial[r] for r in range(groups)])
        saved.append(
            (
                residual, root_first, rows_first, queries, keys, values, log_total, attended,
                middle, root_second, rows_second, gates, gate_ups, hiddens, expert_sum,
            )
        )
        residual = middle + expert_sum
    hidden_out = residual.reshape(1, row_count, model_width).astype(low)
    grad = out_grad.reshape(row_count, model_width).astype(f32)
    attention_grads, expert_grads, small_grads = [], [], []
    for i in reversed(range(layer_total)):
        (
            residual, root_first, rows_first, queries, keys, values, log_total, attended,
            middle, root_second, rows_second, gates, gate_ups, hiddens, expert_sum,
        ) = saved[i]
        qkv_weight, out_weight = attention_weights[i]
        gate_up_weight, down_weight = expert_weights[i]
        mean_gate = jnp.sum(grad * expert_sum, -1, keepdims=True)
        mean_high = mean_gate.astype(low)
        mean_low = (mean_gate - mean_high.astype(f32)).astype(low)
        sent = jnp.concatenate(
            [
                grad.astype(low),
                mean_high,
                mean_low,
                jnp.zeros((row_count, 126), low),
            ],
            -1,
        )
        received = jnp.concatenate(gather_fsdp(sent), 0)
        mean_gates = received[:, model_width : model_width + 1].astype(f32) + received[
            :, model_width + 1 : model_width + 2
        ].astype(f32)
        received = received[:, :model_width]
        entering = 0.0
        gate_up_grads, down_grads, logit_grads = [], [], []
        for j in range(experts_here):
            plain = dot_t(received, down_weight[j])
            gate_part, up_part = gate_ups[j][:, :FE], gate_ups[j][:, FE:]
            sigmoid_gate = jax.nn.sigmoid(gate_part)
            silu_gate = gate_part * sigmoid_gate
            grad_gate_prob = jnp.sum(plain * (silu_gate * up_part), -1, keepdims=True)
            logit_grads.append(gates[j] * (grad_gate_prob - mean_gates))
            plain = plain * gates[j]
            grad_rows = jnp.concatenate(
                [
                    plain * up_part * sigmoid_gate * (1.0 + gate_part * (1.0 - sigmoid_gate)),
                    plain * silu_gate,
                ],
                -1,
            ).astype(low)
            entering = entering + dot_t(grad_rows, gate_up_weight[j])
            down_grads.append(t_dot(hiddens[j], received).astype(low))
            gate_up_grads.append(t_dot(rows_second, grad_rows).astype(low))
        grad_logits = sum(logit_grads[j] * own_experts[j][None, :] for j in range(experts_here))
        entering = entering + dot_t(grad_logits.astype(low), routers[i])
        grad_router = t_dot(rows_second, grad_logits.astype(low))
        expert_grads.insert(
            0,
            (
                lax.psum_scatter(
                    jnp.stack(gate_up_grads), "ctx", scatter_dimension=1, tiled=True
                ),
                lax.psum_scatter(jnp.stack(down_grads), "ctx", scatter_dimension=1, tiled=True),
            ),
        )
        entering = entering.astype(low).reshape(groups, row_count, model_width)
        grad_second = scatter_fsdp([entering[r] for r in range(groups)])
        grad_middle, gain_second = rms_back(middle, root_second, gains[i][:, 1], grad_second)
        grad_middle = grad_middle + grad
        rows_branch = jnp.concatenate(gather_ctx(grad_middle.astype(low)), 0)
        grad_attended = (
            dot_t(rows_branch, out_weight).astype(low).reshape(seq_rows, kv_here, group_size, HEAD_DIM)
        )
        out_weight_grad = t_dot(attended, rows_branch).astype(low)
        scores = (
            jnp.einsum("qhgd,khd->hgqk", queries, keys, preferred_element_type=f32) * score_scale
        )
        probs = jnp.where(visible, jnp.exp(scores - log_total), 0.0)
        grad_values = jnp.einsum(
            "hgqk,qhgd->khd", probs.astype(low), grad_attended, preferred_element_type=f32
        )
        grad_probs = jnp.einsum("qhgd,khd->hgqk", grad_attended, values, preferred_element_type=f32)
        grad_scores = (
            probs * (grad_probs - jnp.sum(probs * grad_probs, -1, keepdims=True))
        ).astype(low)
        grad_queries = score_scale * jnp.einsum(
            "hgqk,khd->qhgd", grad_scores, keys, preferred_element_type=f32
        )
        grad_keys = score_scale * jnp.einsum(
            "hgqk,qhgd->khd", grad_scores, queries, preferred_element_type=f32
        )
        grad_qkv = jnp.concatenate(
            [
                rotate(
                    grad_queries.reshape(seq_rows, kv_here * group_size, HEAD_DIM), places, -1.0
                ).reshape(seq_rows, q_part),
                rotate(grad_keys, places, -1.0).reshape(seq_rows, kv_part),
                grad_values.reshape(seq_rows, kv_part),
            ],
            -1,
        ).astype(low)
        back = dot_t(grad_qkv, qkv_weight).astype(low).reshape(ctx_total, row_count, model_width)
        grad_first = scatter_ctx([back[r] for r in range(4)])
        qkv_weight_grad = t_dot(rows_first, grad_qkv).astype(low)
        grad_input, gain_first = rms_back(residual, root_first, gains[i][:, 0], grad_first)
        grad = grad_input + grad_middle
        packed = jnp.concatenate(
            [
                qkv_weight_grad.reshape(ctx_total, groups, share, q_part + 2 * kv_part).transpose(
                    1, 0, 2, 3
                ),
                out_weight_grad.reshape(groups, share, ctx_total, q_part).transpose(0, 2, 1, 3),
            ],
            -1,
        )
        packed = packed.reshape(groups * ctx_total, share, packed.shape[-1])
        packed = lax.psum_scatter(packed, "fsdp", scatter_dimension=0, tiled=True)
        query_blocks = lax.all_to_all(
            packed[..., : q_part + 2 * kv_part], "ctx", split_axis=0, concat_axis=0, tiled=True
        )
        query_blocks = query_blocks.transpose(1, 0, 2).astype(f32)
        attention_grads.insert(
            0,
            (
                query_blocks[..., :q_part].reshape(share, model_width),
                jnp.concatenate(
                    [
                        query_blocks[..., q_part : q_part + kv_part].reshape(share, kv_width),
                        query_blocks[..., q_part + kv_part :].reshape(share, kv_width),
                    ],
                    -1,
                ),
                packed[..., q_part + 2 * kv_part :]
                .transpose(1, 0, 2)
                .reshape(share, model_width)
                .astype(f32),
            ),
        )
        small_grads.insert(
            0, jnp.concatenate([grad_router, gain_first[:, None], gain_second[:, None]], -1)
        )
    small_sum = lax.psum_scatter(jnp.stack(small_grads), both, scatter_dimension=1, tiled=True)
    return (
        hidden_out,
        grad.reshape(1, row_count, model_width),
        jnp.stack([g[0] for g in attention_grads]),
        jnp.stack([g[1] for g in attention_grads]),
        jnp.stack([g[2] for g in attention_grads]),
        small_sum[..., :expert_total],
        small_sum[..., expert_total:],
        jnp.stack([g[0] for g in expert_grads]).astype(f32),
        jnp.stack([g[1] for g in expert_grads]).astype(f32),
    )


def solution(mesh):
    split = mesh.shape["ctx"] == 4 and mesh.shape["fsdp"] == 8
    return jax.shard_map(
        split_ranks if split else on_device,
        mesh=mesh,
        in_specs=(
            P("fsdp", "ctx", None),
            P(None, ("ctx", "fsdp"), None),
            P(None, ("ctx", "fsdp"), None),
            P(None, ("ctx", "fsdp"), None),
            P(None, ("ctx", "fsdp"), None),
            P(None, ("ctx", "fsdp"), None),
            P(None, "fsdp", "ctx", None),
            P(None, "fsdp", "ctx", None),
            P(None, "fsdp", "ctx", None),
            P("fsdp", "ctx", None),
        ),
        out_specs=(
            P("fsdp", "ctx", None),
            P("fsdp", "ctx", None),
            P(None, ("ctx", "fsdp"), None),
            P(None, ("ctx", "fsdp"), None),
            P(None, ("ctx", "fsdp"), None),
            P(None, ("ctx", "fsdp"), None),
            P(None, ("ctx", "fsdp"), None),
            P(None, "fsdp", "ctx", None),
            P(None, "fsdp", "ctx", None),
        ),
        check_vma=False,
    )
```

```python
import math

import jax
import jax.numpy as jnp
from jax import lax
from jax.experimental import pallas as pl
from jax.experimental.pallas import tpu as pltpu
from jax.sharding import PartitionSpec as P

HEADS = 24
KV_HEADS = 8
HEAD_DIM = 64
FE = 512
TOP = 8


highest = lax.Precision.HIGHEST
epsilon = 1e-06
rope_base = 10000.0
masked_score = -1e30


def row_positions(first_row, row_total, row_count, shards):
    indices = first_row + jnp.arange(row_total, dtype=jnp.int32)
    shard_of = indices // row_count
    within = indices % row_count
    half_rows = row_count // 2
    return jnp.where(
        within < half_rows,
        shard_of * half_rows + within,
        (2 * shards - 1 - shard_of) * half_rows + within - half_rows,
    )


def rotate(values_in, places, direction):
    half_dim = values_in.shape[-1] // 2
    frequency = rope_base ** (-jnp.arange(half_dim, dtype=jnp.float32) / half_dim)
    angles = places.astype(jnp.float32)[:, None] * frequency[None, :]
    cosine_part = jnp.cos(angles)[:, None, :]
    sine_part = direction * jnp.sin(angles)[:, None, :]
    front_half = values_in[..., :half_dim]
    back_half = values_in[..., half_dim:]
    return jnp.concatenate(
        [
            front_half * cosine_part - back_half * sine_part,
            back_half * cosine_part + front_half * sine_part,
        ],
        -1,
    )


def rms_scaled(residual, gain_vector):
    inverse_root = lax.rsqrt(jnp.mean(residual * residual, -1, keepdims=True) + epsilon)
    return (residual * inverse_root * gain_vector, inverse_root)


def rms_back(residual, inverse_root, gain_vector, grad_normed):
    grad_gain = jnp.sum(grad_normed * residual * inverse_root, 0)
    weighted = gain_vector * grad_normed
    cubed = inverse_root * inverse_root * inverse_root
    grad_residual = inverse_root * weighted - residual * cubed * jnp.mean(
        residual * weighted, -1, keepdims=True
    )
    return (grad_residual, grad_gain)


def route_table(routing_rows, expert_total, row_count, capacity):
    top_count = routing_rows.shape[1]
    chosen_mask = (
        routing_rows[:, :, None] == jnp.arange(expert_total, dtype=jnp.int32)[None, None, :]
    )
    expert_used = jnp.sum(chosen_mask.astype(jnp.int32), 1)
    slot_all = jnp.cumsum(expert_used, 0) - expert_used
    slot_taken = jnp.sum(jnp.where(chosen_mask, slot_all[:, None, :], 0), -1)
    target_slots = routing_rows * capacity + slot_taken
    entry_rows = jnp.full((expert_total * capacity,), row_count * top_count, jnp.int32)
    entry_rows = entry_rows.at[target_slots.reshape(-1)].set(
        jnp.arange(row_count * top_count, dtype=jnp.int32)
    )
    return (chosen_mask, target_slots, entry_rows)


def fold_keys(running, key_piece, queries, query_places, row_count, shards, kv_width):
    piece_rows = key_piece.shape[0]
    step_rows = math.gcd(piece_rows, row_count)
    step_total = piece_rows // step_rows
    blocks_in = key_piece.reshape(step_total, step_rows, key_piece.shape[1])
    heads_kv = queries.shape[1]
    head_size = queries.shape[3]
    score_scale = head_size ** (-0.5)

    def fold_one_step(state_in, inputs):
        block_rows, block_index = inputs
        key_places = row_positions(block_index * step_rows, step_rows, row_count, shards)
        key_rows = block_rows[:, :kv_width].reshape(step_rows, heads_kv, head_size)
        value_rows = block_rows[:, kv_width:].reshape(step_rows, heads_kv, head_size)
        scores = (
            jnp.einsum("qhgd,khd->hgqk", queries, key_rows, preferred_element_type=jnp.float32)
            * score_scale
        )
        visible = query_places[:, None] >= key_places[None, :]
        scores = jnp.where(visible, scores, masked_score)
        old_top, old_total, old_sum = state_in
        new_top = jnp.maximum(old_top, jnp.max(scores, -1))
        shrink = jnp.exp(old_top - new_top)
        weights = jnp.where(visible, jnp.exp(scores - new_top[..., None]), 0.0)
        new_total = old_total * shrink + jnp.sum(weights, -1)
        new_sum = old_sum * shrink[..., None] + jnp.einsum(
            "hgqk,khd->hgqd",
            weights.astype(jnp.bfloat16),
            value_rows,
            preferred_element_type=jnp.float32,
        )
        return ((new_top, new_total, new_sum), None)

    running, _ = lax.scan(
        fold_one_step, running, (blocks_in, jnp.arange(step_total, dtype=jnp.int32))
    )
    return running


def attend_back(
    queries,
    query_places,
    gathered,
    out_exact,
    grad_attended,
    log_total,
    row_count,
    shards,
    kv_width,
):
    heads_kv = queries.shape[1]
    head_size = queries.shape[3]
    score_scale = head_size ** (-0.5)
    delta_rows = jnp.transpose(
        jnp.sum(grad_attended.astype(jnp.float32) * out_exact, -1), (1, 2, 0)
    )
    blocks_in = gathered.reshape(shards, row_count, gathered.shape[1])

    def attend_one_step(grad_queries, inputs):
        block_rows, block_index = inputs
        key_places = row_positions(block_index * row_count, row_count, row_count, shards)
        key_rows = block_rows[:, :kv_width].reshape(row_count, heads_kv, head_size)
        value_rows = block_rows[:, kv_width:].reshape(row_count, heads_kv, head_size)
        scores = (
            jnp.einsum("qhgd,khd->hgqk", queries, key_rows, preferred_element_type=jnp.float32)
            * score_scale
        )
        visible = query_places[:, None] >= key_places[None, :]
        probabilities = jnp.where(visible, jnp.exp(scores - log_total[..., None]), 0.0)
        rounded = probabilities.astype(jnp.bfloat16)
        grad_values = jnp.einsum(
            "hgqk,qhgd->khd", rounded, grad_attended, preferred_element_type=jnp.float32
        )
        grad_probs = jnp.einsum(
            "qhgd,khd->hgqk", grad_attended, value_rows, preferred_element_type=jnp.float32
        )
        grad_scores = (probabilities * (grad_probs - delta_rows[..., None])).astype(jnp.bfloat16)
        grad_queries = grad_queries + score_scale * jnp.einsum(
            "hgqk,khd->qhgd", grad_scores, key_rows, preferred_element_type=jnp.float32
        )
        grad_keys = score_scale * jnp.einsum(
            "hgqk,qhgd->khd", grad_scores, queries, preferred_element_type=jnp.float32
        )
        return (
            grad_queries,
            jnp.concatenate(
                [grad_keys.reshape(row_count, kv_width), grad_values.reshape(row_count, kv_width)],
                -1,
            ),
        )

    start_grad = jnp.zeros(queries.shape, jnp.float32)
    grad_queries, grad_blocks = lax.scan(
        attend_one_step, start_grad, (blocks_in, jnp.arange(shards, dtype=jnp.int32))
    )
    return (grad_queries, grad_blocks.reshape(shards * row_count, gathered.shape[1]))


def on_device(
    hidden_in,
    w_query,
    w_key_value,
    w_output,
    w_router,
    norm_gains,
    w_gate_up,
    w_down,
    expert_ids,
    out_grad,
):
    shards = lax.axis_size("ctx")
    groups = lax.axis_size("fsdp")
    shard_index = lax.axis_index("ctx")
    row_count = hidden_in.shape[1]
    model_width = hidden_in.shape[2]
    layer_total = w_query.shape[0]
    experts_here = w_gate_up.shape[1]
    expert_total = experts_here * groups
    capacity = min(row_count, 3 * row_count * TOP // (2 * expert_total))
    kv_width = w_key_value.shape[2] // 2
    group_size = HEADS // KV_HEADS
    query_places = row_positions(shard_index * row_count, row_count, row_count, shards)
    residual = hidden_in.reshape(row_count, model_width).astype(jnp.float32)
    saved = []
    for layer_index in range(layer_total):
        query_weight, key_value_weight, output_weight, router_weight, gains = (
            lax.all_gather(w_query[layer_index], ("ctx", "fsdp"), axis=0, tiled=True),
            lax.all_gather(w_key_value[layer_index], ("ctx", "fsdp"), axis=0, tiled=True),
            lax.all_gather(w_output[layer_index], ("ctx", "fsdp"), axis=0, tiled=True),
            lax.all_gather(w_router[layer_index], ("ctx", "fsdp"), axis=0, tiled=True),
            lax.all_gather(norm_gains[layer_index], ("ctx", "fsdp"), axis=0, tiled=True),
        )
        gate_up_weight, down_weight = (
            lax.all_gather(w_gate_up[layer_index], "ctx", axis=1, tiled=True),
            lax.all_gather(w_down[layer_index], "ctx", axis=1, tiled=True),
        )
        gain_pair = gains.astype(jnp.float32)
        normed_first, root_first = rms_scaled(residual, gain_pair[:, 0])
        normed_first_low = normed_first.astype(jnp.bfloat16)
        query_raw = jnp.dot(normed_first_low, query_weight, preferred_element_type=jnp.float32)
        key_value_raw = jnp.dot(
            normed_first_low, key_value_weight, preferred_element_type=jnp.float32
        )
        queries = rotate(query_raw.reshape(row_count, HEADS, HEAD_DIM), query_places, 1.0).astype(
            jnp.bfloat16
        )
        queries = queries.reshape(row_count, KV_HEADS, group_size, HEAD_DIM)
        key_turned = rotate(
            key_value_raw[:, :kv_width].reshape(row_count, KV_HEADS, HEAD_DIM), query_places, 1.0
        )
        key_value_low = jnp.concatenate(
            [key_turned.reshape(row_count, kv_width), key_value_raw[:, kv_width:]], -1
        ).astype(jnp.bfloat16)
        start_state = (
            jnp.full((KV_HEADS, group_size, row_count), masked_score, jnp.float32),
            jnp.zeros((KV_HEADS, group_size, row_count), jnp.float32),
            jnp.zeros((KV_HEADS, group_size, row_count, HEAD_DIM), jnp.float32),
        )
        top_score, score_total, accumulated = fold_keys(
            start_state,
            lax.all_gather(key_value_low, "ctx", axis=0, tiled=True),
            queries,
            query_places,
            row_count,
            shards,
            kv_width,
        )
        out_exact = jnp.transpose(accumulated / score_total[..., None], (2, 0, 1, 3))
        log_total = top_score + jnp.log(score_total)
        attended = out_exact.reshape(row_count, model_width).astype(jnp.bfloat16)
        middle = residual + jnp.dot(attended, output_weight, preferred_element_type=jnp.float32)
        normed_second, root_second = rms_scaled(middle, gain_pair[:, 1])
        normed_second_low = normed_second.astype(jnp.bfloat16)
        chosen_mask, target_slots, entry_rows = route_table(
            expert_ids[layer_index].reshape(row_count, TOP), expert_total, row_count, capacity
        )
        padded_rows = jnp.concatenate(
            [normed_second_low, jnp.zeros((1, model_width), jnp.bfloat16)], 0
        )
        send_buffer = padded_rows[jnp.minimum(entry_rows // TOP, row_count)].reshape(
            groups, experts_here, capacity, model_width
        )
        received = lax.all_to_all(send_buffer, "fsdp", split_axis=0, concat_axis=0, tiled=True)
        gate_up = jnp.einsum(
            "serd,edf->serf", received, gate_up_weight, preferred_element_type=jnp.float32
        )
        hidden = (jax.nn.silu(gate_up[..., :FE]) * gate_up[..., FE:]).astype(jnp.bfloat16)
        expert_out = jnp.einsum(
            "serf,efd->serd", hidden, down_weight, preferred_element_type=jnp.float32
        ).astype(jnp.bfloat16)
        returned = lax.all_to_all(
            expert_out, "fsdp", split_axis=0, concat_axis=0, tiled=True
        ).reshape(expert_total * capacity, model_width)
        picked = returned[target_slots]
        logits = jnp.dot(normed_second_low, router_weight, preferred_element_type=jnp.float32)
        chosen_logits = jnp.sum(jnp.where(chosen_mask, logits[:, None, :], 0.0), -1)
        gate_probs = jax.nn.softmax(chosen_logits, axis=-1)
        expert_sum = jnp.sum(gate_probs[..., None] * picked.astype(jnp.float32), 1)
        saved.append(
            (
                residual,
                root_first,
                normed_first_low,
                queries,
                key_value_low,
                out_exact,
                log_total,
                attended,
                middle,
                root_second,
                normed_second_low,
                chosen_mask,
                target_slots,
                entry_rows,
                received,
                gate_up,
                hidden,
                picked,
                gate_probs,
                query_weight,
                key_value_weight,
                output_weight,
                router_weight,
                gain_pair,
                gate_up_weight,
                down_weight,
            )
        )
        residual = middle + expert_sum
    hidden_out = residual.reshape(1, row_count, model_width).astype(jnp.bfloat16)
    grad_residual = out_grad.reshape(row_count, model_width).astype(jnp.float32)
    (
        query_parts,
        key_value_parts,
        output_parts,
        router_parts,
        gain_parts,
        gate_up_parts,
        down_parts,
    ) = ([], [], [], [], [], [], [])
    for layer_index in reversed(range(layer_total)):
        (
            layer_input,
            root_first,
            normed_first_low,
            queries,
            key_value_low,
            out_exact,
            log_total,
            attended,
            middle,
            root_second,
            normed_second_low,
            chosen_mask,
            target_slots,
            entry_rows,
            received,
            gate_up,
            hidden,
            picked,
            gate_probs,
            query_weight,
            key_value_weight,
            output_weight,
            router_weight,
            gain_pair,
            gate_up_weight,
            down_weight,
        ) = saved[layer_index]
        grad_gates = jnp.sum(grad_residual[:, None, :] * picked.astype(jnp.float32), -1)
        grad_leaving = (
            (gate_probs[..., None] * grad_residual[:, None, :])
            .astype(jnp.bfloat16)
            .reshape(row_count * TOP, model_width)
        )
        grad_padded = jnp.concatenate([grad_leaving, jnp.zeros((1, model_width), jnp.bfloat16)], 0)
        grad_send = grad_padded[entry_rows].reshape(groups, experts_here, capacity, model_width)
        grad_received = lax.all_to_all(grad_send, "fsdp", split_axis=0, concat_axis=0, tiled=True)
        grad_hidden = jnp.einsum(
            "serd,efd->serf", grad_received, down_weight, preferred_element_type=jnp.float32
        )
        grad_down_part = jnp.einsum(
            "serf,serd->efd", hidden, grad_received, preferred_element_type=jnp.float32
        )
        gate_part = gate_up[..., :FE]
        up_part = gate_up[..., FE:]
        sigmoid_gate = jax.nn.sigmoid(gate_part)
        grad_gate = grad_hidden * up_part * sigmoid_gate * (1.0 + gate_part * (1.0 - sigmoid_gate))
        grad_up = grad_hidden * gate_part * sigmoid_gate
        grad_gate_up_rows = jnp.concatenate([grad_gate, grad_up], -1).astype(jnp.bfloat16)
        grad_gate_up_part = jnp.einsum(
            "serd,serf->edf", received, grad_gate_up_rows, preferred_element_type=jnp.float32
        )
        grad_entering = jnp.einsum(
            "serf,edf->serd", grad_gate_up_rows, gate_up_weight, preferred_element_type=jnp.float32
        ).astype(jnp.bfloat16)
        grad_returned = lax.all_to_all(
            grad_entering, "fsdp", split_axis=0, concat_axis=0, tiled=True
        ).reshape(expert_total * capacity, model_width)
        grad_normed_second = jnp.sum(grad_returned[target_slots].astype(jnp.float32), 1)
        gate_mean = jnp.sum(gate_probs * grad_gates, -1, keepdims=True)
        grad_chosen = gate_probs * (grad_gates - gate_mean)
        grad_logits = jnp.sum(jnp.where(chosen_mask, grad_chosen[..., None], 0.0), 1)
        grad_router_part = jnp.dot(
            normed_second_low.astype(jnp.float32).T, grad_logits, precision=highest
        )
        grad_normed_second = grad_normed_second + jnp.dot(
            grad_logits, router_weight.astype(jnp.float32).T, precision=highest
        )
        grad_middle, grad_gain_second = rms_back(
            middle, root_second, gain_pair[:, 1], grad_normed_second
        )
        grad_middle = grad_middle + grad_residual
        grad_branch = grad_middle.astype(jnp.bfloat16)
        grad_output_part = jnp.einsum(
            "rd,re->de", attended, grad_branch, preferred_element_type=jnp.float32
        )
        grad_attended = jnp.einsum(
            "re,de->rd", grad_branch, output_weight, preferred_element_type=jnp.float32
        ).astype(jnp.bfloat16)
        grad_attended = grad_attended.reshape(row_count, KV_HEADS, group_size, HEAD_DIM)
        gathered = lax.all_gather(key_value_low, "ctx", axis=0, tiled=True)
        grad_queries, grad_key_value_all = attend_back(
            queries,
            query_places,
            gathered,
            out_exact,
            grad_attended,
            log_total,
            row_count,
            shards,
            kv_width,
        )
        grad_key_value_own = lax.psum_scatter(
            grad_key_value_all.astype(jnp.bfloat16), "ctx", scatter_dimension=0, tiled=True
        ).astype(jnp.float32)
        grad_keys = rotate(
            grad_key_value_own[:, :kv_width].reshape(row_count, KV_HEADS, HEAD_DIM),
            query_places,
            -1.0,
        )
        grad_key_value_low = jnp.concatenate(
            [grad_keys.reshape(row_count, kv_width), grad_key_value_own[:, kv_width:]], -1
        ).astype(jnp.bfloat16)
        grad_query_low = (
            rotate(grad_queries.reshape(row_count, HEADS, HEAD_DIM), query_places, -1.0)
            .reshape(row_count, model_width)
            .astype(jnp.bfloat16)
        )
        grad_query_part = jnp.einsum(
            "rd,re->de", normed_first_low, grad_query_low, preferred_element_type=jnp.float32
        )
        grad_key_value_part = jnp.einsum(
            "rd,re->de", normed_first_low, grad_key_value_low, preferred_element_type=jnp.float32
        )
        grad_normed_first = jnp.einsum(
            "re,de->rd", grad_query_low, query_weight, preferred_element_type=jnp.float32
        ) + jnp.einsum(
            "re,de->rd", grad_key_value_low, key_value_weight, preferred_element_type=jnp.float32
        )
        grad_input, grad_gain_first = rms_back(
            layer_input, root_first, gain_pair[:, 0], grad_normed_first
        )
        grad_residual = grad_input + grad_middle
        grad_gain_part = jnp.stack([grad_gain_first, grad_gain_second], -1)
        query_parts.insert(0, grad_query_part)
        key_value_parts.insert(0, grad_key_value_part)
        output_parts.insert(0, grad_output_part)
        router_parts.insert(0, grad_router_part)
        gain_parts.insert(0, grad_gain_part)
        gate_up_parts.insert(0, grad_gate_up_part)
        down_parts.insert(0, grad_down_part)
    stacked_query = jnp.stack(query_parts, 0)
    stacked_key_value = jnp.stack(key_value_parts, 0)
    stacked_output = jnp.stack(output_parts, 0)
    stacked_router = jnp.stack(router_parts, 0)
    stacked_gains = jnp.stack(gain_parts, 0)
    stacked_gate_up = jnp.stack(gate_up_parts, 0)
    stacked_down = jnp.stack(down_parts, 0)
    stacked_query, stacked_key_value, stacked_output, stacked_router, stacked_gains = (
        lax.psum_scatter(stacked_query, ("ctx", "fsdp"), scatter_dimension=1, tiled=True),
        lax.psum_scatter(stacked_key_value, ("ctx", "fsdp"), scatter_dimension=1, tiled=True),
        lax.psum_scatter(stacked_output, ("ctx", "fsdp"), scatter_dimension=1, tiled=True),
        lax.psum_scatter(stacked_router, ("ctx", "fsdp"), scatter_dimension=1, tiled=True),
        lax.psum_scatter(stacked_gains, ("ctx", "fsdp"), scatter_dimension=1, tiled=True),
    )
    stacked_gate_up, stacked_down = (
        lax.psum_scatter(
            stacked_gate_up.astype(jnp.bfloat16), "ctx", scatter_dimension=2, tiled=True
        ).astype(jnp.float32),
        lax.psum_scatter(
            stacked_down.astype(jnp.bfloat16), "ctx", scatter_dimension=2, tiled=True
        ).astype(jnp.float32),
    )
    grad_hidden = grad_residual.reshape(1, row_count, model_width)
    return (
        hidden_out,
        grad_hidden,
        stacked_query,
        stacked_key_value,
        stacked_output,
        stacked_router,
        stacked_gains,
        stacked_gate_up,
        stacked_down,
    )


NN = (((1,), (0,)), ((), ()))
NT = (((1,), (1,)), ((), ()))
TN = (((0,), (0,)), ((), ()))
FE_STEP = 256


def mm(a, b, dims=NN):
    return lax.dot_general(a, b, dims, preferred_element_type=jnp.float32)


def whole(shape):
    return pl.BlockSpec(shape, lambda *_: (0,) * len(shape))


def anywhere():
    return pl.BlockSpec(memory_space=pl.ANY)


def kernel_params(mebibytes):
    return pltpu.CompilerParams(vmem_limit_bytes=mebibytes * 1024 * 1024)


def shaped(shape, dtype=jnp.bfloat16):
    return jax.ShapeDtypeStruct(shape, dtype)


def experts_forward_body(
    rows_0, rows_1, mask, router, own, w_gate, w_up, w_down, *refs
):
    out_0, out_1, all_rows, all_gate, all_up, all_probs, total = refs[-7:]
    expert, piece = pl.program_id(0), pl.program_id(1)
    first = jnp.logical_and(expert == 0, piece == 0)
    last = jnp.logical_and(expert == pl.num_programs(0) - 1, piece == pl.num_programs(1) - 1)
    count = rows_0.shape[0]

    @pl.when(first)
    def _():
        all_rows[:count, :] = rows_0[...]
        all_rows[count:, :] = rows_1[...]
        logits = mm(all_rows[...], router[...]) + mask[...]
        weights = jnp.exp(logits - jnp.max(logits, -1, keepdims=True))
        all_probs[...] = weights / jnp.sum(weights, -1, keepdims=True)
        total[...] = jnp.zeros_like(total)

    chosen = jnp.sum(all_probs[...] * own[pl.ds(expert, 1), :], -1, keepdims=True)
    gate = mm(all_rows[...], w_gate[0])
    up = mm(all_rows[...], w_up[0])
    all_gate[...] = gate.astype(jnp.bfloat16)
    all_up[...] = up.astype(jnp.bfloat16)
    hidden = (gate * jax.nn.sigmoid(gate) * up * chosen).astype(jnp.bfloat16)
    total[...] += mm(hidden, w_down[0])

    @pl.when(last)
    def _():
        out_0[...] = total[:count, :].astype(jnp.bfloat16)
        out_1[...] = total[count:, :].astype(jnp.bfloat16)


def experts_forward(group, groups, rows, mask, router, own, w_gate_up, w_down, kept):
    block, width = rows[0].shape
    count = 2 * block
    expert_count, hidden_width = w_down.shape[0], w_down.shape[1]
    steps = hidden_width // FE_STEP
    flat = shaped((groups * count, expert_count * hidden_width))
    flat_spec = pl.BlockSpec((count, FE_STEP), lambda e, p: (group, e * steps + p))
    lanes_spec = pl.BlockSpec((count, 128), lambda e, p: (group, 0))
    inputs = [*rows, mask, router, own, w_gate_up, w_gate_up, w_down, *kept]
    return pl.pallas_call(
        experts_forward_body,
        grid=(expert_count, steps),
        in_specs=[
            whole((block, width)),
            whole((block, width)),
            lanes_spec,
            whole(router.shape),
            whole(own.shape),
            pl.BlockSpec((1, width, FE_STEP), lambda e, p: (e, 0, p)),
            pl.BlockSpec((1, width, FE_STEP), lambda e, p: (e, 0, steps + p)),
            pl.BlockSpec((1, FE_STEP, width), lambda e, p: (e, p, 0)),
        ]
        + [anywhere()] * len(kept),
        out_specs=[
            whole((block, width)),
            whole((block, width)),
            pl.BlockSpec((count, width), lambda e, p: (group, 0)),
            flat_spec,
            flat_spec,
            lanes_spec,
        ],
        out_shape=[
            shaped((block, width)),
            shaped((block, width)),
            shaped((groups * count, width)),
            flat,
            flat,
            shaped((groups * count, 128), jnp.float32),
        ],
        input_output_aliases={8 + i: 2 + i for i in range(len(kept))},
        scratch_shapes=[pltpu.VMEM((count, width), jnp.float32)],
        compiler_params=kernel_params(24),
        cost_estimate=pl.CostEstimate(
            flops=6 * count * width * expert_count * hidden_width,
            bytes_accessed=6 * width * expert_count * hidden_width,
            transcendentals=count * expert_count * hidden_width,
        ),
    )(*inputs)


def experts_backward_body(
    grads_0, grads_1, probs, gate_in, up_in, router, own, w_gate, w_up, w_down, *refs
):
    out_0, out_1, all_grads, all_grad_gate, all_grad_up, all_hidden, all_logits = refs[-10:-3]
    total, dots, mean = refs[-3:]
    expert, piece = pl.program_id(0), pl.program_id(1)
    first = jnp.logical_and(expert == 0, piece == 0)
    last_piece = piece == pl.num_programs(1) - 1
    last = jnp.logical_and(expert == pl.num_programs(0) - 1, last_piece)
    count, width = out_0.shape

    @pl.when(first)
    def _():
        for at, grads in ((0, grads_0), (count, grads_1)):
            all_grads[at : at + count, :] = grads[:, :width]
            mean[at : at + count, :] = grads[:, width : width + 1].astype(jnp.float32) + grads[
                :, width + 1 : width + 2
            ].astype(jnp.float32)
        total[...] = jnp.zeros_like(total)
        all_logits[...] = jnp.zeros_like(all_logits)

    @pl.when(piece == 0)
    def _():
        dots[...] = jnp.zeros_like(dots)

    mine = own[pl.ds(expert, 1), :]
    chosen = jnp.sum(probs[...] * mine, -1, keepdims=True)
    plain = mm(all_grads[...], w_down[0], NT)
    gate = gate_in[...].astype(jnp.float32)
    up = up_in[...].astype(jnp.float32)
    sigmoid_gate = jax.nn.sigmoid(gate)
    silu_gate = gate * sigmoid_gate
    hidden = silu_gate * up
    dots[...] += jnp.sum(plain * hidden, -1, keepdims=True)
    all_hidden[...] = (hidden * chosen).astype(jnp.bfloat16)
    plain = plain * chosen
    grad_gate = (plain * up * sigmoid_gate * (1.0 + gate * (1.0 - sigmoid_gate))).astype(
        jnp.bfloat16
    )
    grad_up = (plain * silu_gate).astype(jnp.bfloat16)
    all_grad_gate[...] = grad_gate
    all_grad_up[...] = grad_up
    total[...] += mm(grad_gate, w_gate[0], NT) + mm(grad_up, w_up[0], NT)

    @pl.when(last_piece)
    def _():
        all_logits[...] += (chosen * (dots[...] - mean[...]) * mine).astype(jnp.bfloat16)

    @pl.when(last)
    def _():
        result = (total[...] + mm(all_logits[...], router[...], NT)).astype(jnp.bfloat16)
        out_0[...] = result[:count, :]
        out_1[...] = result[count:, :]


def experts_backward(group, groups, grads, probs, gate, up, router, own, w_gate_up, w_down, kept):
    block, width = grads[0].shape[0], w_down.shape[2]
    count = 2 * block
    expert_count, hidden_width = w_down.shape[0], w_down.shape[1]
    steps = hidden_width // FE_STEP
    flat = shaped((groups * count, expert_count * hidden_width))
    flat_spec = pl.BlockSpec((count, FE_STEP), lambda e, p: (group, e * steps + p))
    lanes_spec = pl.BlockSpec((count, 128), lambda e, p: (group, 0))
    inputs = [*grads, probs, gate, up, router, own, w_gate_up, w_gate_up, w_down, *kept]
    return pl.pallas_call(
        experts_backward_body,
        grid=(expert_count, steps),
        in_specs=[
            whole(grads[0].shape),
            whole(grads[1].shape),
            lanes_spec,
            flat_spec,
            flat_spec,
            whole(router.shape),
            whole(own.shape),
            pl.BlockSpec((1, width, FE_STEP), lambda e, p: (e, 0, p)),
            pl.BlockSpec((1, width, FE_STEP), lambda e, p: (e, 0, steps + p)),
            pl.BlockSpec((1, FE_STEP, width), lambda e, p: (e, p, 0)),
        ]
        + [anywhere()] * len(kept),
        out_specs=[
            whole((block, width)),
            whole((block, width)),
            pl.BlockSpec((count, width), lambda e, p: (group, 0)),
            flat_spec,
            flat_spec,
            flat_spec,
            lanes_spec,
        ],
        out_shape=[
            shaped((block, width)),
            shaped((block, width)),
            shaped((groups * count, width)),
            flat,
            flat,
            flat,
            shaped((groups * count, 128)),
        ],
        input_output_aliases={10 + i: 2 + i for i in range(len(kept))},
        scratch_shapes=[
            pltpu.VMEM((count, width), jnp.float32),
            pltpu.VMEM((count, 1), jnp.float32),
            pltpu.VMEM((count, 1), jnp.float32),
        ],
        compiler_params=kernel_params(24),
        cost_estimate=pl.CostEstimate(
            flops=6 * count * width * expert_count * hidden_width,
            bytes_accessed=6 * width * expert_count * hidden_width,
            transcendentals=count * expert_count * hidden_width,
        ),
    )(*inputs)


def turn(block, cosine, sine, lane):
    half = HEAD_DIM // 2
    other = jnp.where(
        lane % HEAD_DIM < half, pltpu.roll(block, 128 - half, 1), pltpu.roll(block, half, 1)
    )
    return block * cosine + other * sine


def attention_forward_body(
    rows_0, rows_1, rows_2, rows_3, w_qkv, w_out, cosine, sine, place_column, place_row,
    out_0, out_1, out_2, out_3, all_rows, qkv, attended, logs,
):
    rows, outs = (rows_0, rows_1, rows_2, rows_3), (out_0, out_1, out_2, out_3)
    count = rows_0.shape[0]
    q_width, total_width = attended.shape[1], qkv.shape[1]
    kv_width = (total_width - q_width) // 2
    group = HEADS // KV_HEADS
    for r in range(4):
        span = pl.ds(r * count, count)
        all_rows[span, :] = rows[r][...]
        raw = mm(rows[r][...], w_qkv[:, :total_width])
        lane = lax.broadcasted_iota(jnp.int32, (count, 128), 1)
        for j in range((q_width + kv_width) // 128):
            turned = turn(raw[:, 128 * j : 128 * j + 128], cosine[span, :], sine[span, :], lane)
            if 128 * j < q_width:
                turned = turned * HEAD_DIM ** (-0.5)
            qkv[span, 128 * j : 128 * j + 128] = turned.astype(jnp.bfloat16)
        qkv[span, q_width + kv_width :] = raw[:, q_width + kv_width :].astype(jnp.bfloat16)
    visible = place_column[...] >= place_row[...]
    for head in range(q_width // HEAD_DIM):
        at, of = head * HEAD_DIM, (head // group) * HEAD_DIM
        queries = qkv[:, at : at + HEAD_DIM]
        keys = qkv[:, q_width + of : q_width + of + HEAD_DIM]
        values = qkv[:, q_width + kv_width + of : q_width + kv_width + of + HEAD_DIM]
        scores = jnp.where(visible, mm(queries, keys, NT), masked_score)
        top = jnp.max(scores, -1, keepdims=True)
        weights = jnp.exp(scores - top)
        total = jnp.sum(weights, -1, keepdims=True)
        logs[:, head : head + 1] = top + jnp.log(total)
        probs = (weights * (1.0 / total)).astype(jnp.bfloat16)
        attended[:, at : at + HEAD_DIM] = mm(probs, values).astype(jnp.bfloat16)
    for r in range(4):
        outs[r][...] = mm(attended[pl.ds(r * count, count), :], w_out[...]).astype(jnp.bfloat16)


def attention_forward(rows, w_qkv, w_out, total_width, tables):
    count, width = rows[0].shape
    seq = 4 * count
    q_width = w_out.shape[0]
    outs = pl.pallas_call(
        attention_forward_body,
        out_shape=[shaped((count, width))] * 4
        + [
            shaped((seq, width)),
            shaped((seq, total_width)),
            shaped((seq, q_width)),
            shaped((seq, 128), jnp.float32),
        ],
        compiler_params=kernel_params(24),
        cost_estimate=pl.CostEstimate(
            flops=2 * seq * width * (total_width + q_width) + 4 * seq * seq * q_width,
            bytes_accessed=2 * (seq * width * 2 + width * (total_width + q_width)),
            transcendentals=seq * seq * (q_width // HEAD_DIM),
        ),
    )(*rows, w_qkv, w_out, *tables)
    return outs[:4], outs[4], outs[5], outs[6], outs[7]


def attention_backward_body(
    grad_0, grad_1, grad_2, grad_3, rows,
    w_qkv, w_out, qkv, logs, cosine, sine, place_column, place_row,
    out_0, out_1, out_2, out_3, all_grads, grad_qkv, gain_sum, grad_attended, raw,
):
    grads, outs = (grad_0, grad_1, grad_2, grad_3), (out_0, out_1, out_2, out_3)
    count, seq = grad_0.shape[0], qkv.shape[0]
    q_width, total_width = grad_attended.shape[1], qkv.shape[1]
    kv_width = (total_width - q_width) // 2
    group = HEADS // KV_HEADS
    scale = HEAD_DIM ** (-0.5)
    for r in range(4):
        span = pl.ds(r * count, count)
        all_grads[span, :] = grads[r][...]
        grad_attended[span, :] = mm(grads[r][...], w_out[...], NT).astype(jnp.bfloat16)
    visible = place_column[...] >= place_row[...]
    for kv_head in range(kv_width // HEAD_DIM):
        k_at = q_width + kv_head * HEAD_DIM
        v_at = k_at + kv_width
        keys, values = qkv[:, k_at : k_at + HEAD_DIM], qkv[:, v_at : v_at + HEAD_DIM]
        grad_keys = jnp.zeros((HEAD_DIM, seq), jnp.float32)
        grad_values = jnp.zeros((HEAD_DIM, seq), jnp.float32)
        for head in range(kv_head * group, (kv_head + 1) * group):
            at = head * HEAD_DIM
            queries = qkv[:, at : at + HEAD_DIM]
            grad_head = grad_attended[:, at : at + HEAD_DIM]
            scores = mm(queries, keys, NT)
            probs = jnp.where(visible, jnp.exp(scores - logs[:, head : head + 1]), 0.0)
            grad_values += mm(grad_head.T, probs.astype(jnp.bfloat16))
            weighted = probs * mm(grad_head, values, NT)
            grad_scores = (weighted - probs * jnp.sum(weighted, -1, keepdims=True)).astype(
                jnp.bfloat16
            )
            raw[:, at : at + HEAD_DIM] = mm(grad_scores, keys) * scale
            grad_keys += mm(queries.T, grad_scores)
        raw[:, k_at : k_at + HEAD_DIM] = grad_keys.T
        raw[:, v_at : v_at + HEAD_DIM] = grad_values.T
    gain_sum[...] = jnp.zeros_like(gain_sum)
    for r in range(4):
        span = pl.ds(r * count, count)
        lane = lax.broadcasted_iota(jnp.int32, (count, 128), 1)
        for j in range((q_width + kv_width) // 128):
            part = slice(128 * j, 128 * j + 128)
            grad_qkv[span, part] = turn(
                raw[span, part], cosine[span, :], -sine[span, :], lane
            ).astype(jnp.bfloat16)
        grad_qkv[span, q_width + kv_width :] = raw[span, q_width + kv_width :].astype(jnp.bfloat16)
        back = mm(grad_qkv[span, :], w_qkv[:, :total_width], NT)
        outs[r][...] = back.astype(jnp.bfloat16)
        gain_sum[...] += jnp.sum(back * rows[span, :].astype(jnp.float32), 0, keepdims=True)


def attention_backward(grads, rows, w_qkv, w_out, qkv, logs, tables):
    count, width = grads[0].shape
    seq = 4 * count
    q_width, total_width = w_out.shape[0], qkv.shape[1]
    outs = pl.pallas_call(
        attention_backward_body,
        out_shape=[shaped((count, width))] * 4
        + [
            shaped((seq, width)),
            shaped((seq, total_width)),
            shaped((1, width), jnp.float32),
        ],
        scratch_shapes=[
            pltpu.VMEM((seq, q_width), jnp.bfloat16),
            pltpu.VMEM((seq, total_width), jnp.float32),
        ],
        compiler_params=kernel_params(32),
        cost_estimate=pl.CostEstimate(
            flops=2 * seq * width * (total_width + q_width) + 10 * seq * seq * q_width,
            bytes_accessed=2 * (seq * width * 3 + width * (total_width + q_width)),
            transcendentals=seq * seq * (q_width // HEAD_DIM),
        ),
    )(*grads, rows, w_qkv, w_out, qkv, logs, *tables)
    return outs[:4], outs[4], outs[5], outs[6]


def assemble_body(members, *refs):
    shards, (qkv, out), sems = refs[:8], refs[8:10], refs[10]
    share = shards[0].shape[1]
    q_part = out.shape[1] // 4
    front = qkv.shape[3]
    copies = []
    for r in range(8):
        copies.append(
            pltpu.make_async_copy(
                shards[r].at[:, :, :front], qkv.at[:, members[r]], sems.at[5 * r]
            )
        )
        for j in range(4):
            copies.append(
                pltpu.make_async_copy(
                    shards[r].at[j, :, front:],
                    out.at[
                        pl.ds(pl.multiple_of(members[r] * share, share), share),
                        j * q_part : (j + 1) * q_part,
                    ],
                    sems.at[5 * r + 1 + j],
                )
            )
    for copy in copies:
        copy.start()
    for copy in copies:
        copy.wait()


def assemble(members, shards, front):
    four, share, width = shards[0].shape
    q_part = width - front
    return pl.pallas_call(
        assemble_body,
        in_specs=[pl.BlockSpec(memory_space=pltpu.SMEM)] + [anywhere()] * 8,
        out_specs=[anywhere()] * 2,
        out_shape=[shaped((four, 8, share, front)), shaped((8 * share, four * q_part))],
        scratch_shapes=[pltpu.SemaphoreType.DMA((40,))],
    )(members, *shards)


def rotate_ranks(values_in, axis_name, total, target_of):
    return lax.ppermute(values_in, axis_name, [(i, target_of(i)) for i in range(total)])


def swap_y(values_in):
    return rotate_ranks(values_in, "fsdp", 8, lambda i: i ^ 1)


def move_z(values_in, steps):
    return rotate_ranks(values_in, "fsdp", 8, lambda i: (i + 2 * steps) % 8)


def swap_core(values_in):
    return rotate_ranks(values_in, "ctx", 4, lambda i: i ^ 1)


def swap_x(values_in):
    return rotate_ranks(values_in, "ctx", 4, lambda i: i ^ 2)


def after(value, *others):
    return lax.optimization_barrier((value, *others))[0]


def wide(value):
    return value.astype(jnp.float32)


def fsdp_members(index):
    z, y = index // 2, index % 2
    return [((z + dz) % 4) * 2 + (y ^ dy) for dz in (0, 3, 1, 2) for dy in (0, 1)]


def gather_fsdp(block, work):
    half = block.shape[0] // 2
    below = move_z(block, 1)
    own = (block, swap_y(block))
    work(0, own)
    above = move_z(after(block, below), -1)
    below = (below, swap_y(below))
    work(1, below)
    far_first = move_z(after(below[0][:half], above), 1)
    far_second = move_z(above[half:], -1)
    above = (above, swap_y(above))
    work(2, above)
    far = jnp.concatenate([far_first, far_second], 0)
    far = (far, swap_y(far))
    work(3, far)
    return [*own, *below, *above, *far]


def scatter_fsdp(parts, beside=(0.0, 0.0, 0.0)):
    half = parts[0].shape[0] // 2
    low = jnp.bfloat16
    far = (wide(parts[6]) + wide(swap_y(parts[7]))).astype(low)
    above = wide(parts[4]) + wide(swap_y(parts[5]))
    far = after(far, beside[0])
    first, second = move_z(far[:half], 1), move_z(far[half:], -1)
    below = wide(parts[2]) + wide(swap_y(after(parts[3], far)))
    above = jnp.concatenate([above[:half] + wide(first), above[half:]], 0).astype(low)
    from_below = move_z(after(above, beside[1]), 1)
    own = wide(parts[0]) + wide(swap_y(after(parts[1], above)))
    below = jnp.concatenate([below[:half], below[half:] + wide(second)], 0).astype(low)
    from_above = move_z(after(below, beside[2]), -1)
    return own + wide(from_below) + wide(from_above)


def gather_ctx(block):
    across = swap_x(block)
    return [block, swap_core(block), across, swap_core(across)]


def scatter_ctx(parts, *beside):
    across = wide(parts[2]) + wide(swap_core(parts[3]))
    own = wide(parts[0]) + wide(swap_core(parts[1]))
    across = swap_x(across.astype(jnp.bfloat16))
    if beside:
        across = after(across, *beside)
    return own + wide(across)


def split_ranks(
    hidden_in,
    w_query,
    w_key_value,
    w_output,
    w_router,
    norm_gains,
    w_gate_up,
    w_down,
    expert_ids,
    out_grad,
):
    both = ("ctx", "fsdp")
    ctx_total, groups = 4, 8
    ctx_index, group_index = lax.axis_index("ctx"), lax.axis_index("fsdp")
    row_count, model_width = hidden_in.shape[1], hidden_in.shape[2]
    layer_total, share, _ = w_query.shape
    experts_here = w_gate_up.shape[1]
    expert_total = experts_here * groups
    kv_width = w_key_value.shape[2] // 2
    q_part, kv_part = model_width // ctx_total, kv_width // ctx_total
    qkv_part = q_part + 2 * kv_part
    pair_total = groups // 2
    low = jnp.bfloat16
    f32 = jnp.float32

    def dot_tn(a, b):
        return mm(a, b, TN)

    members = jnp.stack(fsdp_members(group_index)).astype(jnp.int32)
    expert_lane = jnp.arange(128, dtype=jnp.int32)
    own_experts = (
        expert_lane[None, :] == group_index * experts_here + jnp.arange(8, dtype=jnp.int32)[:, None]
    ).astype(f32)
    places = jnp.concatenate(
        [row_positions((ctx_index ^ r) * row_count, row_count, row_count, ctx_total) for r in range(4)]
    )
    half_dim = HEAD_DIM // 2
    frequency = rope_base ** (-jnp.arange(half_dim, dtype=f32) / half_dim)
    angles = places.astype(f32)[:, None] * frequency[None, :]
    cosine, sine = jnp.cos(angles), jnp.sin(angles)
    tables = (
        jnp.concatenate([cosine] * 4, -1),
        jnp.concatenate([-sine, sine, -sine, sine], -1),
        places[:, None],
        places[None, :],
    )

    hidden_rows = gather_ctx(hidden_in.reshape(row_count, model_width))
    small = jnp.concatenate(
        [norm_gains[i] for i in range(layer_total)] + [w_router[i] for i in range(layer_total)], -1
    )
    small_width = small.shape[1]
    ids = expert_ids.reshape(layer_total, row_count, TOP)

    def weight_blocks(i, *more):
        blocks = jnp.concatenate(
            [
                w_query[i].reshape(share, ctx_total, q_part),
                w_key_value[i, :, :kv_width].reshape(share, ctx_total, kv_part),
                w_key_value[i, :, kv_width:].reshape(share, ctx_total, kv_part),
                *more,
            ],
            -1,
        ).transpose(1, 0, 2)
        return lax.all_to_all(blocks, "ctx", split_axis=0, concat_axis=0, tiled=True)

    def out_blocks(i):
        return w_output[i].reshape(share, ctx_total, q_part).transpose(1, 0, 2)

    front = qkv_part + 128
    blocks = weight_blocks(
        0, jnp.broadcast_to(small[:, None, :], (share, ctx_total, small_width))
    )
    ids_low = jnp.concatenate([ids[i] for i in range(layer_total)], -1).astype(low)
    ids_width = ids_low.shape[1]
    ids_low = jnp.pad(ids_low, ((0, ctx_total * share - row_count), (0, 0)))
    packed = jnp.concatenate(
        [
            blocks,
            ids_low.reshape(ctx_total, share, ids_width),
            jnp.zeros((ctx_total, share, front - qkv_part - small_width - ids_width), low),
            out_blocks(0),
        ],
        -1,
    )
    shards = gather_fsdp(packed.reshape(ctx_total * share, front + q_part), lambda *_: None)
    shards = [shard.reshape(ctx_total, share, front + q_part) for shard in shards]
    qkv_weight, out_weight = assemble(members, shards, front)
    qkv_weight = qkv_weight.reshape(model_width, front)
    small = qkv_weight[:, qkv_part : qkv_part + small_width]
    ids_all = jnp.concatenate(
        [
            shard[..., qkv_part + small_width : qkv_part + small_width + ids_width].reshape(
                ctx_total * share, ids_width
            )[:row_count]
            for shard in shards
        ],
        0,
    ).astype(jnp.int32)
    gains = [wide(small[:, 2 * i : 2 * i + 2]) for i in range(layer_total)]
    routers, masks = [], []
    for i in range(layer_total):
        at = 2 * layer_total + expert_total * i
        routers.append(jnp.pad(small[:, at : at + expert_total], ((0, 0), (0, 128 - expert_total))))
        chosen = jnp.any(
            ids_all[:, TOP * i : TOP * (i + 1), None] == expert_lane[None, None, :], 1
        )
        masks.append(jnp.where(chosen, 0.0, masked_score).astype(f32))

    attention_weights = [(qkv_weight, out_weight)]
    for i in range(1, layer_total):
        packed = jnp.concatenate([weight_blocks(i), out_blocks(i)], -1)
        gathered = lax.all_gather(packed, "fsdp", axis=0, tiled=False)
        attention_weights.append(
            (
                gathered[..., :qkv_part].transpose(1, 0, 2, 3).reshape(model_width, qkv_part),
                gathered[..., qkv_part:].transpose(0, 2, 1, 3).reshape(q_part, model_width),
            )
        )
    expert_weights = [
        (
            lax.all_gather(w_gate_up[i], "ctx", axis=1, tiled=True),
            lax.all_gather(w_down[i], "ctx", axis=1, tiled=True),
        )
        for i in range(layer_total)
    ]

    residual = wide(hidden_in.reshape(row_count, model_width))
    saved = []
    for i in range(layer_total):
        qkv_weight, out_weight = attention_weights[i]
        normed, root_first = rms_scaled(residual, gains[i][:, 0])
        if i == 0:
            rows = [
                rms_scaled(wide(block), gains[i][:, 0])[0].astype(low) for block in hidden_rows
            ]
        else:
            rows = gather_ctx(normed.astype(low))
        branch, rows_first, qkv, attended, logs = attention_forward(
            rows, qkv_weight, out_weight, qkv_part, tables
        )
        middle = residual + scatter_ctx(branch)
        normed_second, root_second = rms_scaled(middle, gains[i][:, 1])
        parts, kept = [None] * groups, []

        def forward_work(group, pair):
            outs = experts_forward(
                group, pair_total, pair, masks[i], routers[i], own_experts, *expert_weights[i], kept
            )
            parts[2 * group], parts[2 * group + 1] = outs[:2]
            kept[:] = outs[2:]

        gather_fsdp(normed_second.astype(low), forward_work)
        rows_second, gate, up, probs = kept
        expert_sum = scatter_fsdp(parts)
        saved.append(
            (
                residual, root_first, rows_first, qkv, attended, logs,
                middle, root_second, rows_second, gate, up, probs, expert_sum,
            )
        )
        residual = middle + expert_sum
    hidden_out = residual.reshape(1, row_count, model_width).astype(low)
    grad = wide(out_grad.reshape(row_count, model_width))
    attention_grads, expert_grads, small_grads = [], [], []
    for i in reversed(range(layer_total)):
        (
            residual, root_first, rows_first, qkv, attended, logs,
            middle, root_second, rows_second, gate, up, probs, expert_sum,
        ) = saved[i]
        qkv_weight, out_weight = attention_weights[i]
        mean_gate = jnp.sum(grad * expert_sum, -1, keepdims=True)
        mean_high = mean_gate.astype(low)
        mean_low = (mean_gate - wide(mean_high)).astype(low)
        sent = jnp.concatenate(
            [grad.astype(low), mean_high, mean_low, jnp.zeros((row_count, 126), low)], -1
        )
        parts, kept = [None] * groups, []

        def backward_work(group, pair):
            outs = experts_backward(
                group, pair_total, pair, probs, gate, up, routers[i], own_experts,
                *expert_weights[i], kept,
            )
            parts[2 * group], parts[2 * group + 1] = outs[:2]
            kept[:] = outs[2:]

        gather_fsdp(sent, backward_work)
        grads_second, grad_gate, grad_up, hidden, grad_logits = kept
        gate_grads = dot_tn(rows_second, grad_gate).astype(low)
        up_grads = dot_tn(rows_second, grad_up).astype(low)
        down_grads = dot_tn(hidden, grads_second).astype(low)
        grad_router = dot_tn(rows_second, grad_logits)[:, :expert_total]
        grad_second = scatter_fsdp(parts, (gate_grads, up_grads, down_grads))
        expert_grads.insert(
            0,
            (
                lax.psum_scatter(gate_grads, "ctx", scatter_dimension=0, tiled=True),
                lax.psum_scatter(up_grads, "ctx", scatter_dimension=0, tiled=True),
                lax.psum_scatter(
                    down_grads.reshape(experts_here, FE, model_width),
                    "ctx",
                    scatter_dimension=1,
                    tiled=True,
                ),
            ),
        )
        grad_middle, gain_second = rms_back(middle, root_second, gains[i][:, 1], grad_second)
        grad_middle = grad_middle + grad
        back, rows_branch, grad_qkv, gain_first = attention_backward(
            gather_ctx(grad_middle.astype(low)), rows_first, qkv_weight, out_weight, qkv, logs, tables
        )
        gain_first = gain_first[0] / gains[i][:, 0]
        qkv_grads = dot_tn(rows_first, grad_qkv).astype(low)
        out_grads = dot_tn(attended, rows_branch).astype(low)
        grad_first = scatter_ctx(back, qkv_grads, out_grads)
        grad_input, _ = rms_back(residual, root_first, gains[i][:, 0], grad_first)
        grad = grad_input + grad_middle
        qkv_grads = qkv_grads.reshape(ctx_total, groups, share, qkv_part)
        out_grads = out_grads.reshape(groups, share, ctx_total, q_part)
        if i == 0:
            packs = [
                jnp.concatenate(
                    [
                        lax.dynamic_index_in_dim(qkv_grads, members[r], 1, False),
                        lax.dynamic_index_in_dim(out_grads, members[r], 0, False).transpose(1, 0, 2),
                    ],
                    -1,
                ).reshape(ctx_total * share, qkv_part + q_part)
                for r in range(groups)
            ]
            packed = scatter_fsdp(packs).reshape(ctx_total, share, qkv_part + q_part)
        else:
            packed = jnp.concatenate(
                [qkv_grads.transpose(1, 0, 2, 3), out_grads.transpose(0, 2, 1, 3)], -1
            ).reshape(groups * ctx_total, share, qkv_part + q_part)
            packed = lax.psum_scatter(packed, "fsdp", scatter_dimension=0, tiled=True)
        query_blocks = lax.all_to_all(
            packed[..., :qkv_part].astype(low), "ctx", split_axis=0, concat_axis=0, tiled=True
        )
        query_blocks = wide(query_blocks.transpose(1, 0, 2))
        attention_grads.insert(
            0,
            (
                query_blocks[..., :q_part].reshape(share, model_width),
                jnp.concatenate(
                    [
                        query_blocks[..., q_part : q_part + kv_part].reshape(share, kv_width),
                        query_blocks[..., q_part + kv_part :].reshape(share, kv_width),
                    ],
                    -1,
                ),
                wide(packed[..., qkv_part:].transpose(1, 0, 2).reshape(share, model_width)),
            ),
        )
        small_grads.insert(
            0,
            lax.psum_scatter(
                jnp.concatenate([grad_router, gain_first[:, None], gain_second[:, None]], -1),
                both,
                scatter_dimension=0,
                tiled=True,
            ),
        )
    small_sum = jnp.stack(small_grads)
    gate_up_out = [
        jnp.concatenate(
            [part.reshape(model_width // ctx_total, experts_here, FE) for part in grads[:2]], -1
        ).transpose(1, 0, 2)
        for grads in expert_grads
    ]
    return (
        hidden_out,
        grad.reshape(1, row_count, model_width),
        jnp.stack([g[0] for g in attention_grads]),
        jnp.stack([g[1] for g in attention_grads]),
        jnp.stack([g[2] for g in attention_grads]),
        small_sum[..., :expert_total],
        small_sum[..., expert_total:],
        wide(jnp.stack(gate_up_out)),
        wide(jnp.stack([g[2] for g in expert_grads])),
    )


def solution(mesh):
    split = mesh.shape["ctx"] == 4 and mesh.shape["fsdp"] == 8
    return jax.shard_map(
        split_ranks if split else on_device,
        mesh=mesh,
        in_specs=(
            P("fsdp", "ctx", None),
            P(None, ("ctx", "fsdp"), None),
            P(None, ("ctx", "fsdp"), None),
            P(None, ("ctx", "fsdp"), None),
            P(None, ("ctx", "fsdp"), None),
            P(None, ("ctx", "fsdp"), None),
            P(None, "fsdp", "ctx", None),
            P(None, "fsdp", "ctx", None),
            P(None, "fsdp", "ctx", None),
            P("fsdp", "ctx", None),
        ),
        out_specs=(
            P("fsdp", "ctx", None),
            P("fsdp", "ctx", None),
            P(None, ("ctx", "fsdp"), None),
            P(None, ("ctx", "fsdp"), None),
            P(None, ("ctx", "fsdp"), None),
            P(None, ("ctx", "fsdp"), None),
            P(None, ("ctx", "fsdp"), None),
            P(None, "fsdp", "ctx", None),
            P(None, "fsdp", "ctx", None),
        ),
        check_vma=False,
    )
```

```python
import functools
import math

import jax
import jax.numpy as jnp
from jax import lax
from jax.experimental import pallas as pl
from jax.experimental.pallas import tpu as pltpu
from jax.sharding import PartitionSpec as P

HEADS = 24
KV_HEADS = 8
HEAD_DIM = 64
FE = 512
TOP = 8


highest = lax.Precision.HIGHEST
epsilon = 1e-06
rope_base = 10000.0
masked_score = -1e30


def row_positions(first_row, row_total, row_count, shards):
    indices = first_row + jnp.arange(row_total, dtype=jnp.int32)
    shard_of = indices // row_count
    within = indices % row_count
    half_rows = row_count // 2
    return jnp.where(
        within < half_rows,
        shard_of * half_rows + within,
        (2 * shards - 1 - shard_of) * half_rows + within - half_rows,
    )


def rotate(values_in, places, direction):
    half_dim = values_in.shape[-1] // 2
    frequency = rope_base ** (-jnp.arange(half_dim, dtype=jnp.float32) / half_dim)
    angles = places.astype(jnp.float32)[:, None] * frequency[None, :]
    cosine_part = jnp.cos(angles)[:, None, :]
    sine_part = direction * jnp.sin(angles)[:, None, :]
    front_half = values_in[..., :half_dim]
    back_half = values_in[..., half_dim:]
    return jnp.concatenate(
        [
            front_half * cosine_part - back_half * sine_part,
            back_half * cosine_part + front_half * sine_part,
        ],
        -1,
    )


def rms_scaled(residual, gain_vector):
    inverse_root = lax.rsqrt(jnp.mean(residual * residual, -1, keepdims=True) + epsilon)
    return (residual * inverse_root * gain_vector, inverse_root)


def rms_back(residual, inverse_root, gain_vector, grad_normed):
    grad_gain = jnp.sum(grad_normed * residual * inverse_root, 0)
    weighted = gain_vector * grad_normed
    cubed = inverse_root * inverse_root * inverse_root
    grad_residual = inverse_root * weighted - residual * cubed * jnp.mean(
        residual * weighted, -1, keepdims=True
    )
    return (grad_residual, grad_gain)


def route_table(routing_rows, expert_total, row_count, capacity):
    top_count = routing_rows.shape[1]
    chosen_mask = (
        routing_rows[:, :, None] == jnp.arange(expert_total, dtype=jnp.int32)[None, None, :]
    )
    expert_used = jnp.sum(chosen_mask.astype(jnp.int32), 1)
    slot_all = jnp.cumsum(expert_used, 0) - expert_used
    slot_taken = jnp.sum(jnp.where(chosen_mask, slot_all[:, None, :], 0), -1)
    target_slots = routing_rows * capacity + slot_taken
    entry_rows = jnp.full((expert_total * capacity,), row_count * top_count, jnp.int32)
    entry_rows = entry_rows.at[target_slots.reshape(-1)].set(
        jnp.arange(row_count * top_count, dtype=jnp.int32)
    )
    return (chosen_mask, target_slots, entry_rows)


def fold_keys(running, key_piece, queries, query_places, row_count, shards, kv_width):
    piece_rows = key_piece.shape[0]
    step_rows = math.gcd(piece_rows, row_count)
    step_total = piece_rows // step_rows
    blocks_in = key_piece.reshape(step_total, step_rows, key_piece.shape[1])
    heads_kv = queries.shape[1]
    head_size = queries.shape[3]
    score_scale = head_size ** (-0.5)

    def fold_one_step(state_in, inputs):
        block_rows, block_index = inputs
        key_places = row_positions(block_index * step_rows, step_rows, row_count, shards)
        key_rows = block_rows[:, :kv_width].reshape(step_rows, heads_kv, head_size)
        value_rows = block_rows[:, kv_width:].reshape(step_rows, heads_kv, head_size)
        scores = (
            jnp.einsum("qhgd,khd->hgqk", queries, key_rows, preferred_element_type=jnp.float32)
            * score_scale
        )
        visible = query_places[:, None] >= key_places[None, :]
        scores = jnp.where(visible, scores, masked_score)
        old_top, old_total, old_sum = state_in
        new_top = jnp.maximum(old_top, jnp.max(scores, -1))
        shrink = jnp.exp(old_top - new_top)
        weights = jnp.where(visible, jnp.exp(scores - new_top[..., None]), 0.0)
        new_total = old_total * shrink + jnp.sum(weights, -1)
        new_sum = old_sum * shrink[..., None] + jnp.einsum(
            "hgqk,khd->hgqd",
            weights.astype(jnp.bfloat16),
            value_rows,
            preferred_element_type=jnp.float32,
        )
        return ((new_top, new_total, new_sum), None)

    running, _ = lax.scan(
        fold_one_step, running, (blocks_in, jnp.arange(step_total, dtype=jnp.int32))
    )
    return running


def attend_back(
    queries,
    query_places,
    gathered,
    out_exact,
    grad_attended,
    log_total,
    row_count,
    shards,
    kv_width,
):
    heads_kv = queries.shape[1]
    head_size = queries.shape[3]
    score_scale = head_size ** (-0.5)
    delta_rows = jnp.transpose(
        jnp.sum(grad_attended.astype(jnp.float32) * out_exact, -1), (1, 2, 0)
    )
    blocks_in = gathered.reshape(shards, row_count, gathered.shape[1])

    def attend_one_step(grad_queries, inputs):
        block_rows, block_index = inputs
        key_places = row_positions(block_index * row_count, row_count, row_count, shards)
        key_rows = block_rows[:, :kv_width].reshape(row_count, heads_kv, head_size)
        value_rows = block_rows[:, kv_width:].reshape(row_count, heads_kv, head_size)
        scores = (
            jnp.einsum("qhgd,khd->hgqk", queries, key_rows, preferred_element_type=jnp.float32)
            * score_scale
        )
        visible = query_places[:, None] >= key_places[None, :]
        probabilities = jnp.where(visible, jnp.exp(scores - log_total[..., None]), 0.0)
        rounded = probabilities.astype(jnp.bfloat16)
        grad_values = jnp.einsum(
            "hgqk,qhgd->khd", rounded, grad_attended, preferred_element_type=jnp.float32
        )
        grad_probs = jnp.einsum(
            "qhgd,khd->hgqk", grad_attended, value_rows, preferred_element_type=jnp.float32
        )
        grad_scores = (probabilities * (grad_probs - delta_rows[..., None])).astype(jnp.bfloat16)
        grad_queries = grad_queries + score_scale * jnp.einsum(
            "hgqk,khd->qhgd", grad_scores, key_rows, preferred_element_type=jnp.float32
        )
        grad_keys = score_scale * jnp.einsum(
            "hgqk,qhgd->khd", grad_scores, queries, preferred_element_type=jnp.float32
        )
        return (
            grad_queries,
            jnp.concatenate(
                [grad_keys.reshape(row_count, kv_width), grad_values.reshape(row_count, kv_width)],
                -1,
            ),
        )

    start_grad = jnp.zeros(queries.shape, jnp.float32)
    grad_queries, grad_blocks = lax.scan(
        attend_one_step, start_grad, (blocks_in, jnp.arange(shards, dtype=jnp.int32))
    )
    return (grad_queries, grad_blocks.reshape(shards * row_count, gathered.shape[1]))


def on_device(
    hidden_in,
    w_query,
    w_key_value,
    w_output,
    w_router,
    norm_gains,
    w_gate_up,
    w_down,
    expert_ids,
    out_grad,
):
    shards = lax.axis_size("ctx")
    groups = lax.axis_size("fsdp")
    shard_index = lax.axis_index("ctx")
    row_count = hidden_in.shape[1]
    model_width = hidden_in.shape[2]
    layer_total = w_query.shape[0]
    experts_here = w_gate_up.shape[1]
    expert_total = experts_here * groups
    capacity = min(row_count, 3 * row_count * TOP // (2 * expert_total))
    kv_width = w_key_value.shape[2] // 2
    group_size = HEADS // KV_HEADS
    query_places = row_positions(shard_index * row_count, row_count, row_count, shards)
    residual = hidden_in.reshape(row_count, model_width).astype(jnp.float32)
    saved = []
    for layer_index in range(layer_total):
        query_weight, key_value_weight, output_weight, router_weight, gains = (
            lax.all_gather(w_query[layer_index], ("ctx", "fsdp"), axis=0, tiled=True),
            lax.all_gather(w_key_value[layer_index], ("ctx", "fsdp"), axis=0, tiled=True),
            lax.all_gather(w_output[layer_index], ("ctx", "fsdp"), axis=0, tiled=True),
            lax.all_gather(w_router[layer_index], ("ctx", "fsdp"), axis=0, tiled=True),
            lax.all_gather(norm_gains[layer_index], ("ctx", "fsdp"), axis=0, tiled=True),
        )
        gate_up_weight, down_weight = (
            lax.all_gather(w_gate_up[layer_index], "ctx", axis=1, tiled=True),
            lax.all_gather(w_down[layer_index], "ctx", axis=1, tiled=True),
        )
        gain_pair = gains.astype(jnp.float32)
        normed_first, root_first = rms_scaled(residual, gain_pair[:, 0])
        normed_first_low = normed_first.astype(jnp.bfloat16)
        query_raw = jnp.dot(normed_first_low, query_weight, preferred_element_type=jnp.float32)
        key_value_raw = jnp.dot(
            normed_first_low, key_value_weight, preferred_element_type=jnp.float32
        )
        queries = rotate(query_raw.reshape(row_count, HEADS, HEAD_DIM), query_places, 1.0).astype(
            jnp.bfloat16
        )
        queries = queries.reshape(row_count, KV_HEADS, group_size, HEAD_DIM)
        key_turned = rotate(
            key_value_raw[:, :kv_width].reshape(row_count, KV_HEADS, HEAD_DIM), query_places, 1.0
        )
        key_value_low = jnp.concatenate(
            [key_turned.reshape(row_count, kv_width), key_value_raw[:, kv_width:]], -1
        ).astype(jnp.bfloat16)
        start_state = (
            jnp.full((KV_HEADS, group_size, row_count), masked_score, jnp.float32),
            jnp.zeros((KV_HEADS, group_size, row_count), jnp.float32),
            jnp.zeros((KV_HEADS, group_size, row_count, HEAD_DIM), jnp.float32),
        )
        top_score, score_total, accumulated = fold_keys(
            start_state,
            lax.all_gather(key_value_low, "ctx", axis=0, tiled=True),
            queries,
            query_places,
            row_count,
            shards,
            kv_width,
        )
        out_exact = jnp.transpose(accumulated / score_total[..., None], (2, 0, 1, 3))
        log_total = top_score + jnp.log(score_total)
        attended = out_exact.reshape(row_count, model_width).astype(jnp.bfloat16)
        middle = residual + jnp.dot(attended, output_weight, preferred_element_type=jnp.float32)
        normed_second, root_second = rms_scaled(middle, gain_pair[:, 1])
        normed_second_low = normed_second.astype(jnp.bfloat16)
        chosen_mask, target_slots, entry_rows = route_table(
            expert_ids[layer_index].reshape(row_count, TOP), expert_total, row_count, capacity
        )
        padded_rows = jnp.concatenate(
            [normed_second_low, jnp.zeros((1, model_width), jnp.bfloat16)], 0
        )
        send_buffer = padded_rows[jnp.minimum(entry_rows // TOP, row_count)].reshape(
            groups, experts_here, capacity, model_width
        )
        received = lax.all_to_all(send_buffer, "fsdp", split_axis=0, concat_axis=0, tiled=True)
        gate_up = jnp.einsum(
            "serd,edf->serf", received, gate_up_weight, preferred_element_type=jnp.float32
        )
        hidden = (jax.nn.silu(gate_up[..., :FE]) * gate_up[..., FE:]).astype(jnp.bfloat16)
        expert_out = jnp.einsum(
            "serf,efd->serd", hidden, down_weight, preferred_element_type=jnp.float32
        ).astype(jnp.bfloat16)
        returned = lax.all_to_all(
            expert_out, "fsdp", split_axis=0, concat_axis=0, tiled=True
        ).reshape(expert_total * capacity, model_width)
        picked = returned[target_slots]
        logits = jnp.dot(normed_second_low, router_weight, preferred_element_type=jnp.float32)
        chosen_logits = jnp.sum(jnp.where(chosen_mask, logits[:, None, :], 0.0), -1)
        gate_probs = jax.nn.softmax(chosen_logits, axis=-1)
        expert_sum = jnp.sum(gate_probs[..., None] * picked.astype(jnp.float32), 1)
        saved.append(
            (
                residual,
                root_first,
                normed_first_low,
                queries,
                key_value_low,
                out_exact,
                log_total,
                attended,
                middle,
                root_second,
                normed_second_low,
                chosen_mask,
                target_slots,
                entry_rows,
                received,
                gate_up,
                hidden,
                picked,
                gate_probs,
                query_weight,
                key_value_weight,
                output_weight,
                router_weight,
                gain_pair,
                gate_up_weight,
                down_weight,
            )
        )
        residual = middle + expert_sum
    hidden_out = residual.reshape(1, row_count, model_width).astype(jnp.bfloat16)
    grad_residual = out_grad.reshape(row_count, model_width).astype(jnp.float32)
    (
        query_parts,
        key_value_parts,
        output_parts,
        router_parts,
        gain_parts,
        gate_up_parts,
        down_parts,
    ) = ([], [], [], [], [], [], [])
    for layer_index in reversed(range(layer_total)):
        (
            layer_input,
            root_first,
            normed_first_low,
            queries,
            key_value_low,
            out_exact,
            log_total,
            attended,
            middle,
            root_second,
            normed_second_low,
            chosen_mask,
            target_slots,
            entry_rows,
            received,
            gate_up,
            hidden,
            picked,
            gate_probs,
            query_weight,
            key_value_weight,
            output_weight,
            router_weight,
            gain_pair,
            gate_up_weight,
            down_weight,
        ) = saved[layer_index]
        grad_gates = jnp.sum(grad_residual[:, None, :] * picked.astype(jnp.float32), -1)
        grad_leaving = (
            (gate_probs[..., None] * grad_residual[:, None, :])
            .astype(jnp.bfloat16)
            .reshape(row_count * TOP, model_width)
        )
        grad_padded = jnp.concatenate([grad_leaving, jnp.zeros((1, model_width), jnp.bfloat16)], 0)
        grad_send = grad_padded[entry_rows].reshape(groups, experts_here, capacity, model_width)
        grad_received = lax.all_to_all(grad_send, "fsdp", split_axis=0, concat_axis=0, tiled=True)
        grad_hidden = jnp.einsum(
            "serd,efd->serf", grad_received, down_weight, preferred_element_type=jnp.float32
        )
        grad_down_part = jnp.einsum(
            "serf,serd->efd", hidden, grad_received, preferred_element_type=jnp.float32
        )
        gate_part = gate_up[..., :FE]
        up_part = gate_up[..., FE:]
        sigmoid_gate = jax.nn.sigmoid(gate_part)
        grad_gate = grad_hidden * up_part * sigmoid_gate * (1.0 + gate_part * (1.0 - sigmoid_gate))
        grad_up = grad_hidden * gate_part * sigmoid_gate
        grad_gate_up_rows = jnp.concatenate([grad_gate, grad_up], -1).astype(jnp.bfloat16)
        grad_gate_up_part = jnp.einsum(
            "serd,serf->edf", received, grad_gate_up_rows, preferred_element_type=jnp.float32
        )
        grad_entering = jnp.einsum(
            "serf,edf->serd", grad_gate_up_rows, gate_up_weight, preferred_element_type=jnp.float32
        ).astype(jnp.bfloat16)
        grad_returned = lax.all_to_all(
            grad_entering, "fsdp", split_axis=0, concat_axis=0, tiled=True
        ).reshape(expert_total * capacity, model_width)
        grad_normed_second = jnp.sum(grad_returned[target_slots].astype(jnp.float32), 1)
        gate_mean = jnp.sum(gate_probs * grad_gates, -1, keepdims=True)
        grad_chosen = gate_probs * (grad_gates - gate_mean)
        grad_logits = jnp.sum(jnp.where(chosen_mask, grad_chosen[..., None], 0.0), 1)
        grad_router_part = jnp.dot(
            normed_second_low.astype(jnp.float32).T, grad_logits, precision=highest
        )
        grad_normed_second = grad_normed_second + jnp.dot(
            grad_logits, router_weight.astype(jnp.float32).T, precision=highest
        )
        grad_middle, grad_gain_second = rms_back(
            middle, root_second, gain_pair[:, 1], grad_normed_second
        )
        grad_middle = grad_middle + grad_residual
        grad_branch = grad_middle.astype(jnp.bfloat16)
        grad_output_part = jnp.einsum(
            "rd,re->de", attended, grad_branch, preferred_element_type=jnp.float32
        )
        grad_attended = jnp.einsum(
            "re,de->rd", grad_branch, output_weight, preferred_element_type=jnp.float32
        ).astype(jnp.bfloat16)
        grad_attended = grad_attended.reshape(row_count, KV_HEADS, group_size, HEAD_DIM)
        gathered = lax.all_gather(key_value_low, "ctx", axis=0, tiled=True)
        grad_queries, grad_key_value_all = attend_back(
            queries,
            query_places,
            gathered,
            out_exact,
            grad_attended,
            log_total,
            row_count,
            shards,
            kv_width,
        )
        grad_key_value_own = lax.psum_scatter(
            grad_key_value_all.astype(jnp.bfloat16), "ctx", scatter_dimension=0, tiled=True
        ).astype(jnp.float32)
        grad_keys = rotate(
            grad_key_value_own[:, :kv_width].reshape(row_count, KV_HEADS, HEAD_DIM),
            query_places,
            -1.0,
        )
        grad_key_value_low = jnp.concatenate(
            [grad_keys.reshape(row_count, kv_width), grad_key_value_own[:, kv_width:]], -1
        ).astype(jnp.bfloat16)
        grad_query_low = (
            rotate(grad_queries.reshape(row_count, HEADS, HEAD_DIM), query_places, -1.0)
            .reshape(row_count, model_width)
            .astype(jnp.bfloat16)
        )
        grad_query_part = jnp.einsum(
            "rd,re->de", normed_first_low, grad_query_low, preferred_element_type=jnp.float32
        )
        grad_key_value_part = jnp.einsum(
            "rd,re->de", normed_first_low, grad_key_value_low, preferred_element_type=jnp.float32
        )
        grad_normed_first = jnp.einsum(
            "re,de->rd", grad_query_low, query_weight, preferred_element_type=jnp.float32
        ) + jnp.einsum(
            "re,de->rd", grad_key_value_low, key_value_weight, preferred_element_type=jnp.float32
        )
        grad_input, grad_gain_first = rms_back(
            layer_input, root_first, gain_pair[:, 0], grad_normed_first
        )
        grad_residual = grad_input + grad_middle
        grad_gain_part = jnp.stack([grad_gain_first, grad_gain_second], -1)
        query_parts.insert(0, grad_query_part)
        key_value_parts.insert(0, grad_key_value_part)
        output_parts.insert(0, grad_output_part)
        router_parts.insert(0, grad_router_part)
        gain_parts.insert(0, grad_gain_part)
        gate_up_parts.insert(0, grad_gate_up_part)
        down_parts.insert(0, grad_down_part)
    stacked_query = jnp.stack(query_parts, 0)
    stacked_key_value = jnp.stack(key_value_parts, 0)
    stacked_output = jnp.stack(output_parts, 0)
    stacked_router = jnp.stack(router_parts, 0)
    stacked_gains = jnp.stack(gain_parts, 0)
    stacked_gate_up = jnp.stack(gate_up_parts, 0)
    stacked_down = jnp.stack(down_parts, 0)
    stacked_query, stacked_key_value, stacked_output, stacked_router, stacked_gains = (
        lax.psum_scatter(stacked_query, ("ctx", "fsdp"), scatter_dimension=1, tiled=True),
        lax.psum_scatter(stacked_key_value, ("ctx", "fsdp"), scatter_dimension=1, tiled=True),
        lax.psum_scatter(stacked_output, ("ctx", "fsdp"), scatter_dimension=1, tiled=True),
        lax.psum_scatter(stacked_router, ("ctx", "fsdp"), scatter_dimension=1, tiled=True),
        lax.psum_scatter(stacked_gains, ("ctx", "fsdp"), scatter_dimension=1, tiled=True),
    )
    stacked_gate_up, stacked_down = (
        lax.psum_scatter(
            stacked_gate_up.astype(jnp.bfloat16), "ctx", scatter_dimension=2, tiled=True
        ).astype(jnp.float32),
        lax.psum_scatter(
            stacked_down.astype(jnp.bfloat16), "ctx", scatter_dimension=2, tiled=True
        ).astype(jnp.float32),
    )
    grad_hidden = grad_residual.reshape(1, row_count, model_width)
    return (
        hidden_out,
        grad_hidden,
        stacked_query,
        stacked_key_value,
        stacked_output,
        stacked_router,
        stacked_gains,
        stacked_gate_up,
        stacked_down,
    )


NN = (((1,), (0,)), ((), ()))
NT = (((1,), (1,)), ((), ()))
TN = (((0,), (0,)), ((), ()))
FE_STEP = 256
EXPERT_MIB = 58


def mm(a, b, dims=NN):
    return lax.dot_general(a, b, dims, preferred_element_type=jnp.float32)


def whole(shape):
    return pl.BlockSpec(shape, lambda *_: (0,) * len(shape))


def anywhere():
    return pl.BlockSpec(memory_space=pl.ANY)


def kernel_params(mebibytes):
    return pltpu.CompilerParams(vmem_limit_bytes=mebibytes * 1024 * 1024)


def shaped(shape, dtype=jnp.bfloat16):
    return jax.ShapeDtypeStruct(shape, dtype)


def experts_forward_body(
    first_id, rows_0, rows_1, ids, router, own, w_gate, w_up, w_down, *refs
):
    out_0, out_1, all_rows, all_gate, all_up, all_probs, total = refs[-7:]
    expert, piece = pl.program_id(0), pl.program_id(1)
    first = jnp.logical_and(expert == 0, piece == 0)
    last = jnp.logical_and(expert == pl.num_programs(0) - 1, piece == pl.num_programs(1) - 1)
    count = rows_0.shape[0]

    @pl.when(first)
    def _():
        all_rows[:count, :] = rows_0[...]
        all_rows[count:, :] = rows_1[...]
        lane = lax.broadcasted_iota(jnp.int32, all_probs.shape, 1).astype(jnp.float32)
        chosen_ids = ids[...].astype(jnp.float32)
        listed = lane == chosen_ids[:, first_id : first_id + 1]
        for k in range(1, TOP):
            at = first_id + k
            listed = jnp.logical_or(listed, lane == chosen_ids[:, at : at + 1])
        logits = jnp.where(listed, mm(all_rows[...], router[...]), masked_score)
        weights = jnp.exp(logits - jnp.max(logits, -1, keepdims=True))
        all_probs[...] = weights / jnp.sum(weights, -1, keepdims=True)
        total[...] = jnp.zeros_like(total)

    chosen = jnp.sum(all_probs[...] * own[pl.ds(expert, 1), :], -1, keepdims=True)
    gate = mm(all_rows[...], w_gate[0])
    up = mm(all_rows[...], w_up[0])
    all_gate[...] = gate.astype(jnp.bfloat16)
    all_up[...] = up.astype(jnp.bfloat16)
    hidden = (gate * jax.nn.sigmoid(gate) * up * chosen).astype(jnp.bfloat16)
    total[...] += mm(hidden, w_down[0])

    @pl.when(last)
    def _():
        out_0[...] = total[:count, :].astype(jnp.bfloat16)
        out_1[...] = total[count:, :].astype(jnp.bfloat16)


def experts_forward(group, groups, rows, ids, first_id, router, own, w_gate_up, w_down, kept):
    block, width = rows[0].shape
    count = 2 * block
    expert_count, hidden_width = w_down.shape[0], w_down.shape[1]
    steps = hidden_width // FE_STEP
    flat = shaped((groups * count, expert_count * hidden_width))
    flat_spec = pl.BlockSpec((count, FE_STEP), lambda e, p: (group, e * steps + p))
    lanes_spec = pl.BlockSpec((count, 128), lambda e, p: (group, 0))
    inputs = [*rows, ids, router, own, w_gate_up, w_gate_up, w_down, *kept]
    return pl.pallas_call(
        functools.partial(experts_forward_body, first_id),
        grid=(expert_count, steps),
        in_specs=[
            whole((block, width)),
            whole((block, width)),
            pl.BlockSpec((count, ids.shape[1]), lambda e, p: (group, 0)),
            whole(router.shape),
            whole(own.shape),
            pl.BlockSpec((1, width, FE_STEP), lambda e, p: (e, 0, p)),
            pl.BlockSpec((1, width, FE_STEP), lambda e, p: (e, 0, steps + p)),
            pl.BlockSpec((1, FE_STEP, width), lambda e, p: (e, p, 0)),
        ]
        + [anywhere()] * len(kept),
        out_specs=[
            whole((block, width)),
            whole((block, width)),
            pl.BlockSpec((count, width), lambda e, p: (group, 0)),
            flat_spec,
            flat_spec,
            lanes_spec,
        ],
        out_shape=[
            shaped((block, width)),
            shaped((block, width)),
            shaped((groups * count, width)),
            flat,
            flat,
            shaped((groups * count, 128), jnp.float32),
        ],
        input_output_aliases={8 + i: 2 + i for i in range(len(kept))},
        scratch_shapes=[pltpu.VMEM((count, width), jnp.float32)],
        compiler_params=kernel_params(EXPERT_MIB),
        cost_estimate=pl.CostEstimate(
            flops=6 * count * width * expert_count * hidden_width,
            bytes_accessed=6 * width * expert_count * hidden_width,
            transcendentals=count * expert_count * hidden_width,
        ),
    )(*inputs)


def experts_backward_body(
    grads_0, grads_1, probs, gate_in, up_in, router, own, w_gate, w_up, w_down, *refs
):
    out_0, out_1, all_grads, all_grad_gate, all_grad_up, all_hidden, all_logits = refs[-10:-3]
    total, dots, mean = refs[-3:]
    expert, piece = pl.program_id(0), pl.program_id(1)
    first = jnp.logical_and(expert == 0, piece == 0)
    last_piece = piece == pl.num_programs(1) - 1
    last = jnp.logical_and(expert == pl.num_programs(0) - 1, last_piece)
    count, width = out_0.shape

    @pl.when(first)
    def _():
        for at, grads in ((0, grads_0), (count, grads_1)):
            all_grads[at : at + count, :] = grads[:, :width]
            mean[at : at + count, :] = grads[:, width : width + 1].astype(jnp.float32) + grads[
                :, width + 1 : width + 2
            ].astype(jnp.float32)
        total[...] = jnp.zeros_like(total)
        all_logits[...] = jnp.zeros_like(all_logits)

    @pl.when(piece == 0)
    def _():
        dots[...] = jnp.zeros_like(dots)

    mine = own[pl.ds(expert, 1), :]
    chosen = jnp.sum(probs[...] * mine, -1, keepdims=True)
    plain = mm(all_grads[...], w_down[0], NT)
    gate = gate_in[...].astype(jnp.float32)
    up = up_in[...].astype(jnp.float32)
    sigmoid_gate = jax.nn.sigmoid(gate)
    silu_gate = gate * sigmoid_gate
    hidden = silu_gate * up
    dots[...] += jnp.sum(plain * hidden, -1, keepdims=True)
    all_hidden[...] = (hidden * chosen).astype(jnp.bfloat16)
    plain = plain * chosen
    grad_gate = (plain * up * sigmoid_gate * (1.0 + gate * (1.0 - sigmoid_gate))).astype(
        jnp.bfloat16
    )
    grad_up = (plain * silu_gate).astype(jnp.bfloat16)
    all_grad_gate[...] = grad_gate
    all_grad_up[...] = grad_up
    total[...] += mm(grad_gate, w_gate[0], NT) + mm(grad_up, w_up[0], NT)

    @pl.when(last_piece)
    def _():
        all_logits[...] += (chosen * (dots[...] - mean[...]) * mine).astype(jnp.bfloat16)

    @pl.when(last)
    def _():
        result = (total[...] + mm(all_logits[...], router[...], NT)).astype(jnp.bfloat16)
        out_0[...] = result[:count, :]
        out_1[...] = result[count:, :]


def experts_backward(group, groups, grads, probs, gate, up, router, own, w_gate_up, w_down, kept):
    block, width = grads[0].shape[0], w_down.shape[2]
    count = 2 * block
    expert_count, hidden_width = w_down.shape[0], w_down.shape[1]
    steps = hidden_width // FE_STEP
    flat = shaped((groups * count, expert_count * hidden_width))
    flat_spec = pl.BlockSpec((count, FE_STEP), lambda e, p: (group, e * steps + p))
    lanes_spec = pl.BlockSpec((count, 128), lambda e, p: (group, 0))
    inputs = [*grads, probs, gate, up, router, own, w_gate_up, w_gate_up, w_down, *kept]
    return pl.pallas_call(
        experts_backward_body,
        grid=(expert_count, steps),
        in_specs=[
            whole(grads[0].shape),
            whole(grads[1].shape),
            lanes_spec,
            flat_spec,
            flat_spec,
            whole(router.shape),
            whole(own.shape),
            pl.BlockSpec((1, width, FE_STEP), lambda e, p: (e, 0, p)),
            pl.BlockSpec((1, width, FE_STEP), lambda e, p: (e, 0, steps + p)),
            pl.BlockSpec((1, FE_STEP, width), lambda e, p: (e, p, 0)),
        ]
        + [anywhere()] * len(kept),
        out_specs=[
            whole((block, width)),
            whole((block, width)),
            pl.BlockSpec((count, width), lambda e, p: (group, 0)),
            flat_spec,
            flat_spec,
            flat_spec,
            lanes_spec,
        ],
        out_shape=[
            shaped((block, width)),
            shaped((block, width)),
            shaped((groups * count, width)),
            flat,
            flat,
            flat,
            shaped((groups * count, 128)),
        ],
        input_output_aliases={10 + i: 2 + i for i in range(len(kept))},
        scratch_shapes=[
            pltpu.VMEM((count, width), jnp.float32),
            pltpu.VMEM((count, 1), jnp.float32),
            pltpu.VMEM((count, 1), jnp.float32),
        ],
        compiler_params=kernel_params(EXPERT_MIB),
        cost_estimate=pl.CostEstimate(
            flops=6 * count * width * expert_count * hidden_width,
            bytes_accessed=6 * width * expert_count * hidden_width,
            transcendentals=count * expert_count * hidden_width,
        ),
    )(*inputs)


def turn(block, cosine, sine, lane):
    half = HEAD_DIM // 2
    other = jnp.where(
        lane % HEAD_DIM < half, pltpu.roll(block, 128 - half, 1), pltpu.roll(block, half, 1)
    )
    return block * cosine + other * sine


def attention_forward_body(
    rows_0, rows_1, rows_2, rows_3, w_qkv, w_out, cosine, sine, place_column, place_row,
    out_0, out_1, out_2, out_3, all_rows, qkv, attended, logs,
):
    rows, outs = (rows_0, rows_1, rows_2, rows_3), (out_0, out_1, out_2, out_3)
    count = rows_0.shape[0]
    q_width, total_width = attended.shape[1], qkv.shape[1]
    kv_width = (total_width - q_width) // 2
    group = HEADS // KV_HEADS
    for r in range(4):
        span = pl.ds(r * count, count)
        all_rows[span, :] = rows[r][...]
        raw = mm(rows[r][...], w_qkv[:, :total_width])
        lane = lax.broadcasted_iota(jnp.int32, (count, 128), 1)
        for j in range((q_width + kv_width) // 128):
            turned = turn(raw[:, 128 * j : 128 * j + 128], cosine[span, :], sine[span, :], lane)
            if 128 * j < q_width:
                turned = turned * HEAD_DIM ** (-0.5)
            qkv[span, 128 * j : 128 * j + 128] = turned.astype(jnp.bfloat16)
        qkv[span, q_width + kv_width :] = raw[:, q_width + kv_width :].astype(jnp.bfloat16)
    visible = place_column[...] >= place_row[...]
    for head in range(q_width // HEAD_DIM):
        at, of = head * HEAD_DIM, (head // group) * HEAD_DIM
        queries = qkv[:, at : at + HEAD_DIM]
        keys = qkv[:, q_width + of : q_width + of + HEAD_DIM]
        values = qkv[:, q_width + kv_width + of : q_width + kv_width + of + HEAD_DIM]
        scores = jnp.where(visible, mm(queries, keys, NT), masked_score)
        top = jnp.max(scores, -1, keepdims=True)
        weights = jnp.exp(scores - top)
        total = jnp.sum(weights, -1, keepdims=True)
        logs[:, head : head + 1] = top + jnp.log(total)
        probs = (weights * (1.0 / total)).astype(jnp.bfloat16)
        attended[:, at : at + HEAD_DIM] = mm(probs, values).astype(jnp.bfloat16)
    for r in range(4):
        outs[r][...] = mm(attended[pl.ds(r * count, count), :], w_out[...]).astype(jnp.bfloat16)


def attention_forward(rows, w_qkv, w_out, total_width, tables):
    count, width = rows[0].shape
    seq = 4 * count
    q_width = w_out.shape[0]
    outs = pl.pallas_call(
        attention_forward_body,
        out_shape=[shaped((count, width))] * 4
        + [
            shaped((seq, width)),
            shaped((seq, total_width)),
            shaped((seq, q_width)),
            shaped((seq, 128), jnp.float32),
        ],
        compiler_params=kernel_params(24),
        cost_estimate=pl.CostEstimate(
            flops=2 * seq * width * (total_width + q_width) + 4 * seq * seq * q_width,
            bytes_accessed=2 * (seq * width * 2 + width * (total_width + q_width)),
            transcendentals=seq * seq * (q_width // HEAD_DIM),
        ),
    )(*rows, w_qkv, w_out, *tables)
    return outs[:4], outs[4], outs[5], outs[6], outs[7]


def attention_backward_body(
    grad_0, grad_1, grad_2, grad_3, rows,
    w_qkv, w_out, qkv, logs, cosine, sine, place_column, place_row,
    out_0, out_1, out_2, out_3, all_grads, grad_qkv, gain_sum, grad_attended, raw,
):
    grads, outs = (grad_0, grad_1, grad_2, grad_3), (out_0, out_1, out_2, out_3)
    count, seq = grad_0.shape[0], qkv.shape[0]
    q_width, total_width = grad_attended.shape[1], qkv.shape[1]
    kv_width = (total_width - q_width) // 2
    group = HEADS // KV_HEADS
    scale = HEAD_DIM ** (-0.5)
    for r in range(4):
        span = pl.ds(r * count, count)
        all_grads[span, :] = grads[r][...]
        grad_attended[span, :] = mm(grads[r][...], w_out[...], NT).astype(jnp.bfloat16)
    visible = place_column[...] >= place_row[...]
    for kv_head in range(kv_width // HEAD_DIM):
        k_at = q_width + kv_head * HEAD_DIM
        v_at = k_at + kv_width
        keys, values = qkv[:, k_at : k_at + HEAD_DIM], qkv[:, v_at : v_at + HEAD_DIM]
        grad_keys = jnp.zeros((HEAD_DIM, seq), jnp.float32)
        grad_values = jnp.zeros((HEAD_DIM, seq), jnp.float32)
        for head in range(kv_head * group, (kv_head + 1) * group):
            at = head * HEAD_DIM
            queries = qkv[:, at : at + HEAD_DIM]
            grad_head = grad_attended[:, at : at + HEAD_DIM]
            scores = mm(queries, keys, NT)
            probs = jnp.where(visible, jnp.exp(scores - logs[:, head : head + 1]), 0.0)
            grad_values += mm(grad_head.T, probs.astype(jnp.bfloat16))
            weighted = probs * mm(grad_head, values, NT)
            grad_scores = (weighted - probs * jnp.sum(weighted, -1, keepdims=True)).astype(
                jnp.bfloat16
            )
            raw[:, at : at + HEAD_DIM] = mm(grad_scores, keys) * scale
            grad_keys += mm(queries.T, grad_scores)
        raw[:, k_at : k_at + HEAD_DIM] = grad_keys.T
        raw[:, v_at : v_at + HEAD_DIM] = grad_values.T
    gain_sum[...] = jnp.zeros_like(gain_sum)
    for r in range(4):
        span = pl.ds(r * count, count)
        lane = lax.broadcasted_iota(jnp.int32, (count, 128), 1)
        for j in range((q_width + kv_width) // 128):
            part = slice(128 * j, 128 * j + 128)
            grad_qkv[span, part] = turn(
                raw[span, part], cosine[span, :], -sine[span, :], lane
            ).astype(jnp.bfloat16)
        grad_qkv[span, q_width + kv_width :] = raw[span, q_width + kv_width :].astype(jnp.bfloat16)
        back = mm(grad_qkv[span, :], w_qkv[:, :total_width], NT)
        outs[r][...] = back.astype(jnp.bfloat16)
        gain_sum[...] += jnp.sum(back * rows[span, :].astype(jnp.float32), 0, keepdims=True)


def attention_backward(grads, rows, w_qkv, w_out, qkv, logs, tables):
    count, width = grads[0].shape
    seq = 4 * count
    q_width, total_width = w_out.shape[0], qkv.shape[1]
    outs = pl.pallas_call(
        attention_backward_body,
        out_shape=[shaped((count, width))] * 4
        + [
            shaped((seq, width)),
            shaped((seq, total_width)),
            shaped((1, width), jnp.float32),
        ],
        scratch_shapes=[
            pltpu.VMEM((seq, q_width), jnp.bfloat16),
            pltpu.VMEM((seq, total_width), jnp.float32),
        ],
        compiler_params=kernel_params(32),
        cost_estimate=pl.CostEstimate(
            flops=2 * seq * width * (total_width + q_width) + 10 * seq * seq * q_width,
            bytes_accessed=2 * (seq * width * 3 + width * (total_width + q_width)),
            transcendentals=seq * seq * (q_width // HEAD_DIM),
        ),
    )(*grads, rows, w_qkv, w_out, qkv, logs, *tables)
    return outs[:4], outs[4], outs[5], outs[6]


def place_body(members, *refs):
    shards, outs = refs[:8], refs[8:]
    share = shards[0].shape[1]
    front = outs[0].shape[3]
    for r in range(8):
        for c in range(4):
            outs[0][c, members[r]] = shards[r][c, :, :front]
        for out in outs[1:]:
            q_part = out.shape[1] // 4
            span = pl.ds(pl.multiple_of(members[r] * share, share), share)
            for j in range(4):
                out[span, j * q_part : (j + 1) * q_part] = shards[r][j, :, front:]


def place(members, shards, front):
    four, share, width = shards[0].shape
    outs = [shaped((four, 8, share, front))]
    if width > front:
        outs.append(shaped((8 * share, four * (width - front))))
    return pl.pallas_call(
        place_body,
        in_specs=[pl.BlockSpec(memory_space=pltpu.SMEM)] + [pl.BlockSpec(memory_space=pltpu.VMEM)] * 8,
        out_shape=outs,
        compiler_params=kernel_params(16),
    )(members, *shards)


def rotate_ranks(values_in, axis_name, total, target_of):
    return lax.ppermute(values_in, axis_name, [(i, target_of(i)) for i in range(total)])


def swap_y(values_in):
    return rotate_ranks(values_in, "fsdp", 8, lambda i: i ^ 1)


def move_z(values_in, steps):
    return rotate_ranks(values_in, "fsdp", 8, lambda i: (i + 2 * steps) % 8)


def swap_core(values_in):
    return rotate_ranks(values_in, "ctx", 4, lambda i: i ^ 1)


def swap_x(values_in):
    return rotate_ranks(values_in, "ctx", 4, lambda i: i ^ 2)


def after(value, *others):
    return lax.optimization_barrier((value, *others))[0]


def wide(value):
    return value.astype(jnp.float32)


def fsdp_members(index):
    z, y = index // 2, index % 2
    return [((z + dz) % 4) * 2 + (y ^ dy) for dz in (0, 3, 1, 2) for dy in (0, 1)]


def gather_fsdp(block, work=None):
    half = block.shape[0] // 2
    work = work or (lambda *_: 0.0)
    below = move_z(block, 1)
    own = (block, swap_y(block))
    above = move_z(after(block, below), -1)
    below_mirror = swap_y(below)
    done = work(0, (after(own[0], below), own[1]))
    far_first = move_z(after(below[:half], above, done), 1)
    far_second = move_z(above[half:], -1)
    above_mirror = swap_y(above)
    below = (below, below_mirror)
    done = work(1, (after(below[0], above), below[1]))
    far = jnp.concatenate([far_first, far_second], 0)
    far_mirror = swap_y(after(far, done))
    above = (above, above_mirror)
    work(2, (after(above[0], far), above[1]))
    far = (far, far_mirror)
    work(3, far)
    return [*own, *below, *above, *far]


def gather_small(block):
    own = jnp.stack([block, swap_y(block)])
    return jnp.concatenate([own, move_z(own, 1), move_z(own, -1), move_z(own, 2)], 0)


def scatter_fsdp(parts, beside=None):
    half = parts[0].shape[0] // 2
    low = jnp.bfloat16
    results = []

    def run(start):
        if beside:
            results.append(beside[len(results)](start))
            return results[-1:]
        return []

    far_mirror, above_mirror = swap_y(parts[7]), swap_y(parts[5])
    far = (wide(parts[6]) + wide(far_mirror)).astype(low)
    first, second = move_z(far[:half], 1), move_z(far[half:], -1)
    below_mirror = swap_y(after(parts[3], far))
    done = run(far)
    above = wide(parts[4]) + wide(above_mirror)
    above = jnp.concatenate([above[:half] + wide(first), above[half:]], 0).astype(low)
    from_below = move_z(after(above, *done), 1)
    own_mirror = swap_y(after(parts[1], above))
    done = run(above)
    below = wide(parts[2]) + wide(below_mirror)
    below = jnp.concatenate([below[:half], below[half:] + wide(second)], 0).astype(low)
    from_above = move_z(after(below, *done), -1)
    done = run(below)
    own = wide(parts[0]) + wide(own_mirror)
    return after(own + wide(from_below), *done) + wide(from_above), results


def gather_ctx(block):
    across = swap_x(block)
    return [block, swap_core(block), across, swap_core(across)]


def scatter_ctx(parts, *beside):
    across = wide(parts[2]) + wide(swap_core(parts[3]))
    own = wide(parts[0]) + wide(swap_core(parts[1]))
    across = swap_x(across.astype(jnp.bfloat16))
    if beside:
        across = after(across, *beside)
    return own + wide(across)


def split_ranks(
    hidden_in,
    w_query,
    w_key_value,
    w_output,
    w_router,
    norm_gains,
    w_gate_up,
    w_down,
    expert_ids,
    out_grad,
):
    both = ("ctx", "fsdp")
    ctx_total, groups = 4, 8
    ctx_index, group_index = lax.axis_index("ctx"), lax.axis_index("fsdp")
    row_count, model_width = hidden_in.shape[1], hidden_in.shape[2]
    layer_total, share, _ = w_query.shape
    experts_here = w_gate_up.shape[1]
    expert_total = experts_here * groups
    kv_width = w_key_value.shape[2] // 2
    q_part, kv_part = model_width // ctx_total, kv_width // ctx_total
    qkv_part = q_part + 2 * kv_part
    pair_total = groups // 2
    low = jnp.bfloat16
    f32 = jnp.float32

    core, across = ctx_index % 2, ctx_index // 2

    def cross_core(whole_sum):
        sent = lax.dynamic_index_in_dim(whole_sum, 1 - core, 1, False)
        held = lax.dynamic_index_in_dim(whole_sum, core, 1, False)
        return (wide(held) + wide(swap_core(sent))).astype(low)

    def cross_x(half_sum):
        sent = lax.dynamic_index_in_dim(half_sum, 1 - across, 0, False)
        held = lax.dynamic_index_in_dim(half_sum, across, 0, False)
        return wide(held) + wide(swap_x(sent))

    def dot_tn(a, b):
        return mm(a, b, TN)

    members = jnp.stack(fsdp_members(group_index)).astype(jnp.int32)
    expert_lane = jnp.arange(128, dtype=jnp.int32)
    own_experts = (
        expert_lane[None, :] == group_index * experts_here + jnp.arange(8, dtype=jnp.int32)[:, None]
    ).astype(f32)
    places = jnp.concatenate(
        [row_positions((ctx_index ^ r) * row_count, row_count, row_count, ctx_total) for r in range(4)]
    )
    half_dim = HEAD_DIM // 2
    frequency = rope_base ** (-jnp.arange(half_dim, dtype=f32) / half_dim)
    angles = places.astype(f32)[:, None] * frequency[None, :]
    cosine, sine = jnp.cos(angles), jnp.sin(angles)
    tables = (
        jnp.concatenate([cosine] * 4, -1),
        jnp.concatenate([-sine, sine, -sine, sine], -1),
        places[:, None],
        places[None, :],
    )

    hidden_rows = gather_ctx(hidden_in.reshape(row_count, model_width))
    small = jnp.concatenate(
        [norm_gains[i] for i in range(layer_total)] + [w_router[i] for i in range(layer_total)], -1
    )
    small_width = small.shape[1]
    parts = []
    for i in range(layer_total):
        parts += [
            w_query[i].reshape(share, ctx_total, q_part),
            w_key_value[i, :, :kv_width].reshape(share, ctx_total, kv_part),
            w_key_value[i, :, kv_width:].reshape(share, ctx_total, kv_part),
        ]
    parts.append(jnp.broadcast_to(small[:, None, :], (share, ctx_total, small_width)))
    blocks = jnp.concatenate(parts, -1).transpose(1, 0, 2)
    blocks = lax.all_to_all(blocks, "ctx", split_axis=0, concat_axis=0, tiled=True)

    def layer_shard(i):
        out_blocks = w_output[i].reshape(share, ctx_total, q_part).transpose(1, 0, 2)
        return jnp.concatenate([blocks[..., i * qkv_part : (i + 1) * qkv_part], out_blocks], -1)

    packed = layer_shard(0).reshape(ctx_total * share, qkv_part + q_part)
    shards = gather_fsdp(packed)
    shards = [shard.reshape(ctx_total, share, qkv_part + q_part) for shard in shards]
    qkv_weight, out_weight = place(members, shards, qkv_part)
    attention_weights = [(qkv_weight.reshape(model_width, qkv_part), out_weight)]

    ids_low = jnp.concatenate(
        [expert_ids[i].reshape(row_count, TOP) for i in range(layer_total)], -1
    ).astype(low)
    ids_width = ids_low.shape[1]
    ids_low = jnp.pad(ids_low, ((0, ctx_total * share - row_count), (0, 0)))
    small_rows = jnp.concatenate(
        [
            blocks[..., layer_total * qkv_part :].reshape(ctx_total * share, small_width),
            ids_low,
            jnp.zeros((ctx_total * share, 128 - small_width - ids_width), low),
        ],
        -1,
    )
    small_all = gather_small(small_rows)
    ids_all = small_all[:, :row_count, small_width : small_width + ids_width].reshape(
        groups * row_count, ids_width
    )
    small_all = small_all.reshape(groups, ctx_total, share, 128)
    small = place(members, [small_all[r] for r in range(groups)], 128)[0].reshape(model_width, 128)
    gains = [wide(small[:, 2 * i : 2 * i + 2]) for i in range(layer_total)]
    routers = []
    for i in range(layer_total):
        at = 2 * layer_total + expert_total * i
        routers.append(jnp.pad(small[:, at : at + expert_total], ((0, 0), (0, 128 - expert_total))))

    expert_weights = []
    for i in range(layer_total):
        if i > 0:
            gathered = lax.all_gather(
                after(layer_shard(i), *expert_weights[-1]), "fsdp", axis=0, tiled=False
            )
            attention_weights.append(
                (
                    gathered[..., :qkv_part].transpose(1, 0, 2, 3).reshape(model_width, qkv_part),
                    gathered[..., qkv_part:].transpose(0, 2, 1, 3).reshape(q_part, model_width),
                )
            )
        gate_up = w_gate_up[i] if i == 0 else after(w_gate_up[i], gathered)
        gate_up = lax.all_gather(gate_up, "ctx", axis=1, tiled=True)
        down = lax.all_gather(after(w_down[i], gate_up), "ctx", axis=1, tiled=True)
        expert_weights.append((gate_up, down))

    residual = wide(hidden_in.reshape(row_count, model_width))
    saved = []
    for i in range(layer_total):
        qkv_weight, out_weight = attention_weights[i]
        normed, root_first = rms_scaled(residual, gains[i][:, 0])
        if i == 0:
            rows = [
                rms_scaled(wide(block), gains[i][:, 0])[0].astype(low) for block in hidden_rows
            ]
        else:
            rows = gather_ctx(normed.astype(low))
        branch, rows_first, qkv, attended, logs = attention_forward(
            rows, qkv_weight, out_weight, qkv_part, tables
        )
        middle = residual + scatter_ctx(branch)
        normed_second, root_second = rms_scaled(middle, gains[i][:, 1])
        parts, kept = [None] * groups, []

        def forward_work(group, pair):
            outs = experts_forward(
                group, pair_total, pair, ids_all, TOP * i, routers[i], own_experts,
                *expert_weights[i], kept,
            )
            parts[2 * group], parts[2 * group + 1] = outs[:2]
            kept[:] = outs[2:]
            return outs[0]

        gather_fsdp(normed_second.astype(low), forward_work)
        rows_second, gate, up, probs = kept
        expert_sum, _ = scatter_fsdp(parts)
        saved.append(
            (
                residual, root_first, rows_first, qkv, attended, logs,
                middle, root_second, rows_second, gate, up, probs, expert_sum,
            )
        )
        residual = middle + expert_sum
    hidden_out = residual.reshape(1, row_count, model_width).astype(low)
    grad = wide(out_grad.reshape(row_count, model_width))
    attention_grads, expert_grads, small_grads = [], [], []
    for i in reversed(range(layer_total)):
        (
            residual, root_first, rows_first, qkv, attended, logs,
            middle, root_second, rows_second, gate, up, probs, expert_sum,
        ) = saved[i]
        qkv_weight, out_weight = attention_weights[i]
        mean_gate = jnp.sum(grad * expert_sum, -1, keepdims=True)
        mean_high = mean_gate.astype(low)
        mean_low = (mean_gate - wide(mean_high)).astype(low)
        sent = jnp.concatenate(
            [grad.astype(low), mean_high, mean_low, jnp.zeros((row_count, 126), low)], -1
        )
        parts, kept = [None] * groups, []

        def backward_work(group, pair):
            outs = experts_backward(
                group, pair_total, pair, probs, gate, up, routers[i], own_experts,
                *expert_weights[i], kept,
            )
            parts[2 * group], parts[2 * group + 1] = outs[:2]
            kept[:] = outs[2:]
            return outs[0]

        gather_fsdp(sent, backward_work)
        grads_second, grad_gate, grad_up, hidden, grad_logits = kept
        grad_second, (gate_grads, up_grads, down_grads) = scatter_fsdp(
            parts,
            (
                lambda start: dot_tn(after(rows_second, start), grad_gate).astype(low),
                lambda start: dot_tn(after(rows_second, start), grad_up).astype(low),
                lambda start: dot_tn(after(hidden, start), grads_second).astype(low),
            ),
        )
        grad_router = dot_tn(rows_second, grad_logits)[:, :expert_total]
        cross = [
            cross_core(gate_grads.reshape(2, 2, model_width // ctx_total, -1)),
            cross_core(up_grads.reshape(2, 2, model_width // ctx_total, -1)),
            cross_core(
                down_grads.reshape(experts_here, 2, 2, FE // ctx_total, model_width).transpose(
                    1, 2, 0, 3, 4
                )
            ),
        ]
        expert_grads.insert(0, [cross_x(part) for part in cross])
        grad_middle, gain_second = rms_back(middle, root_second, gains[i][:, 1], grad_second)
        grad_middle = grad_middle + grad
        back, rows_branch, grad_qkv, gain_first = attention_backward(
            gather_ctx(grad_middle.astype(low)), rows_first, qkv_weight, out_weight, qkv, logs, tables
        )
        gain_first = gain_first[0] / gains[i][:, 0]
        qkv_grads = dot_tn(rows_first, grad_qkv).astype(low)
        out_grads = dot_tn(attended, rows_branch).astype(low)
        grad_first = scatter_ctx(back, qkv_grads, out_grads)
        grad_input, _ = rms_back(residual, root_first, gains[i][:, 0], grad_first)
        grad = grad_input + grad_middle
        qkv_grads = qkv_grads.reshape(ctx_total, groups, share, qkv_part)
        out_grads = out_grads.reshape(groups, share, ctx_total, q_part)
        if i == 0:
            packs = [
                jnp.concatenate(
                    [
                        lax.dynamic_index_in_dim(qkv_grads, members[r], 1, False),
                        lax.dynamic_index_in_dim(out_grads, members[r], 0, False).transpose(1, 0, 2),
                    ],
                    -1,
                ).reshape(ctx_total * share, qkv_part + q_part)
                for r in range(groups)
            ]
            packed = scatter_fsdp(packs)[0].reshape(ctx_total, share, qkv_part + q_part)
        else:
            packed = jnp.concatenate(
                [qkv_grads.transpose(1, 0, 2, 3), out_grads.transpose(0, 2, 1, 3)], -1
            ).reshape(groups * ctx_total, share, qkv_part + q_part)
            packed = lax.psum_scatter(packed, "fsdp", scatter_dimension=0, tiled=True)
        query_blocks = lax.all_to_all(
            packed[..., :qkv_part].astype(low), "ctx", split_axis=0, concat_axis=0, tiled=True
        )
        query_blocks = wide(query_blocks.transpose(1, 0, 2))
        attention_grads.insert(
            0,
            (
                query_blocks[..., :q_part].reshape(share, model_width),
                jnp.concatenate(
                    [
                        query_blocks[..., q_part : q_part + kv_part].reshape(share, kv_width),
                        query_blocks[..., q_part + kv_part :].reshape(share, kv_width),
                    ],
                    -1,
                ),
                wide(packed[..., qkv_part:].transpose(1, 0, 2).reshape(share, model_width)),
            ),
        )
        small_grads.insert(
            0,
            lax.psum_scatter(
                jnp.concatenate([grad_router, gain_first[:, None], gain_second[:, None]], -1),
                both,
                scatter_dimension=0,
                tiled=True,
            ),
        )
    small_sum = jnp.stack(small_grads)
    gate_up_out = [
        jnp.concatenate(
            [part.reshape(model_width // ctx_total, experts_here, FE) for part in grads[:2]], -1
        ).transpose(1, 0, 2)
        for grads in expert_grads
    ]
    return (
        hidden_out,
        grad.reshape(1, row_count, model_width),
        jnp.stack([g[0] for g in attention_grads]),
        jnp.stack([g[1] for g in attention_grads]),
        jnp.stack([g[2] for g in attention_grads]),
        small_sum[..., :expert_total],
        small_sum[..., expert_total:],
        wide(jnp.stack(gate_up_out)),
        wide(jnp.stack([g[2] for g in expert_grads])),
    )


def solution(mesh):
    split = mesh.shape["ctx"] == 4 and mesh.shape["fsdp"] == 8
    return jax.shard_map(
        split_ranks if split else on_device,
        mesh=mesh,
        in_specs=(
            P("fsdp", "ctx", None),
            P(None, ("ctx", "fsdp"), None),
            P(None, ("ctx", "fsdp"), None),
            P(None, ("ctx", "fsdp"), None),
            P(None, ("ctx", "fsdp"), None),
            P(None, ("ctx", "fsdp"), None),
            P(None, "fsdp", "ctx", None),
            P(None, "fsdp", "ctx", None),
            P(None, "fsdp", "ctx", None),
            P("fsdp", "ctx", None),
        ),
        out_specs=(
            P("fsdp", "ctx", None),
            P("fsdp", "ctx", None),
            P(None, ("ctx", "fsdp"), None),
            P(None, ("ctx", "fsdp"), None),
            P(None, ("ctx", "fsdp"), None),
            P(None, ("ctx", "fsdp"), None),
            P(None, ("ctx", "fsdp"), None),
            P(None, "fsdp", "ctx", None),
            P(None, "fsdp", "ctx", None),
        ),
        check_vma=False,
    )
```

```python
import functools
import math

import jax
import jax.numpy as jnp
from jax import lax
from jax.experimental import pallas as pl
from jax.experimental.pallas import tpu as pltpu
from jax.sharding import PartitionSpec as P

HEADS = 24
KV_HEADS = 8
HEAD_DIM = 64
FE = 512
TOP = 8


highest = lax.Precision.HIGHEST
epsilon = 1e-06
rope_base = 10000.0
masked_score = -1e30


def row_positions(first_row, row_total, row_count, shards):
    indices = first_row + jnp.arange(row_total, dtype=jnp.int32)
    shard_of = indices // row_count
    within = indices % row_count
    half_rows = row_count // 2
    return jnp.where(
        within < half_rows,
        shard_of * half_rows + within,
        (2 * shards - 1 - shard_of) * half_rows + within - half_rows,
    )


def rotate(values_in, places, direction):
    half_dim = values_in.shape[-1] // 2
    frequency = rope_base ** (-jnp.arange(half_dim, dtype=jnp.float32) / half_dim)
    angles = places.astype(jnp.float32)[:, None] * frequency[None, :]
    cosine_part = jnp.cos(angles)[:, None, :]
    sine_part = direction * jnp.sin(angles)[:, None, :]
    front_half = values_in[..., :half_dim]
    back_half = values_in[..., half_dim:]
    return jnp.concatenate(
        [
            front_half * cosine_part - back_half * sine_part,
            back_half * cosine_part + front_half * sine_part,
        ],
        -1,
    )


def rms_scaled(residual, gain_vector):
    inverse_root = lax.rsqrt(jnp.mean(residual * residual, -1, keepdims=True) + epsilon)
    return (residual * inverse_root * gain_vector, inverse_root)


def rms_back(residual, inverse_root, gain_vector, grad_normed):
    grad_gain = jnp.sum(grad_normed * residual * inverse_root, 0)
    weighted = gain_vector * grad_normed
    cubed = inverse_root * inverse_root * inverse_root
    grad_residual = inverse_root * weighted - residual * cubed * jnp.mean(
        residual * weighted, -1, keepdims=True
    )
    return (grad_residual, grad_gain)


def route_table(routing_rows, expert_total, row_count, capacity):
    top_count = routing_rows.shape[1]
    chosen_mask = (
        routing_rows[:, :, None] == jnp.arange(expert_total, dtype=jnp.int32)[None, None, :]
    )
    expert_used = jnp.sum(chosen_mask.astype(jnp.int32), 1)
    slot_all = jnp.cumsum(expert_used, 0) - expert_used
    slot_taken = jnp.sum(jnp.where(chosen_mask, slot_all[:, None, :], 0), -1)
    target_slots = routing_rows * capacity + slot_taken
    entry_rows = jnp.full((expert_total * capacity,), row_count * top_count, jnp.int32)
    entry_rows = entry_rows.at[target_slots.reshape(-1)].set(
        jnp.arange(row_count * top_count, dtype=jnp.int32)
    )
    return (chosen_mask, target_slots, entry_rows)


def fold_keys(running, key_piece, queries, query_places, row_count, shards, kv_width):
    piece_rows = key_piece.shape[0]
    step_rows = math.gcd(piece_rows, row_count)
    step_total = piece_rows // step_rows
    blocks_in = key_piece.reshape(step_total, step_rows, key_piece.shape[1])
    heads_kv = queries.shape[1]
    head_size = queries.shape[3]
    score_scale = head_size ** (-0.5)

    def fold_one_step(state_in, inputs):
        block_rows, block_index = inputs
        key_places = row_positions(block_index * step_rows, step_rows, row_count, shards)
        key_rows = block_rows[:, :kv_width].reshape(step_rows, heads_kv, head_size)
        value_rows = block_rows[:, kv_width:].reshape(step_rows, heads_kv, head_size)
        scores = (
            jnp.einsum("qhgd,khd->hgqk", queries, key_rows, preferred_element_type=jnp.float32)
            * score_scale
        )
        visible = query_places[:, None] >= key_places[None, :]
        scores = jnp.where(visible, scores, masked_score)
        old_top, old_total, old_sum = state_in
        new_top = jnp.maximum(old_top, jnp.max(scores, -1))
        shrink = jnp.exp(old_top - new_top)
        weights = jnp.where(visible, jnp.exp(scores - new_top[..., None]), 0.0)
        new_total = old_total * shrink + jnp.sum(weights, -1)
        new_sum = old_sum * shrink[..., None] + jnp.einsum(
            "hgqk,khd->hgqd",
            weights.astype(jnp.bfloat16),
            value_rows,
            preferred_element_type=jnp.float32,
        )
        return ((new_top, new_total, new_sum), None)

    running, _ = lax.scan(
        fold_one_step, running, (blocks_in, jnp.arange(step_total, dtype=jnp.int32))
    )
    return running


def attend_back(
    queries,
    query_places,
    gathered,
    out_exact,
    grad_attended,
    log_total,
    row_count,
    shards,
    kv_width,
):
    heads_kv = queries.shape[1]
    head_size = queries.shape[3]
    score_scale = head_size ** (-0.5)
    delta_rows = jnp.transpose(
        jnp.sum(grad_attended.astype(jnp.float32) * out_exact, -1), (1, 2, 0)
    )
    blocks_in = gathered.reshape(shards, row_count, gathered.shape[1])

    def attend_one_step(grad_queries, inputs):
        block_rows, block_index = inputs
        key_places = row_positions(block_index * row_count, row_count, row_count, shards)
        key_rows = block_rows[:, :kv_width].reshape(row_count, heads_kv, head_size)
        value_rows = block_rows[:, kv_width:].reshape(row_count, heads_kv, head_size)
        scores = (
            jnp.einsum("qhgd,khd->hgqk", queries, key_rows, preferred_element_type=jnp.float32)
            * score_scale
        )
        visible = query_places[:, None] >= key_places[None, :]
        probabilities = jnp.where(visible, jnp.exp(scores - log_total[..., None]), 0.0)
        rounded = probabilities.astype(jnp.bfloat16)
        grad_values = jnp.einsum(
            "hgqk,qhgd->khd", rounded, grad_attended, preferred_element_type=jnp.float32
        )
        grad_probs = jnp.einsum(
            "qhgd,khd->hgqk", grad_attended, value_rows, preferred_element_type=jnp.float32
        )
        grad_scores = (probabilities * (grad_probs - delta_rows[..., None])).astype(jnp.bfloat16)
        grad_queries = grad_queries + score_scale * jnp.einsum(
            "hgqk,khd->qhgd", grad_scores, key_rows, preferred_element_type=jnp.float32
        )
        grad_keys = score_scale * jnp.einsum(
            "hgqk,qhgd->khd", grad_scores, queries, preferred_element_type=jnp.float32
        )
        return (
            grad_queries,
            jnp.concatenate(
                [grad_keys.reshape(row_count, kv_width), grad_values.reshape(row_count, kv_width)],
                -1,
            ),
        )

    start_grad = jnp.zeros(queries.shape, jnp.float32)
    grad_queries, grad_blocks = lax.scan(
        attend_one_step, start_grad, (blocks_in, jnp.arange(shards, dtype=jnp.int32))
    )
    return (grad_queries, grad_blocks.reshape(shards * row_count, gathered.shape[1]))


def on_device(
    hidden_in,
    w_query,
    w_key_value,
    w_output,
    w_router,
    norm_gains,
    w_gate_up,
    w_down,
    expert_ids,
    out_grad,
):
    shards = lax.axis_size("ctx")
    groups = lax.axis_size("fsdp")
    shard_index = lax.axis_index("ctx")
    row_count = hidden_in.shape[1]
    model_width = hidden_in.shape[2]
    layer_total = w_query.shape[0]
    experts_here = w_gate_up.shape[1]
    expert_total = experts_here * groups
    capacity = min(row_count, 3 * row_count * TOP // (2 * expert_total))
    kv_width = w_key_value.shape[2] // 2
    group_size = HEADS // KV_HEADS
    query_places = row_positions(shard_index * row_count, row_count, row_count, shards)
    residual = hidden_in.reshape(row_count, model_width).astype(jnp.float32)
    saved = []
    for layer_index in range(layer_total):
        query_weight, key_value_weight, output_weight, router_weight, gains = (
            lax.all_gather(w_query[layer_index], ("ctx", "fsdp"), axis=0, tiled=True),
            lax.all_gather(w_key_value[layer_index], ("ctx", "fsdp"), axis=0, tiled=True),
            lax.all_gather(w_output[layer_index], ("ctx", "fsdp"), axis=0, tiled=True),
            lax.all_gather(w_router[layer_index], ("ctx", "fsdp"), axis=0, tiled=True),
            lax.all_gather(norm_gains[layer_index], ("ctx", "fsdp"), axis=0, tiled=True),
        )
        gate_up_weight, down_weight = (
            lax.all_gather(w_gate_up[layer_index], "ctx", axis=1, tiled=True),
            lax.all_gather(w_down[layer_index], "ctx", axis=1, tiled=True),
        )
        gain_pair = gains.astype(jnp.float32)
        normed_first, root_first = rms_scaled(residual, gain_pair[:, 0])
        normed_first_low = normed_first.astype(jnp.bfloat16)
        query_raw = jnp.dot(normed_first_low, query_weight, preferred_element_type=jnp.float32)
        key_value_raw = jnp.dot(
            normed_first_low, key_value_weight, preferred_element_type=jnp.float32
        )
        queries = rotate(query_raw.reshape(row_count, HEADS, HEAD_DIM), query_places, 1.0).astype(
            jnp.bfloat16
        )
        queries = queries.reshape(row_count, KV_HEADS, group_size, HEAD_DIM)
        key_turned = rotate(
            key_value_raw[:, :kv_width].reshape(row_count, KV_HEADS, HEAD_DIM), query_places, 1.0
        )
        key_value_low = jnp.concatenate(
            [key_turned.reshape(row_count, kv_width), key_value_raw[:, kv_width:]], -1
        ).astype(jnp.bfloat16)
        start_state = (
            jnp.full((KV_HEADS, group_size, row_count), masked_score, jnp.float32),
            jnp.zeros((KV_HEADS, group_size, row_count), jnp.float32),
            jnp.zeros((KV_HEADS, group_size, row_count, HEAD_DIM), jnp.float32),
        )
        top_score, score_total, accumulated = fold_keys(
            start_state,
            lax.all_gather(key_value_low, "ctx", axis=0, tiled=True),
            queries,
            query_places,
            row_count,
            shards,
            kv_width,
        )
        out_exact = jnp.transpose(accumulated / score_total[..., None], (2, 0, 1, 3))
        log_total = top_score + jnp.log(score_total)
        attended = out_exact.reshape(row_count, model_width).astype(jnp.bfloat16)
        middle = residual + jnp.dot(attended, output_weight, preferred_element_type=jnp.float32)
        normed_second, root_second = rms_scaled(middle, gain_pair[:, 1])
        normed_second_low = normed_second.astype(jnp.bfloat16)
        chosen_mask, target_slots, entry_rows = route_table(
            expert_ids[layer_index].reshape(row_count, TOP), expert_total, row_count, capacity
        )
        padded_rows = jnp.concatenate(
            [normed_second_low, jnp.zeros((1, model_width), jnp.bfloat16)], 0
        )
        send_buffer = padded_rows[jnp.minimum(entry_rows // TOP, row_count)].reshape(
            groups, experts_here, capacity, model_width
        )
        received = lax.all_to_all(send_buffer, "fsdp", split_axis=0, concat_axis=0, tiled=True)
        gate_up = jnp.einsum(
            "serd,edf->serf", received, gate_up_weight, preferred_element_type=jnp.float32
        )
        hidden = (jax.nn.silu(gate_up[..., :FE]) * gate_up[..., FE:]).astype(jnp.bfloat16)
        expert_out = jnp.einsum(
            "serf,efd->serd", hidden, down_weight, preferred_element_type=jnp.float32
        ).astype(jnp.bfloat16)
        returned = lax.all_to_all(
            expert_out, "fsdp", split_axis=0, concat_axis=0, tiled=True
        ).reshape(expert_total * capacity, model_width)
        picked = returned[target_slots]
        logits = jnp.dot(normed_second_low, router_weight, preferred_element_type=jnp.float32)
        chosen_logits = jnp.sum(jnp.where(chosen_mask, logits[:, None, :], 0.0), -1)
        gate_probs = jax.nn.softmax(chosen_logits, axis=-1)
        expert_sum = jnp.sum(gate_probs[..., None] * picked.astype(jnp.float32), 1)
        saved.append(
            (
                residual,
                root_first,
                normed_first_low,
                queries,
                key_value_low,
                out_exact,
                log_total,
                attended,
                middle,
                root_second,
                normed_second_low,
                chosen_mask,
                target_slots,
                entry_rows,
                received,
                gate_up,
                hidden,
                picked,
                gate_probs,
                query_weight,
                key_value_weight,
                output_weight,
                router_weight,
                gain_pair,
                gate_up_weight,
                down_weight,
            )
        )
        residual = middle + expert_sum
    hidden_out = residual.reshape(1, row_count, model_width).astype(jnp.bfloat16)
    grad_residual = out_grad.reshape(row_count, model_width).astype(jnp.float32)
    (
        query_parts,
        key_value_parts,
        output_parts,
        router_parts,
        gain_parts,
        gate_up_parts,
        down_parts,
    ) = ([], [], [], [], [], [], [])
    for layer_index in reversed(range(layer_total)):
        (
            layer_input,
            root_first,
            normed_first_low,
            queries,
            key_value_low,
            out_exact,
            log_total,
            attended,
            middle,
            root_second,
            normed_second_low,
            chosen_mask,
            target_slots,
            entry_rows,
            received,
            gate_up,
            hidden,
            picked,
            gate_probs,
            query_weight,
            key_value_weight,
            output_weight,
            router_weight,
            gain_pair,
            gate_up_weight,
            down_weight,
        ) = saved[layer_index]
        grad_gates = jnp.sum(grad_residual[:, None, :] * picked.astype(jnp.float32), -1)
        grad_leaving = (
            (gate_probs[..., None] * grad_residual[:, None, :])
            .astype(jnp.bfloat16)
            .reshape(row_count * TOP, model_width)
        )
        grad_padded = jnp.concatenate([grad_leaving, jnp.zeros((1, model_width), jnp.bfloat16)], 0)
        grad_send = grad_padded[entry_rows].reshape(groups, experts_here, capacity, model_width)
        grad_received = lax.all_to_all(grad_send, "fsdp", split_axis=0, concat_axis=0, tiled=True)
        grad_hidden = jnp.einsum(
            "serd,efd->serf", grad_received, down_weight, preferred_element_type=jnp.float32
        )
        grad_down_part = jnp.einsum(
            "serf,serd->efd", hidden, grad_received, preferred_element_type=jnp.float32
        )
        gate_part = gate_up[..., :FE]
        up_part = gate_up[..., FE:]
        sigmoid_gate = jax.nn.sigmoid(gate_part)
        grad_gate = grad_hidden * up_part * sigmoid_gate * (1.0 + gate_part * (1.0 - sigmoid_gate))
        grad_up = grad_hidden * gate_part * sigmoid_gate
        grad_gate_up_rows = jnp.concatenate([grad_gate, grad_up], -1).astype(jnp.bfloat16)
        grad_gate_up_part = jnp.einsum(
            "serd,serf->edf", received, grad_gate_up_rows, preferred_element_type=jnp.float32
        )
        grad_entering = jnp.einsum(
            "serf,edf->serd", grad_gate_up_rows, gate_up_weight, preferred_element_type=jnp.float32
        ).astype(jnp.bfloat16)
        grad_returned = lax.all_to_all(
            grad_entering, "fsdp", split_axis=0, concat_axis=0, tiled=True
        ).reshape(expert_total * capacity, model_width)
        grad_normed_second = jnp.sum(grad_returned[target_slots].astype(jnp.float32), 1)
        gate_mean = jnp.sum(gate_probs * grad_gates, -1, keepdims=True)
        grad_chosen = gate_probs * (grad_gates - gate_mean)
        grad_logits = jnp.sum(jnp.where(chosen_mask, grad_chosen[..., None], 0.0), 1)
        grad_router_part = jnp.dot(
            normed_second_low.astype(jnp.float32).T, grad_logits, precision=highest
        )
        grad_normed_second = grad_normed_second + jnp.dot(
            grad_logits, router_weight.astype(jnp.float32).T, precision=highest
        )
        grad_middle, grad_gain_second = rms_back(
            middle, root_second, gain_pair[:, 1], grad_normed_second
        )
        grad_middle = grad_middle + grad_residual
        grad_branch = grad_middle.astype(jnp.bfloat16)
        grad_output_part = jnp.einsum(
            "rd,re->de", attended, grad_branch, preferred_element_type=jnp.float32
        )
        grad_attended = jnp.einsum(
            "re,de->rd", grad_branch, output_weight, preferred_element_type=jnp.float32
        ).astype(jnp.bfloat16)
        grad_attended = grad_attended.reshape(row_count, KV_HEADS, group_size, HEAD_DIM)
        gathered = lax.all_gather(key_value_low, "ctx", axis=0, tiled=True)
        grad_queries, grad_key_value_all = attend_back(
            queries,
            query_places,
            gathered,
            out_exact,
            grad_attended,
            log_total,
            row_count,
            shards,
            kv_width,
        )
        grad_key_value_own = lax.psum_scatter(
            grad_key_value_all.astype(jnp.bfloat16), "ctx", scatter_dimension=0, tiled=True
        ).astype(jnp.float32)
        grad_keys = rotate(
            grad_key_value_own[:, :kv_width].reshape(row_count, KV_HEADS, HEAD_DIM),
            query_places,
            -1.0,
        )
        grad_key_value_low = jnp.concatenate(
            [grad_keys.reshape(row_count, kv_width), grad_key_value_own[:, kv_width:]], -1
        ).astype(jnp.bfloat16)
        grad_query_low = (
            rotate(grad_queries.reshape(row_count, HEADS, HEAD_DIM), query_places, -1.0)
            .reshape(row_count, model_width)
            .astype(jnp.bfloat16)
        )
        grad_query_part = jnp.einsum(
            "rd,re->de", normed_first_low, grad_query_low, preferred_element_type=jnp.float32
        )
        grad_key_value_part = jnp.einsum(
            "rd,re->de", normed_first_low, grad_key_value_low, preferred_element_type=jnp.float32
        )
        grad_normed_first = jnp.einsum(
            "re,de->rd", grad_query_low, query_weight, preferred_element_type=jnp.float32
        ) + jnp.einsum(
            "re,de->rd", grad_key_value_low, key_value_weight, preferred_element_type=jnp.float32
        )
        grad_input, grad_gain_first = rms_back(
            layer_input, root_first, gain_pair[:, 0], grad_normed_first
        )
        grad_residual = grad_input + grad_middle
        grad_gain_part = jnp.stack([grad_gain_first, grad_gain_second], -1)
        query_parts.insert(0, grad_query_part)
        key_value_parts.insert(0, grad_key_value_part)
        output_parts.insert(0, grad_output_part)
        router_parts.insert(0, grad_router_part)
        gain_parts.insert(0, grad_gain_part)
        gate_up_parts.insert(0, grad_gate_up_part)
        down_parts.insert(0, grad_down_part)
    stacked_query = jnp.stack(query_parts, 0)
    stacked_key_value = jnp.stack(key_value_parts, 0)
    stacked_output = jnp.stack(output_parts, 0)
    stacked_router = jnp.stack(router_parts, 0)
    stacked_gains = jnp.stack(gain_parts, 0)
    stacked_gate_up = jnp.stack(gate_up_parts, 0)
    stacked_down = jnp.stack(down_parts, 0)
    stacked_query, stacked_key_value, stacked_output, stacked_router, stacked_gains = (
        lax.psum_scatter(stacked_query, ("ctx", "fsdp"), scatter_dimension=1, tiled=True),
        lax.psum_scatter(stacked_key_value, ("ctx", "fsdp"), scatter_dimension=1, tiled=True),
        lax.psum_scatter(stacked_output, ("ctx", "fsdp"), scatter_dimension=1, tiled=True),
        lax.psum_scatter(stacked_router, ("ctx", "fsdp"), scatter_dimension=1, tiled=True),
        lax.psum_scatter(stacked_gains, ("ctx", "fsdp"), scatter_dimension=1, tiled=True),
    )
    stacked_gate_up, stacked_down = (
        lax.psum_scatter(
            stacked_gate_up.astype(jnp.bfloat16), "ctx", scatter_dimension=2, tiled=True
        ).astype(jnp.float32),
        lax.psum_scatter(
            stacked_down.astype(jnp.bfloat16), "ctx", scatter_dimension=2, tiled=True
        ).astype(jnp.float32),
    )
    grad_hidden = grad_residual.reshape(1, row_count, model_width)
    return (
        hidden_out,
        grad_hidden,
        stacked_query,
        stacked_key_value,
        stacked_output,
        stacked_router,
        stacked_gains,
        stacked_gate_up,
        stacked_down,
    )


NN = (((1,), (0,)), ((), ()))
NT = (((1,), (1,)), ((), ()))
TN = (((0,), (0,)), ((), ()))
FE_STEP = 512
KERNEL_MIB = 58


def mm(a, b, dims=NN):
    return lax.dot_general(a, b, dims, preferred_element_type=jnp.float32)


def whole(shape):
    return pl.BlockSpec(shape, lambda *_: (0,) * len(shape))


def anywhere():
    return pl.BlockSpec(memory_space=pl.ANY)


def kernel_params():
    return pltpu.CompilerParams(vmem_limit_bytes=KERNEL_MIB * 1024 * 1024)


def shaped(shape, dtype=jnp.bfloat16):
    return jax.ShapeDtypeStruct(shape, dtype)


RING = (0, 2, 1, 3)


def bring_expert_weights(bring, ctx_ref, quarters, w_gate_up_here, w_down_here, e, p):
    gate_up, down = quarters[:4], quarters[4:]
    hidden_width = w_down_here.shape[1]
    copies = []
    for r in range(4):
        rows = gate_up[r].shape[1]
        at = pl.ds(pl.multiple_of((ctx_ref[0] ^ r) * rows, rows), rows)
        for side in range(2):
            span = slice(side * hidden_width + p * FE_STEP, side * hidden_width + (p + 1) * FE_STEP)
            copies.append(bring(gate_up[r].at[e, :, span], w_gate_up_here.at[e, at, span]))
    if p == 0:
        for r in range(4):
            rows = down[r].shape[1]
            at = pl.ds(pl.multiple_of((ctx_ref[0] ^ r) * rows, rows), rows)
            copies.append(bring(down[r].at[e], w_down_here.at[e, at, :]))
    return copies


def experts_forward_body(group, first_id, lane_offset, ctx_ref, rows_0, rows_1, ids_in, router_in, own_in, *refs):
    (out_0, out_1, all_rows, all_gate, all_up, all_probs) = refs[-19:-13]
    (
        rows, w_gate_up_here, w_down_here, gate_here, up_here, probs, ring_rows,
        ids, router, own, result, in_sems, out_sems,
    ) = refs[-13:]
    block, width = rows_0.shape
    count = 2 * block
    expert_count, hidden_width = w_down_here.shape[0], w_down_here.shape[1]
    steps = hidden_width // FE_STEP
    incoming = []

    def bring(source, target):
        copy = pltpu.make_async_copy(source, target, in_sems.at[len(incoming)])
        copy.start()
        incoming.append(copy)
        return copy

    span = pl.ds(group * count, count)
    row_copies = [
        bring(rows_0, rows.at[:block]),
        bring(rows_1, rows.at[block:]),
        bring(ids_in.at[span], ids),
        bring(router_in, router),
        bring(own_in, own),
    ]
    weight_copies = []
    for e in range(expert_count):
        for p in range(steps):
            weight_copies.append(
                bring_expert_weights(bring, ctx_ref, refs[:8], w_gate_up_here, w_down_here, e, p)
            )
    outgoing = []

    def send(source, target):
        copy = pltpu.make_async_copy(source, target, out_sems.at[len(outgoing)])
        copy.start()
        outgoing.append(copy)

    for copy in row_copies:
        copy.wait()
    lane = lax.broadcasted_iota(jnp.int32, probs.shape, 1).astype(jnp.float32)
    chosen_ids = ids[...].astype(jnp.float32) + lane_offset
    listed = lane == chosen_ids[:, first_id : first_id + 1]
    for k in range(1, TOP):
        at = first_id + k
        listed = jnp.logical_or(listed, lane == chosen_ids[:, at : at + 1])
    logits = jnp.where(listed, mm(rows[...], router[...]), masked_score)
    weights = jnp.exp(logits - jnp.max(logits, -1, keepdims=True))
    gates = weights / jnp.sum(weights, -1, keepdims=True)
    probs[...] = gates
    part = width // 4
    for place, r in enumerate(RING):
        at = pl.multiple_of((ctx_ref[0] ^ r) * part, part)
        ring_rows[:, place * part : (place + 1) * part] = rows[:, pl.ds(at, part)]
    send(ring_rows, all_rows.at[span])
    send(probs, all_probs.at[span])
    total = jnp.zeros((count, width), jnp.float32)
    for e in range(expert_count):
        chosen = jnp.sum(gates * own[e : e + 1, :], -1, keepdims=True)
        for p in range(steps):
            for copy in weight_copies[e * steps + p]:
                copy.wait()
            lower = slice(p * FE_STEP, (p + 1) * FE_STEP)
            upper = slice(hidden_width + p * FE_STEP, hidden_width + (p + 1) * FE_STEP)
            gate = mm(rows[...], w_gate_up_here[e, :, lower])
            up = mm(rows[...], w_gate_up_here[e, :, upper])
            flat = slice(e * hidden_width + p * FE_STEP, e * hidden_width + (p + 1) * FE_STEP)
            gate_here[:, flat] = gate.astype(jnp.bfloat16)
            up_here[:, flat] = up.astype(jnp.bfloat16)
            hidden = (gate * jax.nn.sigmoid(gate) * up * chosen).astype(jnp.bfloat16)
            total = total + mm(hidden, w_down_here[e, lower, :])
    send(gate_here, all_gate.at[span])
    send(up_here, all_up.at[span])
    result[...] = total.astype(jnp.bfloat16)
    send(result.at[:block], out_0)
    send(result.at[block:], out_1)
    for copy in outgoing:
        copy.wait()


def vmem():
    return pl.BlockSpec(memory_space=pltpu.VMEM)


def smem():
    return pl.BlockSpec(memory_space=pltpu.SMEM)


def expert_shapes(weights):
    (count, rows, width), (_, down_rows, down_width) = weights[0].shape, weights[4].shape
    return (count, 4 * rows, width), (count, 4 * down_rows, down_width)


def expert_cost(count, width, expert_count, hidden_width):
    return pl.CostEstimate(
        flops=6 * count * width * expert_count * hidden_width,
        bytes_accessed=6 * width * expert_count * hidden_width,
        transcendentals=count * expert_count * hidden_width,
    )


def experts_forward(
    group, groups, ctx_ref, rows, ids, first_id, lane_offset, router, own, weights, kept
):
    block, width = rows[0].shape
    count = 2 * block
    gate_up_shape, down_shape = expert_shapes(weights)
    expert_count, hidden_width = down_shape[0], down_shape[1]
    flat = expert_count * hidden_width
    low, f32 = jnp.bfloat16, jnp.float32
    inputs = [ctx_ref, *rows, ids, router, own, *weights, *kept]
    return pl.pallas_call(
        functools.partial(experts_forward_body, group, first_id, lane_offset),
        in_specs=[smem()] + [anywhere()] * (13 + len(kept)),
        out_specs=[anywhere()] * 6,
        out_shape=[
            shaped((block, width)),
            shaped((block, width)),
            shaped((groups * count, width)),
            shaped((groups * count, flat)),
            shaped((groups * count, flat)),
            shaped((groups * count, 128), f32),
        ],
        input_output_aliases={14 + i: 2 + i for i in range(len(kept))},
        scratch_shapes=[
            pltpu.VMEM((count, width), low),
            pltpu.VMEM(gate_up_shape, low),
            pltpu.VMEM(down_shape, low),
            pltpu.VMEM((count, flat), low),
            pltpu.VMEM((count, flat), low),
            pltpu.VMEM((count, 128), f32),
            pltpu.VMEM((count, width), low),
            pltpu.VMEM((count, ids.shape[1]), low),
            pltpu.VMEM(router.shape, low),
            pltpu.VMEM(own.shape, f32),
            pltpu.VMEM((count, width), low),
            pltpu.SemaphoreType.DMA((5 + 8 * flat // FE_STEP + 4 * expert_count,)),
            pltpu.SemaphoreType.DMA((6,)),
        ],
        compiler_params=kernel_params(),
        cost_estimate=expert_cost(count, width, expert_count, hidden_width),
    )(*inputs)


def experts_backward_body(group, ctx_ref, grads_0, grads_1, probs_in, gate_in, up_in, router_in, own_in, *refs):
    out_0, out_1, all_grads, all_grad_gate, all_grad_up, all_hidden, all_logits = refs[-23:-16]
    (
        sent, w_gate_up_here, w_down_here, gates, ups, probs, grads, grad_gates, grad_ups,
        hiddens, logits, router, own, result, in_sems, out_sems,
    ) = refs[-16:]
    block, width = out_0.shape
    count = 2 * block
    expert_count, hidden_width = w_down_here.shape[0], w_down_here.shape[1]
    steps = hidden_width // FE_STEP
    rows_here = pl.ds(group * count, count)
    incoming = []

    def bring(source, target):
        copy = pltpu.make_async_copy(source, target, in_sems.at[len(incoming)])
        copy.start()
        incoming.append(copy)
        return copy

    first_copies = [
        bring(grads_0, sent.at[:block]),
        bring(grads_1, sent.at[block:]),
        bring(probs_in.at[rows_here], probs),
        bring(router_in, router),
        bring(own_in, own),
    ]
    weight_copies = []
    for e in range(expert_count):
        for p in range(steps):
            flat = slice(e * hidden_width + p * FE_STEP, e * hidden_width + (p + 1) * FE_STEP)
            weight_copies.append(
                [
                    bring(gate_in.at[rows_here, flat], gates.at[:, flat]),
                    bring(up_in.at[rows_here, flat], ups.at[:, flat]),
                ]
                + bring_expert_weights(bring, ctx_ref, refs[:8], w_gate_up_here, w_down_here, e, p)
            )
    outgoing = []

    def send(source, target):
        copy = pltpu.make_async_copy(source, target, out_sems.at[len(outgoing)])
        copy.start()
        outgoing.append(copy)

    for copy in first_copies:
        copy.wait()
    grads[...] = sent[:, :width]
    mean = sent[:, width : width + 1].astype(jnp.float32) + sent[:, width + 1 : width + 2].astype(
        jnp.float32
    )
    send(grads, all_grads.at[rows_here])
    total = jnp.zeros((count, width), jnp.float32)
    grad_logits = jnp.zeros(probs.shape, jnp.float32)
    quarter = hidden_width // 4
    for e in range(expert_count):
        mine = own[e : e + 1, :]
        chosen = jnp.sum(probs[...] * mine, -1, keepdims=True)
        dots = jnp.zeros((count, 1), jnp.float32)
        for p in range(steps):
            for copy in weight_copies[e * steps + p]:
                copy.wait()
            lower = slice(p * FE_STEP, (p + 1) * FE_STEP)
            upper = slice(hidden_width + p * FE_STEP, hidden_width + (p + 1) * FE_STEP)
            flat = slice(e * hidden_width + p * FE_STEP, e * hidden_width + (p + 1) * FE_STEP)
            plain = mm(grads[...], w_down_here[e, lower, :], NT)
            gate = gates[:, flat].astype(jnp.float32)
            up = ups[:, flat].astype(jnp.float32)
            sigmoid_gate = jax.nn.sigmoid(gate)
            silu_gate = gate * sigmoid_gate
            hidden = silu_gate * up
            dots = dots + jnp.sum(plain * hidden, -1, keepdims=True)
            hidden = (hidden * chosen).astype(jnp.bfloat16)
            for q in range(FE_STEP // quarter):
                r = ctx_ref[0] ^ (p * (FE_STEP // quarter) + q)
                at = jnp.where(r == 1, 2, jnp.where(r == 2, 1, r)) * expert_count + e
                hiddens[:, pl.ds(pl.multiple_of(at * quarter, quarter), quarter)] = hidden[
                    :, q * quarter : (q + 1) * quarter
                ]
            plain = plain * chosen
            grad_gate = (
                plain * up * sigmoid_gate * (1.0 + gate * (1.0 - sigmoid_gate))
            ).astype(jnp.bfloat16)
            grad_up = (plain * silu_gate).astype(jnp.bfloat16)
            grad_gates[:, flat] = grad_gate
            grad_ups[:, flat] = grad_up
            total = (
                total
                + mm(grad_gate, w_gate_up_here[e, :, lower], NT)
                + mm(grad_up, w_gate_up_here[e, :, upper], NT)
            )
        grad_logits = grad_logits + chosen * (dots - mean) * mine
    send(grad_gates, all_grad_gate.at[rows_here])
    send(grad_ups, all_grad_up.at[rows_here])
    send(hiddens, all_hidden.at[rows_here])
    low_logits = grad_logits.astype(jnp.bfloat16)
    logits[...] = low_logits
    send(logits, all_logits.at[rows_here])
    result[...] = (total + mm(low_logits, router[...], NT)).astype(jnp.bfloat16)
    send(result.at[:block], out_0)
    send(result.at[block:], out_1)
    for copy in outgoing:
        copy.wait()


def experts_backward(
    group, groups, ctx_ref, grads, probs, gate, up, router, own, weights, kept
):
    gate_up_shape, down_shape = expert_shapes(weights)
    expert_count, hidden_width, width = down_shape
    block = grads[0].shape[0]
    count = 2 * block
    flat = expert_count * hidden_width
    low, f32 = jnp.bfloat16, jnp.float32
    inputs = [ctx_ref, *grads, probs, gate, up, router, own, *weights, *kept]
    return pl.pallas_call(
        functools.partial(experts_backward_body, group),
        in_specs=[smem()] + [anywhere()] * (15 + len(kept)),
        out_specs=[anywhere()] * 7,
        out_shape=[
            shaped((block, width)),
            shaped((block, width)),
            shaped((groups * count, width)),
            shaped((groups * count, flat)),
            shaped((groups * count, flat)),
            shaped((groups * count, flat)),
            shaped((groups * count, 128)),
        ],
        input_output_aliases={16 + i: 2 + i for i in range(len(kept))},
        scratch_shapes=[
            pltpu.VMEM((count, grads[0].shape[1]), low),
            pltpu.VMEM(gate_up_shape, low),
            pltpu.VMEM(down_shape, low),
            pltpu.VMEM((count, flat), low),
            pltpu.VMEM((count, flat), low),
            pltpu.VMEM((count, 128), f32),
            pltpu.VMEM((count, width), low),
            pltpu.VMEM((count, flat), low),
            pltpu.VMEM((count, flat), low),
            pltpu.VMEM((count, flat), low),
            pltpu.VMEM((count, 128), low),
            pltpu.VMEM(router.shape, low),
            pltpu.VMEM(own.shape, f32),
            pltpu.VMEM((count, width), low),
            pltpu.SemaphoreType.DMA((5 + 10 * flat // FE_STEP + 4 * expert_count,)),
            pltpu.SemaphoreType.DMA((7,)),
        ],
        compiler_params=kernel_params(),
        cost_estimate=expert_cost(count, width, expert_count, hidden_width),
    )(*inputs)


def turn(block, cosine, sine, lane):
    half = HEAD_DIM // 2
    other = jnp.where(
        lane % HEAD_DIM < half, pltpu.roll(block, 128 - half, 1), pltpu.roll(block, half, 1)
    )
    return block * cosine + other * sine


def row_places(ctx, count, axis):
    half = count // 2
    blocks = []
    for r in range(4):
        c = ctx ^ r
        within = lax.broadcasted_iota(jnp.int32, (count, 1) if axis == 0 else (1, count), axis)
        blocks.append(
            jnp.where(within < half, c * half + within, (7 - c) * half + within - half)
        )
    return jnp.concatenate(blocks, axis)


class Copies:
    def __init__(self, sems):
        self.sems, self.all = sems, []

    def start(self, source, target):
        copy = pltpu.make_async_copy(source, target, self.sems.at[len(self.all)])
        copy.start()
        self.all.append(copy)
        return copy

    def wait(self):
        for copy in self.all:
            copy.wait()


def attention_forward_body(
    ctx_ref, rows_0, rows_1, rows_2, rows_3, w_qkv_in, w_out_in, cosine_in, sine_in,
    out_0, out_1, out_2, out_3, all_rows, qkv_out, attended_out, logs_out,
    rows, w_qkv, w_out, cosine, sine, ring_rows, qkv, attended, logs, result, in_sems, out_sems,
):
    sources, outs = (rows_0, rows_1, rows_2, rows_3), (out_0, out_1, out_2, out_3)
    count, width = rows_0.shape
    q_width, total_width = attended.shape[1], qkv.shape[1]
    kv_width = (total_width - q_width) // 2
    group = HEADS // KV_HEADS
    spans = [slice(r * count, (r + 1) * count) for r in range(4)]
    incoming, outgoing = Copies(in_sems), Copies(out_sems)
    first = [incoming.start(w_qkv_in, w_qkv), incoming.start(rows_0, rows.at[spans[0]])]
    tables = [incoming.start(cosine_in, cosine), incoming.start(sine_in, sine)]
    later = [incoming.start(sources[r], rows.at[spans[r]]) for r in range(1, 4)]
    last = incoming.start(w_out_in, w_out)
    for copy in first + tables:
        copy.wait()
    part = width // 4
    lane = lax.broadcasted_iota(jnp.int32, (count, 128), 1)
    for r in range(4):
        span = spans[r]
        if r:
            later[r - 1].wait()
        raw = mm(rows[span, :], w_qkv[...])
        for j in range((q_width + kv_width) // 128):
            turned = turn(raw[:, 128 * j : 128 * j + 128], cosine[span, :], sine[span, :], lane)
            if 128 * j < q_width:
                turned = turned * HEAD_DIM ** (-0.5)
            qkv[span, 128 * j : 128 * j + 128] = turned.astype(jnp.bfloat16)
        qkv[span, q_width + kv_width :] = raw[:, q_width + kv_width :].astype(jnp.bfloat16)
        for place, distance in enumerate(RING):
            at = pl.multiple_of((ctx_ref[0] ^ distance) * part, part)
            ring_rows[span, place * part : (place + 1) * part] = rows[span, pl.ds(at, part)]
    outgoing.start(qkv, qkv_out)
    outgoing.start(ring_rows, all_rows)
    visible = row_places(ctx_ref[0], count, 0) >= row_places(ctx_ref[0], count, 1)
    for head in range(q_width // HEAD_DIM):
        at, of = head * HEAD_DIM, (head // group) * HEAD_DIM
        queries = qkv[:, at : at + HEAD_DIM]
        keys = qkv[:, q_width + of : q_width + of + HEAD_DIM]
        values = qkv[:, q_width + kv_width + of : q_width + kv_width + of + HEAD_DIM]
        scores = jnp.where(visible, mm(queries, keys, NT), masked_score)
        top = jnp.max(scores, -1, keepdims=True)
        weights = jnp.exp(scores - top)
        total = jnp.sum(weights, -1, keepdims=True)
        logs[:, head : head + 1] = top + jnp.log(total)
        probs = (weights * (1.0 / total)).astype(jnp.bfloat16)
        attended[:, at : at + HEAD_DIM] = mm(probs, values).astype(jnp.bfloat16)
    outgoing.start(logs, logs_out)
    outgoing.start(attended, attended_out)
    last.wait()
    for r in (1, 3, 0, 2):
        result[spans[r], :] = mm(attended[spans[r], :], w_out[...]).astype(jnp.bfloat16)
        outgoing.start(result.at[spans[r]], outs[r])
    outgoing.wait()


def attention_forward(ctx_ref, rows, w_qkv, w_out, total_width, tables):
    count, width = rows[0].shape
    seq = 4 * count
    q_width = w_out.shape[0]
    low, f32 = jnp.bfloat16, jnp.float32
    outs = pl.pallas_call(
        attention_forward_body,
        in_specs=[smem()] + [anywhere()] * 8,
        out_specs=[anywhere()] * 8,
        out_shape=[shaped((count, width))] * 4
        + [
            shaped((seq, width)),
            shaped((seq, total_width)),
            shaped((seq, q_width)),
            shaped((seq, 128), f32),
        ],
        scratch_shapes=[
            pltpu.VMEM((seq, width), low),
            pltpu.VMEM(w_qkv.shape, low),
            pltpu.VMEM(w_out.shape, low),
            pltpu.VMEM((seq, 128), f32),
            pltpu.VMEM((seq, 128), f32),
            pltpu.VMEM((seq, width), low),
            pltpu.VMEM((seq, total_width), low),
            pltpu.VMEM((seq, q_width), low),
            pltpu.VMEM((seq, 128), f32),
            pltpu.VMEM((seq, width), low),
            pltpu.SemaphoreType.DMA((8,)),
            pltpu.SemaphoreType.DMA((8,)),
        ],
        compiler_params=kernel_params(),
        cost_estimate=pl.CostEstimate(
            flops=2 * seq * width * (total_width + q_width) + 4 * seq * seq * q_width,
            bytes_accessed=2 * (seq * width * 2 + width * (total_width + q_width)),
            transcendentals=seq * seq * (q_width // HEAD_DIM),
        ),
    )(ctx_ref, *rows, w_qkv, w_out, *tables)
    return outs[:4], outs[4], outs[5], outs[6], outs[7]


def attention_backward_body(
    ctx_ref, grad_0, grad_1, grad_2, grad_3, rows_in, w_qkv_in, w_out_in, qkv_in, logs_in,
    cosine_in, sine_in,
    out_0, out_1, out_2, out_3, all_grads, grad_qkv_out, gain_out,
    grads, rows, w_qkv, w_out, qkv, logs, cosine, sine, grad_attended, raw, grad_qkv, gain_sum,
    result, in_sems, out_sems,
):
    sources, outs = (grad_0, grad_1, grad_2, grad_3), (out_0, out_1, out_2, out_3)
    count, width = grad_0.shape
    seq = 4 * count
    q_width, total_width = grad_attended.shape[1], qkv.shape[1]
    kv_width = (total_width - q_width) // 2
    group = HEADS // KV_HEADS
    scale = HEAD_DIM ** (-0.5)
    spans = [slice(r * count, (r + 1) * count) for r in range(4)]
    incoming, outgoing = Copies(in_sems), Copies(out_sems)
    first = [incoming.start(w_out_in, w_out)]
    branches = [incoming.start(sources[r], grads.at[spans[r]]) for r in range(4)]
    second = [incoming.start(qkv_in, qkv), incoming.start(logs_in, logs)]
    last = [
        incoming.start(cosine_in, cosine),
        incoming.start(sine_in, sine),
        incoming.start(w_qkv_in, w_qkv),
        incoming.start(rows_in, rows),
    ]
    first[0].wait()
    for r in range(4):
        branches[r].wait()
        grad_attended[spans[r], :] = mm(grads[spans[r], :], w_out[...], NT).astype(jnp.bfloat16)
    outgoing.start(grads, all_grads)
    for copy in second:
        copy.wait()
    visible = row_places(ctx_ref[0], count, 0) >= row_places(ctx_ref[0], count, 1)
    for kv_head in range(kv_width // HEAD_DIM):
        k_at = q_width + kv_head * HEAD_DIM
        v_at = k_at + kv_width
        keys, values = qkv[:, k_at : k_at + HEAD_DIM], qkv[:, v_at : v_at + HEAD_DIM]
        grad_keys = jnp.zeros((HEAD_DIM, seq), jnp.float32)
        grad_values = jnp.zeros((HEAD_DIM, seq), jnp.float32)
        for head in range(kv_head * group, (kv_head + 1) * group):
            at = head * HEAD_DIM
            queries = qkv[:, at : at + HEAD_DIM]
            grad_head = grad_attended[:, at : at + HEAD_DIM]
            scores = mm(queries, keys, NT)
            probs = jnp.where(visible, jnp.exp(scores - logs[:, head : head + 1]), 0.0)
            grad_values += mm(grad_head.T, probs.astype(jnp.bfloat16))
            weighted = probs * mm(grad_head, values, NT)
            grad_scores = (weighted - probs * jnp.sum(weighted, -1, keepdims=True)).astype(
                jnp.bfloat16
            )
            raw[:, at : at + HEAD_DIM] = mm(grad_scores, keys) * scale
            grad_keys += mm(queries.T, grad_scores)
        raw[:, k_at : k_at + HEAD_DIM] = grad_keys.T
        raw[:, v_at : v_at + HEAD_DIM] = grad_values.T
    for copy in last:
        copy.wait()
    gain_sum[...] = jnp.zeros_like(gain_sum)
    lane = lax.broadcasted_iota(jnp.int32, (count, 128), 1)
    part = width // 4
    for r in (1, 3, 0, 2):
        span = spans[r]
        for j in range((q_width + kv_width) // 128):
            columns = slice(128 * j, 128 * j + 128)
            grad_qkv[span, columns] = turn(
                raw[span, columns], cosine[span, :], -sine[span, :], lane
            ).astype(jnp.bfloat16)
        grad_qkv[span, q_width + kv_width :] = raw[span, q_width + kv_width :].astype(jnp.bfloat16)
        result[span, :] = mm(grad_qkv[span, :], w_qkv[...], NT).astype(jnp.bfloat16)
        outgoing.start(result.at[span], outs[r])
    outgoing.start(grad_qkv, grad_qkv_out)
    for r in range(4):
        span = spans[r]
        for place, distance in enumerate(RING):
            at = pl.multiple_of((ctx_ref[0] ^ distance) * part, part)
            spot = slice(place * part, (place + 1) * part)
            gain_sum[:, spot] += jnp.sum(
                result[span, pl.ds(at, part)].astype(jnp.float32)
                * rows[span, spot].astype(jnp.float32),
                0,
                keepdims=True,
            )
    outgoing.start(gain_sum, gain_out)
    outgoing.wait()


def attention_backward(ctx_ref, grads, rows, w_qkv, w_out, qkv, logs, tables):
    count, width = grads[0].shape
    seq = 4 * count
    q_width, total_width = w_out.shape[0], qkv.shape[1]
    low, f32 = jnp.bfloat16, jnp.float32
    outs = pl.pallas_call(
        attention_backward_body,
        in_specs=[smem()] + [anywhere()] * 11,
        out_specs=[anywhere()] * 7,
        out_shape=[shaped((count, width))] * 4
        + [
            shaped((seq, width)),
            shaped((seq, total_width)),
            shaped((1, width), f32),
        ],
        scratch_shapes=[
            pltpu.VMEM((seq, width), low),
            pltpu.VMEM((seq, width), low),
            pltpu.VMEM(w_qkv.shape, low),
            pltpu.VMEM(w_out.shape, low),
            pltpu.VMEM((seq, total_width), low),
            pltpu.VMEM((seq, 128), f32),
            pltpu.VMEM((seq, 128), f32),
            pltpu.VMEM((seq, 128), f32),
            pltpu.VMEM((seq, q_width), low),
            pltpu.VMEM((seq, total_width), f32),
            pltpu.VMEM((seq, total_width), low),
            pltpu.VMEM((1, width), f32),
            pltpu.VMEM((seq, width), low),
            pltpu.SemaphoreType.DMA((11,)),
            pltpu.SemaphoreType.DMA((7,)),
        ],
        compiler_params=kernel_params(),
        cost_estimate=pl.CostEstimate(
            flops=2 * seq * width * (total_width + q_width) + 10 * seq * seq * q_width,
            bytes_accessed=2 * (seq * width * 3 + width * (total_width + q_width)),
            transcendentals=seq * seq * (q_width // HEAD_DIM),
        ),
    )(ctx_ref, *grads, rows, w_qkv, w_out, qkv, logs, *tables)
    return outs[:4], outs[4], outs[5], outs[6]


def place_body(members, shares, *refs):
    shards = [refs[0].at[r] for r in range(8)] if refs[0].shape[0] == 8 else refs[:8]
    outs = refs[1:] if refs[0].shape[0] == 8 else refs[8:]
    front = outs[0].shape[3]
    for r in range(8):
        for c in range(4):
            outs[0][members[8 + c], members[r]] = shards[r][c, :, :front]
        for out in outs[1:]:
            q_part = out.shape[1] // 4
            span = pl.ds(pl.multiple_of(members[r] * shares, shares), shares)
            for j in range(4):
                out[span, j * q_part : (j + 1) * q_part] = shards[r][j, :, front:]


def place(members, shards, front):
    four, share, width = shards[0].shape[-3:]
    outs = [shaped((four, 8, share, front))]
    if width > front:
        outs.append(shaped((8 * share, four * (width - front))))
    return pl.pallas_call(
        lambda members_ref, *refs: place_body(members_ref, share, *refs),
        in_specs=[smem()] + [vmem()] * len(shards),
        out_shape=outs,
        compiler_params=kernel_params(),
    )(members, *shards)


def weight_blocks_body(members, w_query, w_key_value, w_router, gains, *outs):
    layers, share, q_width = w_query.shape
    kv_width = w_key_value.shape[2] // 2
    q_part, kv_part = q_width // 4, kv_width // 4
    experts = w_router.shape[2]
    small = outs[0].shape[1] - 128
    for r in range(4):
        c = members[8 + r]
        outs[r][:, small:] = jnp.zeros((share, 128), jnp.bfloat16)
        for i in range(layers):
            at = i * (q_part + 2 * kv_part)
            outs[r][:, at : at + q_part] = w_query[
                i, :, pl.ds(pl.multiple_of(c * q_part, q_part), q_part)
            ]
            for side in range(2):
                to = at + q_part + side * kv_part
                outs[r][:, to : to + kv_part] = w_key_value[
                    i, :, pl.ds(pl.multiple_of(side * kv_width + c * kv_part, kv_part), kv_part)
                ]
            at = small + i * experts
            outs[r][:, at : at + experts] = w_router[i]
            at = small + layers * experts + 2 * i
            outs[r][:, at : at + 2] = gains[i]


def weight_blocks(members, w_query, w_key_value, w_router, gains):
    layers, share, q_width = w_query.shape
    block = shaped((share, layers * (q_width + w_key_value.shape[2]) // 4 + 128))
    return pl.pallas_call(
        weight_blocks_body,
        in_specs=[smem()] + [vmem()] * 4,
        out_shape=[block] * 4,
        compiler_params=kernel_params(),
    )(members, w_query, w_key_value, w_router, gains)


def pack_shards_body(front, block_0, block_1, block_2, block_3, w_output, ids, *outs):
    blocks, small_rows = (block_0, block_1, block_2, block_3), outs[-1]
    layers, share, width = w_output.shape
    count, top = ids.shape[1:]
    small_rows[...] = jnp.zeros_like(small_rows)
    for r in range(4):
        span = slice(r * share, (r + 1) * share)
        for i in range(layers):
            outs[i][span, :front] = blocks[r][:, i * front : (i + 1) * front]
            outs[i][span, front:] = w_output[i, :, r * (width // 4) : (r + 1) * (width // 4)]
        small_rows[span, :] = blocks[r][:, layers * front :]
    for i in range(layers):
        at = 64 + top * i
        small_rows[:count, at : at + top] = ids[i].astype(jnp.float32).astype(jnp.bfloat16)


def pack_shards(blocks, w_output, ids, front):
    layers, share, width = w_output.shape
    return pl.pallas_call(
        functools.partial(pack_shards_body, front),
        in_specs=[vmem()] * 6,
        out_shape=[shaped((4 * share, front + width // 4))] * layers + [shaped((4 * share, 128))],
        compiler_params=kernel_params(),
    )(*blocks, w_output, ids)


def pack_grads_body(members, qkv, small, out, *parts):
    front, lanes = qkv.shape[3], small.shape[3]
    q_part = out.shape[1] // 4
    share = qkv.shape[2]
    for r in range(8):
        m = members[r]
        part = parts[r] if len(parts) > 1 else parts[0].at[r]
        for place, distance in enumerate(RING):
            part[distance, :, :front] = qkv[place, m]
            part[distance, :, front : front + lanes] = small[place, m]
        for j in range(4):
            part[j, :, front + lanes :] = out[
                pl.ds(pl.multiple_of(m * share, share), share), j * q_part : (j + 1) * q_part
            ]


def pack_grads(members, qkv, small, out, apart):
    four, eight, share, front = qkv.shape
    shape = (four, share, front + small.shape[3] + out.shape[1] // 4)
    return pl.pallas_call(
        pack_grads_body,
        in_specs=[smem()] + [vmem()] * 3,
        out_shape=[shaped(shape)] * 8 if apart else [shaped((eight, *shape))],
        compiler_params=kernel_params(),
    )(members, qkv, small, out)


def finish_attention_body(layers, members, *refs):
    blocks, outs = refs[: 5 * layers], refs[5 * layers :]
    query, key_value, output, router, gains = outs
    experts, lane_count = router.shape[2], layers * router.shape[2]
    q_part, kv_part = query.shape[2] // 4, key_value.shape[2] // 8
    front = q_part + 2 * kv_part
    kv_width = 4 * kv_part
    for i in range(layers):
        lanes = jnp.zeros((query.shape[1], 128), jnp.float32)
        for r in range(4):
            c = members[8 + r]
            block = blocks[5 * i + r]
            query[i, :, pl.ds(pl.multiple_of(c * q_part, q_part), q_part)] = block[
                :, :q_part
            ].astype(jnp.float32)
            for side in range(2):
                at = pl.multiple_of(side * kv_width + c * kv_part, kv_part)
                key_value[i, :, pl.ds(at, kv_part)] = block[
                    :, q_part + side * kv_part : q_part + (side + 1) * kv_part
                ].astype(jnp.float32)
            lanes = lanes + block[:, front:].astype(jnp.float32)
        router[i] = lanes[:, i * experts : (i + 1) * experts]
        gains[i] = lanes[:, lane_count : lane_count + 2]
        own = blocks[5 * i + 4]
        for j in range(4):
            output[i, :, j * q_part : (j + 1) * q_part] = own[j].astype(jnp.float32)


def finish_attention(members, layers, expert_total):
    share, q_part = layers[0][4].shape[1:]
    front = layers[0][0].shape[1] - 128
    total = len(layers)
    f32 = jnp.float32
    return pl.pallas_call(
        functools.partial(finish_attention_body, total),
        in_specs=[smem()] + [vmem()] * (5 * total),
        out_shape=[
            shaped((total, share, 4 * q_part), f32),
            shaped((total, share, 4 * (front - q_part)), f32),
            shaped((total, share, 4 * q_part), f32),
            shaped((total, share, expert_total), f32),
            shaped((total, share, 2), f32),
        ],
        compiler_params=kernel_params(),
    )(members, *[block for layer in layers for block in layer])


def finish_experts_body(
    gate_held, gate_sent, up_held, up_sent, down_held, down_sent, *refs
):
    gate_up, down = refs[-2:]
    half = gate_up.shape[3] // 2
    gate_up[0, 0, :, :half] = gate_held[...].astype(jnp.float32) + gate_sent[...].astype(jnp.float32)
    gate_up[0, 0, :, half:] = up_held[...].astype(jnp.float32) + up_sent[...].astype(jnp.float32)
    down[0, 0] = down_held[...].astype(jnp.float32) + down_sent[...].astype(jnp.float32)


def finish_experts(layer, layers, experts, held, sent, kept):
    rows, flat = sent[0].shape
    half = flat // experts
    down_rows, width = sent[2].shape[0] // experts, sent[2].shape[1]
    gate_spec = pl.BlockSpec((rows, half), lambda e: (0, e))
    down_spec = pl.BlockSpec((down_rows, width), lambda e: (e, 0))
    return pl.pallas_call(
        finish_experts_body,
        grid=(experts,),
        in_specs=[gate_spec] * 4 + [down_spec] * 2 + [anywhere()] * len(kept),
        out_specs=[
            pl.BlockSpec((1, 1, rows, 2 * half), lambda e: (layer, e, 0, 0)),
            pl.BlockSpec((1, 1, down_rows, width), lambda e: (layer, e, 0, 0)),
        ],
        out_shape=[
            shaped((layers, experts, rows, 2 * half), jnp.float32),
            shaped((layers, experts, down_rows, width), jnp.float32),
        ],
        input_output_aliases={6 + i: i for i in range(len(kept))},
        compiler_params=kernel_params(),
    )(held[0], sent[0], held[1], sent[1], held[2], sent[2], *kept)


def rotate_ranks(values_in, axis_name, total, target_of):
    return lax.ppermute(values_in, axis_name, [(i, target_of(i)) for i in range(total)])


def swap_y(values_in):
    return rotate_ranks(values_in, "fsdp", 8, lambda i: i ^ 1)


def move_z(values_in, steps):
    return rotate_ranks(values_in, "fsdp", 8, lambda i: (i + 2 * steps) % 8)


def swap_core(values_in):
    return rotate_ranks(values_in, "ctx", 4, lambda i: i ^ 1)


def swap_x(values_in):
    return rotate_ranks(values_in, "ctx", 4, lambda i: i ^ 2)


def swap_both(values_in):
    return rotate_ranks(values_in, "ctx", 4, lambda i: i ^ 3)


def to_members(blocks):
    return [blocks[0], swap_core(blocks[1]), swap_x(blocks[2]), swap_both(blocks[3])]


def after(value, *others):
    return lax.optimization_barrier((value, *others))[0]


def wide(value):
    return value.astype(jnp.float32)


def fsdp_members(index):
    z, y = index // 2, index % 2
    return [((z + dz) % 4) * 2 + (y ^ dy) for dz in (0, 3, 2, 1) for dy in (0, 1)]


def gather_fsdp(block, work=None):
    below = move_z(block, 1)
    own_mirror = swap_y(block)
    if work is None:
        far = move_z(after(below, own_mirror), 1)
        below_mirror = swap_y(after(below, own_mirror))
        above = move_z(after(block, far, below_mirror), -1)
        far_mirror = swap_y(after(far, below_mirror))
        above_mirror = swap_y(after(above, far_mirror))
        return [block, own_mirror, below, below_mirror, far, far_mirror, above, above_mirror]
    far = move_z(below, 1)
    below_mirror = swap_y(below)
    done = work(0, (after(block, below), own_mirror))
    above = move_z(after(block, far, done), -1)
    far_mirror = swap_y(after(far, done))
    done = work(1, (after(below, far), below_mirror))
    above_mirror = swap_y(after(above, done))
    done = work(2, (after(far, above), far_mirror))
    work(3, (after(above, done), above_mirror))


def scatter_fsdp(parts, beside=None):
    low = jnp.bfloat16
    results = []

    def run(start):
        if beside:
            results.append(beside[len(results)](start))
            return jax.tree.leaves(results[-1])
        return []

    far = (wide(parts[4]) + wide(swap_y(parts[5]))).astype(low)
    from_far = move_z(far, 1)
    above_mirror = swap_y(parts[7])
    done = run(far)
    above = (wide(parts[6]) + wide(above_mirror) + wide(from_far)).astype(low)
    from_below = move_z(after(above, *done), 1)
    below_mirror = swap_y(after(parts[3], above))
    done = run(above)
    below = (wide(parts[2]) + wide(below_mirror)).astype(low)
    from_above = move_z(after(below, *done), -1)
    own_mirror = swap_y(after(parts[1], below))
    done = run(below)
    own = wide(parts[0]) + wide(own_mirror) + wide(from_below)
    return after(own, *done) + wide(from_above), results


def gather_ctx(block):
    across = swap_x(block)
    return [block, swap_core(block), across, swap_core(across)]


def scatter_ctx(parts, *beside):
    across = wide(parts[2]) + wide(swap_core(parts[3]))
    own = wide(parts[0]) + wide(swap_core(parts[1]))
    across = swap_x(across.astype(jnp.bfloat16))
    if beside:
        across = after(across, *beside)
    return own + wide(across)


def split_ranks(
    hidden_in,
    w_query,
    w_key_value,
    w_output,
    w_router,
    norm_gains,
    w_gate_up,
    w_down,
    expert_ids,
    out_grad,
):
    both = ("ctx", "fsdp")
    ctx_total, groups = 4, 8
    ctx_index, group_index = lax.axis_index("ctx"), lax.axis_index("fsdp")
    row_count, model_width = hidden_in.shape[1], hidden_in.shape[2]
    layer_total, share, _ = w_query.shape
    experts_here = w_gate_up.shape[1]
    expert_total = experts_here * groups
    kv_width = w_key_value.shape[2] // 2
    q_part, kv_part = model_width // ctx_total, kv_width // ctx_total
    qkv_part = q_part + 2 * kv_part
    pair_total = groups // 2
    low = jnp.bfloat16
    f32 = jnp.float32

    def dot_tn(a, b):
        return mm(a, b, TN)

    ctx_members = [ctx_index ^ r for r in range(ctx_total)]
    members = jnp.stack([*fsdp_members(group_index), *ctx_members]).astype(jnp.int32)
    natural_members = jnp.stack([*range(groups), *ctx_members]).astype(jnp.int32)
    ring_members = jnp.stack([ctx_members[r] for r in RING])
    ctx_ref = ctx_index.reshape(1).astype(jnp.int32)
    expert_lane = jnp.arange(128, dtype=jnp.int32)
    own_experts = [
        (
            expert_lane[None, :]
            == expert_total * i
            + group_index * experts_here
            + jnp.arange(8, dtype=jnp.int32)[:, None]
        ).astype(f32)
        for i in range(layer_total)
    ]
    gain_lane = expert_total * layer_total

    def ring(vector):
        return jnp.take(vector.reshape(ctx_total, -1), ring_members, axis=0).reshape(-1)

    def gather_experts(i, start):
        return [*gather_ctx(after(w_gate_up[i], start)), *gather_ctx(after(w_down[i], start))]

    places = jnp.concatenate(
        [row_positions((ctx_index ^ r) * row_count, row_count, row_count, ctx_total) for r in range(4)]
    )
    half_dim = HEAD_DIM // 2
    frequency = rope_base ** (-jnp.arange(half_dim, dtype=f32) / half_dim)
    angles = places.astype(f32)[:, None] * frequency[None, :]
    cosine, sine = jnp.cos(angles), jnp.sin(angles)
    tables = (
        jnp.concatenate([cosine] * 4, -1),
        jnp.concatenate([-sine, sine, -sine, sine], -1),
    )

    blocks = to_members(weight_blocks(members, w_query, w_key_value, w_router, norm_gains))
    hidden_rows = gather_ctx(after(hidden_in.reshape(row_count, model_width), blocks[2]))
    *layer_shards, small_rows = pack_shards(
        blocks, w_output, expert_ids.reshape(layer_total, row_count, TOP), qkv_part
    )
    shards = gather_fsdp(layer_shards[0])
    expert_weights = [gather_experts(0, small_rows)]
    small_pair = jnp.stack([small_rows, swap_y(small_rows)])
    small_pair = after(small_pair, shards[2])
    small_all = jnp.concatenate(
        [small_pair, move_z(small_pair, 1), move_z(small_pair, 2), move_z(small_pair, -1)], 0
    )
    small_all = after(small_all, shards[6])
    ids_all = small_all[:, :row_count, 64 : 64 + layer_total * TOP].reshape(groups * row_count, -1)
    small = place(members, [small_all.reshape(groups, ctx_total, share, 128)], 128)[0]
    small = small.reshape(model_width, 128)
    gains = [
        wide(small[:, gain_lane + 2 * i : gain_lane + 2 * i + 2]).T for i in range(layer_total)
    ]
    ring_gains = [ring(gains[i][0]) for i in range(layer_total)]

    def place_layer(members, shards):
        shards = [shard.reshape(-1, ctx_total, share, qkv_part + q_part) for shard in shards]
        if len(shards) > 1:
            shards = [shard[0] for shard in shards]
        qkv_weight, out_weight = place(members, shards, qkv_part)
        return qkv_weight.reshape(model_width, qkv_part), out_weight

    attention_weights = [place_layer(members, shards)]
    later_weights = [
        lax.all_gather(after(shard, shards[7]), "fsdp", axis=0, tiled=False)
        for shard in layer_shards[1:]
    ]

    residual = wide(hidden_in.reshape(row_count, model_width))
    saved = []
    for i in range(layer_total):
        qkv_weight, out_weight = attention_weights[i]
        normed, root_first = rms_scaled(residual, gains[i][0])
        if i == 0:
            rows = [
                rms_scaled(wide(block), gains[i][0])[0].astype(low) for block in hidden_rows
            ]
        else:
            rows = gather_ctx(normed.astype(low))
        branch, rows_first, qkv, attended, logs = attention_forward(
            ctx_ref, rows, qkv_weight, out_weight, qkv_part, tables
        )
        middle = residual + scatter_ctx(branch, *(expert_weights[0] if i == 0 else ()))
        normed_second, root_second = rms_scaled(middle, gains[i][1])
        parts, kept = [None] * groups, []

        def forward_work(group, pair):
            outs = experts_forward(
                group, pair_total, ctx_ref, pair, ids_all, TOP * i, expert_total * i, small,
                own_experts[i], expert_weights[i], kept,
            )
            parts[2 * group], parts[2 * group + 1] = outs[:2]
            kept[:] = outs[2:]
            return outs[0]

        gather_fsdp(normed_second.astype(low), forward_work)
        rows_second, gate, up, probs = kept
        beside = None
        if i + 1 < layer_total:
            gathered = gather_experts(i + 1, parts[0])
            beside = (
                lambda start: [],
                lambda start: place_layer(natural_members, [after(later_weights[i], start)]),
                lambda start: gathered,
            )
        expert_sum, placed = scatter_fsdp(parts, beside)
        if beside:
            attention_weights.append(placed[1])
            expert_weights.append(gathered)
        saved.append(
            (
                residual, root_first, rows_first, qkv, attended, logs,
                middle, root_second, rows_second, gate, up, probs, expert_sum,
            )
        )
        residual = middle + expert_sum
    hidden_out = residual.reshape(1, row_count, model_width).astype(low)
    grad = wide(out_grad.reshape(row_count, model_width))
    attention_grads, expert_grads = [], []

    def finish_layer(i, pairs, start, kept):
        held, sent = [pair[0] for pair in pairs], [pair[1] for pair in pairs]
        held[0] = after(held[0], start)
        return finish_experts(i, layer_total, experts_here, held, sent, kept)

    for i in reversed(range(layer_total)):
        (
            residual, root_first, rows_first, qkv, attended, logs,
            middle, root_second, rows_second, gate, up, probs, expert_sum,
        ) = saved[i]
        qkv_weight, out_weight = attention_weights[i]
        mean_gate = jnp.sum(grad * expert_sum, -1, keepdims=True)
        mean_high = mean_gate.astype(low)
        mean_low = (mean_gate - wide(mean_high)).astype(low)
        lanes = jnp.where(expert_lane == 0, mean_high, jnp.where(expert_lane == 1, mean_low, 0))
        sent = jnp.concatenate([grad.astype(low), lanes.astype(low)], -1)
        parts, kept = [None] * groups, []

        def backward_work(group, pair):
            if i + 1 < layer_total:
                done = (packed, expert_grads[0][0][1], expert_grads[0][1][1], expert_grads[0][2][1])
                pair = (after(pair[0], done[group]), pair[1])
            outs = experts_backward(
                group, pair_total, ctx_ref, pair, probs, gate, up, small, own_experts[i],
                expert_weights[i], kept,
            )
            parts[2 * group], parts[2 * group + 1] = outs[:2]
            kept[:] = outs[2:]
            return outs[0]

        gather_fsdp(sent, backward_work)
        grads_second, grad_gate, grad_up, hidden, grad_logits = kept
        half_width, half_hidden = model_width // 2, hidden.shape[1] // 2

        def to_other_core(start):
            ours = after(rows_second, start)[:, half_width:]
            return [
                swap_core(dot_tn(part, grads).astype(low))
                for part, grads in (
                    (ours, grad_gate),
                    (ours, grad_up),
                    (hidden[:, half_hidden:], grads_second),
                )
            ]

        def add_core(start):
            ours = after(rows_second, start)[:, :half_width]
            return [
                (dot_tn(part, grads) + wide(other)).astype(low)
                for part, grads, other in (
                    (ours, grad_gate, came[0]),
                    (ours, grad_up, came[1]),
                    (hidden[:, :half_hidden], grads_second, came[2]),
                )
            ]

        came = []

        def first_beside(start):
            came[:] = to_other_core(start)
            return came

        def second_beside(start):
            came[:] = add_core(start)
            return came

        def third_beside(start):
            if i + 1 < layer_total:
                return finish_layer(i + 1, expert_grads[0], start, [])
            return []

        grad_second, finished = scatter_fsdp(parts, (first_beside, second_beside, third_beside))
        halves = [(part[: part.shape[0] // 2], part[part.shape[0] // 2 :]) for part in came]
        small_grads = dot_tn(rows_second, grad_logits)
        grad_middle, gain_second = rms_back(middle, root_second, gains[i][1], grad_second)
        grad_middle = grad_middle + grad
        branch_grads = gather_ctx(grad_middle.astype(low))
        crossed = []
        if i == 0:
            crossed.append(swap_x(halves[0][1]))
            crossed.append(swap_x(after(halves[1][1], crossed[0], branch_grads[3])))
            crossed.append(swap_x(after(halves[2][1], crossed[1])))
            rows_first = after(rows_first, crossed[0])
        back, rows_branch, grad_qkv, gain_first = attention_backward(
            ctx_ref, branch_grads, rows_first, qkv_weight, out_weight, qkv,
            logs, tables,
        )
        gain_first = gain_first[0] / ring_gains[i]
        gain_second = ring(gain_second)
        small_grads = jnp.where(
            expert_lane == gain_lane,
            gain_first[:, None],
            jnp.where(expert_lane == gain_lane + 1, gain_second[:, None], small_grads),
        ).astype(low)
        if crossed:
            small_grads = after(small_grads, crossed[1])
        qkv_grads = dot_tn(rows_first, grad_qkv).astype(low)
        out_grads = dot_tn(attended, rows_branch).astype(low)
        grad_first = scatter_ctx(back, qkv_grads, out_grads)
        grad_input, _ = rms_back(residual, root_first, gains[i][0], grad_first)
        grad = grad_input + grad_middle
        crossed = crossed or [swap_x(after(sent_half, grad)) for _, sent_half in halves]
        expert_grads.insert(0, [(half[0], sent) for half, sent in zip(halves, crossed, strict=True)])
        packs = pack_grads(
            members if i == 0 else natural_members,
            qkv_grads.reshape(ctx_total, groups, share, qkv_part),
            small_grads.reshape(ctx_total, groups, share, 128),
            out_grads,
            i == 0,
        )
        shard_shape = (ctx_total, share, qkv_part + 128 + q_part)
        if i == 0:
            flat = (ctx_total * share, shard_shape[2])
            packed = scatter_fsdp([pack.reshape(flat) for pack in packs])[0].astype(low)
        else:
            packed = packs[0].reshape(groups * ctx_total, *shard_shape[1:])
            attention_grads.insert(0, lax.psum_scatter(packed, "fsdp", scatter_dimension=0, tiled=True))
        if i == 0:
            attention_grads.insert(0, packed.reshape(shard_shape))
    front = qkv_part + 128
    blocks = to_members(
        [jnp.concatenate([part[r, :, :front] for part in attention_grads], -1) for r in range(ctx_total)]
    )
    query_out, key_value_out, output_out, router_out, gains_out = finish_attention(
        members,
        [
            [block[:, i * front : (i + 1) * front] for block in blocks] + [part[..., front:]]
            for i, part in enumerate(attention_grads)
        ],
        expert_total,
    )
    outs = finish_layer(0, expert_grads[0], attention_grads[0], finished[2])
    return (
        hidden_out,
        grad.reshape(1, row_count, model_width),
        query_out,
        key_value_out,
        output_out,
        router_out,
        gains_out,
        outs[0],
        outs[1],
    )


def solution(mesh):
    split = mesh.shape["ctx"] == 4 and mesh.shape["fsdp"] == 8
    return jax.shard_map(
        split_ranks if split else on_device,
        mesh=mesh,
        in_specs=(
            P("fsdp", "ctx", None),
            P(None, ("ctx", "fsdp"), None),
            P(None, ("ctx", "fsdp"), None),
            P(None, ("ctx", "fsdp"), None),
            P(None, ("ctx", "fsdp"), None),
            P(None, ("ctx", "fsdp"), None),
            P(None, "fsdp", "ctx", None),
            P(None, "fsdp", "ctx", None),
            P(None, "fsdp", "ctx", None),
            P("fsdp", "ctx", None),
        ),
        out_specs=(
            P("fsdp", "ctx", None),
            P("fsdp", "ctx", None),
            P(None, ("ctx", "fsdp"), None),
            P(None, ("ctx", "fsdp"), None),
            P(None, ("ctx", "fsdp"), None),
            P(None, ("ctx", "fsdp"), None),
            P(None, ("ctx", "fsdp"), None),
            P(None, "fsdp", "ctx", None),
            P(None, "fsdp", "ctx", None),
        ),
        check_vma=False,
    )
```

```python
import functools
import math

import jax
import jax.numpy as jnp
from jax import lax
from jax.experimental import pallas as pl
from jax.experimental.pallas import tpu as pltpu
from jax.sharding import PartitionSpec as P

HEADS = 24
KV_HEADS = 8
HEAD_DIM = 64
FE = 512
TOP = 8


highest = lax.Precision.HIGHEST
epsilon = 1e-06
rope_base = 10000.0
masked_score = -1e30


def row_positions(first_row, row_total, row_count, shards):
    indices = first_row + jnp.arange(row_total, dtype=jnp.int32)
    shard_of = indices // row_count
    within = indices % row_count
    half_rows = row_count // 2
    return jnp.where(
        within < half_rows,
        shard_of * half_rows + within,
        (2 * shards - 1 - shard_of) * half_rows + within - half_rows,
    )


def rotate(values_in, places, direction):
    half_dim = values_in.shape[-1] // 2
    frequency = rope_base ** (-jnp.arange(half_dim, dtype=jnp.float32) / half_dim)
    angles = places.astype(jnp.float32)[:, None] * frequency[None, :]
    cosine_part = jnp.cos(angles)[:, None, :]
    sine_part = direction * jnp.sin(angles)[:, None, :]
    front_half = values_in[..., :half_dim]
    back_half = values_in[..., half_dim:]
    return jnp.concatenate(
        [
            front_half * cosine_part - back_half * sine_part,
            back_half * cosine_part + front_half * sine_part,
        ],
        -1,
    )


def rms_scaled(residual, gain_vector):
    inverse_root = lax.rsqrt(jnp.mean(residual * residual, -1, keepdims=True) + epsilon)
    return (residual * inverse_root * gain_vector, inverse_root)


def rms_back(residual, inverse_root, gain_vector, grad_normed):
    grad_gain = jnp.sum(grad_normed * residual * inverse_root, 0)
    weighted = gain_vector * grad_normed
    cubed = inverse_root * inverse_root * inverse_root
    grad_residual = inverse_root * weighted - residual * cubed * jnp.mean(
        residual * weighted, -1, keepdims=True
    )
    return (grad_residual, grad_gain)


def route_table(routing_rows, expert_total, row_count, capacity):
    top_count = routing_rows.shape[1]
    chosen_mask = (
        routing_rows[:, :, None] == jnp.arange(expert_total, dtype=jnp.int32)[None, None, :]
    )
    expert_used = jnp.sum(chosen_mask.astype(jnp.int32), 1)
    slot_all = jnp.cumsum(expert_used, 0) - expert_used
    slot_taken = jnp.sum(jnp.where(chosen_mask, slot_all[:, None, :], 0), -1)
    target_slots = routing_rows * capacity + slot_taken
    entry_rows = jnp.full((expert_total * capacity,), row_count * top_count, jnp.int32)
    entry_rows = entry_rows.at[target_slots.reshape(-1)].set(
        jnp.arange(row_count * top_count, dtype=jnp.int32)
    )
    return (chosen_mask, target_slots, entry_rows)


def fold_keys(running, key_piece, queries, query_places, row_count, shards, kv_width):
    piece_rows = key_piece.shape[0]
    step_rows = math.gcd(piece_rows, row_count)
    step_total = piece_rows // step_rows
    blocks_in = key_piece.reshape(step_total, step_rows, key_piece.shape[1])
    heads_kv = queries.shape[1]
    head_size = queries.shape[3]
    score_scale = head_size ** (-0.5)

    def fold_one_step(state_in, inputs):
        block_rows, block_index = inputs
        key_places = row_positions(block_index * step_rows, step_rows, row_count, shards)
        key_rows = block_rows[:, :kv_width].reshape(step_rows, heads_kv, head_size)
        value_rows = block_rows[:, kv_width:].reshape(step_rows, heads_kv, head_size)
        scores = (
            jnp.einsum("qhgd,khd->hgqk", queries, key_rows, preferred_element_type=jnp.float32)
            * score_scale
        )
        visible = query_places[:, None] >= key_places[None, :]
        scores = jnp.where(visible, scores, masked_score)
        old_top, old_total, old_sum = state_in
        new_top = jnp.maximum(old_top, jnp.max(scores, -1))
        shrink = jnp.exp(old_top - new_top)
        weights = jnp.where(visible, jnp.exp(scores - new_top[..., None]), 0.0)
        new_total = old_total * shrink + jnp.sum(weights, -1)
        new_sum = old_sum * shrink[..., None] + jnp.einsum(
            "hgqk,khd->hgqd",
            weights.astype(jnp.bfloat16),
            value_rows,
            preferred_element_type=jnp.float32,
        )
        return ((new_top, new_total, new_sum), None)

    running, _ = lax.scan(
        fold_one_step, running, (blocks_in, jnp.arange(step_total, dtype=jnp.int32))
    )
    return running


def attend_back(
    queries,
    query_places,
    gathered,
    out_exact,
    grad_attended,
    log_total,
    row_count,
    shards,
    kv_width,
):
    heads_kv = queries.shape[1]
    head_size = queries.shape[3]
    score_scale = head_size ** (-0.5)
    delta_rows = jnp.transpose(
        jnp.sum(grad_attended.astype(jnp.float32) * out_exact, -1), (1, 2, 0)
    )
    blocks_in = gathered.reshape(shards, row_count, gathered.shape[1])

    def attend_one_step(grad_queries, inputs):
        block_rows, block_index = inputs
        key_places = row_positions(block_index * row_count, row_count, row_count, shards)
        key_rows = block_rows[:, :kv_width].reshape(row_count, heads_kv, head_size)
        value_rows = block_rows[:, kv_width:].reshape(row_count, heads_kv, head_size)
        scores = (
            jnp.einsum("qhgd,khd->hgqk", queries, key_rows, preferred_element_type=jnp.float32)
            * score_scale
        )
        visible = query_places[:, None] >= key_places[None, :]
        probabilities = jnp.where(visible, jnp.exp(scores - log_total[..., None]), 0.0)
        rounded = probabilities.astype(jnp.bfloat16)
        grad_values = jnp.einsum(
            "hgqk,qhgd->khd", rounded, grad_attended, preferred_element_type=jnp.float32
        )
        grad_probs = jnp.einsum(
            "qhgd,khd->hgqk", grad_attended, value_rows, preferred_element_type=jnp.float32
        )
        grad_scores = (probabilities * (grad_probs - delta_rows[..., None])).astype(jnp.bfloat16)
        grad_queries = grad_queries + score_scale * jnp.einsum(
            "hgqk,khd->qhgd", grad_scores, key_rows, preferred_element_type=jnp.float32
        )
        grad_keys = score_scale * jnp.einsum(
            "hgqk,qhgd->khd", grad_scores, queries, preferred_element_type=jnp.float32
        )
        return (
            grad_queries,
            jnp.concatenate(
                [grad_keys.reshape(row_count, kv_width), grad_values.reshape(row_count, kv_width)],
                -1,
            ),
        )

    start_grad = jnp.zeros(queries.shape, jnp.float32)
    grad_queries, grad_blocks = lax.scan(
        attend_one_step, start_grad, (blocks_in, jnp.arange(shards, dtype=jnp.int32))
    )
    return (grad_queries, grad_blocks.reshape(shards * row_count, gathered.shape[1]))


def on_device(
    hidden_in,
    w_query,
    w_key_value,
    w_output,
    w_router,
    norm_gains,
    w_gate_up,
    w_down,
    expert_ids,
    out_grad,
):
    shards = lax.axis_size("ctx")
    groups = lax.axis_size("fsdp")
    shard_index = lax.axis_index("ctx")
    row_count = hidden_in.shape[1]
    model_width = hidden_in.shape[2]
    layer_total = w_query.shape[0]
    experts_here = w_gate_up.shape[1]
    expert_total = experts_here * groups
    capacity = min(row_count, 3 * row_count * TOP // (2 * expert_total))
    kv_width = w_key_value.shape[2] // 2
    group_size = HEADS // KV_HEADS
    query_places = row_positions(shard_index * row_count, row_count, row_count, shards)
    residual = hidden_in.reshape(row_count, model_width).astype(jnp.float32)
    saved = []
    for layer_index in range(layer_total):
        query_weight, key_value_weight, output_weight, router_weight, gains = (
            lax.all_gather(w_query[layer_index], ("ctx", "fsdp"), axis=0, tiled=True),
            lax.all_gather(w_key_value[layer_index], ("ctx", "fsdp"), axis=0, tiled=True),
            lax.all_gather(w_output[layer_index], ("ctx", "fsdp"), axis=0, tiled=True),
            lax.all_gather(w_router[layer_index], ("ctx", "fsdp"), axis=0, tiled=True),
            lax.all_gather(norm_gains[layer_index], ("ctx", "fsdp"), axis=0, tiled=True),
        )
        gate_up_weight, down_weight = (
            lax.all_gather(w_gate_up[layer_index], "ctx", axis=1, tiled=True),
            lax.all_gather(w_down[layer_index], "ctx", axis=1, tiled=True),
        )
        gain_pair = gains.astype(jnp.float32)
        normed_first, root_first = rms_scaled(residual, gain_pair[:, 0])
        normed_first_low = normed_first.astype(jnp.bfloat16)
        query_raw = jnp.dot(normed_first_low, query_weight, preferred_element_type=jnp.float32)
        key_value_raw = jnp.dot(
            normed_first_low, key_value_weight, preferred_element_type=jnp.float32
        )
        queries = rotate(query_raw.reshape(row_count, HEADS, HEAD_DIM), query_places, 1.0).astype(
            jnp.bfloat16
        )
        queries = queries.reshape(row_count, KV_HEADS, group_size, HEAD_DIM)
        key_turned = rotate(
            key_value_raw[:, :kv_width].reshape(row_count, KV_HEADS, HEAD_DIM), query_places, 1.0
        )
        key_value_low = jnp.concatenate(
            [key_turned.reshape(row_count, kv_width), key_value_raw[:, kv_width:]], -1
        ).astype(jnp.bfloat16)
        start_state = (
            jnp.full((KV_HEADS, group_size, row_count), masked_score, jnp.float32),
            jnp.zeros((KV_HEADS, group_size, row_count), jnp.float32),
            jnp.zeros((KV_HEADS, group_size, row_count, HEAD_DIM), jnp.float32),
        )
        top_score, score_total, accumulated = fold_keys(
            start_state,
            lax.all_gather(key_value_low, "ctx", axis=0, tiled=True),
            queries,
            query_places,
            row_count,
            shards,
            kv_width,
        )
        out_exact = jnp.transpose(accumulated / score_total[..., None], (2, 0, 1, 3))
        log_total = top_score + jnp.log(score_total)
        attended = out_exact.reshape(row_count, model_width).astype(jnp.bfloat16)
        middle = residual + jnp.dot(attended, output_weight, preferred_element_type=jnp.float32)
        normed_second, root_second = rms_scaled(middle, gain_pair[:, 1])
        normed_second_low = normed_second.astype(jnp.bfloat16)
        chosen_mask, target_slots, entry_rows = route_table(
            expert_ids[layer_index].reshape(row_count, TOP), expert_total, row_count, capacity
        )
        padded_rows = jnp.concatenate(
            [normed_second_low, jnp.zeros((1, model_width), jnp.bfloat16)], 0
        )
        send_buffer = padded_rows[jnp.minimum(entry_rows // TOP, row_count)].reshape(
            groups, experts_here, capacity, model_width
        )
        received = lax.all_to_all(send_buffer, "fsdp", split_axis=0, concat_axis=0, tiled=True)
        gate_up = jnp.einsum(
            "serd,edf->serf", received, gate_up_weight, preferred_element_type=jnp.float32
        )
        hidden = (jax.nn.silu(gate_up[..., :FE]) * gate_up[..., FE:]).astype(jnp.bfloat16)
        expert_out = jnp.einsum(
            "serf,efd->serd", hidden, down_weight, preferred_element_type=jnp.float32
        ).astype(jnp.bfloat16)
        returned = lax.all_to_all(
            expert_out, "fsdp", split_axis=0, concat_axis=0, tiled=True
        ).reshape(expert_total * capacity, model_width)
        picked = returned[target_slots]
        logits = jnp.dot(normed_second_low, router_weight, preferred_element_type=jnp.float32)
        chosen_logits = jnp.sum(jnp.where(chosen_mask, logits[:, None, :], 0.0), -1)
        gate_probs = jax.nn.softmax(chosen_logits, axis=-1)
        expert_sum = jnp.sum(gate_probs[..., None] * picked.astype(jnp.float32), 1)
        saved.append(
            (
                residual,
                root_first,
                normed_first_low,
                queries,
                key_value_low,
                out_exact,
                log_total,
                attended,
                middle,
                root_second,
                normed_second_low,
                chosen_mask,
                target_slots,
                entry_rows,
                received,
                gate_up,
                hidden,
                picked,
                gate_probs,
                query_weight,
                key_value_weight,
                output_weight,
                router_weight,
                gain_pair,
                gate_up_weight,
                down_weight,
            )
        )
        residual = middle + expert_sum
    hidden_out = residual.reshape(1, row_count, model_width).astype(jnp.bfloat16)
    grad_residual = out_grad.reshape(row_count, model_width).astype(jnp.float32)
    (
        query_parts,
        key_value_parts,
        output_parts,
        router_parts,
        gain_parts,
        gate_up_parts,
        down_parts,
    ) = ([], [], [], [], [], [], [])
    for layer_index in reversed(range(layer_total)):
        (
            layer_input,
            root_first,
            normed_first_low,
            queries,
            key_value_low,
            out_exact,
            log_total,
            attended,
            middle,
            root_second,
            normed_second_low,
            chosen_mask,
            target_slots,
            entry_rows,
            received,
            gate_up,
            hidden,
            picked,
            gate_probs,
            query_weight,
            key_value_weight,
            output_weight,
            router_weight,
            gain_pair,
            gate_up_weight,
            down_weight,
        ) = saved[layer_index]
        grad_gates = jnp.sum(grad_residual[:, None, :] * picked.astype(jnp.float32), -1)
        grad_leaving = (
            (gate_probs[..., None] * grad_residual[:, None, :])
            .astype(jnp.bfloat16)
            .reshape(row_count * TOP, model_width)
        )
        grad_padded = jnp.concatenate([grad_leaving, jnp.zeros((1, model_width), jnp.bfloat16)], 0)
        grad_send = grad_padded[entry_rows].reshape(groups, experts_here, capacity, model_width)
        grad_received = lax.all_to_all(grad_send, "fsdp", split_axis=0, concat_axis=0, tiled=True)
        grad_hidden = jnp.einsum(
            "serd,efd->serf", grad_received, down_weight, preferred_element_type=jnp.float32
        )
        grad_down_part = jnp.einsum(
            "serf,serd->efd", hidden, grad_received, preferred_element_type=jnp.float32
        )
        gate_part = gate_up[..., :FE]
        up_part = gate_up[..., FE:]
        sigmoid_gate = jax.nn.sigmoid(gate_part)
        grad_gate = grad_hidden * up_part * sigmoid_gate * (1.0 + gate_part * (1.0 - sigmoid_gate))
        grad_up = grad_hidden * gate_part * sigmoid_gate
        grad_gate_up_rows = jnp.concatenate([grad_gate, grad_up], -1).astype(jnp.bfloat16)
        grad_gate_up_part = jnp.einsum(
            "serd,serf->edf", received, grad_gate_up_rows, preferred_element_type=jnp.float32
        )
        grad_entering = jnp.einsum(
            "serf,edf->serd", grad_gate_up_rows, gate_up_weight, preferred_element_type=jnp.float32
        ).astype(jnp.bfloat16)
        grad_returned = lax.all_to_all(
            grad_entering, "fsdp", split_axis=0, concat_axis=0, tiled=True
        ).reshape(expert_total * capacity, model_width)
        grad_normed_second = jnp.sum(grad_returned[target_slots].astype(jnp.float32), 1)
        gate_mean = jnp.sum(gate_probs * grad_gates, -1, keepdims=True)
        grad_chosen = gate_probs * (grad_gates - gate_mean)
        grad_logits = jnp.sum(jnp.where(chosen_mask, grad_chosen[..., None], 0.0), 1)
        grad_router_part = jnp.dot(
            normed_second_low.astype(jnp.float32).T, grad_logits, precision=highest
        )
        grad_normed_second = grad_normed_second + jnp.dot(
            grad_logits, router_weight.astype(jnp.float32).T, precision=highest
        )
        grad_middle, grad_gain_second = rms_back(
            middle, root_second, gain_pair[:, 1], grad_normed_second
        )
        grad_middle = grad_middle + grad_residual
        grad_branch = grad_middle.astype(jnp.bfloat16)
        grad_output_part = jnp.einsum(
            "rd,re->de", attended, grad_branch, preferred_element_type=jnp.float32
        )
        grad_attended = jnp.einsum(
            "re,de->rd", grad_branch, output_weight, preferred_element_type=jnp.float32
        ).astype(jnp.bfloat16)
        grad_attended = grad_attended.reshape(row_count, KV_HEADS, group_size, HEAD_DIM)
        gathered = lax.all_gather(key_value_low, "ctx", axis=0, tiled=True)
        grad_queries, grad_key_value_all = attend_back(
            queries,
            query_places,
            gathered,
            out_exact,
            grad_attended,
            log_total,
            row_count,
            shards,
            kv_width,
        )
        grad_key_value_own = lax.psum_scatter(
            grad_key_value_all.astype(jnp.bfloat16), "ctx", scatter_dimension=0, tiled=True
        ).astype(jnp.float32)
        grad_keys = rotate(
            grad_key_value_own[:, :kv_width].reshape(row_count, KV_HEADS, HEAD_DIM),
            query_places,
            -1.0,
        )
        grad_key_value_low = jnp.concatenate(
            [grad_keys.reshape(row_count, kv_width), grad_key_value_own[:, kv_width:]], -1
        ).astype(jnp.bfloat16)
        grad_query_low = (
            rotate(grad_queries.reshape(row_count, HEADS, HEAD_DIM), query_places, -1.0)
            .reshape(row_count, model_width)
            .astype(jnp.bfloat16)
        )
        grad_query_part = jnp.einsum(
            "rd,re->de", normed_first_low, grad_query_low, preferred_element_type=jnp.float32
        )
        grad_key_value_part = jnp.einsum(
            "rd,re->de", normed_first_low, grad_key_value_low, preferred_element_type=jnp.float32
        )
        grad_normed_first = jnp.einsum(
            "re,de->rd", grad_query_low, query_weight, preferred_element_type=jnp.float32
        ) + jnp.einsum(
            "re,de->rd", grad_key_value_low, key_value_weight, preferred_element_type=jnp.float32
        )
        grad_input, grad_gain_first = rms_back(
            layer_input, root_first, gain_pair[:, 0], grad_normed_first
        )
        grad_residual = grad_input + grad_middle
        grad_gain_part = jnp.stack([grad_gain_first, grad_gain_second], -1)
        query_parts.insert(0, grad_query_part)
        key_value_parts.insert(0, grad_key_value_part)
        output_parts.insert(0, grad_output_part)
        router_parts.insert(0, grad_router_part)
        gain_parts.insert(0, grad_gain_part)
        gate_up_parts.insert(0, grad_gate_up_part)
        down_parts.insert(0, grad_down_part)
    stacked_query = jnp.stack(query_parts, 0)
    stacked_key_value = jnp.stack(key_value_parts, 0)
    stacked_output = jnp.stack(output_parts, 0)
    stacked_router = jnp.stack(router_parts, 0)
    stacked_gains = jnp.stack(gain_parts, 0)
    stacked_gate_up = jnp.stack(gate_up_parts, 0)
    stacked_down = jnp.stack(down_parts, 0)
    stacked_query, stacked_key_value, stacked_output, stacked_router, stacked_gains = (
        lax.psum_scatter(stacked_query, ("ctx", "fsdp"), scatter_dimension=1, tiled=True),
        lax.psum_scatter(stacked_key_value, ("ctx", "fsdp"), scatter_dimension=1, tiled=True),
        lax.psum_scatter(stacked_output, ("ctx", "fsdp"), scatter_dimension=1, tiled=True),
        lax.psum_scatter(stacked_router, ("ctx", "fsdp"), scatter_dimension=1, tiled=True),
        lax.psum_scatter(stacked_gains, ("ctx", "fsdp"), scatter_dimension=1, tiled=True),
    )
    stacked_gate_up, stacked_down = (
        lax.psum_scatter(
            stacked_gate_up.astype(jnp.bfloat16), "ctx", scatter_dimension=2, tiled=True
        ).astype(jnp.float32),
        lax.psum_scatter(
            stacked_down.astype(jnp.bfloat16), "ctx", scatter_dimension=2, tiled=True
        ).astype(jnp.float32),
    )
    grad_hidden = grad_residual.reshape(1, row_count, model_width)
    return (
        hidden_out,
        grad_hidden,
        stacked_query,
        stacked_key_value,
        stacked_output,
        stacked_router,
        stacked_gains,
        stacked_gate_up,
        stacked_down,
    )


NN = (((1,), (0,)), ((), ()))
NT = (((1,), (1,)), ((), ()))
TN = (((0,), (0,)), ((), ()))
FE_STEP = 512
KERNEL_MIB = 58


def mm(a, b, dims=NN):
    return lax.dot_general(a, b, dims, preferred_element_type=jnp.float32)


def whole(shape):
    return pl.BlockSpec(shape, lambda *_: (0,) * len(shape))


def anywhere():
    return pl.BlockSpec(memory_space=pl.ANY)


def kernel_params():
    return pltpu.CompilerParams(vmem_limit_bytes=KERNEL_MIB * 1024 * 1024)


def shaped(shape, dtype=jnp.bfloat16):
    return jax.ShapeDtypeStruct(shape, dtype)


RING = (0, 2, 1, 3)


def bring_expert_weights(bring, ctx_ref, weights, w_gate_up_here, w_down_here, e, p):
    hidden_width, width = w_down_here.shape[1:]
    copies = []
    for side in range(2):
        span = slice(side * hidden_width + p * FE_STEP, side * hidden_width + (p + 1) * FE_STEP)
        if len(weights) == 1:
            copies.append(bring(weights[0].at[e, :, span], w_gate_up_here.at[e, :, span]))
            continue
        for r in range(4):
            quarter = weights[4 * e + r]
            rows = quarter.shape[0]
            at = pl.ds(pl.multiple_of((ctx_ref[0] ^ r) * rows, rows), rows)
            copies.append(bring(quarter.at[:, span], w_gate_up_here.at[e, at, span]))
    if p == 0:
        rows, part = hidden_width // 4, width // 3
        for r in range(4):
            if len(weights) > 1:
                at = pl.ds(pl.multiple_of((ctx_ref[0] ^ r) * rows, rows), rows)
                copies.append(bring(weights[-4 + r].at[e], w_down_here.at[e, at, :]))
                continue
            for b in range(3):
                source = slice((3 * r + b) * rows, (3 * r + b + 1) * rows)
                copies.append(
                    bring(
                        weights[0].at[e, source, 2 * hidden_width :],
                        w_down_here.at[e, r * rows : (r + 1) * rows, b * part : (b + 1) * part],
                    )
                )
    return copies


def join_experts(gate_up, down):
    part = down.shape[2] // 3
    return jnp.concatenate(
        [gate_up, jnp.concatenate([down[:, :, b * part : (b + 1) * part] for b in range(3)], 1)], -1
    )


def experts_forward_body(weight_total, group, first_id, lane_offset, ctx_ref, rows_0, rows_1, ids_0, ids_1, router_in, own_in, *refs):
    (out_0, out_1, all_rows, all_gate, all_up, all_probs) = refs[-19:-13]
    (
        rows, w_gate_up_here, w_down_here, gate_here, up_here, probs, ring_rows,
        ids, router, own, result, in_sems, out_sems,
    ) = refs[-13:]
    block, width = rows_0.shape
    count = 2 * block
    expert_count, hidden_width = w_down_here.shape[0], w_down_here.shape[1]
    steps = hidden_width // FE_STEP
    incoming = []

    def bring(source, target):
        copy = pltpu.make_async_copy(source, target, in_sems.at[len(incoming)])
        copy.start()
        incoming.append(copy)
        return copy

    span = pl.ds(group * count, count)
    ids_at = ids_0.shape[1] - 128
    row_copies = [
        bring(rows_0, rows.at[:block]),
        bring(rows_1, rows.at[block:]),
        bring(ids_0.at[:block, ids_at:], ids.at[:block]),
        bring(ids_1.at[:block, ids_at:], ids.at[block:]),
        bring(router_in, router),
        bring(own_in, own),
    ]
    weight_copies = []
    for e in range(expert_count):
        for p in range(steps):
            weight_copies.append(
                bring_expert_weights(bring, ctx_ref, refs[:weight_total], w_gate_up_here, w_down_here, e, p)
            )
    outgoing = []

    def send(source, target):
        copy = pltpu.make_async_copy(source, target, out_sems.at[len(outgoing)])
        copy.start()
        outgoing.append(copy)

    for copy in row_copies:
        copy.wait()
    lane = lax.broadcasted_iota(jnp.int32, probs.shape, 1).astype(jnp.float32)
    chosen_ids = ids[...].astype(jnp.float32) + lane_offset
    listed = lane == chosen_ids[:, first_id : first_id + 1]
    for k in range(1, TOP):
        at = first_id + k
        listed = jnp.logical_or(listed, lane == chosen_ids[:, at : at + 1])
    logits = jnp.where(listed, mm(rows[...], router[...]), masked_score)
    weights = jnp.exp(logits - jnp.max(logits, -1, keepdims=True))
    gates = weights / jnp.sum(weights, -1, keepdims=True)
    probs[...] = gates
    part = width // 4
    for place, r in enumerate(RING):
        at = pl.multiple_of((ctx_ref[0] ^ r) * part, part)
        ring_rows[:, place * part : (place + 1) * part] = rows[:, pl.ds(at, part)]
    send(ring_rows, all_rows.at[span])
    send(probs, all_probs.at[span])
    total = jnp.zeros((count, width), jnp.float32)
    for e in range(expert_count):
        chosen = jnp.sum(gates * own[e : e + 1, :], -1, keepdims=True)
        for p in range(steps):
            for copy in weight_copies[e * steps + p]:
                copy.wait()
            lower = slice(p * FE_STEP, (p + 1) * FE_STEP)
            upper = slice(hidden_width + p * FE_STEP, hidden_width + (p + 1) * FE_STEP)
            gate = mm(rows[...], w_gate_up_here[e, :, lower])
            up = mm(rows[...], w_gate_up_here[e, :, upper])
            flat = slice(e * hidden_width + p * FE_STEP, e * hidden_width + (p + 1) * FE_STEP)
            gate_here[:, flat] = gate.astype(jnp.bfloat16)
            up_here[:, flat] = up.astype(jnp.bfloat16)
            hidden = (gate * jax.nn.sigmoid(gate) * up * chosen).astype(jnp.bfloat16)
            total = total + mm(hidden, w_down_here[e, lower, :])
    send(gate_here, all_gate.at[span])
    send(up_here, all_up.at[span])
    result[...] = total.astype(jnp.bfloat16)
    send(result.at[:block], out_0)
    send(result.at[block:], out_1)
    for copy in outgoing:
        copy.wait()


def vmem():
    return pl.BlockSpec(memory_space=pltpu.VMEM)


def smem():
    return pl.BlockSpec(memory_space=pltpu.SMEM)


def expert_shapes(weights):
    if len(weights) == 1:
        count, width, columns = weights[0].shape
        hidden_width = (columns - width // 3) // 2
    else:
        count, rows, width = weights[-1].shape
        hidden_width = 4 * rows
    return (count, width, 2 * hidden_width), (count, hidden_width, width)


def expert_cost(count, width, expert_count, hidden_width):
    return pl.CostEstimate(
        flops=6 * count * width * expert_count * hidden_width,
        bytes_accessed=6 * width * expert_count * hidden_width,
        transcendentals=count * expert_count * hidden_width,
    )


def experts_forward(
    group, groups, ctx_ref, rows, ids, first_id, lane_offset, router, own, weights, kept
):
    block, width = rows[0].shape
    count = 2 * block
    gate_up_shape, down_shape = expert_shapes(weights)
    expert_count, hidden_width = down_shape[0], down_shape[1]
    flat = expert_count * hidden_width
    low, f32 = jnp.bfloat16, jnp.float32
    inputs = [ctx_ref, *rows, *ids, router, own, *weights, *kept]
    return pl.pallas_call(
        functools.partial(experts_forward_body, len(weights), group, first_id, lane_offset),
        in_specs=[smem()] + [anywhere()] * (6 + len(weights) + len(kept)),
        out_specs=[anywhere()] * 6,
        out_shape=[
            shaped((block, width)),
            shaped((block, width)),
            shaped((groups * count, width)),
            shaped((groups * count, flat)),
            shaped((groups * count, flat)),
            shaped((groups * count, 128), f32),
        ],
        input_output_aliases={7 + len(weights) + i: 2 + i for i in range(len(kept))},
        scratch_shapes=[
            pltpu.VMEM((count, width), low),
            pltpu.VMEM(gate_up_shape, low),
            pltpu.VMEM(down_shape, low),
            pltpu.VMEM((count, flat), low),
            pltpu.VMEM((count, flat), low),
            pltpu.VMEM((count, 128), f32),
            pltpu.VMEM((count, width), low),
            pltpu.VMEM((count, 128), low),
            pltpu.VMEM(router.shape, low),
            pltpu.VMEM(own.shape, f32),
            pltpu.VMEM((count, width), low),
            pltpu.SemaphoreType.DMA((6 + 8 * flat // FE_STEP + 24 * expert_count,)),
            pltpu.SemaphoreType.DMA((6,)),
        ],
        compiler_params=kernel_params(),
        cost_estimate=expert_cost(count, width, expert_count, hidden_width),
    )(*inputs)


def experts_backward_body(weight_total, ring, group, ctx_ref, grads_0, grads_1, probs_in, gate_in, up_in, router_in, own_in, *refs):
    out_0, out_1, all_grads, all_grad_gate, all_grad_up, all_hidden, all_logits = refs[-23:-16]
    (
        sent, w_gate_up_here, w_down_here, gates, ups, probs, grads, grad_gates, grad_ups,
        hiddens, logits, router, own, result, in_sems, out_sems,
    ) = refs[-16:]
    block, width = out_0.shape
    count = 2 * block
    expert_count, hidden_width = w_down_here.shape[0], w_down_here.shape[1]
    steps = hidden_width // FE_STEP
    rows_here = pl.ds(group * count, count)
    incoming = []

    def bring(source, target):
        copy = pltpu.make_async_copy(source, target, in_sems.at[len(incoming)])
        copy.start()
        incoming.append(copy)
        return copy

    first_copies = [
        bring(grads_0, sent.at[:block]),
        bring(grads_1, sent.at[block:]),
        bring(probs_in.at[rows_here], probs),
        bring(router_in, router),
        bring(own_in, own),
    ]
    weight_copies = []
    for e in range(expert_count):
        for p in range(steps):
            flat = slice(e * hidden_width + p * FE_STEP, e * hidden_width + (p + 1) * FE_STEP)
            weight_copies.append(
                [
                    bring(gate_in.at[rows_here, flat], gates.at[:, flat]),
                    bring(up_in.at[rows_here, flat], ups.at[:, flat]),
                ]
                + bring_expert_weights(bring, ctx_ref, refs[:weight_total], w_gate_up_here, w_down_here, e, p)
            )
    outgoing = []

    def send(source, target):
        copy = pltpu.make_async_copy(source, target, out_sems.at[len(outgoing)])
        copy.start()
        outgoing.append(copy)

    for copy in first_copies:
        copy.wait()
    grads[...] = sent[:, :width]
    mean = sent[:, width : width + 1].astype(jnp.float32) + sent[:, width + 1 : width + 2].astype(
        jnp.float32
    )
    send(grads, all_grads.at[rows_here])
    total = jnp.zeros((count, width), jnp.float32)
    grad_logits = jnp.zeros(probs.shape, jnp.float32)
    quarter = hidden_width // 4
    for e in range(expert_count):
        mine = own[e : e + 1, :]
        chosen = jnp.sum(probs[...] * mine, -1, keepdims=True)
        dots = jnp.zeros((count, 1), jnp.float32)
        for p in range(steps):
            for copy in weight_copies[e * steps + p]:
                copy.wait()
            lower = slice(p * FE_STEP, (p + 1) * FE_STEP)
            upper = slice(hidden_width + p * FE_STEP, hidden_width + (p + 1) * FE_STEP)
            flat = slice(e * hidden_width + p * FE_STEP, e * hidden_width + (p + 1) * FE_STEP)
            plain = mm(grads[...], w_down_here[e, lower, :], NT)
            gate = gates[:, flat].astype(jnp.float32)
            up = ups[:, flat].astype(jnp.float32)
            sigmoid_gate = jax.nn.sigmoid(gate)
            silu_gate = gate * sigmoid_gate
            hidden = silu_gate * up
            dots = dots + jnp.sum(plain * hidden, -1, keepdims=True)
            hidden = (hidden * chosen).astype(jnp.bfloat16)
            for q in range(FE_STEP // quarter):
                at = p * (FE_STEP // quarter) + q
                if ring:
                    r = ctx_ref[0] ^ at
                    at = jnp.where(r == 1, 2, jnp.where(r == 2, 1, r))
                at = at * expert_count + e
                hiddens[:, pl.ds(pl.multiple_of(at * quarter, quarter), quarter)] = hidden[
                    :, q * quarter : (q + 1) * quarter
                ]
            plain = plain * chosen
            grad_gate = (
                plain * up * sigmoid_gate * (1.0 + gate * (1.0 - sigmoid_gate))
            ).astype(jnp.bfloat16)
            grad_up = (plain * silu_gate).astype(jnp.bfloat16)
            grad_gates[:, flat] = grad_gate
            grad_ups[:, flat] = grad_up
            total = (
                total
                + mm(grad_gate, w_gate_up_here[e, :, lower], NT)
                + mm(grad_up, w_gate_up_here[e, :, upper], NT)
            )
        grad_logits = grad_logits + chosen * (dots - mean) * mine
    send(grad_gates, all_grad_gate.at[rows_here])
    send(grad_ups, all_grad_up.at[rows_here])
    send(hiddens, all_hidden.at[rows_here])
    low_logits = grad_logits.astype(jnp.bfloat16)
    logits[...] = low_logits
    send(logits, all_logits.at[rows_here])
    result[...] = (total + mm(low_logits, router[...], NT)).astype(jnp.bfloat16)
    send(result.at[:block], out_0)
    send(result.at[block:], out_1)
    for copy in outgoing:
        copy.wait()


def experts_backward(
    group, groups, ctx_ref, grads, probs, gate, up, router, own, weights, kept, ring
):
    gate_up_shape, down_shape = expert_shapes(weights)
    expert_count, hidden_width, width = down_shape
    block = grads[0].shape[0]
    count = 2 * block
    flat = expert_count * hidden_width
    low, f32 = jnp.bfloat16, jnp.float32
    inputs = [ctx_ref, *grads, probs, gate, up, router, own, *weights, *kept]
    return pl.pallas_call(
        functools.partial(experts_backward_body, len(weights), ring, group),
        in_specs=[smem()] + [anywhere()] * (7 + len(weights) + len(kept)),
        out_specs=[anywhere()] * 7,
        out_shape=[
            shaped((block, width)),
            shaped((block, width)),
            shaped((groups * count, width)),
            shaped((groups * count, flat)),
            shaped((groups * count, flat)),
            shaped((groups * count, flat)),
            shaped((groups * count, 128)),
        ],
        input_output_aliases={8 + len(weights) + i: 2 + i for i in range(len(kept))},
        scratch_shapes=[
            pltpu.VMEM((count, grads[0].shape[1]), low),
            pltpu.VMEM(gate_up_shape, low),
            pltpu.VMEM(down_shape, low),
            pltpu.VMEM((count, flat), low),
            pltpu.VMEM((count, flat), low),
            pltpu.VMEM((count, 128), f32),
            pltpu.VMEM((count, width), low),
            pltpu.VMEM((count, flat), low),
            pltpu.VMEM((count, flat), low),
            pltpu.VMEM((count, flat), low),
            pltpu.VMEM((count, 128), low),
            pltpu.VMEM(router.shape, low),
            pltpu.VMEM(own.shape, f32),
            pltpu.VMEM((count, width), low),
            pltpu.SemaphoreType.DMA((5 + 10 * flat // FE_STEP + 24 * expert_count,)),
            pltpu.SemaphoreType.DMA((7,)),
        ],
        compiler_params=kernel_params(),
        cost_estimate=expert_cost(count, width, expert_count, hidden_width),
    )(*inputs)


def turn(block, cosine, sine, lane):
    half = HEAD_DIM // 2
    other = jnp.where(
        lane % HEAD_DIM < half, pltpu.roll(block, 128 - half, 1), pltpu.roll(block, half, 1)
    )
    return block * cosine + other * sine


def row_places(ctx, count, axis):
    half = count // 2
    blocks = []
    for r in range(4):
        c = ctx ^ r
        within = lax.broadcasted_iota(jnp.int32, (count, 1) if axis == 0 else (1, count), axis)
        blocks.append(
            jnp.where(within < half, c * half + within, (7 - c) * half + within - half)
        )
    return jnp.concatenate(blocks, axis)


class Copies:
    def __init__(self, sems):
        self.sems, self.all = sems, []

    def start(self, source, target):
        copy = pltpu.make_async_copy(source, target, self.sems.at[len(self.all)])
        copy.start()
        self.all.append(copy)
        return copy

    def wait(self):
        for copy in self.all:
            copy.wait()


def attention_forward_body(
    ctx_ref, rows_0, rows_1, rows_2, rows_3, w_qkv_in, w_out_in, cosine_in, sine_in,
    out_0, out_1, out_2, out_3, all_rows, qkv_out, attended_out, logs_out,
    rows, w_qkv, w_out, cosine, sine, ring_rows, qkv, attended, logs, result, in_sems, out_sems,
):
    sources, outs = (rows_0, rows_1, rows_2, rows_3), (out_0, out_1, out_2, out_3)
    count, width = rows_0.shape
    q_width, total_width = attended.shape[1], qkv.shape[1]
    kv_width = (total_width - q_width) // 2
    group = HEADS // KV_HEADS
    spans = [slice(r * count, (r + 1) * count) for r in range(4)]
    incoming, outgoing = Copies(in_sems), Copies(out_sems)
    first = [incoming.start(w_qkv_in, w_qkv), incoming.start(rows_0, rows.at[spans[0]])]
    tables = [incoming.start(cosine_in, cosine), incoming.start(sine_in, sine)]
    later = [incoming.start(sources[r], rows.at[spans[r]]) for r in range(1, 4)]
    last = incoming.start(w_out_in, w_out)
    for copy in first + tables:
        copy.wait()
    part = width // 4
    lane = lax.broadcasted_iota(jnp.int32, (count, 128), 1)
    for r in range(4):
        span = spans[r]
        if r:
            later[r - 1].wait()
        raw = mm(rows[span, :], w_qkv[...])
        for j in range((q_width + kv_width) // 128):
            turned = turn(raw[:, 128 * j : 128 * j + 128], cosine[span, :], sine[span, :], lane)
            if 128 * j < q_width:
                turned = turned * HEAD_DIM ** (-0.5)
            qkv[span, 128 * j : 128 * j + 128] = turned.astype(jnp.bfloat16)
        qkv[span, q_width + kv_width :] = raw[:, q_width + kv_width :].astype(jnp.bfloat16)
        for place, distance in enumerate(RING):
            at = pl.multiple_of((ctx_ref[0] ^ distance) * part, part)
            ring_rows[span, place * part : (place + 1) * part] = rows[span, pl.ds(at, part)]
    outgoing.start(qkv, qkv_out)
    outgoing.start(ring_rows, all_rows)
    visible = row_places(ctx_ref[0], count, 0) >= row_places(ctx_ref[0], count, 1)
    for head in range(q_width // HEAD_DIM):
        at, of = head * HEAD_DIM, (head // group) * HEAD_DIM
        queries = qkv[:, at : at + HEAD_DIM]
        keys = qkv[:, q_width + of : q_width + of + HEAD_DIM]
        values = qkv[:, q_width + kv_width + of : q_width + kv_width + of + HEAD_DIM]
        scores = jnp.where(visible, mm(queries, keys, NT), masked_score)
        top = jnp.max(scores, -1, keepdims=True)
        weights = jnp.exp(scores - top)
        total = jnp.sum(weights, -1, keepdims=True)
        logs[:, head : head + 1] = top + jnp.log(total)
        probs = (weights * (1.0 / total)).astype(jnp.bfloat16)
        attended[:, at : at + HEAD_DIM] = mm(probs, values).astype(jnp.bfloat16)
    outgoing.start(logs, logs_out)
    outgoing.start(attended, attended_out)
    last.wait()
    for r in (1, 3, 0, 2):
        result[spans[r], :] = mm(attended[spans[r], :], w_out[...]).astype(jnp.bfloat16)
        outgoing.start(result.at[spans[r]], outs[r])
    outgoing.wait()


def attention_forward(ctx_ref, rows, w_qkv, w_out, total_width, tables):
    count, width = rows[0].shape
    seq = 4 * count
    q_width = w_out.shape[0]
    low, f32 = jnp.bfloat16, jnp.float32
    outs = pl.pallas_call(
        attention_forward_body,
        in_specs=[smem()] + [anywhere()] * 8,
        out_specs=[anywhere()] * 8,
        out_shape=[shaped((count, width))] * 4
        + [
            shaped((seq, width)),
            shaped((seq, total_width)),
            shaped((seq, q_width)),
            shaped((seq, 128), f32),
        ],
        scratch_shapes=[
            pltpu.VMEM((seq, width), low),
            pltpu.VMEM(w_qkv.shape, low),
            pltpu.VMEM(w_out.shape, low),
            pltpu.VMEM((seq, 128), f32),
            pltpu.VMEM((seq, 128), f32),
            pltpu.VMEM((seq, width), low),
            pltpu.VMEM((seq, total_width), low),
            pltpu.VMEM((seq, q_width), low),
            pltpu.VMEM((seq, 128), f32),
            pltpu.VMEM((seq, width), low),
            pltpu.SemaphoreType.DMA((8,)),
            pltpu.SemaphoreType.DMA((8,)),
        ],
        compiler_params=kernel_params(),
        cost_estimate=pl.CostEstimate(
            flops=2 * seq * width * (total_width + q_width) + 4 * seq * seq * q_width,
            bytes_accessed=2 * (seq * width * 2 + width * (total_width + q_width)),
            transcendentals=seq * seq * (q_width // HEAD_DIM),
        ),
    )(ctx_ref, *rows, w_qkv, w_out, *tables)
    return outs[:4], outs[4], outs[5], outs[6], outs[7]


def attention_backward_body(
    ctx_ref, grad_0, grad_1, grad_2, grad_3, rows_in, w_qkv_in, w_out_in, qkv_in, logs_in,
    cosine_in, sine_in,
    out_0, out_1, out_2, out_3, all_grads, grad_qkv_out, gain_out,
    grads, rows, w_qkv, w_out, qkv, logs, cosine, sine, grad_attended, raw, grad_qkv, gain_sum,
    result, in_sems, out_sems,
):
    sources, outs = (grad_0, grad_1, grad_2, grad_3), (out_0, out_1, out_2, out_3)
    count, width = grad_0.shape
    seq = 4 * count
    q_width, total_width = grad_attended.shape[1], qkv.shape[1]
    kv_width = (total_width - q_width) // 2
    group = HEADS // KV_HEADS
    scale = HEAD_DIM ** (-0.5)
    spans = [slice(r * count, (r + 1) * count) for r in range(4)]
    incoming, outgoing = Copies(in_sems), Copies(out_sems)
    first = [incoming.start(w_out_in, w_out)]
    branches = [incoming.start(sources[r], grads.at[spans[r]]) for r in range(4)]
    second = [incoming.start(qkv_in, qkv), incoming.start(logs_in, logs)]
    last = [
        incoming.start(cosine_in, cosine),
        incoming.start(sine_in, sine),
        incoming.start(w_qkv_in, w_qkv),
        incoming.start(rows_in, rows),
    ]
    first[0].wait()
    for r in range(4):
        branches[r].wait()
        grad_attended[spans[r], :] = mm(grads[spans[r], :], w_out[...], NT).astype(jnp.bfloat16)
    outgoing.start(grads, all_grads)
    for copy in second:
        copy.wait()
    visible = row_places(ctx_ref[0], count, 0) >= row_places(ctx_ref[0], count, 1)
    for kv_head in range(kv_width // HEAD_DIM):
        k_at = q_width + kv_head * HEAD_DIM
        v_at = k_at + kv_width
        keys, values = qkv[:, k_at : k_at + HEAD_DIM], qkv[:, v_at : v_at + HEAD_DIM]
        grad_keys = jnp.zeros((HEAD_DIM, seq), jnp.float32)
        grad_values = jnp.zeros((HEAD_DIM, seq), jnp.float32)
        for head in range(kv_head * group, (kv_head + 1) * group):
            at = head * HEAD_DIM
            queries = qkv[:, at : at + HEAD_DIM]
            grad_head = grad_attended[:, at : at + HEAD_DIM]
            scores = mm(queries, keys, NT)
            probs = jnp.where(visible, jnp.exp(scores - logs[:, head : head + 1]), 0.0)
            grad_values += mm(grad_head.T, probs.astype(jnp.bfloat16))
            weighted = probs * mm(grad_head, values, NT)
            grad_scores = (weighted - probs * jnp.sum(weighted, -1, keepdims=True)).astype(
                jnp.bfloat16
            )
            raw[:, at : at + HEAD_DIM] = mm(grad_scores, keys) * scale
            grad_keys += mm(queries.T, grad_scores)
        raw[:, k_at : k_at + HEAD_DIM] = grad_keys.T
        raw[:, v_at : v_at + HEAD_DIM] = grad_values.T
    for copy in last:
        copy.wait()
    gain_sum[...] = jnp.zeros_like(gain_sum)
    lane = lax.broadcasted_iota(jnp.int32, (count, 128), 1)
    part = width // 4
    for r in (1, 3, 0, 2):
        span = spans[r]
        for j in range((q_width + kv_width) // 128):
            columns = slice(128 * j, 128 * j + 128)
            grad_qkv[span, columns] = turn(
                raw[span, columns], cosine[span, :], -sine[span, :], lane
            ).astype(jnp.bfloat16)
        grad_qkv[span, q_width + kv_width :] = raw[span, q_width + kv_width :].astype(jnp.bfloat16)
        result[span, :] = mm(grad_qkv[span, :], w_qkv[...], NT).astype(jnp.bfloat16)
        outgoing.start(result.at[span], outs[r])
    outgoing.start(grad_qkv, grad_qkv_out)
    for r in range(4):
        span = spans[r]
        for place, distance in enumerate(RING):
            at = pl.multiple_of((ctx_ref[0] ^ distance) * part, part)
            spot = slice(place * part, (place + 1) * part)
            gain_sum[:, spot] += jnp.sum(
                result[span, pl.ds(at, part)].astype(jnp.float32)
                * rows[span, spot].astype(jnp.float32),
                0,
                keepdims=True,
            )
    outgoing.start(gain_sum, gain_out)
    outgoing.wait()


def attention_backward(ctx_ref, grads, rows, w_qkv, w_out, qkv, logs, tables):
    count, width = grads[0].shape
    seq = 4 * count
    q_width, total_width = w_out.shape[0], qkv.shape[1]
    low, f32 = jnp.bfloat16, jnp.float32
    outs = pl.pallas_call(
        attention_backward_body,
        in_specs=[smem()] + [anywhere()] * 11,
        out_specs=[anywhere()] * 7,
        out_shape=[shaped((count, width))] * 4
        + [
            shaped((seq, width)),
            shaped((seq, total_width)),
            shaped((1, width), f32),
        ],
        scratch_shapes=[
            pltpu.VMEM((seq, width), low),
            pltpu.VMEM((seq, width), low),
            pltpu.VMEM(w_qkv.shape, low),
            pltpu.VMEM(w_out.shape, low),
            pltpu.VMEM((seq, total_width), low),
            pltpu.VMEM((seq, 128), f32),
            pltpu.VMEM((seq, 128), f32),
            pltpu.VMEM((seq, 128), f32),
            pltpu.VMEM((seq, q_width), low),
            pltpu.VMEM((seq, total_width), f32),
            pltpu.VMEM((seq, total_width), low),
            pltpu.VMEM((1, width), f32),
            pltpu.VMEM((seq, width), low),
            pltpu.SemaphoreType.DMA((11,)),
            pltpu.SemaphoreType.DMA((7,)),
        ],
        compiler_params=kernel_params(),
        cost_estimate=pl.CostEstimate(
            flops=2 * seq * width * (total_width + q_width) + 10 * seq * seq * q_width,
            bytes_accessed=2 * (seq * width * 3 + width * (total_width + q_width)),
            transcendentals=seq * seq * (q_width // HEAD_DIM),
        ),
    )(ctx_ref, *grads, rows, w_qkv, w_out, qkv, logs, *tables)
    return outs[:4], outs[4], outs[5], outs[6]


def place_body(members, share, first, *refs):
    shards, outs = refs[:8], refs[8:]
    front = outs[0].shape[3]
    for r in range(8):
        for c in range(4):
            outs[0][members[8 + c], members[r]] = shards[r][c, :, first : first + front]
        for out in outs[1:]:
            q_part = out.shape[1] // 4
            span = pl.ds(pl.multiple_of(members[r] * share, share), share)
            for j in range(4):
                out[span, j * q_part : (j + 1) * q_part] = shards[r][
                    j, :, first + front : first + front + q_part
                ]


def place(members, shards, first, front, rest):
    four, share, width = shards[0].shape
    outs = [shaped((four, 8, share, front))]
    if rest:
        outs.append(shaped((8 * share, four * rest)))
    return pl.pallas_call(
        lambda members_ref, *refs: place_body(members_ref, share, first, *refs),
        in_specs=[smem()] + [vmem()] * 8,
        out_shape=outs,
        compiler_params=kernel_params(),
    )(members, *shards)


def turned(block):
    return block.astype(jnp.float32).T.astype(jnp.bfloat16)


def weight_blocks_body(members, w_query, w_key_value, w_router, gains, *outs):
    layers, share, q_width = w_query.shape
    kv_width = w_key_value.shape[2] // 2
    q_part, kv_part = q_width // 4, kv_width // 4
    experts = w_router.shape[1]
    small = outs[0].shape[1] - 128
    for r in range(4):
        c = members[8 + r]
        outs[r][:, small:] = jnp.zeros((share, 128), jnp.bfloat16)
        for i in range(layers):
            at = i * (q_part + 2 * kv_part)
            outs[r][:, at : at + q_part] = w_query[
                i, :, pl.ds(pl.multiple_of(c * q_part, q_part), q_part)
            ]
            for side in range(2):
                to = at + q_part + side * kv_part
                outs[r][:, to : to + kv_part] = w_key_value[
                    i, :, pl.ds(pl.multiple_of(side * kv_width + c * kv_part, kv_part), kv_part)
                ]
            at = small + i * experts
            outs[r][:, at : at + experts] = turned(w_router[i])
            at = small + layers * experts + 2 * i
            outs[r][:, at : at + 2] = turned(gains[i])


def weight_blocks(members, w_query, w_key_value, w_router, gains):
    layers, share, q_width = w_query.shape
    block = shaped((share, layers * (q_width + w_key_value.shape[2]) // 4 + 128))
    return pl.pallas_call(
        weight_blocks_body,
        in_specs=[smem()] + [vmem()] * 4,
        out_shape=[block] * 4,
        compiler_params=kernel_params(),
    )(members, w_query, w_key_value, w_router, gains)


def pack_shards_body(front, block_0, block_1, block_2, block_3, w_output, ids, shard):
    blocks = (block_0, block_1, block_2, block_3)
    layers, share, width = w_output.shape
    part = front + width // 4
    top, count = ids.shape[1:]
    for r in range(4):
        span = slice(r * share, (r + 1) * share)
        for i in range(layers):
            shard[span, i * part : i * part + front] = blocks[r][:, i * front : (i + 1) * front]
            shard[span, i * part + front : (i + 1) * part] = w_output[
                i, :, r * (width // 4) : (r + 1) * (width // 4)
            ]
        shard[span, layers * part :] = blocks[r][:, layers * front :]
    for i in range(layers):
        at = layers * part + 64 + top * i
        shard[:count, at : at + top] = turned(ids[i])


def pack_shards(blocks, w_output, ids, front):
    layers, share, width = w_output.shape
    return pl.pallas_call(
        functools.partial(pack_shards_body, front),
        in_specs=[vmem()] * 6,
        out_shape=shaped((4 * share, layers * (front + width // 4) + 128)),
        compiler_params=kernel_params(),
    )(*blocks, w_output, ids)


def pack_grads_body(members, qkv, small, out, *parts):
    front, lanes = qkv.shape[3], small.shape[3]
    q_part = out.shape[1] // 4
    share = qkv.shape[2]
    for r in range(8):
        m = members[r]
        part = parts[r] if len(parts) > 1 else parts[0].at[r]
        for place, distance in enumerate(RING):
            part[distance, :, :front] = qkv[place, m]
            part[distance, :, front : front + lanes] = small[place, m]
        for j in range(4):
            part[j, :, front + lanes :] = out[
                pl.ds(pl.multiple_of(m * share, share), share), j * q_part : (j + 1) * q_part
            ]


def pack_grads(members, qkv, small, out, apart):
    four, eight, share, front = qkv.shape
    shape = (four, share, front + small.shape[3] + out.shape[1] // 4)
    return pl.pallas_call(
        pack_grads_body,
        in_specs=[smem()] + [vmem()] * 3,
        out_shape=[shaped(shape)] * 8 if apart else [shaped((eight, *shape))],
        compiler_params=kernel_params(),
    )(members, qkv, small, out)


def finish_attention_body(layers, members, *refs):
    blocks, outs = refs[: 5 * layers], refs[5 * layers :]
    query, key_value, output, router, gains = outs
    experts, lane_count = router.shape[1], layers * router.shape[1]
    q_part, kv_part = query.shape[2] // 4, key_value.shape[2] // 8
    front = q_part + 2 * kv_part
    kv_width = 4 * kv_part
    for i in range(layers):
        lanes = jnp.zeros((query.shape[1], 128), jnp.float32)
        for r in range(4):
            c = members[8 + r]
            block = blocks[5 * i + r]
            query[i, :, pl.ds(pl.multiple_of(c * q_part, q_part), q_part)] = block[
                :, :q_part
            ].astype(jnp.float32)
            for side in range(2):
                at = pl.multiple_of(side * kv_width + c * kv_part, kv_part)
                key_value[i, :, pl.ds(at, kv_part)] = block[
                    :, q_part + side * kv_part : q_part + (side + 1) * kv_part
                ].astype(jnp.float32)
            lanes = lanes + block[:, front:].astype(jnp.float32)
        lanes = lanes.T
        router[i] = lanes[i * experts : (i + 1) * experts, :]
        gains[i] = lanes[lane_count : lane_count + 2, :]
        own = blocks[5 * i + 4]
        for j in range(4):
            output[i, :, j * q_part : (j + 1) * q_part] = own[j].astype(jnp.float32)


def finish_attention(members, layers, expert_total):
    share, q_part = layers[0][4].shape[1:]
    front = layers[0][0].shape[1] - 128
    total = len(layers)
    f32 = jnp.float32
    return pl.pallas_call(
        functools.partial(finish_attention_body, total),
        in_specs=[smem()] + [vmem()] * (5 * total),
        out_shape=[
            shaped((total, share, 4 * q_part), f32),
            shaped((total, share, 4 * (front - q_part)), f32),
            shaped((total, share, 4 * q_part), f32),
            shaped((total, expert_total, share), f32),
            shaped((total, 2, share), f32),
        ],
        compiler_params=kernel_params(),
    )(members, *[block for layer in layers for block in layer])


def finish_experts_body(down_total, *refs):
    gate_up, down = refs[-2:]
    half = gate_up.shape[3] // 2

    def total(first, count):
        values = [ref[...].astype(jnp.float32) for ref in refs[first : first + count]]
        return sum(values[1:], values[0])

    gate_up[0, 0, :, :half] = total(0, 2)
    gate_up[0, 0, :, half:] = total(2, 2)
    down[0, 0] = total(4, down_total)


def finish_experts(layer, layers, experts, held, sent, kept):
    rows, flat = held[0].shape
    half = flat // experts
    down_rows, width = held[2].shape[0] // experts, held[2].shape[1]
    gate_spec = pl.BlockSpec((rows, half), lambda e: (0, e))
    down_spec = pl.BlockSpec((down_rows, width), lambda e: (e, 0))
    downs = [part for part in (held[2], sent[2]) if part is not None]
    inputs = [held[0], sent[0], held[1], sent[1], *downs]
    return pl.pallas_call(
        functools.partial(finish_experts_body, len(downs)),
        grid=(experts,),
        in_specs=[gate_spec] * 4 + [down_spec] * len(downs) + [anywhere()] * len(kept),
        out_specs=[
            pl.BlockSpec((1, 1, rows, 2 * half), lambda e: (layer, e, 0, 0)),
            pl.BlockSpec((1, 1, down_rows, width), lambda e: (layer, e, 0, 0)),
        ],
        out_shape=[
            shaped((layers, experts, rows, 2 * half), jnp.float32),
            shaped((layers, experts, down_rows, width), jnp.float32),
        ],
        input_output_aliases={len(inputs) + i: i for i in range(len(kept))},
        compiler_params=kernel_params(),
    )(*inputs, *kept)


def rotate_ranks(values_in, axis_name, total, target_of):
    return lax.ppermute(values_in, axis_name, [(i, target_of(i)) for i in range(total)])


def swap_y(values_in):
    return rotate_ranks(values_in, "fsdp", 8, lambda i: i ^ 1)


def move_z(values_in, steps):
    return rotate_ranks(values_in, "fsdp", 8, lambda i: (i + 2 * steps) % 8)


def swap_core(values_in):
    return rotate_ranks(values_in, "ctx", 4, lambda i: i ^ 1)


def swap_x(values_in):
    return rotate_ranks(values_in, "ctx", 4, lambda i: i ^ 2)


def swap_both(values_in):
    return rotate_ranks(values_in, "ctx", 4, lambda i: i ^ 3)


def to_members(blocks):
    return [blocks[0], swap_core(blocks[1]), swap_x(blocks[2]), swap_both(blocks[3])]


def after(value, *others):
    return lax.optimization_barrier((value, *others))[0]


def wide(value):
    return value.astype(jnp.float32)


def fsdp_members(index):
    z, y = index // 2, index % 2
    return [((z + dz) % 4) * 2 + (y ^ dy) for dz in (0, 3, 2, 1) for dy in (0, 1)]


def gather_fsdp(block, work=None, beside=()):
    below = move_z(block, 1)
    own_mirror = swap_y(block)
    if work is None:
        below, own_mirror = after(below, own_mirror, beside[0]), after(own_mirror, below)
        far = move_z(below, 1)
        below_mirror = swap_y(after(below, own_mirror))
        far = after(far, below_mirror, beside[1])
        above = move_z(after(block, far), -1)
        far_mirror = swap_y(far)
        above = after(above, far_mirror, beside[2])
        above_mirror = swap_y(above)
        return [block, own_mirror, below, below_mirror, far, far_mirror, above, above_mirror]
    far = move_z(below, 1)
    below_mirror = swap_y(below)
    done = work(0, (after(block, below), own_mirror))
    above = move_z(after(block, far, done), -1)
    far_mirror = swap_y(after(far, done))
    done = work(1, (after(below, far), below_mirror))
    above_mirror = swap_y(after(above, done))
    work(2, (after(far, above), far_mirror))
    work(3, (above, above_mirror))
    return above_mirror


def scatter_fsdp(parts, beside=None, start=None, middle=None, late=None):
    low = jnp.bfloat16
    results = []

    def run(start):
        if beside:
            results.append(beside[len(results)](start))
            return jax.tree.leaves(results[-1])
        return []

    def held(value, *others):
        return after(value, *[other for other in others if other is not None])

    far = (wide(parts[4]) + wide(swap_y(held(parts[5], start)))).astype(low)
    from_far = move_z(far, 1)
    above_mirror = swap_y(held(parts[7], start))
    done = run(far)
    above = (wide(parts[6]) + wide(above_mirror) + wide(from_far)).astype(low)
    above = held(above, middle)
    from_below = move_z(above, 1)
    below_mirror = swap_y(after(parts[3], above))
    later = run(above)
    below = held((wide(parts[2]) + wide(below_mirror)).astype(low), late)
    from_above = move_z(after(below, *done), -1)
    own_mirror = swap_y(after(parts[1], below))
    done = later + run(below)
    own = wide(parts[0]) + wide(own_mirror) + wide(from_below)
    return after(own, *done) + wide(from_above), results, below


def gather_ctx(block):
    across = swap_x(block)
    return [block, swap_core(block), across, swap_core(across)]


def scatter_ctx(parts, beside=()):
    across = wide(parts[2]) + wide(swap_core(parts[3]))
    own = wide(parts[0]) + wide(swap_core(parts[1]))
    across = swap_x(across.astype(jnp.bfloat16))
    return own + wide(after(across, *beside))


def split_ranks(
    hidden_in,
    w_query,
    w_key_value,
    w_output,
    w_router,
    norm_gains,
    w_gate_up,
    w_down,
    expert_ids,
    out_grad,
):
    both = ("ctx", "fsdp")
    ctx_total, groups = 4, 8
    ctx_index, group_index = lax.axis_index("ctx"), lax.axis_index("fsdp")
    row_count, model_width = hidden_in.shape[1], hidden_in.shape[2]
    layer_total, share, _ = w_query.shape
    experts_here = w_gate_up.shape[1]
    expert_total = experts_here * groups
    kv_width = w_key_value.shape[2] // 2
    q_part, kv_part = model_width // ctx_total, kv_width // ctx_total
    qkv_part = q_part + 2 * kv_part
    pair_total = groups // 2
    low = jnp.bfloat16
    f32 = jnp.float32

    def dot_tn(a, b):
        return mm(a, b, TN)

    ctx_members = [ctx_index ^ r for r in range(ctx_total)]
    members = jnp.stack([*fsdp_members(group_index), *ctx_members]).astype(jnp.int32)
    natural_members = jnp.stack([*range(groups), *ctx_members]).astype(jnp.int32)
    ring_members = jnp.stack([ctx_members[r] for r in RING])
    ctx_ref = ctx_index.reshape(1).astype(jnp.int32)
    expert_lane = jnp.arange(128, dtype=jnp.int32)
    own_experts = [
        (
            expert_lane[None, :]
            == expert_total * i
            + group_index * experts_here
            + jnp.arange(8, dtype=jnp.int32)[:, None]
        ).astype(f32)
        for i in range(layer_total)
    ]
    gain_lane = expert_total * layer_total

    def ring(vector):
        return jnp.take(vector.reshape(ctx_total, -1), ring_members, axis=0).reshape(-1)

    places = jnp.concatenate(
        [row_positions((ctx_index ^ r) * row_count, row_count, row_count, ctx_total) for r in range(4)]
    )
    half_dim = HEAD_DIM // 2
    frequency = rope_base ** (-jnp.arange(half_dim, dtype=f32) / half_dim)
    angles = places.astype(f32)[:, None] * frequency[None, :]
    cosine, sine = jnp.cos(angles), jnp.sin(angles)
    tables = (
        jnp.concatenate([cosine] * 4, -1),
        jnp.concatenate([-sine, sine, -sine, sine], -1),
    )

    blocks = to_members(
        weight_blocks(
            members, w_query, w_key_value, w_router.transpose(0, 2, 1), norm_gains.transpose(0, 2, 1)
        )
    )
    packed = pack_shards(
        blocks,
        w_output,
        expert_ids.reshape(layer_total, row_count, TOP).transpose(0, 2, 1),
        qkv_part,
    )
    expert_weights, start = [[]], packed
    for part in [*(w_gate_up[0, e] for e in range(experts_here)), w_down[0]]:
        expert_weights[0].extend(gather_ctx(after(part, start)))
        start = expert_weights[0][-2]
    hidden_rows = gather_ctx(
        after(hidden_in.reshape(row_count, model_width), expert_weights[0][6])
    )
    flat_shards = gather_fsdp(packed, None, [expert_weights[0][2], expert_weights[0][6], 0.0])
    shards = [shard.reshape(ctx_total, share, -1) for shard in flat_shards]
    layer_part = qkv_part + q_part
    small = place(members, shards, layer_total * layer_part, 128, 0)[0].reshape(model_width, 128)
    gains = [
        wide(small[:, gain_lane + 2 * i : gain_lane + 2 * i + 2]).T for i in range(layer_total)
    ]
    ring_gains = [ring(gains[i][0]) for i in range(layer_total)]

    def place_layer(i, start):
        qkv_weight, out_weight = place(
            members, [after(shards[0], start), *shards[1:]], i * layer_part, qkv_part, q_part
        )
        return qkv_weight.reshape(model_width, qkv_part), out_weight

    attention_weights = [place_layer(0, expert_weights[0][10])]
    residual = wide(hidden_in.reshape(row_count, model_width))
    saved = []
    for i in range(layer_total):
        qkv_weight, out_weight = attention_weights[i]
        normed, root_first = rms_scaled(residual, gains[i][0])
        if i == 0:
            rows = [
                rms_scaled(wide(block), gains[i][0])[0].astype(low) for block in hidden_rows
            ]
        else:
            rows = gather_ctx(normed.astype(low))
        branch, rows_first, qkv, attended, logs = attention_forward(
            ctx_ref, rows, qkv_weight, out_weight, qkv_part, tables
        )
        middle = residual + scatter_ctx(branch)
        normed_second, root_second = rms_scaled(middle, gains[i][1])
        parts, kept = [None] * groups, []

        def forward_work(group, pair):
            outs = experts_forward(
                group, pair_total, ctx_ref, pair, flat_shards[2 * group : 2 * group + 2],
                64 + TOP * i, expert_total * i, small,
                own_experts[i], expert_weights[i], kept,
            )
            parts[2 * group], parts[2 * group + 1] = outs[:2]
            kept[:] = outs[2:]
            return outs[0]

        normed_second = normed_second.astype(low)
        beside = None
        if i == 0:
            joined = join_experts(after(w_gate_up[1], middle), w_down[1])
            expert_weights.append([lax.all_gather(joined, "ctx", axis=1, tiled=True)])
            beside = (lambda start: [], lambda start: place_layer(1, start), lambda start: [])
        last = gather_fsdp(normed_second, forward_work)
        rows_second, gate, up, probs = kept
        expert_sum, placed, _ = scatter_fsdp(parts, beside, last)
        if beside:
            attention_weights.append(placed[1])
        saved.append(
            (
                residual, root_first, rows_first, qkv, attended, logs,
                middle, root_second, rows_second, gate, up, probs, expert_sum,
            )
        )
        residual = middle + expert_sum
    hidden_out = residual.reshape(1, row_count, model_width).astype(low)
    grad = wide(out_grad.reshape(row_count, model_width))
    expert_grads = []

    def add_core(start, pairs, came):
        sums = [
            (dot_tn(after(part, start)[:, :half], grads) + wide(other)).astype(low)
            for (part, half, grads), other in zip(pairs, came, strict=True)
        ]
        return [(part[: part.shape[0] // 2], part[part.shape[0] // 2 :]) for part in sums]

    def finish_layer(i, pairs, start, kept):
        held, sent = [pair[0] for pair in pairs], [pair[1] for pair in pairs]
        held[0] = after(held[0], start)
        return finish_experts(i, layer_total, experts_here, held, sent, kept)

    for i in reversed(range(layer_total)):
        (
            residual, root_first, rows_first, qkv, attended, logs,
            middle, root_second, rows_second, gate, up, probs, expert_sum,
        ) = saved[i]
        qkv_weight, out_weight = attention_weights[i]
        mean_gate = jnp.sum(grad * expert_sum, -1, keepdims=True)
        mean_high = mean_gate.astype(low)
        mean_low = (mean_gate - wide(mean_high)).astype(low)
        lanes = jnp.where(expert_lane == 0, mean_high, jnp.where(expert_lane == 1, mean_low, 0))
        sent = jnp.concatenate([grad.astype(low), lanes.astype(low)], -1)
        parts, kept = [None] * groups, []
        if i == 0:
            halves = add_core(sent, *pending)
            expert_grads.insert(0, [(half[0], swap_x(half[1])) for half in halves] + [upper_down])

        def backward_work(group, pair):
            if i == 0 and group == 0:
                pair = (after(pair[0], *jax.tree.leaves(halves)), pair[1])
            if i == 0 and group == 3:
                pair = (after(pair[0], expert_grads[0][0][1]), pair[1])
            outs = experts_backward(
                group, pair_total, ctx_ref, pair, probs, gate, up, small, own_experts[i],
                expert_weights[i], kept, i == 0,
            )
            parts[2 * group], parts[2 * group + 1] = outs[:2]
            kept[:] = outs[2:]
            return outs[0]

        last = gather_fsdp(sent, backward_work)
        grads_second, grad_gate, grad_up, hidden, grad_logits = kept
        half_width, half_hidden = model_width // 2, hidden.shape[1] // 2

        came, whole_down = [], []
        pairs = [(rows_second, half_width, grad_gate), (rows_second, half_width, grad_up)]
        if i == 0:
            pairs.append((hidden, half_hidden, grads_second))

        def first_beside(start):
            for part, half, grads in pairs:
                came.append(swap_core(dot_tn(after(part, start)[:, half:], grads).astype(low)))
            if i > 0:
                whole_down.append(dot_tn(after(hidden, start), grads_second).astype(low))
            return came + whole_down

        last_gate = [expert_grads[0][1][1]] if i == 0 else []
        grad_second, _, _ = scatter_fsdp(
            parts, (lambda start: last_gate, first_beside, lambda start: []), last
        )
        small_grads = dot_tn(rows_second, grad_logits)
        grad_middle, gain_second = rms_back(middle, root_second, gains[i][1], grad_second)
        grad_middle = grad_middle + grad
        branch_rows = grad_middle.astype(low)
        branch_grads = gather_ctx(branch_rows)
        if i > 0:
            pending = pairs, came
        back, rows_branch, grad_qkv, gain_first = attention_backward(
            ctx_ref, branch_grads, rows_first, qkv_weight, out_weight, qkv,
            logs, tables,
        )
        gain_first = gain_first[0] / ring_gains[i]
        gain_second = ring(gain_second)
        small_grads = jnp.where(
            expert_lane == gain_lane,
            gain_first[:, None],
            jnp.where(expert_lane == gain_lane + 1, gain_second[:, None], small_grads),
        ).astype(low)
        if i == 0:
            far = (wide(packs[4]) + wide(swap_y(after(packs[5], grad_second)))).astype(low)
            above_mirror, from_far = swap_y(after(packs[7], grad_second)), move_z(far, 1)
            above = (wide(packs[6]) + wide(above_mirror) + wide(from_far)).astype(low)
            above = after(above, back[0])
            from_below, below_mirror = move_z(above, 1), swap_y(after(packs[3], above))
            rows_first = after(rows_first, above)
        qkv_grads = dot_tn(rows_first, grad_qkv).astype(low)
        out_grads = dot_tn(attended, rows_branch).astype(low)
        layer_packs = pack_grads(
            members,
            qkv_grads.reshape(ctx_total, groups, share, qkv_part),
            small_grads.reshape(ctx_total, groups, share, 128),
            out_grads,
            True,
        )
        flat_packs = [pack.reshape(ctx_total * share, -1) for pack in layer_packs]
        if i == 0:
            below = after((wide(packs[2]) + wide(below_mirror)).astype(low), layer_packs[0])
            from_above, own_mirror = move_z(below, -1), swap_y(after(packs[1], below))
            upper = wide(packs[0]) + wide(own_mirror) + wide(from_below) + wide(from_above)
            halves = add_core(below, pairs[:1], came[:1])
            crossed = [swap_x(halves[0][1])]

            def second_beside(start):
                halves.extend(add_core(start, pairs[1:], came[1:]))
                crossed.extend(swap_x(half[1]) for half in halves[1:])
                return jax.tree.leaves(halves)

            beside = [
                second_beside,
                lambda start: [crossed[0], finish_layer(1, expert_grads[0], start, [])],
                lambda start: crossed[1],
            ]
            lower, finished, _ = scatter_fsdp(flat_packs, beside, below, None, upper)
            expert_grads.insert(
                0, [(half[0], other) for half, other in zip(halves, crossed, strict=True)]
            )
            attention_grads = [lower, upper]
            layer_packs = [upper]
        grad_first = scatter_ctx(back, layer_packs)
        grad_input, _ = rms_back(residual, root_first, gains[i][0], grad_first)
        grad = grad_input + grad_middle
        if i > 0:
            parts = after(whole_down[0], grad).reshape(ctx_total, -1, model_width)
            upper_down = lax.psum_scatter(parts, "ctx", scatter_dimension=0, tiled=True)
            upper_down = (upper_down.reshape(-1, model_width), None)
        packs = flat_packs
    attention_grads = [
        part.astype(low).reshape(ctx_total, share, -1) for part in attention_grads
    ]
    front = qkv_part + 128
    blocks = to_members(
        [jnp.concatenate([part[r, :, :front] for part in attention_grads], -1) for r in range(ctx_total)]
    )
    query_out, key_value_out, output_out, router_out, gains_out = finish_attention(
        members,
        [
            [block[:, i * front : (i + 1) * front] for block in blocks] + [part[..., front:]]
            for i, part in enumerate(attention_grads)
        ],
        expert_total,
    )
    outs = finish_layer(0, expert_grads[0], attention_grads[0], finished[1][1])
    return (
        hidden_out,
        grad.reshape(1, row_count, model_width),
        query_out,
        key_value_out,
        output_out,
        router_out.transpose(0, 2, 1),
        gains_out.transpose(0, 2, 1),
        outs[0],
        outs[1],
    )


def solution(mesh):
    split = mesh.shape["ctx"] == 4 and mesh.shape["fsdp"] == 8
    return jax.shard_map(
        split_ranks if split else on_device,
        mesh=mesh,
        in_specs=(
            P("fsdp", "ctx", None),
            P(None, ("ctx", "fsdp"), None),
            P(None, ("ctx", "fsdp"), None),
            P(None, ("ctx", "fsdp"), None),
            P(None, ("ctx", "fsdp"), None),
            P(None, ("ctx", "fsdp"), None),
            P(None, "fsdp", "ctx", None),
            P(None, "fsdp", "ctx", None),
            P(None, "fsdp", "ctx", None),
            P("fsdp", "ctx", None),
        ),
        out_specs=(
            P("fsdp", "ctx", None),
            P("fsdp", "ctx", None),
            P(None, ("ctx", "fsdp"), None),
            P(None, ("ctx", "fsdp"), None),
            P(None, ("ctx", "fsdp"), None),
            P(None, ("ctx", "fsdp"), None),
            P(None, ("ctx", "fsdp"), None),
            P(None, "fsdp", "ctx", None),
            P(None, "fsdp", "ctx", None),
        ),
        check_vma=False,
    )
```

```python
import functools
import math

import jax
import jax.numpy as jnp
from jax import lax
from jax.experimental import pallas as pl
from jax.experimental.pallas import tpu as pltpu
from jax.sharding import PartitionSpec as P

HEADS = 24
KV_HEADS = 8
HEAD_DIM = 64
FE = 512
TOP = 8


highest = lax.Precision.HIGHEST
epsilon = 1e-06
rope_base = 10000.0
masked_score = -1e30


def row_positions(first_row, row_total, row_count, shards):
    indices = first_row + jnp.arange(row_total, dtype=jnp.int32)
    shard_of = indices // row_count
    within = indices % row_count
    half_rows = row_count // 2
    return jnp.where(
        within < half_rows,
        shard_of * half_rows + within,
        (2 * shards - 1 - shard_of) * half_rows + within - half_rows,
    )


def rotate(values_in, places, direction):
    half_dim = values_in.shape[-1] // 2
    frequency = rope_base ** (-jnp.arange(half_dim, dtype=jnp.float32) / half_dim)
    angles = places.astype(jnp.float32)[:, None] * frequency[None, :]
    cosine_part = jnp.cos(angles)[:, None, :]
    sine_part = direction * jnp.sin(angles)[:, None, :]
    front_half = values_in[..., :half_dim]
    back_half = values_in[..., half_dim:]
    return jnp.concatenate(
        [
            front_half * cosine_part - back_half * sine_part,
            back_half * cosine_part + front_half * sine_part,
        ],
        -1,
    )


def rms_scaled(residual, gain_vector):
    inverse_root = lax.rsqrt(jnp.mean(residual * residual, -1, keepdims=True) + epsilon)
    return (residual * inverse_root * gain_vector, inverse_root)


def rms_back(residual, inverse_root, gain_vector, grad_normed):
    grad_gain = jnp.sum(grad_normed * residual * inverse_root, 0)
    weighted = gain_vector * grad_normed
    cubed = inverse_root * inverse_root * inverse_root
    grad_residual = inverse_root * weighted - residual * cubed * jnp.mean(
        residual * weighted, -1, keepdims=True
    )
    return (grad_residual, grad_gain)


def route_table(routing_rows, expert_total, row_count, capacity):
    top_count = routing_rows.shape[1]
    chosen_mask = (
        routing_rows[:, :, None] == jnp.arange(expert_total, dtype=jnp.int32)[None, None, :]
    )
    expert_used = jnp.sum(chosen_mask.astype(jnp.int32), 1)
    slot_all = jnp.cumsum(expert_used, 0) - expert_used
    slot_taken = jnp.sum(jnp.where(chosen_mask, slot_all[:, None, :], 0), -1)
    target_slots = routing_rows * capacity + slot_taken
    entry_rows = jnp.full((expert_total * capacity,), row_count * top_count, jnp.int32)
    entry_rows = entry_rows.at[target_slots.reshape(-1)].set(
        jnp.arange(row_count * top_count, dtype=jnp.int32)
    )
    return (chosen_mask, target_slots, entry_rows)


def fold_keys(running, key_piece, queries, query_places, row_count, shards, kv_width):
    piece_rows = key_piece.shape[0]
    step_rows = math.gcd(piece_rows, row_count)
    step_total = piece_rows // step_rows
    blocks_in = key_piece.reshape(step_total, step_rows, key_piece.shape[1])
    heads_kv = queries.shape[1]
    head_size = queries.shape[3]
    score_scale = head_size ** (-0.5)

    def fold_one_step(state_in, inputs):
        block_rows, block_index = inputs
        key_places = row_positions(block_index * step_rows, step_rows, row_count, shards)
        key_rows = block_rows[:, :kv_width].reshape(step_rows, heads_kv, head_size)
        value_rows = block_rows[:, kv_width:].reshape(step_rows, heads_kv, head_size)
        scores = (
            jnp.einsum("qhgd,khd->hgqk", queries, key_rows, preferred_element_type=jnp.float32)
            * score_scale
        )
        visible = query_places[:, None] >= key_places[None, :]
        scores = jnp.where(visible, scores, masked_score)
        old_top, old_total, old_sum = state_in
        new_top = jnp.maximum(old_top, jnp.max(scores, -1))
        shrink = jnp.exp(old_top - new_top)
        weights = jnp.where(visible, jnp.exp(scores - new_top[..., None]), 0.0)
        new_total = old_total * shrink + jnp.sum(weights, -1)
        new_sum = old_sum * shrink[..., None] + jnp.einsum(
            "hgqk,khd->hgqd",
            weights.astype(jnp.bfloat16),
            value_rows,
            preferred_element_type=jnp.float32,
        )
        return ((new_top, new_total, new_sum), None)

    running, _ = lax.scan(
        fold_one_step, running, (blocks_in, jnp.arange(step_total, dtype=jnp.int32))
    )
    return running


def attend_back(
    queries,
    query_places,
    gathered,
    out_exact,
    grad_attended,
    log_total,
    row_count,
    shards,
    kv_width,
):
    heads_kv = queries.shape[1]
    head_size = queries.shape[3]
    score_scale = head_size ** (-0.5)
    delta_rows = jnp.transpose(
        jnp.sum(grad_attended.astype(jnp.float32) * out_exact, -1), (1, 2, 0)
    )
    blocks_in = gathered.reshape(shards, row_count, gathered.shape[1])

    def attend_one_step(grad_queries, inputs):
        block_rows, block_index = inputs
        key_places = row_positions(block_index * row_count, row_count, row_count, shards)
        key_rows = block_rows[:, :kv_width].reshape(row_count, heads_kv, head_size)
        value_rows = block_rows[:, kv_width:].reshape(row_count, heads_kv, head_size)
        scores = (
            jnp.einsum("qhgd,khd->hgqk", queries, key_rows, preferred_element_type=jnp.float32)
            * score_scale
        )
        visible = query_places[:, None] >= key_places[None, :]
        probabilities = jnp.where(visible, jnp.exp(scores - log_total[..., None]), 0.0)
        rounded = probabilities.astype(jnp.bfloat16)
        grad_values = jnp.einsum(
            "hgqk,qhgd->khd", rounded, grad_attended, preferred_element_type=jnp.float32
        )
        grad_probs = jnp.einsum(
            "qhgd,khd->hgqk", grad_attended, value_rows, preferred_element_type=jnp.float32
        )
        grad_scores = (probabilities * (grad_probs - delta_rows[..., None])).astype(jnp.bfloat16)
        grad_queries = grad_queries + score_scale * jnp.einsum(
            "hgqk,khd->qhgd", grad_scores, key_rows, preferred_element_type=jnp.float32
        )
        grad_keys = score_scale * jnp.einsum(
            "hgqk,qhgd->khd", grad_scores, queries, preferred_element_type=jnp.float32
        )
        return (
            grad_queries,
            jnp.concatenate(
                [grad_keys.reshape(row_count, kv_width), grad_values.reshape(row_count, kv_width)],
                -1,
            ),
        )

    start_grad = jnp.zeros(queries.shape, jnp.float32)
    grad_queries, grad_blocks = lax.scan(
        attend_one_step, start_grad, (blocks_in, jnp.arange(shards, dtype=jnp.int32))
    )
    return (grad_queries, grad_blocks.reshape(shards * row_count, gathered.shape[1]))


def on_device(
    hidden_in,
    w_query,
    w_key_value,
    w_output,
    w_router,
    norm_gains,
    w_gate_up,
    w_down,
    expert_ids,
    out_grad,
):
    shards = lax.axis_size("ctx")
    groups = lax.axis_size("fsdp")
    shard_index = lax.axis_index("ctx")
    row_count = hidden_in.shape[1]
    model_width = hidden_in.shape[2]
    layer_total = w_query.shape[0]
    experts_here = w_gate_up.shape[1]
    expert_total = experts_here * groups
    capacity = min(row_count, 3 * row_count * TOP // (2 * expert_total))
    kv_width = w_key_value.shape[2] // 2
    group_size = HEADS // KV_HEADS
    query_places = row_positions(shard_index * row_count, row_count, row_count, shards)
    residual = hidden_in.reshape(row_count, model_width).astype(jnp.float32)
    saved = []
    for layer_index in range(layer_total):
        query_weight, key_value_weight, output_weight, router_weight, gains = (
            lax.all_gather(w_query[layer_index], ("ctx", "fsdp"), axis=0, tiled=True),
            lax.all_gather(w_key_value[layer_index], ("ctx", "fsdp"), axis=0, tiled=True),
            lax.all_gather(w_output[layer_index], ("ctx", "fsdp"), axis=0, tiled=True),
            lax.all_gather(w_router[layer_index], ("ctx", "fsdp"), axis=0, tiled=True),
            lax.all_gather(norm_gains[layer_index], ("ctx", "fsdp"), axis=0, tiled=True),
        )
        gate_up_weight, down_weight = (
            lax.all_gather(w_gate_up[layer_index], "ctx", axis=1, tiled=True),
            lax.all_gather(w_down[layer_index], "ctx", axis=1, tiled=True),
        )
        gain_pair = gains.astype(jnp.float32)
        normed_first, root_first = rms_scaled(residual, gain_pair[:, 0])
        normed_first_low = normed_first.astype(jnp.bfloat16)
        query_raw = jnp.dot(normed_first_low, query_weight, preferred_element_type=jnp.float32)
        key_value_raw = jnp.dot(
            normed_first_low, key_value_weight, preferred_element_type=jnp.float32
        )
        queries = rotate(query_raw.reshape(row_count, HEADS, HEAD_DIM), query_places, 1.0).astype(
            jnp.bfloat16
        )
        queries = queries.reshape(row_count, KV_HEADS, group_size, HEAD_DIM)
        key_turned = rotate(
            key_value_raw[:, :kv_width].reshape(row_count, KV_HEADS, HEAD_DIM), query_places, 1.0
        )
        key_value_low = jnp.concatenate(
            [key_turned.reshape(row_count, kv_width), key_value_raw[:, kv_width:]], -1
        ).astype(jnp.bfloat16)
        start_state = (
            jnp.full((KV_HEADS, group_size, row_count), masked_score, jnp.float32),
            jnp.zeros((KV_HEADS, group_size, row_count), jnp.float32),
            jnp.zeros((KV_HEADS, group_size, row_count, HEAD_DIM), jnp.float32),
        )
        top_score, score_total, accumulated = fold_keys(
            start_state,
            lax.all_gather(key_value_low, "ctx", axis=0, tiled=True),
            queries,
            query_places,
            row_count,
            shards,
            kv_width,
        )
        out_exact = jnp.transpose(accumulated / score_total[..., None], (2, 0, 1, 3))
        log_total = top_score + jnp.log(score_total)
        attended = out_exact.reshape(row_count, model_width).astype(jnp.bfloat16)
        middle = residual + jnp.dot(attended, output_weight, preferred_element_type=jnp.float32)
        normed_second, root_second = rms_scaled(middle, gain_pair[:, 1])
        normed_second_low = normed_second.astype(jnp.bfloat16)
        chosen_mask, target_slots, entry_rows = route_table(
            expert_ids[layer_index].reshape(row_count, TOP), expert_total, row_count, capacity
        )
        padded_rows = jnp.concatenate(
            [normed_second_low, jnp.zeros((1, model_width), jnp.bfloat16)], 0
        )
        send_buffer = padded_rows[jnp.minimum(entry_rows // TOP, row_count)].reshape(
            groups, experts_here, capacity, model_width
        )
        received = lax.all_to_all(send_buffer, "fsdp", split_axis=0, concat_axis=0, tiled=True)
        gate_up = jnp.einsum(
            "serd,edf->serf", received, gate_up_weight, preferred_element_type=jnp.float32
        )
        hidden = (jax.nn.silu(gate_up[..., :FE]) * gate_up[..., FE:]).astype(jnp.bfloat16)
        expert_out = jnp.einsum(
            "serf,efd->serd", hidden, down_weight, preferred_element_type=jnp.float32
        ).astype(jnp.bfloat16)
        returned = lax.all_to_all(
            expert_out, "fsdp", split_axis=0, concat_axis=0, tiled=True
        ).reshape(expert_total * capacity, model_width)
        picked = returned[target_slots]
        logits = jnp.dot(normed_second_low, router_weight, preferred_element_type=jnp.float32)
        chosen_logits = jnp.sum(jnp.where(chosen_mask, logits[:, None, :], 0.0), -1)
        gate_probs = jax.nn.softmax(chosen_logits, axis=-1)
        expert_sum = jnp.sum(gate_probs[..., None] * picked.astype(jnp.float32), 1)
        saved.append(
            (
                residual,
                root_first,
                normed_first_low,
                queries,
                key_value_low,
                out_exact,
                log_total,
                attended,
                middle,
                root_second,
                normed_second_low,
                chosen_mask,
                target_slots,
                entry_rows,
                received,
                gate_up,
                hidden,
                picked,
                gate_probs,
                query_weight,
                key_value_weight,
                output_weight,
                router_weight,
                gain_pair,
                gate_up_weight,
                down_weight,
            )
        )
        residual = middle + expert_sum
    hidden_out = residual.reshape(1, row_count, model_width).astype(jnp.bfloat16)
    grad_residual = out_grad.reshape(row_count, model_width).astype(jnp.float32)
    (
        query_parts,
        key_value_parts,
        output_parts,
        router_parts,
        gain_parts,
        gate_up_parts,
        down_parts,
    ) = ([], [], [], [], [], [], [])
    for layer_index in reversed(range(layer_total)):
        (
            layer_input,
            root_first,
            normed_first_low,
            queries,
            key_value_low,
            out_exact,
            log_total,
            attended,
            middle,
            root_second,
            normed_second_low,
            chosen_mask,
            target_slots,
            entry_rows,
            received,
            gate_up,
            hidden,
            picked,
            gate_probs,
            query_weight,
            key_value_weight,
            output_weight,
            router_weight,
            gain_pair,
            gate_up_weight,
            down_weight,
        ) = saved[layer_index]
        grad_gates = jnp.sum(grad_residual[:, None, :] * picked.astype(jnp.float32), -1)
        grad_leaving = (
            (gate_probs[..., None] * grad_residual[:, None, :])
            .astype(jnp.bfloat16)
            .reshape(row_count * TOP, model_width)
        )
        grad_padded = jnp.concatenate([grad_leaving, jnp.zeros((1, model_width), jnp.bfloat16)], 0)
        grad_send = grad_padded[entry_rows].reshape(groups, experts_here, capacity, model_width)
        grad_received = lax.all_to_all(grad_send, "fsdp", split_axis=0, concat_axis=0, tiled=True)
        grad_hidden = jnp.einsum(
            "serd,efd->serf", grad_received, down_weight, preferred_element_type=jnp.float32
        )
        grad_down_part = jnp.einsum(
            "serf,serd->efd", hidden, grad_received, preferred_element_type=jnp.float32
        )
        gate_part = gate_up[..., :FE]
        up_part = gate_up[..., FE:]
        sigmoid_gate = jax.nn.sigmoid(gate_part)
        grad_gate = grad_hidden * up_part * sigmoid_gate * (1.0 + gate_part * (1.0 - sigmoid_gate))
        grad_up = grad_hidden * gate_part * sigmoid_gate
        grad_gate_up_rows = jnp.concatenate([grad_gate, grad_up], -1).astype(jnp.bfloat16)
        grad_gate_up_part = jnp.einsum(
            "serd,serf->edf", received, grad_gate_up_rows, preferred_element_type=jnp.float32
        )
        grad_entering = jnp.einsum(
            "serf,edf->serd", grad_gate_up_rows, gate_up_weight, preferred_element_type=jnp.float32
        ).astype(jnp.bfloat16)
        grad_returned = lax.all_to_all(
            grad_entering, "fsdp", split_axis=0, concat_axis=0, tiled=True
        ).reshape(expert_total * capacity, model_width)
        grad_normed_second = jnp.sum(grad_returned[target_slots].astype(jnp.float32), 1)
        gate_mean = jnp.sum(gate_probs * grad_gates, -1, keepdims=True)
        grad_chosen = gate_probs * (grad_gates - gate_mean)
        grad_logits = jnp.sum(jnp.where(chosen_mask, grad_chosen[..., None], 0.0), 1)
        grad_router_part = jnp.dot(
            normed_second_low.astype(jnp.float32).T, grad_logits, precision=highest
        )
        grad_normed_second = grad_normed_second + jnp.dot(
            grad_logits, router_weight.astype(jnp.float32).T, precision=highest
        )
        grad_middle, grad_gain_second = rms_back(
            middle, root_second, gain_pair[:, 1], grad_normed_second
        )
        grad_middle = grad_middle + grad_residual
        grad_branch = grad_middle.astype(jnp.bfloat16)
        grad_output_part = jnp.einsum(
            "rd,re->de", attended, grad_branch, preferred_element_type=jnp.float32
        )
        grad_attended = jnp.einsum(
            "re,de->rd", grad_branch, output_weight, preferred_element_type=jnp.float32
        ).astype(jnp.bfloat16)
        grad_attended = grad_attended.reshape(row_count, KV_HEADS, group_size, HEAD_DIM)
        gathered = lax.all_gather(key_value_low, "ctx", axis=0, tiled=True)
        grad_queries, grad_key_value_all = attend_back(
            queries,
            query_places,
            gathered,
            out_exact,
            grad_attended,
            log_total,
            row_count,
            shards,
            kv_width,
        )
        grad_key_value_own = lax.psum_scatter(
            grad_key_value_all.astype(jnp.bfloat16), "ctx", scatter_dimension=0, tiled=True
        ).astype(jnp.float32)
        grad_keys = rotate(
            grad_key_value_own[:, :kv_width].reshape(row_count, KV_HEADS, HEAD_DIM),
            query_places,
            -1.0,
        )
        grad_key_value_low = jnp.concatenate(
            [grad_keys.reshape(row_count, kv_width), grad_key_value_own[:, kv_width:]], -1
        ).astype(jnp.bfloat16)
        grad_query_low = (
            rotate(grad_queries.reshape(row_count, HEADS, HEAD_DIM), query_places, -1.0)
            .reshape(row_count, model_width)
            .astype(jnp.bfloat16)
        )
        grad_query_part = jnp.einsum(
            "rd,re->de", normed_first_low, grad_query_low, preferred_element_type=jnp.float32
        )
        grad_key_value_part = jnp.einsum(
            "rd,re->de", normed_first_low, grad_key_value_low, preferred_element_type=jnp.float32
        )
        grad_normed_first = jnp.einsum(
            "re,de->rd", grad_query_low, query_weight, preferred_element_type=jnp.float32
        ) + jnp.einsum(
            "re,de->rd", grad_key_value_low, key_value_weight, preferred_element_type=jnp.float32
        )
        grad_input, grad_gain_first = rms_back(
            layer_input, root_first, gain_pair[:, 0], grad_normed_first
        )
        grad_residual = grad_input + grad_middle
        grad_gain_part = jnp.stack([grad_gain_first, grad_gain_second], -1)
        query_parts.insert(0, grad_query_part)
        key_value_parts.insert(0, grad_key_value_part)
        output_parts.insert(0, grad_output_part)
        router_parts.insert(0, grad_router_part)
        gain_parts.insert(0, grad_gain_part)
        gate_up_parts.insert(0, grad_gate_up_part)
        down_parts.insert(0, grad_down_part)
    stacked_query = jnp.stack(query_parts, 0)
    stacked_key_value = jnp.stack(key_value_parts, 0)
    stacked_output = jnp.stack(output_parts, 0)
    stacked_router = jnp.stack(router_parts, 0)
    stacked_gains = jnp.stack(gain_parts, 0)
    stacked_gate_up = jnp.stack(gate_up_parts, 0)
    stacked_down = jnp.stack(down_parts, 0)
    stacked_query, stacked_key_value, stacked_output, stacked_router, stacked_gains = (
        lax.psum_scatter(stacked_query, ("ctx", "fsdp"), scatter_dimension=1, tiled=True),
        lax.psum_scatter(stacked_key_value, ("ctx", "fsdp"), scatter_dimension=1, tiled=True),
        lax.psum_scatter(stacked_output, ("ctx", "fsdp"), scatter_dimension=1, tiled=True),
        lax.psum_scatter(stacked_router, ("ctx", "fsdp"), scatter_dimension=1, tiled=True),
        lax.psum_scatter(stacked_gains, ("ctx", "fsdp"), scatter_dimension=1, tiled=True),
    )
    stacked_gate_up, stacked_down = (
        lax.psum_scatter(
            stacked_gate_up.astype(jnp.bfloat16), "ctx", scatter_dimension=2, tiled=True
        ).astype(jnp.float32),
        lax.psum_scatter(
            stacked_down.astype(jnp.bfloat16), "ctx", scatter_dimension=2, tiled=True
        ).astype(jnp.float32),
    )
    grad_hidden = grad_residual.reshape(1, row_count, model_width)
    return (
        hidden_out,
        grad_hidden,
        stacked_query,
        stacked_key_value,
        stacked_output,
        stacked_router,
        stacked_gains,
        stacked_gate_up,
        stacked_down,
    )


NN = (((1,), (0,)), ((), ()))
NT = (((1,), (1,)), ((), ()))
TN = (((0,), (0,)), ((), ()))
FE_STEP = 512
KERNEL_MIB = 58


def mm(a, b, dims=NN):
    return lax.dot_general(a, b, dims, preferred_element_type=jnp.float32)


def whole(shape):
    return pl.BlockSpec(shape, lambda *_: (0,) * len(shape))


def anywhere():
    return pl.BlockSpec(memory_space=pl.ANY)


def kernel_params():
    return pltpu.CompilerParams(vmem_limit_bytes=KERNEL_MIB * 1024 * 1024)


def shaped(shape, dtype=jnp.bfloat16):
    return jax.ShapeDtypeStruct(shape, dtype)


RING = (0, 2, 1, 3)


def bring_expert_weights(bring, ctx_ref, weights, w_gate_up_here, w_down_here, e, p, down_first=False):
    hidden_width, width = w_down_here.shape[1:]
    copies, downs = [], []

    def bring_gate_up():
        for side in range(2):
            span = slice(side * hidden_width + p * FE_STEP, side * hidden_width + (p + 1) * FE_STEP)
            if len(weights) == 1:
                copies.append(bring(weights[0].at[e, :, span], w_gate_up_here.at[e, :, span]))
                continue
            for r in range(4):
                quarter = weights[4 * e + r]
                rows = quarter.shape[0]
                at = pl.ds(pl.multiple_of((ctx_ref[0] ^ r) * rows, rows), rows)
                copies.append(bring(quarter.at[:, span], w_gate_up_here.at[e, at, span]))

    def bring_down():
        if p == 0:
            rows, part = hidden_width // 4, width // 3
            for r in range(4):
                if len(weights) > 1:
                    at = pl.ds(pl.multiple_of((ctx_ref[0] ^ r) * rows, rows), rows)
                    downs.append(bring(weights[-4 + r].at[e], w_down_here.at[e, at, :]))
                    continue
                for b in range(3):
                    source = slice((3 * r + b) * rows, (3 * r + b + 1) * rows)
                    downs.append(
                        bring(
                            weights[0].at[e, source, 2 * hidden_width :],
                            w_down_here.at[e, r * rows : (r + 1) * rows, b * part : (b + 1) * part],
                        )
                    )

    for part in (bring_down, bring_gate_up) if down_first else (bring_gate_up, bring_down):
        part()
    return copies, downs


def join_experts(gate_up, down):
    part = down.shape[2] // 3
    return jnp.concatenate(
        [gate_up, jnp.concatenate([down[:, :, b * part : (b + 1) * part] for b in range(3)], 1)], -1
    )


def experts_forward_body(weight_total, group, first_id, lane_offset, ctx_ref, rows_0, rows_1, ids_0, ids_1, router_in, own_in, *refs):
    (out_0, out_1, all_rows, all_gate, all_up, all_probs) = refs[-19:-13]
    (
        rows, w_gate_up_here, w_down_here, gate_here, up_here, probs, ring_rows,
        ids, router, own, result, in_sems, out_sems,
    ) = refs[-13:]
    block, width = rows_0.shape
    count = 2 * block
    expert_count, hidden_width = w_down_here.shape[0], w_down_here.shape[1]
    steps = hidden_width // FE_STEP
    incoming = []

    def bring(source, target):
        copy = pltpu.make_async_copy(source, target, in_sems.at[len(incoming)])
        copy.start()
        incoming.append(copy)
        return copy

    span = pl.ds(group * count, count)
    ids_at = ids_0.shape[1] - 128
    row_copies = [
        bring(rows_0, rows.at[:block]),
        bring(rows_1, rows.at[block:]),
        bring(ids_0.at[:block, ids_at:], ids.at[:block]),
        bring(ids_1.at[:block, ids_at:], ids.at[block:]),
        bring(router_in, router),
        bring(own_in, own),
    ]
    weight_copies = []
    for e in range(expert_count):
        for p in range(steps):
            weight_copies.append(
                bring_expert_weights(bring, ctx_ref, refs[:weight_total], w_gate_up_here, w_down_here, e, p)
            )
    outgoing = []

    def send(source, target):
        copy = pltpu.make_async_copy(source, target, out_sems.at[len(outgoing)])
        copy.start()
        outgoing.append(copy)

    for copy in row_copies:
        copy.wait()
    lane = lax.broadcasted_iota(jnp.int32, probs.shape, 1).astype(jnp.float32)
    chosen_ids = ids[...].astype(jnp.float32) + lane_offset
    listed = lane == chosen_ids[:, first_id : first_id + 1]
    for k in range(1, TOP):
        at = first_id + k
        listed = jnp.logical_or(listed, lane == chosen_ids[:, at : at + 1])
    logits = jnp.where(listed, mm(rows[...], router[...]), masked_score)
    weights = jnp.exp(logits - jnp.max(logits, -1, keepdims=True))
    gates = weights / jnp.sum(weights, -1, keepdims=True)
    probs[...] = gates
    part = width // 4
    for place, r in enumerate(RING):
        at = pl.multiple_of((ctx_ref[0] ^ r) * part, part)
        ring_rows[:, place * part : (place + 1) * part] = rows[:, pl.ds(at, part)]
    send(ring_rows, all_rows.at[span])
    send(probs, all_probs.at[span])
    total = jnp.zeros((count, width), jnp.float32)
    for e in range(expert_count):
        chosen = jnp.sum(gates * own[e : e + 1, :], -1, keepdims=True)
        for p in range(steps):
            for copy in weight_copies[e * steps + p][0]:
                copy.wait()
            lower = slice(p * FE_STEP, (p + 1) * FE_STEP)
            upper = slice(hidden_width + p * FE_STEP, hidden_width + (p + 1) * FE_STEP)
            gate = mm(rows[...], w_gate_up_here[e, :, lower])
            up = mm(rows[...], w_gate_up_here[e, :, upper])
            flat = slice(e * hidden_width + p * FE_STEP, e * hidden_width + (p + 1) * FE_STEP)
            gate_here[:, flat] = gate.astype(jnp.bfloat16)
            up_here[:, flat] = up.astype(jnp.bfloat16)
            hidden = (gate * jax.nn.sigmoid(gate) * up * chosen).astype(jnp.bfloat16)
            for copy in weight_copies[e * steps + p][1]:
                copy.wait()
            total = total + mm(hidden, w_down_here[e, lower, :])
    send(gate_here, all_gate.at[span])
    send(up_here, all_up.at[span])
    result[...] = total.astype(jnp.bfloat16)
    send(result.at[:block], out_0)
    send(result.at[block:], out_1)
    for copy in outgoing:
        copy.wait()


def vmem():
    return pl.BlockSpec(memory_space=pltpu.VMEM)


def smem():
    return pl.BlockSpec(memory_space=pltpu.SMEM)


def expert_shapes(weights):
    if len(weights) == 1:
        count, width, columns = weights[0].shape
        hidden_width = (columns - width // 3) // 2
    else:
        count, rows, width = weights[-1].shape
        hidden_width = 4 * rows
    return (count, width, 2 * hidden_width), (count, hidden_width, width)


def expert_cost(count, width, expert_count, hidden_width):
    return pl.CostEstimate(
        flops=6 * count * width * expert_count * hidden_width,
        bytes_accessed=6 * width * expert_count * hidden_width,
        transcendentals=count * expert_count * hidden_width,
    )


def experts_forward(
    group, groups, ctx_ref, rows, ids, first_id, lane_offset, router, own, weights, kept
):
    block, width = rows[0].shape
    count = 2 * block
    gate_up_shape, down_shape = expert_shapes(weights)
    expert_count, hidden_width = down_shape[0], down_shape[1]
    flat = expert_count * hidden_width
    low, f32 = jnp.bfloat16, jnp.float32
    inputs = [ctx_ref, *rows, *ids, router, own, *weights, *kept]
    return pl.pallas_call(
        functools.partial(experts_forward_body, len(weights), group, first_id, lane_offset),
        in_specs=[smem()] + [anywhere()] * (6 + len(weights) + len(kept)),
        out_specs=[anywhere()] * 6,
        out_shape=[
            shaped((block, width)),
            shaped((block, width)),
            shaped((groups * count, width)),
            shaped((groups * count, flat)),
            shaped((groups * count, flat)),
            shaped((groups * count, 128), f32),
        ],
        input_output_aliases={7 + len(weights) + i: 2 + i for i in range(len(kept))},
        scratch_shapes=[
            pltpu.VMEM((count, width), low),
            pltpu.VMEM(gate_up_shape, low),
            pltpu.VMEM(down_shape, low),
            pltpu.VMEM((count, flat), low),
            pltpu.VMEM((count, flat), low),
            pltpu.VMEM((count, 128), f32),
            pltpu.VMEM((count, width), low),
            pltpu.VMEM((count, 128), low),
            pltpu.VMEM(router.shape, low),
            pltpu.VMEM(own.shape, f32),
            pltpu.VMEM((count, width), low),
            pltpu.SemaphoreType.DMA((6 + 8 * flat // FE_STEP + 24 * expert_count,)),
            pltpu.SemaphoreType.DMA((6,)),
        ],
        compiler_params=kernel_params(),
        cost_estimate=expert_cost(count, width, expert_count, hidden_width),
    )(*inputs)


def experts_backward_body(weight_total, ring, group, ctx_ref, grads_0, grads_1, probs_in, gate_in, up_in, router_in, own_in, *refs):
    out_0, out_1, all_grads, all_grad_gate, all_grad_up, all_hidden, all_logits = refs[-23:-16]
    (
        sent, w_gate_up_here, w_down_here, gates, ups, probs, grads, grad_gates, grad_ups,
        hiddens, logits, router, own, result, in_sems, out_sems,
    ) = refs[-16:]
    block, width = out_0.shape
    count = 2 * block
    expert_count, hidden_width = w_down_here.shape[0], w_down_here.shape[1]
    steps = hidden_width // FE_STEP
    rows_here = pl.ds(group * count, count)
    incoming = []

    def bring(source, target):
        copy = pltpu.make_async_copy(source, target, in_sems.at[len(incoming)])
        copy.start()
        incoming.append(copy)
        return copy

    first_copies = [
        bring(grads_0, sent.at[:block]),
        bring(grads_1, sent.at[block:]),
        bring(probs_in.at[rows_here], probs),
        bring(router_in, router),
        bring(own_in, own),
    ]
    weight_copies = []
    for e in range(expert_count):
        for p in range(steps):
            flat = slice(e * hidden_width + p * FE_STEP, e * hidden_width + (p + 1) * FE_STEP)
            rows_copies = [
                bring(gate_in.at[rows_here, flat], gates.at[:, flat]),
                bring(up_in.at[rows_here, flat], ups.at[:, flat]),
            ]
            gate_up_copies, down_copies = bring_expert_weights(
                bring, ctx_ref, refs[:weight_total], w_gate_up_here, w_down_here, e, p, True
            )
            weight_copies.append((rows_copies + down_copies, gate_up_copies))
    outgoing = []

    def send(source, target):
        copy = pltpu.make_async_copy(source, target, out_sems.at[len(outgoing)])
        copy.start()
        outgoing.append(copy)

    for copy in first_copies:
        copy.wait()
    grads[...] = sent[:, :width]
    mean = sent[:, width : width + 1].astype(jnp.float32) + sent[:, width + 1 : width + 2].astype(
        jnp.float32
    )
    send(grads, all_grads.at[rows_here])
    total = jnp.zeros((count, width), jnp.float32)
    grad_logits = jnp.zeros(probs.shape, jnp.float32)
    quarter = hidden_width // 4
    for e in range(expert_count):
        mine = own[e : e + 1, :]
        chosen = jnp.sum(probs[...] * mine, -1, keepdims=True)
        dots = jnp.zeros((count, 1), jnp.float32)
        for p in range(steps):
            for copy in weight_copies[e * steps + p][0]:
                copy.wait()
            lower = slice(p * FE_STEP, (p + 1) * FE_STEP)
            upper = slice(hidden_width + p * FE_STEP, hidden_width + (p + 1) * FE_STEP)
            flat = slice(e * hidden_width + p * FE_STEP, e * hidden_width + (p + 1) * FE_STEP)
            plain = mm(grads[...], w_down_here[e, lower, :], NT)
            gate = gates[:, flat].astype(jnp.float32)
            up = ups[:, flat].astype(jnp.float32)
            sigmoid_gate = jax.nn.sigmoid(gate)
            silu_gate = gate * sigmoid_gate
            hidden = silu_gate * up
            dots = dots + jnp.sum(plain * hidden, -1, keepdims=True)
            hidden = (hidden * chosen).astype(jnp.bfloat16)
            for q in range(FE_STEP // quarter):
                at = p * (FE_STEP // quarter) + q
                if ring:
                    r = ctx_ref[0] ^ at
                    at = jnp.where(r == 1, 2, jnp.where(r == 2, 1, r))
                at = at * expert_count + e
                hiddens[:, pl.ds(pl.multiple_of(at * quarter, quarter), quarter)] = hidden[
                    :, q * quarter : (q + 1) * quarter
                ]
            plain = plain * chosen
            grad_gate = (
                plain * up * sigmoid_gate * (1.0 + gate * (1.0 - sigmoid_gate))
            ).astype(jnp.bfloat16)
            grad_up = (plain * silu_gate).astype(jnp.bfloat16)
            grad_gates[:, flat] = grad_gate
            grad_ups[:, flat] = grad_up
            for copy in weight_copies[e * steps + p][1]:
                copy.wait()
            total = (
                total
                + mm(grad_gate, w_gate_up_here[e, :, lower], NT)
                + mm(grad_up, w_gate_up_here[e, :, upper], NT)
            )
        grad_logits = grad_logits + chosen * (dots - mean) * mine
    send(grad_gates, all_grad_gate.at[rows_here])
    send(grad_ups, all_grad_up.at[rows_here])
    send(hiddens, all_hidden.at[rows_here])
    low_logits = grad_logits.astype(jnp.bfloat16)
    logits[...] = low_logits
    send(logits, all_logits.at[rows_here])
    result[...] = (total + mm(low_logits, router[...], NT)).astype(jnp.bfloat16)
    send(result.at[:block], out_0)
    send(result.at[block:], out_1)
    for copy in outgoing:
        copy.wait()


def experts_backward(
    group, groups, ctx_ref, grads, probs, gate, up, router, own, weights, kept, ring
):
    gate_up_shape, down_shape = expert_shapes(weights)
    expert_count, hidden_width, width = down_shape
    block = grads[0].shape[0]
    count = 2 * block
    flat = expert_count * hidden_width
    low, f32 = jnp.bfloat16, jnp.float32
    inputs = [ctx_ref, *grads, probs, gate, up, router, own, *weights, *kept]
    return pl.pallas_call(
        functools.partial(experts_backward_body, len(weights), ring, group),
        in_specs=[smem()] + [anywhere()] * (7 + len(weights) + len(kept)),
        out_specs=[anywhere()] * 7,
        out_shape=[
            shaped((block, width)),
            shaped((block, width)),
            shaped((groups * count, width)),
            shaped((groups * count, flat)),
            shaped((groups * count, flat)),
            shaped((groups * count, flat)),
            shaped((groups * count, 128)),
        ],
        input_output_aliases={8 + len(weights) + i: 2 + i for i in range(len(kept))},
        scratch_shapes=[
            pltpu.VMEM((count, grads[0].shape[1]), low),
            pltpu.VMEM(gate_up_shape, low),
            pltpu.VMEM(down_shape, low),
            pltpu.VMEM((count, flat), low),
            pltpu.VMEM((count, flat), low),
            pltpu.VMEM((count, 128), f32),
            pltpu.VMEM((count, width), low),
            pltpu.VMEM((count, flat), low),
            pltpu.VMEM((count, flat), low),
            pltpu.VMEM((count, flat), low),
            pltpu.VMEM((count, 128), low),
            pltpu.VMEM(router.shape, low),
            pltpu.VMEM(own.shape, f32),
            pltpu.VMEM((count, width), low),
            pltpu.SemaphoreType.DMA((5 + 10 * flat // FE_STEP + 24 * expert_count,)),
            pltpu.SemaphoreType.DMA((7,)),
        ],
        compiler_params=kernel_params(),
        cost_estimate=expert_cost(count, width, expert_count, hidden_width),
    )(*inputs)


def turn(block, cosine, sine, lane):
    half = HEAD_DIM // 2
    other = jnp.where(
        lane % HEAD_DIM < half, pltpu.roll(block, 128 - half, 1), pltpu.roll(block, half, 1)
    )
    return block * cosine + other * sine


def row_places(ctx, count, axis):
    half = count // 2
    blocks = []
    for r in range(4):
        c = ctx ^ r
        within = lax.broadcasted_iota(jnp.int32, (count, 1) if axis == 0 else (1, count), axis)
        blocks.append(
            jnp.where(within < half, c * half + within, (7 - c) * half + within - half)
        )
    return jnp.concatenate(blocks, axis)


class Copies:
    def __init__(self, sems):
        self.sems, self.all = sems, []

    def start(self, source, target):
        copy = pltpu.make_async_copy(source, target, self.sems.at[len(self.all)])
        copy.start()
        self.all.append(copy)
        return copy

    def wait(self):
        for copy in self.all:
            copy.wait()


def attention_forward_body(
    gain_lane, ctx_ref, rows_0, rows_1, rows_2, rows_3, w_qkv_in, w_out_in, cosine_in, sine_in, small_in, root_in,
    out_0, out_1, out_2, out_3, all_rows, qkv_out, attended_out, logs_out,
    rows, w_qkv, w_out, cosine, sine, small, root, ring_rows, qkv, attended, logs, result, in_sems, out_sems,
):
    sources, outs = (rows_0, rows_1, rows_2, rows_3), (out_0, out_1, out_2, out_3)
    count, width = rows_0.shape
    q_width, total_width = attended.shape[1], qkv.shape[1]
    kv_width = (total_width - q_width) // 2
    group = HEADS // KV_HEADS
    spans = [slice(r * count, (r + 1) * count) for r in range(4)]
    incoming, outgoing = Copies(in_sems), Copies(out_sems)
    first = [incoming.start(w_qkv_in, w_qkv), incoming.start(rows_0, rows.at[spans[0]])]
    tables = [incoming.start(cosine_in, cosine), incoming.start(sine_in, sine)]
    if gain_lane is not None:
        tables.append(incoming.start(small_in, small))
        tables.append(incoming.start(root_in, root))
    later = [incoming.start(sources[r], rows.at[spans[r]]) for r in range(1, 4)]
    last = incoming.start(w_out_in, w_out)
    for copy in first + tables:
        copy.wait()
    part = width // 4
    lane = lax.broadcasted_iota(jnp.int32, (count, 128), 1)
    if gain_lane is not None:
        gain = small[...].astype(jnp.float32).T[gain_lane : gain_lane + 1, :]
    for r in range(4):
        span = spans[r]
        if r:
            later[r - 1].wait()
        if gain_lane is not None:
            value = rows[span, :].astype(jnp.float32)
            rows[span, :] = (value * root[span, :1] * gain).astype(jnp.bfloat16)
        raw = mm(rows[span, :], w_qkv[...])
        for j in range((q_width + kv_width) // 128):
            turned = turn(raw[:, 128 * j : 128 * j + 128], cosine[span, :], sine[span, :], lane)
            if 128 * j < q_width:
                turned = turned * HEAD_DIM ** (-0.5)
            qkv[span, 128 * j : 128 * j + 128] = turned.astype(jnp.bfloat16)
        qkv[span, q_width + kv_width :] = raw[:, q_width + kv_width :].astype(jnp.bfloat16)
        for place, distance in enumerate(RING):
            at = pl.multiple_of((ctx_ref[0] ^ distance) * part, part)
            ring_rows[span, place * part : (place + 1) * part] = rows[span, pl.ds(at, part)]
    outgoing.start(qkv, qkv_out)
    outgoing.start(ring_rows, all_rows)
    visible = row_places(ctx_ref[0], count, 0) >= row_places(ctx_ref[0], count, 1)
    for head in range(q_width // HEAD_DIM):
        at, of = head * HEAD_DIM, (head // group) * HEAD_DIM
        queries = qkv[:, at : at + HEAD_DIM]
        keys = qkv[:, q_width + of : q_width + of + HEAD_DIM]
        values = qkv[:, q_width + kv_width + of : q_width + kv_width + of + HEAD_DIM]
        scores = jnp.where(visible, mm(queries, keys, NT), masked_score)
        top = jnp.max(scores, -1, keepdims=True)
        weights = jnp.exp(scores - top)
        total = jnp.sum(weights, -1, keepdims=True)
        logs[:, head : head + 1] = top + jnp.log(total)
        probs = (weights * (1.0 / total)).astype(jnp.bfloat16)
        attended[:, at : at + HEAD_DIM] = mm(probs, values).astype(jnp.bfloat16)
    outgoing.start(logs, logs_out)
    outgoing.start(attended, attended_out)
    last.wait()
    for r in (1, 3, 0, 2):
        result[spans[r], :] = mm(attended[spans[r], :], w_out[...]).astype(jnp.bfloat16)
        outgoing.start(result.at[spans[r]], outs[r])
    outgoing.wait()


def attention_forward(ctx_ref, rows, w_qkv, w_out, total_width, tables, small, roots, gain_lane):
    count, width = rows[0].shape
    seq = 4 * count
    q_width = w_out.shape[0]
    low, f32 = jnp.bfloat16, jnp.float32
    outs = pl.pallas_call(
        functools.partial(attention_forward_body, gain_lane),
        in_specs=[smem()] + [anywhere()] * 10,
        out_specs=[anywhere()] * 8,
        out_shape=[shaped((count, width))] * 4
        + [
            shaped((seq, width)),
            shaped((seq, total_width)),
            shaped((seq, q_width)),
            shaped((seq, 128), f32),
        ],
        scratch_shapes=[
            pltpu.VMEM((seq, width), low),
            pltpu.VMEM(w_qkv.shape, low),
            pltpu.VMEM(w_out.shape, low),
            pltpu.VMEM((seq, 128), f32),
            pltpu.VMEM((seq, 128), f32),
            pltpu.VMEM(small.shape, low),
            pltpu.VMEM(roots.shape, f32),
            pltpu.VMEM((seq, width), low),
            pltpu.VMEM((seq, total_width), low),
            pltpu.VMEM((seq, q_width), low),
            pltpu.VMEM((seq, 128), f32),
            pltpu.VMEM((seq, width), low),
            pltpu.SemaphoreType.DMA((10,)),
            pltpu.SemaphoreType.DMA((8,)),
        ],
        compiler_params=kernel_params(),
        cost_estimate=pl.CostEstimate(
            flops=2 * seq * width * (total_width + q_width) + 4 * seq * seq * q_width,
            bytes_accessed=2 * (seq * width * 2 + width * (total_width + q_width)),
            transcendentals=seq * seq * (q_width // HEAD_DIM),
        ),
    )(ctx_ref, *rows, w_qkv, w_out, *tables, small, roots)
    return outs[:4], outs[4], outs[5], outs[6], outs[7]


def attention_backward_body(
    ctx_ref, grad_0, grad_1, grad_2, grad_3, rows_in, w_qkv_in, w_out_in, qkv_in, logs_in,
    cosine_in, sine_in,
    out_0, out_1, out_2, out_3, all_grads, grad_qkv_out, gain_out,
    grads, rows, w_qkv, w_out, qkv, logs, cosine, sine, grad_attended, raw, grad_qkv, gain_sum,
    result, in_sems, out_sems,
):
    sources, outs = (grad_0, grad_1, grad_2, grad_3), (out_0, out_1, out_2, out_3)
    count, width = grad_0.shape
    seq = 4 * count
    q_width, total_width = grad_attended.shape[1], qkv.shape[1]
    kv_width = (total_width - q_width) // 2
    group = HEADS // KV_HEADS
    scale = HEAD_DIM ** (-0.5)
    spans = [slice(r * count, (r + 1) * count) for r in range(4)]
    incoming, outgoing = Copies(in_sems), Copies(out_sems)
    first = [incoming.start(w_out_in, w_out)]
    branches = [incoming.start(sources[r], grads.at[spans[r]]) for r in range(4)]
    second = [incoming.start(qkv_in, qkv), incoming.start(logs_in, logs)]
    last = [
        incoming.start(cosine_in, cosine),
        incoming.start(sine_in, sine),
        incoming.start(w_qkv_in, w_qkv),
        incoming.start(rows_in, rows),
    ]
    first[0].wait()
    for r in range(4):
        branches[r].wait()
        grad_attended[spans[r], :] = mm(grads[spans[r], :], w_out[...], NT).astype(jnp.bfloat16)
    outgoing.start(grads, all_grads)
    for copy in second:
        copy.wait()
    visible = row_places(ctx_ref[0], count, 0) >= row_places(ctx_ref[0], count, 1)
    for kv_head in range(kv_width // HEAD_DIM):
        k_at = q_width + kv_head * HEAD_DIM
        v_at = k_at + kv_width
        keys, values = qkv[:, k_at : k_at + HEAD_DIM], qkv[:, v_at : v_at + HEAD_DIM]
        grad_keys = jnp.zeros((HEAD_DIM, seq), jnp.float32)
        grad_values = jnp.zeros((HEAD_DIM, seq), jnp.float32)
        for head in range(kv_head * group, (kv_head + 1) * group):
            at = head * HEAD_DIM
            queries = qkv[:, at : at + HEAD_DIM]
            grad_head = grad_attended[:, at : at + HEAD_DIM]
            scores = mm(queries, keys, NT)
            probs = jnp.where(visible, jnp.exp(scores - logs[:, head : head + 1]), 0.0)
            grad_values += mm(grad_head.T, probs.astype(jnp.bfloat16))
            weighted = probs * mm(grad_head, values, NT)
            grad_scores = (weighted - probs * jnp.sum(weighted, -1, keepdims=True)).astype(
                jnp.bfloat16
            )
            raw[:, at : at + HEAD_DIM] = mm(grad_scores, keys) * scale
            grad_keys += mm(queries.T, grad_scores)
        raw[:, k_at : k_at + HEAD_DIM] = grad_keys.T
        raw[:, v_at : v_at + HEAD_DIM] = grad_values.T
    for copy in last:
        copy.wait()
    gain_sum[...] = jnp.zeros_like(gain_sum)
    lane = lax.broadcasted_iota(jnp.int32, (count, 128), 1)
    part = width // 4
    for r in (1, 3, 0, 2):
        span = spans[r]
        for j in range((q_width + kv_width) // 128):
            columns = slice(128 * j, 128 * j + 128)
            grad_qkv[span, columns] = turn(
                raw[span, columns], cosine[span, :], -sine[span, :], lane
            ).astype(jnp.bfloat16)
        grad_qkv[span, q_width + kv_width :] = raw[span, q_width + kv_width :].astype(jnp.bfloat16)
        result[span, :] = mm(grad_qkv[span, :], w_qkv[...], NT).astype(jnp.bfloat16)
        outgoing.start(result.at[span], outs[r])
    outgoing.start(grad_qkv, grad_qkv_out)
    for r in range(4):
        span = spans[r]
        for place, distance in enumerate(RING):
            at = pl.multiple_of((ctx_ref[0] ^ distance) * part, part)
            spot = slice(place * part, (place + 1) * part)
            gain_sum[:, spot] += jnp.sum(
                result[span, pl.ds(at, part)].astype(jnp.float32)
                * rows[span, spot].astype(jnp.float32),
                0,
                keepdims=True,
            )
    outgoing.start(gain_sum, gain_out)
    outgoing.wait()


def attention_backward(ctx_ref, grads, rows, w_qkv, w_out, qkv, logs, tables):
    count, width = grads[0].shape
    seq = 4 * count
    q_width, total_width = w_out.shape[0], qkv.shape[1]
    low, f32 = jnp.bfloat16, jnp.float32
    outs = pl.pallas_call(
        attention_backward_body,
        in_specs=[smem()] + [anywhere()] * 11,
        out_specs=[anywhere()] * 7,
        out_shape=[shaped((count, width))] * 4
        + [
            shaped((seq, width)),
            shaped((seq, total_width)),
            shaped((1, width), f32),
        ],
        scratch_shapes=[
            pltpu.VMEM((seq, width), low),
            pltpu.VMEM((seq, width), low),
            pltpu.VMEM(w_qkv.shape, low),
            pltpu.VMEM(w_out.shape, low),
            pltpu.VMEM((seq, total_width), low),
            pltpu.VMEM((seq, 128), f32),
            pltpu.VMEM((seq, 128), f32),
            pltpu.VMEM((seq, 128), f32),
            pltpu.VMEM((seq, q_width), low),
            pltpu.VMEM((seq, total_width), f32),
            pltpu.VMEM((seq, total_width), low),
            pltpu.VMEM((1, width), f32),
            pltpu.VMEM((seq, width), low),
            pltpu.SemaphoreType.DMA((11,)),
            pltpu.SemaphoreType.DMA((7,)),
        ],
        compiler_params=kernel_params(),
        cost_estimate=pl.CostEstimate(
            flops=2 * seq * width * (total_width + q_width) + 10 * seq * seq * q_width,
            bytes_accessed=2 * (seq * width * 3 + width * (total_width + q_width)),
            transcendentals=seq * seq * (q_width // HEAD_DIM),
        ),
    )(ctx_ref, *grads, rows, w_qkv, w_out, qkv, logs, *tables)
    return outs[:4], outs[4], outs[5], outs[6]


def place_body(members, share, total, parts, *refs):
    shards, outs = refs[:total], list(refs[total:])

    def rows_of(r, c, columns):
        if r < 7 or total == 8:
            return shards[r][c, :, columns]
        return shards[7 + c // 2][c % 2, :, columns]

    for first, front, rest in parts:
        out = outs.pop(0)
        for r in range(8):
            for c in range(4):
                out[members[8 + c], members[r]] = rows_of(r, c, slice(first, first + front))
        if not rest:
            continue
        out = outs.pop(0)
        for r in range(8):
            span = pl.ds(pl.multiple_of(members[r] * share, share), share)
            for j in range(4):
                out[span, j * rest : (j + 1) * rest] = rows_of(
                    r, j, slice(first + front, first + front + rest)
                )


def place(members, shards, parts):
    four, share, width = shards[0].shape
    outs = []
    for _, front, rest in parts:
        outs.append(shaped((four, 8, share, front)))
        if rest:
            outs.append(shaped((8 * share, four * rest)))
    return pl.pallas_call(
        lambda members_ref, *refs: place_body(members_ref, share, len(shards), parts, *refs),
        in_specs=[smem()] + [vmem()] * len(shards),
        out_shape=outs,
        compiler_params=kernel_params(),
    )(members, *shards)


def turned(block):
    return block.astype(jnp.float32).T.astype(jnp.bfloat16)


def weight_blocks_body(members, w_query, w_key_value, w_router, gains, *outs):
    layers, share, q_width = w_query.shape
    kv_width = w_key_value.shape[2] // 2
    q_part, kv_part = q_width // 4, kv_width // 4
    experts = w_router.shape[1]
    small = outs[0].shape[1] - 128
    for r in range(4):
        c = members[8 + r]
        outs[r][:, small:] = jnp.zeros((share, 128), jnp.bfloat16)
        for i in range(layers):
            at = i * (q_part + 2 * kv_part)
            outs[r][:, at : at + q_part] = w_query[
                i, :, pl.ds(pl.multiple_of(c * q_part, q_part), q_part)
            ]
            for side in range(2):
                to = at + q_part + side * kv_part
                outs[r][:, to : to + kv_part] = w_key_value[
                    i, :, pl.ds(pl.multiple_of(side * kv_width + c * kv_part, kv_part), kv_part)
                ]
            at = small + i * experts
            outs[r][:, at : at + experts] = turned(w_router[i])
            at = small + layers * experts + 2 * i
            outs[r][:, at : at + 2] = turned(gains[i])


def weight_blocks(members, w_query, w_key_value, w_router, gains):
    layers, share, q_width = w_query.shape
    block = shaped((share, layers * (q_width + w_key_value.shape[2]) // 4 + 128))
    return pl.pallas_call(
        weight_blocks_body,
        in_specs=[smem()] + [vmem()] * 4,
        out_shape=[block] * 4,
        compiler_params=kernel_params(),
    )(members, w_query, w_key_value, w_router, gains)


def pack_shards_body(front, block_0, block_1, block_2, block_3, w_output, ids, shard):
    blocks = (block_0, block_1, block_2, block_3)
    layers, share, width = w_output.shape
    part = front + width // 4
    top, count = ids.shape[1:]
    for r in range(4):
        span = slice(r * share, (r + 1) * share)
        for i in range(layers):
            shard[span, i * part : i * part + front] = blocks[r][:, i * front : (i + 1) * front]
            shard[span, i * part + front : (i + 1) * part] = w_output[
                i, :, r * (width // 4) : (r + 1) * (width // 4)
            ]
        shard[span, layers * part :] = blocks[r][:, layers * front :]
    for i in range(layers):
        at = layers * part + 64 + top * i
        shard[:count, at : at + top] = turned(ids[i])


def pack_shards(blocks, w_output, ids, front):
    layers, share, width = w_output.shape
    return pl.pallas_call(
        functools.partial(pack_shards_body, front),
        in_specs=[vmem()] * 6,
        out_shape=shaped((4 * share, layers * (front + width // 4) + 128)),
        compiler_params=kernel_params(),
    )(*blocks, w_output, ids)


def pack_grads_body(members, qkv, small, out, *parts):
    front, lanes = qkv.shape[3], small.shape[3]
    q_part = out.shape[1] // 4
    share = qkv.shape[2]
    for r in range(8):
        m = members[r]
        part = parts[r] if len(parts) > 1 else parts[0].at[r]
        for place, distance in enumerate(RING):
            part[distance, :, :front] = qkv[place, m]
            part[distance, :, front : front + lanes] = small[place, m]
        for j in range(4):
            part[j, :, front + lanes :] = out[
                pl.ds(pl.multiple_of(m * share, share), share), j * q_part : (j + 1) * q_part
            ]


def pack_grads(members, qkv, small, out, apart):
    four, eight, share, front = qkv.shape
    shape = (four, share, front + small.shape[3] + out.shape[1] // 4)
    return pl.pallas_call(
        pack_grads_body,
        in_specs=[smem()] + [vmem()] * 3,
        out_shape=[shaped(shape)] * 8 if apart else [shaped((eight, *shape))],
        compiler_params=kernel_params(),
    )(members, qkv, small, out)


def finish_attention_body(layers, members, *refs):
    blocks, outs = refs[: 5 * layers], refs[5 * layers :]
    query, key_value, output, router, gains = outs
    experts, lane_count = router.shape[1], layers * router.shape[1]
    q_part, kv_part = query.shape[2] // 4, key_value.shape[2] // 8
    front = q_part + 2 * kv_part
    kv_width = 4 * kv_part
    for i in range(layers):
        lanes = jnp.zeros((query.shape[1], 128), jnp.float32)
        for r in range(4):
            c = members[8 + r]
            block = blocks[5 * i + r]
            query[i, :, pl.ds(pl.multiple_of(c * q_part, q_part), q_part)] = block[
                :, :q_part
            ].astype(jnp.float32)
            for side in range(2):
                at = pl.multiple_of(side * kv_width + c * kv_part, kv_part)
                key_value[i, :, pl.ds(at, kv_part)] = block[
                    :, q_part + side * kv_part : q_part + (side + 1) * kv_part
                ].astype(jnp.float32)
            lanes = lanes + block[:, front:].astype(jnp.float32)
        lanes = lanes.T
        router[i] = lanes[i * experts : (i + 1) * experts, :]
        gains[i] = lanes[lane_count : lane_count + 2, :]
        own = blocks[5 * i + 4]
        for j in range(4):
            output[i, :, j * q_part : (j + 1) * q_part] = own[j].astype(jnp.float32)


def finish_attention(members, layers, expert_total):
    share, q_part = layers[0][4].shape[1:]
    front = layers[0][0].shape[1] - 128
    total = len(layers)
    f32 = jnp.float32
    return pl.pallas_call(
        functools.partial(finish_attention_body, total),
        in_specs=[smem()] + [vmem()] * (5 * total),
        out_shape=[
            shaped((total, share, 4 * q_part), f32),
            shaped((total, share, 4 * (front - q_part)), f32),
            shaped((total, share, 4 * q_part), f32),
            shaped((total, expert_total, share), f32),
            shaped((total, 2, share), f32),
        ],
        compiler_params=kernel_params(),
    )(members, *[block for layer in layers for block in layer])


def finish_experts_body(down_total, *refs):
    gate_up, down = refs[-2:]
    half = gate_up.shape[3] // 2

    def total(first, count):
        values = [ref[...].astype(jnp.float32) for ref in refs[first : first + count]]
        return sum(values[1:], values[0])

    gate_up[0, 0, :, :half] = total(0, 2)
    gate_up[0, 0, :, half:] = total(2, 2)
    down[0, 0] = total(4, down_total)


def finish_experts(layer, layers, experts, held, sent, kept):
    rows, flat = held[0].shape
    half = flat // experts
    down_rows, width = held[2].shape[0] // experts, held[2].shape[1]
    gate_spec = pl.BlockSpec((rows, half), lambda e: (0, e))
    down_spec = pl.BlockSpec((down_rows, width), lambda e: (e, 0))
    downs = [part for part in (held[2], sent[2]) if part is not None]
    inputs = [held[0], sent[0], held[1], sent[1], *downs]
    return pl.pallas_call(
        functools.partial(finish_experts_body, len(downs)),
        grid=(experts,),
        in_specs=[gate_spec] * 4 + [down_spec] * len(downs) + [anywhere()] * len(kept),
        out_specs=[
            pl.BlockSpec((1, 1, rows, 2 * half), lambda e: (layer, e, 0, 0)),
            pl.BlockSpec((1, 1, down_rows, width), lambda e: (layer, e, 0, 0)),
        ],
        out_shape=[
            shaped((layers, experts, rows, 2 * half), jnp.float32),
            shaped((layers, experts, down_rows, width), jnp.float32),
        ],
        input_output_aliases={len(inputs) + i: i for i in range(len(kept))},
        compiler_params=kernel_params(),
    )(*inputs, *kept)


def rotate_ranks(values_in, axis_name, total, target_of):
    return lax.ppermute(values_in, axis_name, [(i, target_of(i)) for i in range(total)])


def swap_y(values_in):
    return rotate_ranks(values_in, "fsdp", 8, lambda i: i ^ 1)


def move_z(values_in, steps):
    return rotate_ranks(values_in, "fsdp", 8, lambda i: (i + 2 * steps) % 8)


def swap_core(values_in):
    return rotate_ranks(values_in, "ctx", 4, lambda i: i ^ 1)


def swap_x(values_in):
    return rotate_ranks(values_in, "ctx", 4, lambda i: i ^ 2)


def swap_both(values_in):
    return rotate_ranks(values_in, "ctx", 4, lambda i: i ^ 3)


def to_members(blocks):
    return [blocks[0], swap_core(blocks[1]), swap_x(blocks[2]), swap_both(blocks[3])]


def after(value, *others):
    return lax.optimization_barrier((value, *others))[0]


def wide(value):
    return value.astype(jnp.float32)


def fsdp_members(index):
    z, y = index // 2, index % 2
    return [((z + dz) % 4) * 2 + (y ^ dy) for dz in (0, 3, 2, 1) for dy in (0, 1)]


def gather_fsdp(block, work=None, beside=()):
    below = move_z(block, 1)
    own_mirror = swap_y(block)
    if work is None:
        below, own_mirror = after(below, own_mirror, beside[0]), after(own_mirror, below)
        far = move_z(below, 1)
        below_mirror = swap_y(after(below, own_mirror))
        far = after(far, below_mirror, beside[1])
        above = move_z(after(block, far), -1)
        far_mirror = swap_y(far)
        above = after(above, far_mirror, beside[2])
        half = block.shape[0] // 2
        above_mirrors = [swap_y(above[:half]), move_z(after(own_mirror, above)[half:], -1)]
        return [block, own_mirror, below, below_mirror, far, far_mirror, above, *above_mirrors]
    far = move_z(below, 1)
    below_mirror = swap_y(below)
    done = work(0, (after(block, below), own_mirror))
    above = move_z(after(block, far, done), -1)
    far_mirror = swap_y(after(far, done))
    done = work(1, (after(below, far), below_mirror))
    above_mirror = swap_y(after(above, done))
    work(2, (after(far, above), far_mirror))
    work(3, (above, above_mirror))
    return above_mirror


def scatter_fsdp(parts, beside=None, start=None, middle=None, late=None):
    low = jnp.bfloat16
    results = []

    def run(start):
        if beside:
            results.append(beside[len(results)](start))
            return jax.tree.leaves(results[-1])
        return []

    def held(value, *others):
        return after(value, *[other for other in others if other is not None])

    far = (wide(parts[4]) + wide(swap_y(held(parts[5], start)))).astype(low)
    from_far = move_z(far, 1)
    above_mirror = swap_y(held(parts[7], start))
    done = run(far)
    above = (wide(parts[6]) + wide(above_mirror) + wide(from_far)).astype(low)
    above = held(above, middle)
    from_below = move_z(above, 1)
    below_mirror = swap_y(after(parts[3], above))
    later = run(above)
    below = held((wide(parts[2]) + wide(below_mirror)).astype(low), late)
    from_above = move_z(after(below, *done), -1)
    own_mirror = swap_y(after(parts[1], below))
    done = later + run(below)
    own = wide(parts[0]) + wide(own_mirror) + wide(from_below)
    return after(own, *done) + wide(from_above), results, below


def gather_ctx(block):
    across = swap_x(block)
    return [block, swap_core(block), across, swap_core(across)]


def scatter_ctx(parts, beside=()):
    across = wide(parts[2]) + wide(swap_core(parts[3]))
    own = wide(parts[0]) + wide(swap_core(parts[1]))
    across = swap_x(across.astype(jnp.bfloat16))
    return own + wide(after(across, *beside))


def split_ranks(
    hidden_in,
    w_query,
    w_key_value,
    w_output,
    w_router,
    norm_gains,
    w_gate_up,
    w_down,
    expert_ids,
    out_grad,
):
    both = ("ctx", "fsdp")
    ctx_total, groups = 4, 8
    ctx_index, group_index = lax.axis_index("ctx"), lax.axis_index("fsdp")
    row_count, model_width = hidden_in.shape[1], hidden_in.shape[2]
    layer_total, share, _ = w_query.shape
    experts_here = w_gate_up.shape[1]
    expert_total = experts_here * groups
    kv_width = w_key_value.shape[2] // 2
    q_part, kv_part = model_width // ctx_total, kv_width // ctx_total
    qkv_part = q_part + 2 * kv_part
    pair_total = groups // 2
    low = jnp.bfloat16
    f32 = jnp.float32

    def dot_tn(a, b):
        return mm(a, b, TN)

    ctx_members = [ctx_index ^ r for r in range(ctx_total)]
    members = jnp.stack([*fsdp_members(group_index), *ctx_members]).astype(jnp.int32)
    natural_members = jnp.stack([*range(groups), *ctx_members]).astype(jnp.int32)
    ring_members = jnp.stack([ctx_members[r] for r in RING])
    ctx_ref = ctx_index.reshape(1).astype(jnp.int32)
    expert_lane = jnp.arange(128, dtype=jnp.int32)
    own_experts = [
        (
            expert_lane[None, :]
            == expert_total * i
            + group_index * experts_here
            + jnp.arange(8, dtype=jnp.int32)[:, None]
        ).astype(f32)
        for i in range(layer_total)
    ]
    gain_lane = expert_total * layer_total

    def ring(vector):
        return jnp.take(vector.reshape(ctx_total, -1), ring_members, axis=0).reshape(-1)

    places = jnp.concatenate(
        [row_positions((ctx_index ^ r) * row_count, row_count, row_count, ctx_total) for r in range(4)]
    )
    half_dim = HEAD_DIM // 2
    frequency = rope_base ** (-jnp.arange(half_dim, dtype=f32) / half_dim)
    angles = places.astype(f32)[:, None] * frequency[None, :]
    cosine, sine = jnp.cos(angles), jnp.sin(angles)
    tables = (
        jnp.concatenate([cosine] * 4, -1),
        jnp.concatenate([-sine, sine, -sine, sine], -1),
    )

    blocks = to_members(
        weight_blocks(
            members, w_query, w_key_value, w_router.transpose(0, 2, 1), norm_gains.transpose(0, 2, 1)
        )
    )
    packed = pack_shards(
        blocks,
        w_output,
        expert_ids.reshape(layer_total, row_count, TOP).transpose(0, 2, 1),
        qkv_part,
    )
    expert_weights, start = [[]], packed
    for part in [*(w_gate_up[0, e] for e in range(experts_here)), w_down[0]]:
        expert_weights[0].extend(gather_ctx(after(part, start)))
        start = expert_weights[0][-2]
    hidden_rows = gather_ctx(
        after(hidden_in.reshape(row_count, model_width), expert_weights[0][6])
    )
    hidden_roots = jnp.concatenate(
        [
            jnp.broadcast_to(rms_scaled(wide(block), 1.0)[1], (row_count, 128))
            for block in hidden_rows
        ],
        0,
    )
    joined = join_experts(after(w_gate_up[1], hidden_rows[1]), w_down[1])
    flat_shards = gather_fsdp(
        packed,
        None,
        [expert_weights[0][2], expert_weights[0][6], after(hidden_roots, joined)],
    )
    shards = [shard.reshape(-1, share, shard.shape[1]) for shard in flat_shards]
    flat_shards[7:] = [jnp.concatenate(flat_shards[7:], 0)]
    layer_part = qkv_part + q_part
    ready = after(shards[0], *expert_weights[0])
    small, qkv_weight, out_weight = place(
        members,
        [ready, *shards[1:]],
        [(layer_total * layer_part, 128, 0), (0, qkv_part, q_part)],
    )
    small = small.reshape(model_width, 128)
    attention_weights = [(qkv_weight.reshape(model_width, qkv_part), out_weight)]
    gains = [
        wide(small[:, gain_lane + 2 * i : gain_lane + 2 * i + 2]).T for i in range(layer_total)
    ]
    ring_gains = [ring(gains[i][0]) for i in range(layer_total)]

    def place_layer(i, start):
        qkv_weight, out_weight = place(
            members,
            [after(shards[0], start), *shards[1:]],
            [(i * layer_part, qkv_part, q_part)],
        )
        return qkv_weight.reshape(model_width, qkv_part), out_weight

    residual = wide(hidden_in.reshape(row_count, model_width))
    saved = []
    for i in range(layer_total):
        qkv_weight, out_weight = attention_weights[i]
        normed, root_first = rms_scaled(residual, gains[i][0])
        rows = hidden_rows if i == 0 else gather_ctx(normed.astype(low))
        branch, rows_first, qkv, attended, logs = attention_forward(
            ctx_ref, rows, qkv_weight, out_weight, qkv_part, tables, small,
            hidden_roots, gain_lane if i == 0 else None,
        )
        middle = residual + scatter_ctx(branch)
        normed_second, root_second = rms_scaled(middle, gains[i][1])
        parts, kept = [None] * groups, []

        def forward_work(group, pair):
            outs = experts_forward(
                group, pair_total, ctx_ref, pair, flat_shards[2 * group : 2 * group + 2],
                64 + TOP * i, expert_total * i, small,
                own_experts[i], expert_weights[i], kept,
            )
            parts[2 * group], parts[2 * group + 1] = outs[:2]
            kept[:] = outs[2:]
            return outs[0]

        normed_second = normed_second.astype(low)
        beside = None
        if i == 0:
            joined = after(joined, middle)
            expert_weights.append([lax.all_gather(joined, "ctx", axis=1, tiled=True)])
            beside = (lambda start: [], lambda start: place_layer(1, start), lambda start: [])
        last = gather_fsdp(normed_second, forward_work)
        rows_second, gate, up, probs = kept
        expert_sum, placed, _ = scatter_fsdp(parts, beside, last)
        if beside:
            attention_weights.append(placed[1])
        saved.append(
            (
                residual, root_first, rows_first, qkv, attended, logs,
                middle, root_second, rows_second, gate, up, probs, expert_sum,
            )
        )
        residual = middle + expert_sum
    hidden_out = residual.reshape(1, row_count, model_width).astype(low)
    grad = wide(out_grad.reshape(row_count, model_width))
    expert_grads = []

    def add_core(start, pairs, came):
        sums = [
            (dot_tn(after(part, start)[:, :half], grads) + wide(other)).astype(low)
            for (part, half, grads), other in zip(pairs, came, strict=True)
        ]
        return [(part[: part.shape[0] // 2], part[part.shape[0] // 2 :]) for part in sums]

    def finish_layer(i, pairs, start, kept):
        held, sent = [pair[0] for pair in pairs], [pair[1] for pair in pairs]
        held[0] = after(held[0], start)
        return finish_experts(i, layer_total, experts_here, held, sent, kept)

    for i in reversed(range(layer_total)):
        (
            residual, root_first, rows_first, qkv, attended, logs,
            middle, root_second, rows_second, gate, up, probs, expert_sum,
        ) = saved[i]
        qkv_weight, out_weight = attention_weights[i]
        mean_gate = jnp.sum(grad * expert_sum, -1, keepdims=True)
        mean_high = mean_gate.astype(low)
        mean_low = (mean_gate - wide(mean_high)).astype(low)
        lanes = jnp.where(expert_lane == 0, mean_high, jnp.where(expert_lane == 1, mean_low, 0))
        sent = jnp.concatenate([grad.astype(low), lanes.astype(low)], -1)
        parts, kept = [None] * groups, []
        if i == 0:
            whole_down = dot_tn(after(upper_hidden, sent), upper_grads).astype(low)
            halves = add_core(sent, *pending)
            upper_down = lax.psum_scatter(
                whole_down.reshape(ctx_total, -1, model_width), "ctx", scatter_dimension=0, tiled=True
            )
            upper_down = (upper_down.reshape(-1, model_width), None)
            expert_grads.insert(0, [(half[0], swap_x(half[1])) for half in halves] + [upper_down])

        def backward_work(group, pair):
            if i == 0 and group == 0:
                pair = (after(pair[0], whole_down, *jax.tree.leaves(halves)), pair[1])
            if i == 0 and group == 3:
                pair = (after(pair[0], expert_grads[0][0][1]), pair[1])
            outs = experts_backward(
                group, pair_total, ctx_ref, pair, probs, gate, up, small, own_experts[i],
                expert_weights[i], kept, i == 0,
            )
            parts[2 * group], parts[2 * group + 1] = outs[:2]
            kept[:] = outs[2:]
            return outs[0]

        last = gather_fsdp(sent, backward_work)
        grads_second, grad_gate, grad_up, hidden, grad_logits = kept
        half_width, half_hidden = model_width // 2, hidden.shape[1] // 2

        came = []
        pairs = [(rows_second, half_width, grad_gate), (rows_second, half_width, grad_up)]
        if i == 0:
            pairs.append((hidden, half_hidden, grads_second))

        def first_beside(start):
            for part, half, grads in pairs:
                came.append(swap_core(dot_tn(after(part, start)[:, half:], grads).astype(low)))
            return came

        last_gate = [expert_grads[0][1][1]] if i == 0 else []
        grad_second, small_grads, _ = scatter_fsdp(
            parts,
            (
                lambda start: [*first_beside(start), *last_gate],
                lambda start: dot_tn(after(rows_second, start), grad_logits),
                lambda start: [],
            ),
            last,
        )
        small_grads = small_grads[1]
        grad_middle, gain_second = rms_back(middle, root_second, gains[i][1], grad_second)
        grad_middle = grad_middle + grad
        branch_rows = grad_middle.astype(low)
        branch_grads = gather_ctx(branch_rows)
        if i > 0:
            pending = pairs, came
            upper_hidden, upper_grads = hidden, grads_second
        back, rows_branch, grad_qkv, gain_first = attention_backward(
            ctx_ref, branch_grads, rows_first, qkv_weight, out_weight, qkv,
            logs, tables,
        )
        gain_first = gain_first[0] / ring_gains[i]
        gain_second = ring(after(gain_second, back[0]))
        small_grads = jnp.where(
            expert_lane == gain_lane,
            gain_first[:, None],
            jnp.where(expert_lane == gain_lane + 1, gain_second[:, None], small_grads),
        ).astype(low)
        if i == 0:
            far = (wide(packs[4]) + wide(swap_y(after(packs[5], grad_second)))).astype(low)
            above_mirror, from_far = swap_y(after(packs[7], grad_second)), move_z(far, 1)
            above = (wide(packs[6]) + wide(above_mirror) + wide(from_far)).astype(low)
            above = after(above, back[0])
            from_below, below_mirror = move_z(above, 1), swap_y(after(packs[3], above))
            rows_first = after(rows_first, above)
        qkv_grads = dot_tn(rows_first, grad_qkv).astype(low)
        out_grads = dot_tn(attended, rows_branch).astype(low)
        layer_packs = pack_grads(
            members,
            qkv_grads.reshape(ctx_total, groups, share, qkv_part),
            small_grads.reshape(ctx_total, groups, share, 128),
            out_grads,
            True,
        )
        flat_packs = [pack.reshape(ctx_total * share, -1) for pack in layer_packs]
        if i == 0:
            below = after((wide(packs[2]) + wide(below_mirror)).astype(low), layer_packs[0])
            from_above, own_mirror = move_z(below, -1), swap_y(after(packs[1], below))
            upper = wide(packs[0]) + wide(own_mirror) + wide(from_below) + wide(from_above)
            halves = add_core(below, pairs[:1], came[:1])
            crossed = [swap_x(halves[0][1])]

            def second_beside(start):
                halves.extend(add_core(start, pairs[1:], came[1:]))
                crossed.extend(swap_x(half[1]) for half in halves[1:])
                return finish_layer(1, expert_grads[0], start, []), halves

            beside = [
                second_beside,
                lambda start: crossed[0],
                lambda start: crossed[1],
            ]
            lower, finished, _ = scatter_fsdp(flat_packs, beside, below, None, upper)
            expert_grads.insert(
                0, [(half[0], other) for half, other in zip(halves, crossed, strict=True)]
            )
            attention_grads = [lower, upper]
            layer_packs = [upper]
        grad_first = scatter_ctx(back, layer_packs)
        grad_input, _ = rms_back(residual, root_first, gains[i][0], grad_first)
        grad = grad_input + grad_middle
        packs = flat_packs
    attention_grads = [
        part.astype(low).reshape(ctx_total, share, -1) for part in attention_grads
    ]
    front = qkv_part + 128
    blocks = to_members(
        [jnp.concatenate([part[r, :, :front] for part in attention_grads], -1) for r in range(ctx_total)]
    )
    query_out, key_value_out, output_out, router_out, gains_out = finish_attention(
        members,
        [
            [block[:, i * front : (i + 1) * front] for block in blocks] + [part[..., front:]]
            for i, part in enumerate(attention_grads)
        ],
        expert_total,
    )
    outs = finish_layer(0, expert_grads[0], attention_grads[0], finished[0][0])
    return (
        hidden_out,
        grad.reshape(1, row_count, model_width),
        query_out,
        key_value_out,
        output_out,
        router_out.transpose(0, 2, 1),
        gains_out.transpose(0, 2, 1),
        outs[0],
        outs[1],
    )


def solution(mesh):
    split = mesh.shape["ctx"] == 4 and mesh.shape["fsdp"] == 8
    return jax.shard_map(
        split_ranks if split else on_device,
        mesh=mesh,
        in_specs=(
            P("fsdp", "ctx", None),
            P(None, ("ctx", "fsdp"), None),
            P(None, ("ctx", "fsdp"), None),
            P(None, ("ctx", "fsdp"), None),
            P(None, ("ctx", "fsdp"), None),
            P(None, ("ctx", "fsdp"), None),
            P(None, "fsdp", "ctx", None),
            P(None, "fsdp", "ctx", None),
            P(None, "fsdp", "ctx", None),
            P("fsdp", "ctx", None),
        ),
        out_specs=(
            P("fsdp", "ctx", None),
            P("fsdp", "ctx", None),
            P(None, ("ctx", "fsdp"), None),
            P(None, ("ctx", "fsdp"), None),
            P(None, ("ctx", "fsdp"), None),
            P(None, ("ctx", "fsdp"), None),
            P(None, ("ctx", "fsdp"), None),
            P(None, "fsdp", "ctx", None),
            P(None, "fsdp", "ctx", None),
        ),
        check_vma=False,
    )
```

```python
import functools
import math

import jax
import jax.numpy as jnp
from jax import lax
from jax.experimental import pallas as pl
from jax.experimental.pallas import tpu as pltpu
from jax.sharding import PartitionSpec as P

HEADS = 24
KV_HEADS = 8
HEAD_DIM = 64
FE = 512
TOP = 8


highest = lax.Precision.HIGHEST
epsilon = 1e-06
rope_base = 10000.0
masked_score = -1e30


def row_positions(first_row, row_total, row_count, shards):
    indices = first_row + jnp.arange(row_total, dtype=jnp.int32)
    shard_of = indices // row_count
    within = indices % row_count
    half_rows = row_count // 2
    return jnp.where(
        within < half_rows,
        shard_of * half_rows + within,
        (2 * shards - 1 - shard_of) * half_rows + within - half_rows,
    )


def rotate(values_in, places, direction):
    half_dim = values_in.shape[-1] // 2
    frequency = rope_base ** (-jnp.arange(half_dim, dtype=jnp.float32) / half_dim)
    angles = places.astype(jnp.float32)[:, None] * frequency[None, :]
    cosine_part = jnp.cos(angles)[:, None, :]
    sine_part = direction * jnp.sin(angles)[:, None, :]
    front_half = values_in[..., :half_dim]
    back_half = values_in[..., half_dim:]
    return jnp.concatenate(
        [
            front_half * cosine_part - back_half * sine_part,
            back_half * cosine_part + front_half * sine_part,
        ],
        -1,
    )


def rms_scaled(residual, gain_vector):
    inverse_root = lax.rsqrt(jnp.mean(residual * residual, -1, keepdims=True) + epsilon)
    return (residual * inverse_root * gain_vector, inverse_root)


def rms_back(residual, inverse_root, gain_vector, grad_normed):
    grad_gain = jnp.sum(grad_normed * residual * inverse_root, 0)
    weighted = gain_vector * grad_normed
    cubed = inverse_root * inverse_root * inverse_root
    grad_residual = inverse_root * weighted - residual * cubed * jnp.mean(
        residual * weighted, -1, keepdims=True
    )
    return (grad_residual, grad_gain)


def route_table(routing_rows, expert_total, row_count, capacity):
    top_count = routing_rows.shape[1]
    chosen_mask = (
        routing_rows[:, :, None] == jnp.arange(expert_total, dtype=jnp.int32)[None, None, :]
    )
    expert_used = jnp.sum(chosen_mask.astype(jnp.int32), 1)
    slot_all = jnp.cumsum(expert_used, 0) - expert_used
    slot_taken = jnp.sum(jnp.where(chosen_mask, slot_all[:, None, :], 0), -1)
    target_slots = routing_rows * capacity + slot_taken
    entry_rows = jnp.full((expert_total * capacity,), row_count * top_count, jnp.int32)
    entry_rows = entry_rows.at[target_slots.reshape(-1)].set(
        jnp.arange(row_count * top_count, dtype=jnp.int32)
    )
    return (chosen_mask, target_slots, entry_rows)


def fold_keys(running, key_piece, queries, query_places, row_count, shards, kv_width):
    piece_rows = key_piece.shape[0]
    step_rows = math.gcd(piece_rows, row_count)
    step_total = piece_rows // step_rows
    blocks_in = key_piece.reshape(step_total, step_rows, key_piece.shape[1])
    heads_kv = queries.shape[1]
    head_size = queries.shape[3]
    score_scale = head_size ** (-0.5)

    def fold_one_step(state_in, inputs):
        block_rows, block_index = inputs
        key_places = row_positions(block_index * step_rows, step_rows, row_count, shards)
        key_rows = block_rows[:, :kv_width].reshape(step_rows, heads_kv, head_size)
        value_rows = block_rows[:, kv_width:].reshape(step_rows, heads_kv, head_size)
        scores = (
            jnp.einsum("qhgd,khd->hgqk", queries, key_rows, preferred_element_type=jnp.float32)
            * score_scale
        )
        visible = query_places[:, None] >= key_places[None, :]
        scores = jnp.where(visible, scores, masked_score)
        old_top, old_total, old_sum = state_in
        new_top = jnp.maximum(old_top, jnp.max(scores, -1))
        shrink = jnp.exp(old_top - new_top)
        weights = jnp.where(visible, jnp.exp(scores - new_top[..., None]), 0.0)
        new_total = old_total * shrink + jnp.sum(weights, -1)
        new_sum = old_sum * shrink[..., None] + jnp.einsum(
            "hgqk,khd->hgqd",
            weights.astype(jnp.bfloat16),
            value_rows,
            preferred_element_type=jnp.float32,
        )
        return ((new_top, new_total, new_sum), None)

    running, _ = lax.scan(
        fold_one_step, running, (blocks_in, jnp.arange(step_total, dtype=jnp.int32))
    )
    return running


def attend_back(
    queries,
    query_places,
    gathered,
    out_exact,
    grad_attended,
    log_total,
    row_count,
    shards,
    kv_width,
):
    heads_kv = queries.shape[1]
    head_size = queries.shape[3]
    score_scale = head_size ** (-0.5)
    delta_rows = jnp.transpose(
        jnp.sum(grad_attended.astype(jnp.float32) * out_exact, -1), (1, 2, 0)
    )
    blocks_in = gathered.reshape(shards, row_count, gathered.shape[1])

    def attend_one_step(grad_queries, inputs):
        block_rows, block_index = inputs
        key_places = row_positions(block_index * row_count, row_count, row_count, shards)
        key_rows = block_rows[:, :kv_width].reshape(row_count, heads_kv, head_size)
        value_rows = block_rows[:, kv_width:].reshape(row_count, heads_kv, head_size)
        scores = (
            jnp.einsum("qhgd,khd->hgqk", queries, key_rows, preferred_element_type=jnp.float32)
            * score_scale
        )
        visible = query_places[:, None] >= key_places[None, :]
        probabilities = jnp.where(visible, jnp.exp(scores - log_total[..., None]), 0.0)
        rounded = probabilities.astype(jnp.bfloat16)
        grad_values = jnp.einsum(
            "hgqk,qhgd->khd", rounded, grad_attended, preferred_element_type=jnp.float32
        )
        grad_probs = jnp.einsum(
            "qhgd,khd->hgqk", grad_attended, value_rows, preferred_element_type=jnp.float32
        )
        grad_scores = (probabilities * (grad_probs - delta_rows[..., None])).astype(jnp.bfloat16)
        grad_queries = grad_queries + score_scale * jnp.einsum(
            "hgqk,khd->qhgd", grad_scores, key_rows, preferred_element_type=jnp.float32
        )
        grad_keys = score_scale * jnp.einsum(
            "hgqk,qhgd->khd", grad_scores, queries, preferred_element_type=jnp.float32
        )
        return (
            grad_queries,
            jnp.concatenate(
                [grad_keys.reshape(row_count, kv_width), grad_values.reshape(row_count, kv_width)],
                -1,
            ),
        )

    start_grad = jnp.zeros(queries.shape, jnp.float32)
    grad_queries, grad_blocks = lax.scan(
        attend_one_step, start_grad, (blocks_in, jnp.arange(shards, dtype=jnp.int32))
    )
    return (grad_queries, grad_blocks.reshape(shards * row_count, gathered.shape[1]))


def on_device(
    hidden_in,
    w_query,
    w_key_value,
    w_output,
    w_router,
    norm_gains,
    w_gate_up,
    w_down,
    expert_ids,
    out_grad,
):
    shards = lax.axis_size("ctx")
    groups = lax.axis_size("fsdp")
    shard_index = lax.axis_index("ctx")
    row_count = hidden_in.shape[1]
    model_width = hidden_in.shape[2]
    layer_total = w_query.shape[0]
    experts_here = w_gate_up.shape[1]
    expert_total = experts_here * groups
    capacity = min(row_count, 3 * row_count * TOP // (2 * expert_total))
    kv_width = w_key_value.shape[2] // 2
    group_size = HEADS // KV_HEADS
    query_places = row_positions(shard_index * row_count, row_count, row_count, shards)
    residual = hidden_in.reshape(row_count, model_width).astype(jnp.float32)
    saved = []
    for layer_index in range(layer_total):
        query_weight, key_value_weight, output_weight, router_weight, gains = (
            lax.all_gather(w_query[layer_index], ("ctx", "fsdp"), axis=0, tiled=True),
            lax.all_gather(w_key_value[layer_index], ("ctx", "fsdp"), axis=0, tiled=True),
            lax.all_gather(w_output[layer_index], ("ctx", "fsdp"), axis=0, tiled=True),
            lax.all_gather(w_router[layer_index], ("ctx", "fsdp"), axis=0, tiled=True),
            lax.all_gather(norm_gains[layer_index], ("ctx", "fsdp"), axis=0, tiled=True),
        )
        gate_up_weight, down_weight = (
            lax.all_gather(w_gate_up[layer_index], "ctx", axis=1, tiled=True),
            lax.all_gather(w_down[layer_index], "ctx", axis=1, tiled=True),
        )
        gain_pair = gains.astype(jnp.float32)
        normed_first, root_first = rms_scaled(residual, gain_pair[:, 0])
        normed_first_low = normed_first.astype(jnp.bfloat16)
        query_raw = jnp.dot(normed_first_low, query_weight, preferred_element_type=jnp.float32)
        key_value_raw = jnp.dot(
            normed_first_low, key_value_weight, preferred_element_type=jnp.float32
        )
        queries = rotate(query_raw.reshape(row_count, HEADS, HEAD_DIM), query_places, 1.0).astype(
            jnp.bfloat16
        )
        queries = queries.reshape(row_count, KV_HEADS, group_size, HEAD_DIM)
        key_turned = rotate(
            key_value_raw[:, :kv_width].reshape(row_count, KV_HEADS, HEAD_DIM), query_places, 1.0
        )
        key_value_low = jnp.concatenate(
            [key_turned.reshape(row_count, kv_width), key_value_raw[:, kv_width:]], -1
        ).astype(jnp.bfloat16)
        start_state = (
            jnp.full((KV_HEADS, group_size, row_count), masked_score, jnp.float32),
            jnp.zeros((KV_HEADS, group_size, row_count), jnp.float32),
            jnp.zeros((KV_HEADS, group_size, row_count, HEAD_DIM), jnp.float32),
        )
        top_score, score_total, accumulated = fold_keys(
            start_state,
            lax.all_gather(key_value_low, "ctx", axis=0, tiled=True),
            queries,
            query_places,
            row_count,
            shards,
            kv_width,
        )
        out_exact = jnp.transpose(accumulated / score_total[..., None], (2, 0, 1, 3))
        log_total = top_score + jnp.log(score_total)
        attended = out_exact.reshape(row_count, model_width).astype(jnp.bfloat16)
        middle = residual + jnp.dot(attended, output_weight, preferred_element_type=jnp.float32)
        normed_second, root_second = rms_scaled(middle, gain_pair[:, 1])
        normed_second_low = normed_second.astype(jnp.bfloat16)
        chosen_mask, target_slots, entry_rows = route_table(
            expert_ids[layer_index].reshape(row_count, TOP), expert_total, row_count, capacity
        )
        padded_rows = jnp.concatenate(
            [normed_second_low, jnp.zeros((1, model_width), jnp.bfloat16)], 0
        )
        send_buffer = padded_rows[jnp.minimum(entry_rows // TOP, row_count)].reshape(
            groups, experts_here, capacity, model_width
        )
        received = lax.all_to_all(send_buffer, "fsdp", split_axis=0, concat_axis=0, tiled=True)
        gate_up = jnp.einsum(
            "serd,edf->serf", received, gate_up_weight, preferred_element_type=jnp.float32
        )
        hidden = (jax.nn.silu(gate_up[..., :FE]) * gate_up[..., FE:]).astype(jnp.bfloat16)
        expert_out = jnp.einsum(
            "serf,efd->serd", hidden, down_weight, preferred_element_type=jnp.float32
        ).astype(jnp.bfloat16)
        returned = lax.all_to_all(
            expert_out, "fsdp", split_axis=0, concat_axis=0, tiled=True
        ).reshape(expert_total * capacity, model_width)
        picked = returned[target_slots]
        logits = jnp.dot(normed_second_low, router_weight, preferred_element_type=jnp.float32)
        chosen_logits = jnp.sum(jnp.where(chosen_mask, logits[:, None, :], 0.0), -1)
        gate_probs = jax.nn.softmax(chosen_logits, axis=-1)
        expert_sum = jnp.sum(gate_probs[..., None] * picked.astype(jnp.float32), 1)
        saved.append(
            (
                residual,
                root_first,
                normed_first_low,
                queries,
                key_value_low,
                out_exact,
                log_total,
                attended,
                middle,
                root_second,
                normed_second_low,
                chosen_mask,
                target_slots,
                entry_rows,
                received,
                gate_up,
                hidden,
                picked,
                gate_probs,
                query_weight,
                key_value_weight,
                output_weight,
                router_weight,
                gain_pair,
                gate_up_weight,
                down_weight,
            )
        )
        residual = middle + expert_sum
    hidden_out = residual.reshape(1, row_count, model_width).astype(jnp.bfloat16)
    grad_residual = out_grad.reshape(row_count, model_width).astype(jnp.float32)
    (
        query_parts,
        key_value_parts,
        output_parts,
        router_parts,
        gain_parts,
        gate_up_parts,
        down_parts,
    ) = ([], [], [], [], [], [], [])
    for layer_index in reversed(range(layer_total)):
        (
            layer_input,
            root_first,
            normed_first_low,
            queries,
            key_value_low,
            out_exact,
            log_total,
            attended,
            middle,
            root_second,
            normed_second_low,
            chosen_mask,
            target_slots,
            entry_rows,
            received,
            gate_up,
            hidden,
            picked,
            gate_probs,
            query_weight,
            key_value_weight,
            output_weight,
            router_weight,
            gain_pair,
            gate_up_weight,
            down_weight,
        ) = saved[layer_index]
        grad_gates = jnp.sum(grad_residual[:, None, :] * picked.astype(jnp.float32), -1)
        grad_leaving = (
            (gate_probs[..., None] * grad_residual[:, None, :])
            .astype(jnp.bfloat16)
            .reshape(row_count * TOP, model_width)
        )
        grad_padded = jnp.concatenate([grad_leaving, jnp.zeros((1, model_width), jnp.bfloat16)], 0)
        grad_send = grad_padded[entry_rows].reshape(groups, experts_here, capacity, model_width)
        grad_received = lax.all_to_all(grad_send, "fsdp", split_axis=0, concat_axis=0, tiled=True)
        grad_hidden = jnp.einsum(
            "serd,efd->serf", grad_received, down_weight, preferred_element_type=jnp.float32
        )
        grad_down_part = jnp.einsum(
            "serf,serd->efd", hidden, grad_received, preferred_element_type=jnp.float32
        )
        gate_part = gate_up[..., :FE]
        up_part = gate_up[..., FE:]
        sigmoid_gate = jax.nn.sigmoid(gate_part)
        grad_gate = grad_hidden * up_part * sigmoid_gate * (1.0 + gate_part * (1.0 - sigmoid_gate))
        grad_up = grad_hidden * gate_part * sigmoid_gate
        grad_gate_up_rows = jnp.concatenate([grad_gate, grad_up], -1).astype(jnp.bfloat16)
        grad_gate_up_part = jnp.einsum(
            "serd,serf->edf", received, grad_gate_up_rows, preferred_element_type=jnp.float32
        )
        grad_entering = jnp.einsum(
            "serf,edf->serd", grad_gate_up_rows, gate_up_weight, preferred_element_type=jnp.float32
        ).astype(jnp.bfloat16)
        grad_returned = lax.all_to_all(
            grad_entering, "fsdp", split_axis=0, concat_axis=0, tiled=True
        ).reshape(expert_total * capacity, model_width)
        grad_normed_second = jnp.sum(grad_returned[target_slots].astype(jnp.float32), 1)
        gate_mean = jnp.sum(gate_probs * grad_gates, -1, keepdims=True)
        grad_chosen = gate_probs * (grad_gates - gate_mean)
        grad_logits = jnp.sum(jnp.where(chosen_mask, grad_chosen[..., None], 0.0), 1)
        grad_router_part = jnp.dot(
            normed_second_low.astype(jnp.float32).T, grad_logits, precision=highest
        )
        grad_normed_second = grad_normed_second + jnp.dot(
            grad_logits, router_weight.astype(jnp.float32).T, precision=highest
        )
        grad_middle, grad_gain_second = rms_back(
            middle, root_second, gain_pair[:, 1], grad_normed_second
        )
        grad_middle = grad_middle + grad_residual
        grad_branch = grad_middle.astype(jnp.bfloat16)
        grad_output_part = jnp.einsum(
            "rd,re->de", attended, grad_branch, preferred_element_type=jnp.float32
        )
        grad_attended = jnp.einsum(
            "re,de->rd", grad_branch, output_weight, preferred_element_type=jnp.float32
        ).astype(jnp.bfloat16)
        grad_attended = grad_attended.reshape(row_count, KV_HEADS, group_size, HEAD_DIM)
        gathered = lax.all_gather(key_value_low, "ctx", axis=0, tiled=True)
        grad_queries, grad_key_value_all = attend_back(
            queries,
            query_places,
            gathered,
            out_exact,
            grad_attended,
            log_total,
            row_count,
            shards,
            kv_width,
        )
        grad_key_value_own = lax.psum_scatter(
            grad_key_value_all.astype(jnp.bfloat16), "ctx", scatter_dimension=0, tiled=True
        ).astype(jnp.float32)
        grad_keys = rotate(
            grad_key_value_own[:, :kv_width].reshape(row_count, KV_HEADS, HEAD_DIM),
            query_places,
            -1.0,
        )
        grad_key_value_low = jnp.concatenate(
            [grad_keys.reshape(row_count, kv_width), grad_key_value_own[:, kv_width:]], -1
        ).astype(jnp.bfloat16)
        grad_query_low = (
            rotate(grad_queries.reshape(row_count, HEADS, HEAD_DIM), query_places, -1.0)
            .reshape(row_count, model_width)
            .astype(jnp.bfloat16)
        )
        grad_query_part = jnp.einsum(
            "rd,re->de", normed_first_low, grad_query_low, preferred_element_type=jnp.float32
        )
        grad_key_value_part = jnp.einsum(
            "rd,re->de", normed_first_low, grad_key_value_low, preferred_element_type=jnp.float32
        )
        grad_normed_first = jnp.einsum(
            "re,de->rd", grad_query_low, query_weight, preferred_element_type=jnp.float32
        ) + jnp.einsum(
            "re,de->rd", grad_key_value_low, key_value_weight, preferred_element_type=jnp.float32
        )
        grad_input, grad_gain_first = rms_back(
            layer_input, root_first, gain_pair[:, 0], grad_normed_first
        )
        grad_residual = grad_input + grad_middle
        grad_gain_part = jnp.stack([grad_gain_first, grad_gain_second], -1)
        query_parts.insert(0, grad_query_part)
        key_value_parts.insert(0, grad_key_value_part)
        output_parts.insert(0, grad_output_part)
        router_parts.insert(0, grad_router_part)
        gain_parts.insert(0, grad_gain_part)
        gate_up_parts.insert(0, grad_gate_up_part)
        down_parts.insert(0, grad_down_part)
    stacked_query = jnp.stack(query_parts, 0)
    stacked_key_value = jnp.stack(key_value_parts, 0)
    stacked_output = jnp.stack(output_parts, 0)
    stacked_router = jnp.stack(router_parts, 0)
    stacked_gains = jnp.stack(gain_parts, 0)
    stacked_gate_up = jnp.stack(gate_up_parts, 0)
    stacked_down = jnp.stack(down_parts, 0)
    stacked_query, stacked_key_value, stacked_output, stacked_router, stacked_gains = (
        lax.psum_scatter(stacked_query, ("ctx", "fsdp"), scatter_dimension=1, tiled=True),
        lax.psum_scatter(stacked_key_value, ("ctx", "fsdp"), scatter_dimension=1, tiled=True),
        lax.psum_scatter(stacked_output, ("ctx", "fsdp"), scatter_dimension=1, tiled=True),
        lax.psum_scatter(stacked_router, ("ctx", "fsdp"), scatter_dimension=1, tiled=True),
        lax.psum_scatter(stacked_gains, ("ctx", "fsdp"), scatter_dimension=1, tiled=True),
    )
    stacked_gate_up, stacked_down = (
        lax.psum_scatter(
            stacked_gate_up.astype(jnp.bfloat16), "ctx", scatter_dimension=2, tiled=True
        ).astype(jnp.float32),
        lax.psum_scatter(
            stacked_down.astype(jnp.bfloat16), "ctx", scatter_dimension=2, tiled=True
        ).astype(jnp.float32),
    )
    grad_hidden = grad_residual.reshape(1, row_count, model_width)
    return (
        hidden_out,
        grad_hidden,
        stacked_query,
        stacked_key_value,
        stacked_output,
        stacked_router,
        stacked_gains,
        stacked_gate_up,
        stacked_down,
    )


NN = (((1,), (0,)), ((), ()))
NT = (((1,), (1,)), ((), ()))
TN = (((0,), (0,)), ((), ()))
FE_STEP = 512
KERNEL_MIB = 58


def mm(a, b, dims=NN):
    return lax.dot_general(a, b, dims, preferred_element_type=jnp.float32)


def whole(shape):
    return pl.BlockSpec(shape, lambda *_: (0,) * len(shape))


def anywhere():
    return pl.BlockSpec(memory_space=pl.ANY)


def kernel_params():
    return pltpu.CompilerParams(vmem_limit_bytes=KERNEL_MIB * 1024 * 1024)


def shaped(shape, dtype=jnp.bfloat16):
    return jax.ShapeDtypeStruct(shape, dtype)


RING = (0, 2, 1, 3)


def bring_expert_weights(bring, ctx_ref, weights, w_gate_up_here, w_down_here, e, p, down_first=False):
    hidden_width, width = w_down_here.shape[1:]
    copies, downs = [], []

    def bring_gate_up():
        for side in range(2):
            span = slice(side * hidden_width + p * FE_STEP, side * hidden_width + (p + 1) * FE_STEP)
            if len(weights) == 1:
                copies.append(bring(weights[0].at[e, :, span], w_gate_up_here.at[e, :, span]))
                continue
            for r in range(4):
                quarter = weights[4 * e + r]
                rows = quarter.shape[0]
                at = pl.ds(pl.multiple_of((ctx_ref[0] ^ r) * rows, rows), rows)
                copies.append(bring(quarter.at[:, span], w_gate_up_here.at[e, at, span]))

    def bring_down():
        if p == 0:
            rows, part = hidden_width // 4, width // 3
            for r in range(4):
                if len(weights) > 1:
                    at = pl.ds(pl.multiple_of((ctx_ref[0] ^ r) * rows, rows), rows)
                    downs.append(bring(weights[-4 + r].at[e], w_down_here.at[e, at, :]))
                    continue
                for b in range(3):
                    source = slice((3 * r + b) * rows, (3 * r + b + 1) * rows)
                    downs.append(
                        bring(
                            weights[0].at[e, source, 2 * hidden_width :],
                            w_down_here.at[e, r * rows : (r + 1) * rows, b * part : (b + 1) * part],
                        )
                    )

    for part in (bring_down, bring_gate_up) if down_first else (bring_gate_up, bring_down):
        part()
    return copies, downs


def join_experts(gate_up, down):
    part = down.shape[2] // 3
    return jnp.concatenate(
        [gate_up, jnp.concatenate([down[:, :, b * part : (b + 1) * part] for b in range(3)], 1)], -1
    )


def experts_forward_body(weight_total, group, first_id, lane_offset, ctx_ref, rows_0, rows_1, ids_0, ids_1, router_in, own_in, *refs):
    (out_0, out_1, all_rows, all_gate, all_up, all_probs) = refs[-19:-13]
    (
        rows, w_gate_up_here, w_down_here, gate_here, up_here, probs, ring_rows,
        ids, router, own, result, in_sems, out_sems,
    ) = refs[-13:]
    block, width = rows_0.shape
    count = 2 * block
    expert_count, hidden_width = w_down_here.shape[0], w_down_here.shape[1]
    steps = hidden_width // FE_STEP
    incoming = []

    def bring(source, target):
        copy = pltpu.make_async_copy(source, target, in_sems.at[len(incoming)])
        copy.start()
        incoming.append(copy)
        return copy

    span = pl.ds(group * count, count)
    ids_at = ids_0.shape[1] - 128
    row_copies = [
        bring(rows_0, rows.at[:block]),
        bring(rows_1, rows.at[block:]),
        bring(ids_0.at[:block, ids_at:], ids.at[:block]),
        bring(ids_1.at[:block, ids_at:], ids.at[block:]),
        bring(router_in, router),
        bring(own_in, own),
    ]
    weight_copies = []
    for e in range(expert_count):
        for p in range(steps):
            weight_copies.append(
                bring_expert_weights(bring, ctx_ref, refs[:weight_total], w_gate_up_here, w_down_here, e, p)
            )
    outgoing = []

    def send(source, target):
        copy = pltpu.make_async_copy(source, target, out_sems.at[len(outgoing)])
        copy.start()
        outgoing.append(copy)

    for copy in row_copies:
        copy.wait()
    lane = lax.broadcasted_iota(jnp.int32, probs.shape, 1).astype(jnp.float32)
    chosen_ids = ids[...].astype(jnp.float32) + lane_offset
    listed = lane == chosen_ids[:, first_id : first_id + 1]
    for k in range(1, TOP):
        at = first_id + k
        listed = jnp.logical_or(listed, lane == chosen_ids[:, at : at + 1])
    logits = jnp.where(listed, mm(rows[...], router[...]), masked_score)
    weights = jnp.exp(logits - jnp.max(logits, -1, keepdims=True))
    gates = weights / jnp.sum(weights, -1, keepdims=True)
    probs[...] = gates
    part = width // 4
    for place, r in enumerate(RING):
        at = pl.multiple_of((ctx_ref[0] ^ r) * part, part)
        ring_rows[:, place * part : (place + 1) * part] = rows[:, pl.ds(at, part)]
    send(ring_rows, all_rows.at[span])
    send(probs, all_probs.at[span])
    total = jnp.zeros((count, width), jnp.float32)
    for e in range(expert_count):
        chosen = jnp.sum(gates * own[e : e + 1, :], -1, keepdims=True)
        for p in range(steps):
            for copy in weight_copies[e * steps + p][0]:
                copy.wait()
            lower = slice(p * FE_STEP, (p + 1) * FE_STEP)
            upper = slice(hidden_width + p * FE_STEP, hidden_width + (p + 1) * FE_STEP)
            gate = mm(rows[...], w_gate_up_here[e, :, lower])
            up = mm(rows[...], w_gate_up_here[e, :, upper])
            flat = slice(e * hidden_width + p * FE_STEP, e * hidden_width + (p + 1) * FE_STEP)
            gate_here[:, flat] = gate.astype(jnp.bfloat16)
            up_here[:, flat] = up.astype(jnp.bfloat16)
            hidden = (gate * jax.nn.sigmoid(gate) * up * chosen).astype(jnp.bfloat16)
            for copy in weight_copies[e * steps + p][1]:
                copy.wait()
            total = total + mm(hidden, w_down_here[e, lower, :])
    send(gate_here, all_gate.at[span])
    send(up_here, all_up.at[span])
    result[...] = total.astype(jnp.bfloat16)
    send(result.at[:block], out_0)
    send(result.at[block:], out_1)
    for copy in outgoing:
        copy.wait()


def vmem():
    return pl.BlockSpec(memory_space=pltpu.VMEM)


def smem():
    return pl.BlockSpec(memory_space=pltpu.SMEM)


def expert_shapes(weights):
    if len(weights) == 1:
        count, width, columns = weights[0].shape
        hidden_width = (columns - width // 3) // 2
    else:
        count, rows, width = weights[-1].shape
        hidden_width = 4 * rows
    return (count, width, 2 * hidden_width), (count, hidden_width, width)


def expert_cost(count, width, expert_count, hidden_width):
    return pl.CostEstimate(
        flops=6 * count * width * expert_count * hidden_width,
        bytes_accessed=6 * width * expert_count * hidden_width,
        transcendentals=count * expert_count * hidden_width,
    )


def experts_forward(
    group, groups, ctx_ref, rows, ids, first_id, lane_offset, router, own, weights, kept
):
    block, width = rows[0].shape
    count = 2 * block
    gate_up_shape, down_shape = expert_shapes(weights)
    expert_count, hidden_width = down_shape[0], down_shape[1]
    flat = expert_count * hidden_width
    low, f32 = jnp.bfloat16, jnp.float32
    inputs = [ctx_ref, *rows, *ids, router, own, *weights, *kept]
    return pl.pallas_call(
        functools.partial(experts_forward_body, len(weights), group, first_id, lane_offset),
        in_specs=[smem()] + [anywhere()] * (6 + len(weights) + len(kept)),
        out_specs=[anywhere()] * 6,
        out_shape=[
            shaped((block, width)),
            shaped((block, width)),
            shaped((groups * count, width)),
            shaped((groups * count, flat)),
            shaped((groups * count, flat)),
            shaped((groups * count, 128), f32),
        ],
        input_output_aliases={7 + len(weights) + i: 2 + i for i in range(len(kept))},
        scratch_shapes=[
            pltpu.VMEM((count, width), low),
            pltpu.VMEM(gate_up_shape, low),
            pltpu.VMEM(down_shape, low),
            pltpu.VMEM((count, flat), low),
            pltpu.VMEM((count, flat), low),
            pltpu.VMEM((count, 128), f32),
            pltpu.VMEM((count, width), low),
            pltpu.VMEM((count, 128), low),
            pltpu.VMEM(router.shape, low),
            pltpu.VMEM(own.shape, f32),
            pltpu.VMEM((count, width), low),
            pltpu.SemaphoreType.DMA((6 + 8 * flat // FE_STEP + 24 * expert_count,)),
            pltpu.SemaphoreType.DMA((6,)),
        ],
        compiler_params=kernel_params(),
        cost_estimate=expert_cost(count, width, expert_count, hidden_width),
    )(*inputs)


def experts_backward_body(weight_total, ring, group, ctx_ref, grads_0, grads_1, probs_in, gate_in, up_in, router_in, own_in, *refs):
    out_0, out_1, all_grads, all_grad_gate, all_grad_up, all_hidden, all_logits = refs[-23:-16]
    (
        sent, w_gate_up_here, w_down_here, gates, ups, probs, grads, grad_gates, grad_ups,
        hiddens, logits, router, own, result, in_sems, out_sems,
    ) = refs[-16:]
    block, width = out_0.shape
    count = 2 * block
    expert_count, hidden_width = w_down_here.shape[0], w_down_here.shape[1]
    steps = hidden_width // FE_STEP
    rows_here = pl.ds(group * count, count)
    incoming = []

    def bring(source, target):
        copy = pltpu.make_async_copy(source, target, in_sems.at[len(incoming)])
        copy.start()
        incoming.append(copy)
        return copy

    first_copies = [
        bring(grads_0, sent.at[:block]),
        bring(grads_1, sent.at[block:]),
        bring(probs_in.at[rows_here], probs),
        bring(router_in, router),
        bring(own_in, own),
    ]
    weight_copies = []
    for e in range(expert_count):
        for p in range(steps):
            flat = slice(e * hidden_width + p * FE_STEP, e * hidden_width + (p + 1) * FE_STEP)
            rows_copies = [
                bring(gate_in.at[rows_here, flat], gates.at[:, flat]),
                bring(up_in.at[rows_here, flat], ups.at[:, flat]),
            ]
            gate_up_copies, down_copies = bring_expert_weights(
                bring, ctx_ref, refs[:weight_total], w_gate_up_here, w_down_here, e, p, True
            )
            weight_copies.append((rows_copies + down_copies, gate_up_copies))
    outgoing = []

    def send(source, target):
        copy = pltpu.make_async_copy(source, target, out_sems.at[len(outgoing)])
        copy.start()
        outgoing.append(copy)

    for copy in first_copies:
        copy.wait()
    grads[...] = sent[:, :width]
    mean = sent[:, width : width + 1].astype(jnp.float32) + sent[:, width + 1 : width + 2].astype(
        jnp.float32
    )
    send(grads, all_grads.at[rows_here])
    total = jnp.zeros((count, width), jnp.float32)
    grad_logits = jnp.zeros(probs.shape, jnp.float32)
    quarter = hidden_width // 4
    for e in range(expert_count):
        mine = own[e : e + 1, :]
        chosen = jnp.sum(probs[...] * mine, -1, keepdims=True)
        dots = jnp.zeros((count, 1), jnp.float32)
        for p in range(steps):
            for copy in weight_copies[e * steps + p][0]:
                copy.wait()
            lower = slice(p * FE_STEP, (p + 1) * FE_STEP)
            upper = slice(hidden_width + p * FE_STEP, hidden_width + (p + 1) * FE_STEP)
            flat = slice(e * hidden_width + p * FE_STEP, e * hidden_width + (p + 1) * FE_STEP)
            plain = mm(grads[...], w_down_here[e, lower, :], NT)
            gate = gates[:, flat].astype(jnp.float32)
            up = ups[:, flat].astype(jnp.float32)
            sigmoid_gate = jax.nn.sigmoid(gate)
            silu_gate = gate * sigmoid_gate
            hidden = silu_gate * up
            dots = dots + jnp.sum(plain * hidden, -1, keepdims=True)
            hidden = (hidden * chosen).astype(jnp.bfloat16)
            for q in range(FE_STEP // quarter):
                at = p * (FE_STEP // quarter) + q
                if ring:
                    r = ctx_ref[0] ^ at
                    at = jnp.where(r == 1, 2, jnp.where(r == 2, 1, r))
                at = at * expert_count + e
                hiddens[:, pl.ds(pl.multiple_of(at * quarter, quarter), quarter)] = hidden[
                    :, q * quarter : (q + 1) * quarter
                ]
            plain = plain * chosen
            grad_gate = (
                plain * up * sigmoid_gate * (1.0 + gate * (1.0 - sigmoid_gate))
            ).astype(jnp.bfloat16)
            grad_up = (plain * silu_gate).astype(jnp.bfloat16)
            grad_gates[:, flat] = grad_gate
            grad_ups[:, flat] = grad_up
            for copy in weight_copies[e * steps + p][1]:
                copy.wait()
            total = (
                total
                + mm(grad_gate, w_gate_up_here[e, :, lower], NT)
                + mm(grad_up, w_gate_up_here[e, :, upper], NT)
            )
        grad_logits = grad_logits + chosen * (dots - mean) * mine
    send(grad_gates, all_grad_gate.at[rows_here])
    send(grad_ups, all_grad_up.at[rows_here])
    send(hiddens, all_hidden.at[rows_here])
    low_logits = grad_logits.astype(jnp.bfloat16)
    logits[...] = low_logits
    send(logits, all_logits.at[rows_here])
    result[...] = (total + mm(low_logits, router[...], NT)).astype(jnp.bfloat16)
    send(result.at[:block], out_0)
    send(result.at[block:], out_1)
    for copy in outgoing:
        copy.wait()


def experts_backward(
    group, groups, ctx_ref, grads, probs, gate, up, router, own, weights, kept, ring
):
    gate_up_shape, down_shape = expert_shapes(weights)
    expert_count, hidden_width, width = down_shape
    block = grads[0].shape[0]
    count = 2 * block
    flat = expert_count * hidden_width
    low, f32 = jnp.bfloat16, jnp.float32
    inputs = [ctx_ref, *grads, probs, gate, up, router, own, *weights, *kept]
    return pl.pallas_call(
        functools.partial(experts_backward_body, len(weights), ring, group),
        in_specs=[smem()] + [anywhere()] * (7 + len(weights) + len(kept)),
        out_specs=[anywhere()] * 7,
        out_shape=[
            shaped((block, width)),
            shaped((block, width)),
            shaped((groups * count, width)),
            shaped((groups * count, flat)),
            shaped((groups * count, flat)),
            shaped((groups * count, flat)),
            shaped((groups * count, 128)),
        ],
        input_output_aliases={8 + len(weights) + i: 2 + i for i in range(len(kept))},
        scratch_shapes=[
            pltpu.VMEM((count, grads[0].shape[1]), low),
            pltpu.VMEM(gate_up_shape, low),
            pltpu.VMEM(down_shape, low),
            pltpu.VMEM((count, flat), low),
            pltpu.VMEM((count, flat), low),
            pltpu.VMEM((count, 128), f32),
            pltpu.VMEM((count, width), low),
            pltpu.VMEM((count, flat), low),
            pltpu.VMEM((count, flat), low),
            pltpu.VMEM((count, flat), low),
            pltpu.VMEM((count, 128), low),
            pltpu.VMEM(router.shape, low),
            pltpu.VMEM(own.shape, f32),
            pltpu.VMEM((count, width), low),
            pltpu.SemaphoreType.DMA((5 + 10 * flat // FE_STEP + 24 * expert_count,)),
            pltpu.SemaphoreType.DMA((7,)),
        ],
        compiler_params=kernel_params(),
        cost_estimate=expert_cost(count, width, expert_count, hidden_width),
    )(*inputs)


def turn(block, cosine, sine, lane):
    half = HEAD_DIM // 2
    other = jnp.where(
        lane % HEAD_DIM < half, pltpu.roll(block, 128 - half, 1), pltpu.roll(block, half, 1)
    )
    return block * cosine + other * sine


def row_places(ctx, count, axis):
    half = count // 2
    blocks = []
    for r in range(4):
        c = ctx ^ r
        within = lax.broadcasted_iota(jnp.int32, (count, 1) if axis == 0 else (1, count), axis)
        blocks.append(
            jnp.where(within < half, c * half + within, (7 - c) * half + within - half)
        )
    return jnp.concatenate(blocks, axis)


class Copies:
    def __init__(self, sems):
        self.sems, self.all = sems, []

    def start(self, source, target):
        copy = pltpu.make_async_copy(source, target, self.sems.at[len(self.all)])
        copy.start()
        self.all.append(copy)
        return copy

    def wait(self):
        for copy in self.all:
            copy.wait()


def attention_forward_body(
    gain_lane, ctx_ref, rows_0, rows_1, rows_2, rows_3, w_qkv_in, w_out_in, cosine_in, sine_in, small_in, root_in,
    out_0, out_1, out_2, out_3, all_rows, qkv_out, attended_out, logs_out,
    rows, w_qkv, w_out, cosine, sine, small, root, ring_rows, qkv, attended, logs, result, in_sems, out_sems,
):
    sources, outs = (rows_0, rows_1, rows_2, rows_3), (out_0, out_1, out_2, out_3)
    count, width = rows_0.shape
    q_width, total_width = attended.shape[1], qkv.shape[1]
    kv_width = (total_width - q_width) // 2
    group = HEADS // KV_HEADS
    spans = [slice(r * count, (r + 1) * count) for r in range(4)]
    incoming, outgoing = Copies(in_sems), Copies(out_sems)
    first = [incoming.start(w_qkv_in, w_qkv), incoming.start(rows_0, rows.at[spans[0]])]
    tables = [incoming.start(cosine_in, cosine), incoming.start(sine_in, sine)]
    if gain_lane is not None:
        tables.append(incoming.start(small_in, small))
        tables.append(incoming.start(root_in, root))
    later = [incoming.start(sources[r], rows.at[spans[r]]) for r in range(1, 4)]
    last = incoming.start(w_out_in, w_out)
    for copy in first + tables:
        copy.wait()
    part = width // 4
    lane = lax.broadcasted_iota(jnp.int32, (count, 128), 1)
    if gain_lane is not None:
        gain = small[...].astype(jnp.float32).T[gain_lane : gain_lane + 1, :]
    for r in range(4):
        span = spans[r]
        if r:
            later[r - 1].wait()
        if gain_lane is not None:
            value = rows[span, :].astype(jnp.float32)
            rows[span, :] = (value * root[span, :1] * gain).astype(jnp.bfloat16)
        raw = mm(rows[span, :], w_qkv[...])
        for j in range((q_width + kv_width) // 128):
            turned = turn(raw[:, 128 * j : 128 * j + 128], cosine[span, :], sine[span, :], lane)
            if 128 * j < q_width:
                turned = turned * HEAD_DIM ** (-0.5)
            qkv[span, 128 * j : 128 * j + 128] = turned.astype(jnp.bfloat16)
        qkv[span, q_width + kv_width :] = raw[:, q_width + kv_width :].astype(jnp.bfloat16)
        for place, distance in enumerate(RING):
            at = pl.multiple_of((ctx_ref[0] ^ distance) * part, part)
            ring_rows[span, place * part : (place + 1) * part] = rows[span, pl.ds(at, part)]
    outgoing.start(qkv, qkv_out)
    outgoing.start(ring_rows, all_rows)
    visible = row_places(ctx_ref[0], count, 0) >= row_places(ctx_ref[0], count, 1)
    for head in range(q_width // HEAD_DIM):
        at, of = head * HEAD_DIM, (head // group) * HEAD_DIM
        queries = qkv[:, at : at + HEAD_DIM]
        keys = qkv[:, q_width + of : q_width + of + HEAD_DIM]
        values = qkv[:, q_width + kv_width + of : q_width + kv_width + of + HEAD_DIM]
        scores = jnp.where(visible, mm(queries, keys, NT), masked_score)
        top = jnp.max(scores, -1, keepdims=True)
        weights = jnp.exp(scores - top)
        total = jnp.sum(weights, -1, keepdims=True)
        logs[:, head : head + 1] = top + jnp.log(total)
        probs = (weights * (1.0 / total)).astype(jnp.bfloat16)
        attended[:, at : at + HEAD_DIM] = mm(probs, values).astype(jnp.bfloat16)
    outgoing.start(logs, logs_out)
    outgoing.start(attended, attended_out)
    last.wait()
    for r in (1, 3, 0, 2):
        result[spans[r], :] = mm(attended[spans[r], :], w_out[...]).astype(jnp.bfloat16)
        outgoing.start(result.at[spans[r]], outs[r])
    outgoing.wait()


def attention_forward(ctx_ref, rows, w_qkv, w_out, total_width, tables, small, roots, gain_lane):
    count, width = rows[0].shape
    seq = 4 * count
    q_width = w_out.shape[0]
    low, f32 = jnp.bfloat16, jnp.float32
    outs = pl.pallas_call(
        functools.partial(attention_forward_body, gain_lane),
        in_specs=[smem()] + [anywhere()] * 10,
        out_specs=[anywhere()] * 8,
        out_shape=[shaped((count, width))] * 4
        + [
            shaped((seq, width)),
            shaped((seq, total_width)),
            shaped((seq, q_width)),
            shaped((seq, 128), f32),
        ],
        scratch_shapes=[
            pltpu.VMEM((seq, width), low),
            pltpu.VMEM(w_qkv.shape, low),
            pltpu.VMEM(w_out.shape, low),
            pltpu.VMEM((seq, 128), f32),
            pltpu.VMEM((seq, 128), f32),
            pltpu.VMEM(small.shape, low),
            pltpu.VMEM(roots.shape, f32),
            pltpu.VMEM((seq, width), low),
            pltpu.VMEM((seq, total_width), low),
            pltpu.VMEM((seq, q_width), low),
            pltpu.VMEM((seq, 128), f32),
            pltpu.VMEM((seq, width), low),
            pltpu.SemaphoreType.DMA((10,)),
            pltpu.SemaphoreType.DMA((8,)),
        ],
        compiler_params=kernel_params(),
        cost_estimate=pl.CostEstimate(
            flops=2 * seq * width * (total_width + q_width) + 4 * seq * seq * q_width,
            bytes_accessed=2 * (seq * width * 2 + width * (total_width + q_width)),
            transcendentals=seq * seq * (q_width // HEAD_DIM),
        ),
    )(ctx_ref, *rows, w_qkv, w_out, *tables, small, roots)
    return outs[:4], outs[4], outs[5], outs[6], outs[7]


def attention_backward_body(
    ctx_ref, grad_0, grad_1, grad_2, grad_3, rows_in, w_qkv_in, w_out_in, qkv_in, logs_in,
    cosine_in, sine_in,
    out_0, out_1, out_2, out_3, all_grads, grad_qkv_out, gain_out,
    grads, rows, w_qkv, w_out, qkv, logs, cosine, sine, grad_attended, raw, grad_qkv, gain_sum,
    result, in_sems, out_sems,
):
    sources, outs = (grad_0, grad_1, grad_2, grad_3), (out_0, out_1, out_2, out_3)
    count, width = grad_0.shape
    seq = 4 * count
    q_width, total_width = grad_attended.shape[1], qkv.shape[1]
    kv_width = (total_width - q_width) // 2
    group = HEADS // KV_HEADS
    scale = HEAD_DIM ** (-0.5)
    spans = [slice(r * count, (r + 1) * count) for r in range(4)]
    incoming, outgoing = Copies(in_sems), Copies(out_sems)
    first = [incoming.start(w_out_in, w_out)]
    branches = [incoming.start(sources[r], grads.at[spans[r]]) for r in range(4)]
    second = [incoming.start(qkv_in, qkv), incoming.start(logs_in, logs)]
    last = [
        incoming.start(cosine_in, cosine),
        incoming.start(sine_in, sine),
        incoming.start(w_qkv_in, w_qkv),
        incoming.start(rows_in, rows),
    ]
    first[0].wait()
    for r in range(4):
        branches[r].wait()
        grad_attended[spans[r], :] = mm(grads[spans[r], :], w_out[...], NT).astype(jnp.bfloat16)
    outgoing.start(grads, all_grads)
    for copy in second:
        copy.wait()
    visible = row_places(ctx_ref[0], count, 0) >= row_places(ctx_ref[0], count, 1)
    for kv_head in range(kv_width // HEAD_DIM):
        k_at = q_width + kv_head * HEAD_DIM
        v_at = k_at + kv_width
        keys, values = qkv[:, k_at : k_at + HEAD_DIM], qkv[:, v_at : v_at + HEAD_DIM]
        grad_keys = jnp.zeros((HEAD_DIM, seq), jnp.float32)
        grad_values = jnp.zeros((HEAD_DIM, seq), jnp.float32)
        for head in range(kv_head * group, (kv_head + 1) * group):
            at = head * HEAD_DIM
            queries = qkv[:, at : at + HEAD_DIM]
            grad_head = grad_attended[:, at : at + HEAD_DIM]
            scores = mm(queries, keys, NT)
            probs = jnp.where(visible, jnp.exp(scores - logs[:, head : head + 1]), 0.0)
            grad_values += mm(grad_head.T, probs.astype(jnp.bfloat16))
            weighted = probs * mm(grad_head, values, NT)
            grad_scores = (weighted - probs * jnp.sum(weighted, -1, keepdims=True)).astype(
                jnp.bfloat16
            )
            raw[:, at : at + HEAD_DIM] = mm(grad_scores, keys) * scale
            grad_keys += mm(queries.T, grad_scores)
        raw[:, k_at : k_at + HEAD_DIM] = grad_keys.T
        raw[:, v_at : v_at + HEAD_DIM] = grad_values.T
    for copy in last:
        copy.wait()
    gain_sum[...] = jnp.zeros_like(gain_sum)
    lane = lax.broadcasted_iota(jnp.int32, (count, 128), 1)
    part = width // 4
    for r in (1, 3, 0, 2):
        span = spans[r]
        for j in range((q_width + kv_width) // 128):
            columns = slice(128 * j, 128 * j + 128)
            grad_qkv[span, columns] = turn(
                raw[span, columns], cosine[span, :], -sine[span, :], lane
            ).astype(jnp.bfloat16)
        grad_qkv[span, q_width + kv_width :] = raw[span, q_width + kv_width :].astype(jnp.bfloat16)
        result[span, :] = mm(grad_qkv[span, :], w_qkv[...], NT).astype(jnp.bfloat16)
        outgoing.start(result.at[span], outs[r])
    outgoing.start(grad_qkv, grad_qkv_out)
    for r in range(4):
        span = spans[r]
        for place, distance in enumerate(RING):
            at = pl.multiple_of((ctx_ref[0] ^ distance) * part, part)
            spot = slice(place * part, (place + 1) * part)
            gain_sum[:, spot] += jnp.sum(
                result[span, pl.ds(at, part)].astype(jnp.float32)
                * rows[span, spot].astype(jnp.float32),
                0,
                keepdims=True,
            )
    outgoing.start(gain_sum, gain_out)
    outgoing.wait()


def attention_backward(ctx_ref, grads, rows, w_qkv, w_out, qkv, logs, tables):
    count, width = grads[0].shape
    seq = 4 * count
    q_width, total_width = w_out.shape[0], qkv.shape[1]
    low, f32 = jnp.bfloat16, jnp.float32
    outs = pl.pallas_call(
        attention_backward_body,
        in_specs=[smem()] + [anywhere()] * 11,
        out_specs=[anywhere()] * 7,
        out_shape=[shaped((count, width))] * 4
        + [
            shaped((seq, width)),
            shaped((seq, total_width)),
            shaped((1, width), f32),
        ],
        scratch_shapes=[
            pltpu.VMEM((seq, width), low),
            pltpu.VMEM((seq, width), low),
            pltpu.VMEM(w_qkv.shape, low),
            pltpu.VMEM(w_out.shape, low),
            pltpu.VMEM((seq, total_width), low),
            pltpu.VMEM((seq, 128), f32),
            pltpu.VMEM((seq, 128), f32),
            pltpu.VMEM((seq, 128), f32),
            pltpu.VMEM((seq, q_width), low),
            pltpu.VMEM((seq, total_width), f32),
            pltpu.VMEM((seq, total_width), low),
            pltpu.VMEM((1, width), f32),
            pltpu.VMEM((seq, width), low),
            pltpu.SemaphoreType.DMA((11,)),
            pltpu.SemaphoreType.DMA((7,)),
        ],
        compiler_params=kernel_params(),
        cost_estimate=pl.CostEstimate(
            flops=2 * seq * width * (total_width + q_width) + 10 * seq * seq * q_width,
            bytes_accessed=2 * (seq * width * 3 + width * (total_width + q_width)),
            transcendentals=seq * seq * (q_width // HEAD_DIM),
        ),
    )(ctx_ref, *grads, rows, w_qkv, w_out, qkv, logs, *tables)
    return outs[:4], outs[4], outs[5], outs[6]


def place_body(members, share, total, parts, *refs):
    shards, outs = refs[:total], list(refs[total:])

    def rows_of(r, c, columns):
        if r < 7 or total == 8:
            return shards[r][c, :, columns]
        return shards[7 + c // 2][c % 2, :, columns]

    for first, front, rest in parts:
        out = outs.pop(0)
        for r in range(8):
            for c in range(4):
                out[members[8 + c], members[r]] = rows_of(r, c, slice(first, first + front))
        if not rest:
            continue
        out = outs.pop(0)
        for r in range(8):
            span = pl.ds(pl.multiple_of(members[r] * share, share), share)
            for j in range(4):
                out[span, j * rest : (j + 1) * rest] = rows_of(
                    r, j, slice(first + front, first + front + rest)
                )


def place(members, shards, parts):
    four, share, width = shards[0].shape
    outs = []
    for _, front, rest in parts:
        outs.append(shaped((four, 8, share, front)))
        if rest:
            outs.append(shaped((8 * share, four * rest)))
    return pl.pallas_call(
        lambda members_ref, *refs: place_body(members_ref, share, len(shards), parts, *refs),
        in_specs=[smem()] + [vmem()] * len(shards),
        out_shape=outs,
        compiler_params=kernel_params(),
    )(members, *shards)


def turned(block):
    return block.astype(jnp.float32).T.astype(jnp.bfloat16)


def weight_blocks_body(members, w_query, w_key_value, w_router, gains, *outs):
    layers, share, q_width = w_query.shape
    kv_width = w_key_value.shape[2] // 2
    q_part, kv_part = q_width // 4, kv_width // 4
    experts = w_router.shape[1]
    small = outs[0].shape[1] - 128
    for r in range(4):
        c = members[8 + r]
        outs[r][:, small:] = jnp.zeros((share, 128), jnp.bfloat16)
        for i in range(layers):
            at = i * (q_part + 2 * kv_part)
            outs[r][:, at : at + q_part] = w_query[
                i, :, pl.ds(pl.multiple_of(c * q_part, q_part), q_part)
            ]
            for side in range(2):
                to = at + q_part + side * kv_part
                outs[r][:, to : to + kv_part] = w_key_value[
                    i, :, pl.ds(pl.multiple_of(side * kv_width + c * kv_part, kv_part), kv_part)
                ]
            at = small + i * experts
            outs[r][:, at : at + experts] = turned(w_router[i])
            at = small + layers * experts + 2 * i
            outs[r][:, at : at + 2] = turned(gains[i])


def weight_blocks(members, w_query, w_key_value, w_router, gains):
    layers, share, q_width = w_query.shape
    block = shaped((share, layers * (q_width + w_key_value.shape[2]) // 4 + 128))
    return pl.pallas_call(
        weight_blocks_body,
        in_specs=[smem()] + [vmem()] * 4,
        out_shape=[block] * 4,
        compiler_params=kernel_params(),
    )(members, w_query, w_key_value, w_router, gains)


def pack_shards_body(front, block_0, block_1, block_2, block_3, w_output, ids, shard):
    blocks = (block_0, block_1, block_2, block_3)
    layers, share, width = w_output.shape
    part = front + width // 4
    top, count = ids.shape[1:]
    for r in range(4):
        span = slice(r * share, (r + 1) * share)
        for i in range(layers):
            shard[span, i * part : i * part + front] = blocks[r][:, i * front : (i + 1) * front]
            shard[span, i * part + front : (i + 1) * part] = w_output[
                i, :, r * (width // 4) : (r + 1) * (width // 4)
            ]
        shard[span, layers * part :] = blocks[r][:, layers * front :]
    for i in range(layers):
        at = layers * part + 64 + top * i
        shard[:count, at : at + top] = turned(ids[i])


def pack_shards(blocks, w_output, ids, front):
    layers, share, width = w_output.shape
    return pl.pallas_call(
        functools.partial(pack_shards_body, front),
        in_specs=[vmem()] * 6,
        out_shape=shaped((4 * share, layers * (front + width // 4) + 128)),
        compiler_params=kernel_params(),
    )(*blocks, w_output, ids)


def pack_grads_body(members, qkv, small, out, *parts):
    front, lanes = qkv.shape[3], small.shape[3]
    q_part = out.shape[1] // 4
    share = qkv.shape[2]
    for r in range(8):
        m = members[r]
        part = parts[r] if len(parts) > 1 else parts[0].at[r]
        for place, distance in enumerate(RING):
            part[distance, :, :front] = qkv[place, m]
            part[distance, :, front : front + lanes] = small[place, m]
        for j in range(4):
            part[j, :, front + lanes :] = out[
                pl.ds(pl.multiple_of(m * share, share), share), j * q_part : (j + 1) * q_part
            ]


def pack_grads(members, qkv, small, out, apart):
    four, eight, share, front = qkv.shape
    shape = (four, share, front + small.shape[3] + out.shape[1] // 4)
    return pl.pallas_call(
        pack_grads_body,
        in_specs=[smem()] + [vmem()] * 3,
        out_shape=[shaped(shape)] * 8 if apart else [shaped((eight, *shape))],
        compiler_params=kernel_params(),
    )(members, qkv, small, out)


def finish_attention_body(layers, members, *refs):
    blocks, outs = refs[: 5 * layers], refs[5 * layers :]
    query, key_value, output, router, gains = outs
    experts, lane_count = router.shape[1], layers * router.shape[1]
    q_part, kv_part = query.shape[2] // 4, key_value.shape[2] // 8
    front = q_part + 2 * kv_part
    kv_width = 4 * kv_part
    for i in range(layers):
        lanes = jnp.zeros((query.shape[1], 128), jnp.float32)
        for r in range(4):
            c = members[8 + r]
            block = blocks[5 * i + r]
            query[i, :, pl.ds(pl.multiple_of(c * q_part, q_part), q_part)] = block[
                :, :q_part
            ].astype(jnp.float32)
            for side in range(2):
                at = pl.multiple_of(side * kv_width + c * kv_part, kv_part)
                key_value[i, :, pl.ds(at, kv_part)] = block[
                    :, q_part + side * kv_part : q_part + (side + 1) * kv_part
                ].astype(jnp.float32)
            lanes = lanes + block[:, front:].astype(jnp.float32)
        lanes = lanes.T
        router[i] = lanes[i * experts : (i + 1) * experts, :]
        gains[i] = lanes[lane_count : lane_count + 2, :]
        own = blocks[5 * i + 4]
        for j in range(4):
            output[i, :, j * q_part : (j + 1) * q_part] = own[j].astype(jnp.float32)


def finish_attention(members, layers, expert_total):
    share, q_part = layers[0][4].shape[1:]
    front = layers[0][0].shape[1] - 128
    total = len(layers)
    f32 = jnp.float32
    return pl.pallas_call(
        functools.partial(finish_attention_body, total),
        in_specs=[smem()] + [vmem()] * (5 * total),
        out_shape=[
            shaped((total, share, 4 * q_part), f32),
            shaped((total, share, 4 * (front - q_part)), f32),
            shaped((total, share, 4 * q_part), f32),
            shaped((total, expert_total, share), f32),
            shaped((total, 2, share), f32),
        ],
        compiler_params=kernel_params(),
    )(members, *[block for layer in layers for block in layer])


def finish_experts_body(down_total, *refs):
    gate_up, down = refs[-2:]
    half = gate_up.shape[3] // 2

    def total(first, count):
        values = [ref[...].astype(jnp.float32) for ref in refs[first : first + count]]
        return sum(values[1:], values[0])

    gate_up[0, 0, :, :half] = total(0, 2)
    gate_up[0, 0, :, half:] = total(2, 2)
    down[0, 0] = total(4, down_total)


def finish_experts(layer, layers, experts, held, sent, kept):
    rows, flat = held[0].shape
    half = flat // experts
    down_rows, width = held[2].shape[0] // experts, held[2].shape[1]
    gate_spec = pl.BlockSpec((rows, half), lambda e: (0, e))
    down_spec = pl.BlockSpec((down_rows, width), lambda e: (e, 0))
    downs = [part for part in (held[2], sent[2]) if part is not None]
    inputs = [held[0], sent[0], held[1], sent[1], *downs]
    return pl.pallas_call(
        functools.partial(finish_experts_body, len(downs)),
        grid=(experts,),
        in_specs=[gate_spec] * 4 + [down_spec] * len(downs) + [anywhere()] * len(kept),
        out_specs=[
            pl.BlockSpec((1, 1, rows, 2 * half), lambda e: (layer, e, 0, 0)),
            pl.BlockSpec((1, 1, down_rows, width), lambda e: (layer, e, 0, 0)),
        ],
        out_shape=[
            shaped((layers, experts, rows, 2 * half), jnp.float32),
            shaped((layers, experts, down_rows, width), jnp.float32),
        ],
        input_output_aliases={len(inputs) + i: i for i in range(len(kept))},
        compiler_params=kernel_params(),
    )(*inputs, *kept)


def rotate_ranks(values_in, axis_name, total, target_of):
    return lax.ppermute(values_in, axis_name, [(i, target_of(i)) for i in range(total)])


def swap_y(values_in):
    return rotate_ranks(values_in, "fsdp", 8, lambda i: i ^ 1)


def move_z(values_in, steps):
    return rotate_ranks(values_in, "fsdp", 8, lambda i: (i + 2 * steps) % 8)


def swap_core(values_in):
    return rotate_ranks(values_in, "ctx", 4, lambda i: i ^ 1)


def swap_x(values_in):
    return rotate_ranks(values_in, "ctx", 4, lambda i: i ^ 2)


def swap_both(values_in):
    return rotate_ranks(values_in, "ctx", 4, lambda i: i ^ 3)


def to_members(blocks):
    return [blocks[0], swap_core(blocks[1]), swap_x(blocks[2]), swap_both(blocks[3])]


def after(value, *others):
    return lax.optimization_barrier((value, *others))[0]


def wide(value):
    return value.astype(jnp.float32)


def fsdp_members(index):
    z, y = index // 2, index % 2
    return [((z + dz) % 4) * 2 + (y ^ dy) for dz in (0, 3, 2, 1) for dy in (0, 1)]


def gather_fsdp(block, work=None, beside=()):
    below = move_z(block, 1)
    own_mirror = swap_y(block)
    if work is None:
        below, own_mirror = after(below, own_mirror, beside[0]), after(own_mirror, below)
        far = move_z(below, 1)
        below_mirror = swap_y(after(below, own_mirror))
        far = after(far, below_mirror, beside[1])
        above = move_z(after(block, far), -1)
        far_mirror = swap_y(far)
        above = after(above, far_mirror, beside[2])
        half = block.shape[0] // 2
        above_mirrors = [swap_y(above[:half]), move_z(after(own_mirror, above)[half:], -1)]
        return [block, own_mirror, below, below_mirror, far, far_mirror, above, *above_mirrors]
    far = move_z(below, 1)
    below_mirror = swap_y(below)
    done = work(0, (after(block, below), own_mirror))
    above = move_z(after(block, far, done), -1)
    far_mirror = swap_y(after(far, done))
    done = work(1, (after(below, far), below_mirror))
    above_mirror = swap_y(after(above, done))
    work(2, (after(far, above), far_mirror))
    work(3, (above, above_mirror))
    return above_mirror


def scatter_fsdp(parts, beside=None, start=None, middle=None, late=None):
    low = jnp.bfloat16
    results = []

    def run(start):
        if beside:
            results.append(beside[len(results)](start))
            return jax.tree.leaves(results[-1])
        return []

    def held(value, *others):
        return after(value, *[other for other in others if other is not None])

    far = (wide(parts[4]) + wide(swap_y(held(parts[5], start)))).astype(low)
    from_far = move_z(far, 1)
    above_mirror = swap_y(held(parts[7], start))
    done = run(far)
    above = (wide(parts[6]) + wide(above_mirror) + wide(from_far)).astype(low)
    above = held(above, middle)
    from_below = move_z(above, 1)
    below_mirror = swap_y(after(parts[3], above))
    later = run(above)
    below = held((wide(parts[2]) + wide(below_mirror)).astype(low), late)
    from_above = move_z(after(below, *done), -1)
    own_mirror = swap_y(after(parts[1], below))
    done = later + run(below)
    own = wide(parts[0]) + wide(own_mirror) + wide(from_below)
    return after(own, *done) + wide(from_above), results, below


def gather_ctx(block):
    across = swap_x(block)
    return [block, swap_core(block), across, swap_core(across)]


def scatter_ctx(parts, beside=()):
    across = wide(parts[2]) + wide(swap_core(parts[3]))
    own = wide(parts[0]) + wide(swap_core(parts[1]))
    across = swap_x(across.astype(jnp.bfloat16))
    return own + wide(after(across, *beside))


def split_ranks(
    hidden_in,
    w_query,
    w_key_value,
    w_output,
    w_router,
    norm_gains,
    w_gate_up,
    w_down,
    expert_ids,
    out_grad,
):
    both = ("ctx", "fsdp")
    ctx_total, groups = 4, 8
    ctx_index, group_index = lax.axis_index("ctx"), lax.axis_index("fsdp")
    row_count, model_width = hidden_in.shape[1], hidden_in.shape[2]
    layer_total, share, _ = w_query.shape
    experts_here = w_gate_up.shape[1]
    expert_total = experts_here * groups
    kv_width = w_key_value.shape[2] // 2
    q_part, kv_part = model_width // ctx_total, kv_width // ctx_total
    qkv_part = q_part + 2 * kv_part
    pair_total = groups // 2
    low = jnp.bfloat16
    f32 = jnp.float32

    def dot_tn(a, b):
        return mm(a, b, TN)

    ctx_members = [ctx_index ^ r for r in range(ctx_total)]
    members = jnp.stack([*fsdp_members(group_index), *ctx_members]).astype(jnp.int32)
    natural_members = jnp.stack([*range(groups), *ctx_members]).astype(jnp.int32)
    ring_members = jnp.stack([ctx_members[r] for r in RING])
    ctx_ref = ctx_index.reshape(1).astype(jnp.int32)
    expert_lane = jnp.arange(128, dtype=jnp.int32)
    own_experts = [
        (
            expert_lane[None, :]
            == expert_total * i
            + group_index * experts_here
            + jnp.arange(8, dtype=jnp.int32)[:, None]
        ).astype(f32)
        for i in range(layer_total)
    ]
    gain_lane = expert_total * layer_total

    def ring(vector):
        return jnp.take(vector.reshape(ctx_total, -1), ring_members, axis=0).reshape(-1)

    places = jnp.concatenate(
        [row_positions((ctx_index ^ r) * row_count, row_count, row_count, ctx_total) for r in range(4)]
    )
    half_dim = HEAD_DIM // 2
    frequency = rope_base ** (-jnp.arange(half_dim, dtype=f32) / half_dim)
    angles = places.astype(f32)[:, None] * frequency[None, :]
    cosine, sine = jnp.cos(angles), jnp.sin(angles)
    tables = (
        jnp.concatenate([cosine] * 4, -1),
        jnp.concatenate([-sine, sine, -sine, sine], -1),
    )

    blocks = to_members(
        weight_blocks(
            members, w_query, w_key_value, w_router.transpose(0, 2, 1), norm_gains.transpose(0, 2, 1)
        )
    )
    packed = pack_shards(
        blocks,
        w_output,
        expert_ids.reshape(layer_total, row_count, TOP).transpose(0, 2, 1),
        qkv_part,
    )
    expert_weights, start = [[]], packed
    for part in [*(w_gate_up[0, e] for e in range(experts_here)), w_down[0]]:
        expert_weights[0].extend(gather_ctx(after(part, start)))
        start = expert_weights[0][-2]
    hidden_rows = gather_ctx(
        after(hidden_in.reshape(row_count, model_width), expert_weights[0][6])
    )
    hidden_roots = jnp.concatenate(
        [
            jnp.broadcast_to(rms_scaled(wide(block), 1.0)[1], (row_count, 128))
            for block in hidden_rows
        ],
        0,
    )
    joined = join_experts(after(w_gate_up[1], hidden_rows[1]), w_down[1])
    flat_shards = gather_fsdp(
        packed,
        None,
        [expert_weights[0][2], expert_weights[0][6], after(hidden_roots, joined)],
    )
    shards = [shard.reshape(-1, share, shard.shape[1]) for shard in flat_shards]
    flat_shards[7:] = [jnp.concatenate(flat_shards[7:], 0)]
    layer_part = qkv_part + q_part
    ready = after(shards[0], *expert_weights[0])
    small, qkv_weight, out_weight = place(
        members,
        [ready, *shards[1:]],
        [(layer_total * layer_part, 128, 0), (0, qkv_part, q_part)],
    )
    small = small.reshape(model_width, 128)
    attention_weights = [(qkv_weight.reshape(model_width, qkv_part), out_weight)]
    gains = [
        wide(small[:, gain_lane + 2 * i : gain_lane + 2 * i + 2]).T for i in range(layer_total)
    ]
    ring_gains = [ring(gains[i][0]) for i in range(layer_total)]

    def place_layer(i, start):
        qkv_weight, out_weight = place(
            members,
            [after(shards[0], start), *shards[1:]],
            [(i * layer_part, qkv_part, q_part)],
        )
        return qkv_weight.reshape(model_width, qkv_part), out_weight

    residual = wide(hidden_in.reshape(row_count, model_width))
    saved = []
    for i in range(layer_total):
        qkv_weight, out_weight = attention_weights[i]
        normed, root_first = rms_scaled(residual, gains[i][0])
        rows = hidden_rows if i == 0 else gather_ctx(normed.astype(low))
        branch, rows_first, qkv, attended, logs = attention_forward(
            ctx_ref, rows, qkv_weight, out_weight, qkv_part, tables, small,
            hidden_roots, gain_lane if i == 0 else None,
        )
        middle = residual + scatter_ctx(branch)
        normed_second, root_second = rms_scaled(middle, gains[i][1])
        parts, kept = [None] * groups, []

        def forward_work(group, pair):
            outs = experts_forward(
                group, pair_total, ctx_ref, pair, flat_shards[2 * group : 2 * group + 2],
                64 + TOP * i, expert_total * i, small,
                own_experts[i], expert_weights[i], kept,
            )
            parts[2 * group], parts[2 * group + 1] = outs[:2]
            kept[:] = outs[2:]
            return outs[0]

        normed_second = normed_second.astype(low)
        beside = None
        if i == 0:
            joined = after(joined, middle)
            expert_weights.append([lax.all_gather(joined, "ctx", axis=1, tiled=True)])
            beside = (lambda start: [], lambda start: place_layer(1, start), lambda start: [])
        last = gather_fsdp(normed_second, forward_work)
        rows_second, gate, up, probs = kept
        expert_sum, placed, _ = scatter_fsdp(parts, beside, last)
        if beside:
            attention_weights.append(placed[1])
        saved.append(
            (
                residual, root_first, rows_first, qkv, attended, logs,
                middle, root_second, rows_second, gate, up, probs, expert_sum,
            )
        )
        residual = middle + expert_sum
    hidden_out = residual.reshape(1, row_count, model_width).astype(low)
    grad = wide(out_grad.reshape(row_count, model_width))
    expert_grads = []

    def add_core(start, pairs, came):
        sums = [
            (dot_tn(after(part, start)[:, :half], grads) + wide(other)).astype(low)
            for (part, half, grads), other in zip(pairs, came, strict=True)
        ]
        return [(part[: part.shape[0] // 2], part[part.shape[0] // 2 :]) for part in sums]

    def finish_layer(i, pairs, start, kept):
        held, sent = [pair[0] for pair in pairs], [pair[1] for pair in pairs]
        held[0] = after(held[0], start)
        return finish_experts(i, layer_total, experts_here, held, sent, kept)

    for i in reversed(range(layer_total)):
        (
            residual, root_first, rows_first, qkv, attended, logs,
            middle, root_second, rows_second, gate, up, probs, expert_sum,
        ) = saved[i]
        qkv_weight, out_weight = attention_weights[i]
        mean_gate = jnp.sum(grad * expert_sum, -1, keepdims=True)
        mean_high = mean_gate.astype(low)
        mean_low = (mean_gate - wide(mean_high)).astype(low)
        lanes = jnp.where(expert_lane == 0, mean_high, jnp.where(expert_lane == 1, mean_low, 0))
        sent = jnp.concatenate([grad.astype(low), lanes.astype(low)], -1)
        parts, kept = [None] * groups, []
        if i == 0:
            whole_down = dot_tn(after(upper_hidden, sent), upper_grads).astype(low)
            halves = add_core(sent, *pending)
            upper_down = lax.psum_scatter(
                whole_down.reshape(ctx_total, -1, model_width), "ctx", scatter_dimension=0, tiled=True
            )
            upper_down = (upper_down.reshape(-1, model_width), None)
            expert_grads.insert(0, [(half[0], swap_x(half[1])) for half in halves] + [upper_down])

        def backward_work(group, pair):
            if i == 0 and group == 0:
                pair = (after(pair[0], whole_down, *jax.tree.leaves(halves)), pair[1])
            if i == 0 and group > 1:
                pair = (after(pair[0], expert_grads[0][group - 2][1]), pair[1])
            outs = experts_backward(
                group, pair_total, ctx_ref, pair, probs, gate, up, small, own_experts[i],
                expert_weights[i], kept, i == 0,
            )
            parts[2 * group], parts[2 * group + 1] = outs[:2]
            kept[:] = outs[2:]
            return outs[0]

        last = gather_fsdp(sent, backward_work)
        grads_second, grad_gate, grad_up, hidden, grad_logits = kept
        half_width, half_hidden = model_width // 2, hidden.shape[1] // 2

        came = []
        pairs = [(rows_second, half_width, grad_gate), (rows_second, half_width, grad_up)]
        if i == 0:
            pairs.append((hidden, half_hidden, grads_second))

        def first_beside(start):
            for part, half, grads in pairs:
                came.append(swap_core(dot_tn(after(part, start)[:, half:], grads).astype(low)))
            return came

        grad_second, small_grads, _ = scatter_fsdp(
            parts,
            (
                first_beside,
                lambda start: dot_tn(after(rows_second, start), grad_logits),
                lambda start: [],
            ),
            last,
        )
        small_grads = small_grads[1]
        grad_middle, gain_second = rms_back(middle, root_second, gains[i][1], grad_second)
        grad_middle = grad_middle + grad
        branch_rows = grad_middle.astype(low)
        branch_grads = gather_ctx(branch_rows)
        if i > 0:
            pending = pairs, came
            upper_hidden, upper_grads = hidden, grads_second
        back, rows_branch, grad_qkv, gain_first = attention_backward(
            ctx_ref, branch_grads, rows_first, qkv_weight, out_weight, qkv,
            logs, tables,
        )
        gain_first = gain_first[0] / ring_gains[i]
        gain_second = ring(after(gain_second, back[0]))
        small_grads = jnp.where(
            expert_lane == gain_lane,
            gain_first[:, None],
            jnp.where(expert_lane == gain_lane + 1, gain_second[:, None], small_grads),
        ).astype(low)
        if i == 0:
            far = (wide(packs[4]) + wide(swap_y(after(packs[5], grad_second)))).astype(low)
            above_mirror, from_far = swap_y(after(packs[7], grad_second)), move_z(far, 1)
            above = (wide(packs[6]) + wide(above_mirror) + wide(from_far)).astype(low)
            above = after(above, back[0])
            from_below, below_mirror = move_z(above, 1), swap_y(after(packs[3], above))
            rows_first = after(rows_first, above)
        qkv_grads = dot_tn(rows_first, grad_qkv).astype(low)
        out_grads = dot_tn(attended, rows_branch).astype(low)
        layer_packs = pack_grads(
            members,
            qkv_grads.reshape(ctx_total, groups, share, qkv_part),
            small_grads.reshape(ctx_total, groups, share, 128),
            out_grads,
            True,
        )
        flat_packs = [pack.reshape(ctx_total * share, -1) for pack in layer_packs]
        if i == 0:
            below = after((wide(packs[2]) + wide(below_mirror)).astype(low), layer_packs[0])
            from_above, own_mirror = move_z(below, -1), swap_y(after(packs[1], below))
            upper = wide(packs[0]) + wide(own_mirror) + wide(from_below) + wide(from_above)
            halves = add_core(below, pairs[:1], came[:1])
            crossed = [swap_x(halves[0][1])]

            def second_beside(start):
                halves.extend(add_core(start, pairs[1:], came[1:]))
                crossed.extend(swap_x(half[1]) for half in halves[1:])
                return finish_layer(1, expert_grads[0], start, []), halves

            beside = [
                second_beside,
                lambda start: crossed[0],
                lambda start: crossed[1],
            ]
            lower, finished, _ = scatter_fsdp(flat_packs, beside, below, None, upper)
            expert_grads.insert(
                0, [(half[0], other) for half, other in zip(halves, crossed, strict=True)]
            )
            attention_grads = [lower, upper]
            layer_packs = [upper]
        grad_first = scatter_ctx(back, layer_packs)
        grad_input, _ = rms_back(residual, root_first, gains[i][0], grad_first)
        grad = grad_input + grad_middle
        packs = flat_packs
    attention_grads = [
        part.astype(low).reshape(ctx_total, share, -1) for part in attention_grads
    ]
    front = qkv_part + 128
    blocks = to_members(
        [jnp.concatenate([part[r, :, :front] for part in attention_grads], -1) for r in range(ctx_total)]
    )
    query_out, key_value_out, output_out, router_out, gains_out = finish_attention(
        members,
        [
            [block[:, i * front : (i + 1) * front] for block in blocks] + [part[..., front:]]
            for i, part in enumerate(attention_grads)
        ],
        expert_total,
    )
    outs = finish_layer(0, expert_grads[0], attention_grads[0], finished[0][0])
    return (
        hidden_out,
        grad.reshape(1, row_count, model_width),
        query_out,
        key_value_out,
        output_out,
        router_out.transpose(0, 2, 1),
        gains_out.transpose(0, 2, 1),
        outs[0],
        outs[1],
    )


def solution(mesh):
    split = mesh.shape["ctx"] == 4 and mesh.shape["fsdp"] == 8
    return jax.shard_map(
        split_ranks if split else on_device,
        mesh=mesh,
        in_specs=(
            P("fsdp", "ctx", None),
            P(None, ("ctx", "fsdp"), None),
            P(None, ("ctx", "fsdp"), None),
            P(None, ("ctx", "fsdp"), None),
            P(None, ("ctx", "fsdp"), None),
            P(None, ("ctx", "fsdp"), None),
            P(None, "fsdp", "ctx", None),
            P(None, "fsdp", "ctx", None),
            P(None, "fsdp", "ctx", None),
            P("fsdp", "ctx", None),
        ),
        out_specs=(
            P("fsdp", "ctx", None),
            P("fsdp", "ctx", None),
            P(None, ("ctx", "fsdp"), None),
            P(None, ("ctx", "fsdp"), None),
            P(None, ("ctx", "fsdp"), None),
            P(None, ("ctx", "fsdp"), None),
            P(None, ("ctx", "fsdp"), None),
            P(None, "fsdp", "ctx", None),
            P(None, "fsdp", "ctx", None),
        ),
        check_vma=False,
    )
```
